32 devices in a mesh: dp: 8 (over z, y), context: 4 (over x, core).
Axes of the slice: x: 2, y: 2, z: 4, core: 2. Of those that a mesh axis runs over, the one named last changes fastest.
Arguments:
- tokens: bfloat16 [64, 512, 768], P('dp', 'context'), may hold values from -6 to 6
- cotangent: float32 [64, 512, 768], P('dp', 'context'), may hold values from -6 to 6
- lengths: int32 [64], P('dp'), may hold values from 1 to 512, as said below
- attention_weights: float32 [4, 768, 768], P(None, ('dp', 'context')), may hold values from -0.21875 to 0.21875
- inner_weights: float32 [768, 3072], P(('dp', 'context')), may hold values from -0.21875 to 0.21875
- outer_weights: float32 [3072, 768], P(('dp', 'context')), may hold values from -0.109375 to 0.109375
- inner_bias: float32 [3072], P(('dp', 'context')), may hold values from -3 to 3
- vectors: float32 [8, 768], P(None, ('dp', 'context')), may hold values from -3 to 3, as said below
- attention_first: float32 [4, 768, 768], P(None, ('dp', 'context')), may hold values from -24 to 24
- attention_second: float32 [4, 768, 768], P(None, ('dp', 'context')), may hold values from 1.31072 to 5.24288
- inner_first: float32 [768, 3072], P(('dp', 'context')), may hold values from -56 to 56
- inner_second: float32 [768, 3072], P(('dp', 'context')), may hold values from 6.5536 to 26.2144
- outer_moment_first: float32 [3072, 768], P(('dp', 'context')), may hold values from -64 to 64
- outer_second: float32 [3072, 768], P(('dp', 'context')), may hold values from 9.8304 to 39.3216
- bias_first: float32 [3072], P(('dp', 'context')), may hold values from -48 to 48
- bias_second: float32 [3072], P(('dp', 'context')), may hold values from 5.24288 to 20.97152
- vector_first: float32 [8, 768], P(None, ('dp', 'context')), may hold values from -80 to 80
- vector_second: float32 [8, 768], P(None, ('dp', 'context')), may hold values from 16.384 to 65.536
Outputs:
- output_tokens: bfloat16 [64, 512, 768], P('dp', 'context')
- input_grad: float32 [64, 512, 768], P('dp', 'context')
- attention_grad: float32 [4, 768, 768], P(None, ('dp', 'context'))
- attention_square: float32 [4, 768, 768], P(None, ('dp', 'context'))
- attention_new: float32 [4, 768, 768], P(None, ('dp', 'context'))
- inner_grad: float32 [768, 3072], P(('dp', 'context'))
- inner_square: float32 [768, 3072], P(('dp', 'context'))
- inner_new: float32 [768, 3072], P(('dp', 'context'))
- outer_grad: float32 [3072, 768], P(('dp', 'context'))
- outer_square: float32 [3072, 768], P(('dp', 'context'))
- outer_new: float32 [3072, 768], P(('dp', 'context'))
- bias_grad: float32 [3072], P(('dp', 'context'))
- bias_square: float32 [3072], P(('dp', 'context'))
- bias_new: float32 [3072], P(('dp', 'context'))
- vector_grad: float32 [8, 768], P(None, ('dp', 'context'))
- vector_square: float32 [8, 768], P(None, ('dp', 'context'))
- vector_new: float32 [8, 768], P(None, ('dp', 'context'))
The draws below stay inside these ranges and needn't reach their ends.
Inputs may be any that keep to these rules, and one draw needn't show every extreme that they name: `lengths`: among the 8 sequences of each index of dp, at least one has length 512. `vectors`: norm gains (rows 4 and 6) lie in 0.5 to 1.5.
All inputs are finite; a program needn't handle non-finite values.
Results may differ from the reference program's by a relative error of at most 0.012.
The reference program's roundings to bfloat16 on the way count: a program that leaves them out, or rounds other values in their place, can miss the bound.
Values may be sent and summed in bfloat16 or wider, within the bound.
No kernel may reach another device: no remote copies, remote signals or barrier semaphores. Data moves between devices by JAX's collectives and lax.ppermute only.
A program may use at most 192 MiB of HBM per device.

```python
import math
import jax
import jax.numpy as jnp
from jax import lax

D = 768
HEADS = 12
HEAD = 64
FF = 3072
LEN = 512
SEQ_DEV = 8
STEP = 10
SEQS = 64


def draw_lengths(key, part):
    key = jax.random.fold_in(key, 11)
    length_key, choose_key = jax.random.split(key)
    draw_rows = jax.random.randint(length_key, (SEQS,), 1, LEN + 1, jnp.int32)
    groups = draw_rows.reshape(SEQS // SEQ_DEV, SEQ_DEV)
    chosen = jax.random.randint(choose_key, (SEQS // SEQ_DEV, 1), 0, SEQ_DEV, jnp.int32)
    places = jnp.arange(SEQ_DEV, dtype=jnp.int32)[None, :]
    return jnp.where(places == chosen, LEN, groups).reshape(SEQS).astype(jnp.int32)


def draw_vectors(key, part):
    key = jax.random.fold_in(key, 5)
    bias_key, gain_key = jax.random.split(key)
    biases = jnp.clip(0.5 * jax.random.normal(bias_key, (8, D), jnp.float32), -3.0, 3.0)
    gain_rows = jax.random.uniform(gain_key, (8, D), jnp.float32, 0.5, 1.5)
    row_index = jnp.arange(8, dtype=jnp.int32)[:, None]
    return jnp.where((row_index == 4) | (row_index == 6), gain_rows, biases)


def levels(own_key, dims, cuts, low, high):
    gain = 1.0
    for dim, blocks in cuts:
        heights = jax.random.uniform(jax.random.fold_in(jax.random.fold_in(own_key, 6), dim), (blocks,), jnp.float32, low / len(cuts), high / len(cuts))
        gain = gain * jnp.repeat(jnp.exp(heights), dims[dim] // blocks).reshape((-1,) + (1,) * (len(dims) - 1 - dim))
    return gain


def gaussian(key, shape, spread, limit, cuts=(), kind=jnp.bfloat16):
    array = spread * jax.random.normal(key, shape, jnp.float32)
    if cuts:
        array = array * levels(key, shape, cuts, -0.22, 0.18)
    return jnp.clip(array, -limit, limit).astype(kind)


def setup_inputs(seed: int = 0) -> dict:
    seeds = jax.random.split(jax.random.key(seed), 19)
    tokens = gaussian(seeds[0], (SEQS, LEN, D), 1.0, 6.0, ((0, 8), (1, 4)))
    cotangent = gaussian(seeds[1], (SEQS, LEN, D), 1.0, 6.0, ((0, 8), (1, 4)), jnp.float32)
    lengths = draw_lengths(jax.random.fold_in(seeds[18], 71), 0)
    attention_weights = gaussian(seeds[3], (4, D, D), D ** -0.5, 0.21875, ((1, 32),), jnp.float32)
    inner_weights = gaussian(seeds[4], (D, FF), D ** -0.5, 0.21875, ((0, 32),), jnp.float32)
    outer_weights = gaussian(seeds[5], (FF, D), FF ** -0.5, 0.109375, ((0, 32),), jnp.float32)
    inner_bias = gaussian(seeds[6], (FF,), 0.5, 3.0, ((0, 32),), jnp.float32)
    vectors = draw_vectors(jax.random.fold_in(seeds[18], 71), 0)
    attention_first = gaussian(seeds[8], (4, D, D), (0.022 * (SEQS * LEN) ** 0.5), 24.0, ((1, 32),), jnp.float32)
    attention_second = jnp.clip(jnp.exp(math.log(5.24288) - 1.3862944 * jax.random.uniform(seeds[9], (4, D, D), jnp.float32) ** levels(seeds[9], (4, D, D), ((1, 32),), -0.2, 0.2)), 1.31072, 5.24288)
    inner_first = gaussian(seeds[10], (D, FF), (0.05 * (SEQS * LEN) ** 0.5), 56.0, ((0, 32),), jnp.float32)
    inner_second = jnp.clip(jnp.exp(math.log(26.2144) - 1.3862944 * jax.random.uniform(seeds[11], (D, FF), jnp.float32) ** levels(seeds[11], (D, FF), ((0, 32),), -0.2, 0.2)), 6.5536, 26.2144)
    outer_moment_first = gaussian(seeds[12], (FF, D), (0.06 * (SEQS * LEN) ** 0.5), 64.0, ((0, 32),), jnp.float32)
    outer_second = jnp.clip(jnp.exp(math.log(39.3216) - 1.3862944 * jax.random.uniform(seeds[13], (FF, D), jnp.float32) ** levels(seeds[13], (FF, D), ((0, 32),), -0.2, 0.2)), 9.8304, 39.3216)
    bias_first = gaussian(seeds[14], (FF,), (0.045 * (SEQS * LEN) ** 0.5), 48.0, ((0, 32),), jnp.float32)
    bias_second = jnp.clip(jnp.exp(math.log(20.97152) - 1.3862944 * jax.random.uniform(seeds[15], (FF,), jnp.float32) ** levels(seeds[15], (FF,), ((0, 32),), -0.2, 0.2)), 5.24288, 20.97152)
    vector_first = gaussian(seeds[16], (8, D), (0.08 * (SEQS * LEN) ** 0.5), 80.0, ((1, 32),), jnp.float32)
    vector_second = jnp.clip(jnp.exp(math.log(65.536) - 1.3862944 * jax.random.uniform(seeds[17], (8, D), jnp.float32) ** levels(seeds[17], (8, D), ((1, 32),), -0.2, 0.2)), 16.384, 65.536)
    return dict(tokens=tokens, cotangent=cotangent, lengths=lengths, attention_weights=attention_weights, inner_weights=inner_weights, outer_weights=outer_weights, inner_bias=inner_bias, vectors=vectors, attention_first=attention_first, attention_second=attention_second, inner_first=inner_first, inner_second=inner_second, outer_moment_first=outer_moment_first, outer_second=outer_second, bias_first=bias_first, bias_second=bias_second, vector_first=vector_first, vector_second=vector_second)


NORM_EPS = 1e-12
BETA_ONE = 0.9
BETA_TWO = 0.999
ADAM_EPS = 1e-06
MATRIX_LEARN_RATE = 0.05
VECTOR_RATE = 0.5
WEIGHT_DECAY = 0.01
MASK_FILL = -1e+30

@jax.custom_vjp
def low(v):
    return lax.optimization_barrier(v.astype(jnp.bfloat16)).astype(jnp.float32)

@jax.custom_vjp
def low_back(v):
    return v

def low_keep(v):
    return (low(v), None)

def low_pass(kept, grad):
    return (grad,)

def back_keep(v):
    return (v, None)

def back_low(kept, grad):
    return (low(grad),)
low.defvjp(low_keep, low_pass)
low_back.defvjp(back_keep, back_low)

def precise_gelu_activation(value_entries):
    return jax.nn.gelu(value_entries, approximate=False)

def normalize(value_entries, gain_row, shift_row):
    centered = value_entries - lax.optimization_barrier(jnp.mean(value_entries, axis=-1, keepdims=True))
    variance = lax.optimization_barrier(jnp.mean(centered * centered, axis=-1, keepdims=True))
    return centered * lax.rsqrt(variance + NORM_EPS) * gain_row + shift_row

def adam_step(weight, gradient, moment_one, moment_two, step_rate, decay_rate):
    first_new = BETA_ONE * moment_one + (1.0 - BETA_ONE) * gradient
    second_new = BETA_TWO * moment_two + (1.0 - BETA_TWO) * gradient * gradient
    first_hat = first_new / (1.0 - BETA_ONE ** STEP)
    second_hat = second_new / (1.0 - BETA_TWO ** STEP)
    updated = weight - step_rate * (first_hat / (jnp.sqrt(second_hat) + ADAM_EPS) + decay_rate * weight)
    return (second_new, updated)

def layer_forward(token_block, attention_weights, inner_weights, outer_weights, inner_bias, vectors, key_valid):
    highest_precision = lax.Precision.HIGHEST
    attention_low = low(attention_weights)
    inner_low = low(inner_weights)
    outer_low = low(outer_weights)
    bias_low = low(inner_bias)
    vector_low = low(vectors)
    seqs_here = token_block.shape[0]

    def project(value_entries, matrix_operand):
        return jnp.einsum('tui,iy->tuy', value_entries, matrix_operand, precision=highest_precision)
    query_rows = low_back(low(project(token_block, attention_low[0]) + vector_low[0]))
    key_rows = low_back(low(project(token_block, attention_low[1])))
    value_rows = low_back(low(project(token_block, attention_low[2]) + vector_low[1]))
    shape_heads = (seqs_here, LEN, HEADS, HEAD)
    scores = jnp.einsum('sqhc,skhc->shqk', query_rows.reshape(shape_heads), key_rows.reshape(shape_heads), precision=highest_precision) * HEAD ** (-0.5)
    scores = low_back(scores)
    masked = jnp.where(key_valid[:, None, None, :], scores, MASK_FILL)
    row_peak = lax.optimization_barrier(jnp.max(masked, axis=-1, keepdims=True))
    exponent = jnp.exp(masked - row_peak)
    attention_probability = exponent / lax.optimization_barrier(jnp.sum(exponent, axis=-1, keepdims=True))
    mixed_rows = jnp.einsum('shqk,skhc->sqhc', low(attention_probability), value_rows.reshape(shape_heads), precision=highest_precision)
    mixed_rows = low_back(low(mixed_rows.reshape(seqs_here, LEN, D)))
    branch = low_back(project(mixed_rows, attention_low[3]) + vector_low[2])
    normed = normalize(token_block + branch, vector_low[4], vector_low[5])
    hidden_pre = low_back(project(low(normed), inner_low) + bias_low)
    activated = low(precise_gelu_activation(hidden_pre))
    ffn_out = low_back(project(activated, outer_low) + vector_low[3])
    return normalize(normed + ffn_out, vector_low[6], vector_low[7])

def reference(tokens, cotangent, lengths, attention_weights, inner_weights, outer_weights, inner_bias, vectors, attention_first, attention_second, inner_first, inner_second, outer_moment_first, outer_second, bias_first, bias_second, vector_first, vector_second):
    per_block = max(1, 4096 // LEN)
    while SEQS % per_block != 0:
        per_block = per_block - 1
    block_count = SEQS // per_block
    token_blocks = tokens.astype(jnp.float32).reshape(block_count, per_block, LEN, D)
    cotangent_blocks = cotangent.astype(jnp.float32).reshape(block_count, per_block, LEN, D)
    length_blocks = lengths.reshape(block_count, per_block)
    params = (attention_weights, inner_weights, outer_weights, inner_bias, vectors)
    positions = jnp.arange(LEN, dtype=jnp.int32)

    def one_block(totals, block_data):
        token_block, cotangent_block, length_block = block_data
        key_valid = positions[None, :] < length_block[:, None]

        def forward_here(inputs, *weights):
            return layer_forward(inputs, *weights, key_valid)
        result, pullback = jax.vjp(forward_here, token_block, *params)
        gradients = pullback(cotangent_block)
        totals = tuple((summed + fresh for summed, fresh in zip(totals, gradients[1:])))
        return (totals, (result.astype(jnp.bfloat16), gradients[0]))
    zeros_init = tuple((jnp.zeros(parameter.shape, jnp.float32) for parameter in params))
    totals, (outputs, input_grads) = lax.scan(one_block, zeros_init, (token_blocks, cotangent_blocks, length_blocks))
    output_tokens = outputs.reshape(SEQS, LEN, D)
    input_grad = input_grads.reshape(SEQS, LEN, D)
    attention_grad, inner_grad, outer_grad, bias_grad, vector_grad = totals
    attention_square, attention_new = adam_step(attention_weights, attention_grad, attention_first, attention_second, MATRIX_LEARN_RATE, WEIGHT_DECAY)
    inner_square, inner_new = adam_step(inner_weights, inner_grad, inner_first, inner_second, MATRIX_LEARN_RATE, WEIGHT_DECAY)
    outer_square, outer_new = adam_step(outer_weights, outer_grad, outer_moment_first, outer_second, MATRIX_LEARN_RATE, WEIGHT_DECAY)
    bias_square, bias_new = adam_step(inner_bias, bias_grad, bias_first, bias_second, VECTOR_RATE, 0.0)
    vector_square, vector_new = adam_step(vectors, vector_grad, vector_first, vector_second, VECTOR_RATE, 0.0)
    return (output_tokens, input_grad, attention_grad, attention_square, attention_new, inner_grad, inner_square, inner_new, outer_grad, outer_square, outer_new, bias_grad, bias_square, bias_new, vector_grad, vector_square, vector_new)
```

```python
import jax
import jax.numpy as jnp
from jax import lax
from jax.sharding import PartitionSpec as P

HEADS = 12
HEAD = 64
STEP = 10

NORM_EPS = 1e-12
BETA_ONE = 0.9
BETA_TWO = 0.999
ADAM_EPS = 1e-06
MATRIX_LEARN_RATE = 0.05
VECTOR_RATE = 0.5
WEIGHT_DECAY = 0.01
MASK_FILL = -1e30

BOTH = ("dp", "context")
LOW = jnp.bfloat16
WIDE = jnp.float32


def adam_step(weight, gradient, moment_one, moment_two, step_rate, decay_rate):
    first_new = BETA_ONE * moment_one + (1.0 - BETA_ONE) * gradient
    second_new = BETA_TWO * moment_two + (1.0 - BETA_TWO) * gradient * gradient
    first_hat = first_new / (1.0 - BETA_ONE**STEP)
    second_hat = second_new / (1.0 - BETA_TWO**STEP)
    updated = weight - step_rate * (
        first_hat / (jnp.sqrt(second_hat) + ADAM_EPS) + decay_rate * weight
    )
    return (second_new, updated)


def matmul(left, right):
    return jnp.dot(left, right, preferred_element_type=WIDE)


def contract_rows(left, right):
    return lax.dot_general(left, right, (((0,), (0,)), ((), ())), preferred_element_type=WIDE)


def times_transpose(left, right):
    return lax.dot_general(left, right, (((1,), (1,)), ((), ())), preferred_element_type=WIDE)


def swap_bit(value, bit, count):
    return lax.ppermute(value, BOTH, [(i, i ^ (1 << bit)) for i in range(count)])


def my_bit(bit):
    return (lax.axis_index(BOTH) >> bit) & 1


def join(mine, other, bit, axis):
    flag = my_bit(bit) == 1
    return jnp.where(
        flag, jnp.stack([other, mine], axis=axis), jnp.stack([mine, other], axis=axis)
    )


def gather_all(shard, count):
    bits = count.bit_length() - 1
    held = shard
    for place, bit in enumerate(range(bits - 1, 2, -1)):
        held = join(held, swap_bit(held, bit, count), bit, place)
    place = bits - 3
    half = shard.shape[1] // 2
    first, second = held[..., :half], held[..., half:]
    first = join(first, swap_bit(first, 2, count), 2, place)
    second = join(second, swap_bit(second, 1, count), 1, place)
    first = join(first, swap_bit(first, 1, count), 1, place + 1)
    second = join(second, swap_bit(second, 2, count), 2, place)
    held = jnp.concatenate([first, second], axis=-1)
    held = join(held, swap_bit(held, 0, count), 0, place + 2)
    return held.reshape((count,) + shard.shape)


def halve(partial, bit, axis, count):
    mine = my_bit(bit)
    sent = lax.dynamic_index_in_dim(partial, 1 - mine, axis, keepdims=False)
    kept = lax.dynamic_index_in_dim(partial, mine, axis, keepdims=False)
    return kept.astype(WIDE) + swap_bit(sent, bit, count).astype(WIDE)


def reduce_shards(partial, count, kind=LOW):
    bits = count.bit_length() - 1
    rows, columns = partial.shape[1:]
    partial = partial.astype(kind).reshape((2,) * bits + (rows, columns))
    partial = halve(partial, 0, bits - 1, count).astype(kind)
    half = columns // 2
    first, second = partial[..., :half], partial[..., half:]
    place = bits - 3
    first = halve(first, 1, place + 1, count).astype(kind)
    second = halve(second, 2, place, count).astype(kind)
    first = halve(first, 2, place, count).astype(kind)
    second = halve(second, 1, place, count).astype(kind)
    partial = jnp.concatenate([first, second], axis=-1)
    for place, bit in reversed(list(enumerate(range(bits - 1, 2, -1)))):
        partial = halve(partial, bit, place, count)
        if place:
            partial = partial.astype(kind)
    return partial


def swap_context(value, offset, parts):
    return lax.ppermute(value, "context", [(i, i ^ offset) for i in range(parts)])


def to_sequences(value, parts):
    seqs, here, width = value.shape
    own = seqs // parts
    me = lax.axis_index("context")
    whole = jnp.zeros((own, parts * here, width), value.dtype)
    for offset in range(parts):
        peer = me ^ offset
        block = lax.dynamic_slice_in_dim(value, peer * own, own, 0)
        if offset:
            block = swap_context(block, offset, parts)
        whole = lax.dynamic_update_slice_in_dim(whole, block, peer * here, 1)
    return whole


def to_positions(value, parts):
    own, length, width = value.shape
    here = length // parts
    me = lax.axis_index("context")
    whole = jnp.zeros((own * parts, here, width), value.dtype)
    for offset in range(parts):
        peer = me ^ offset
        block = lax.dynamic_slice_in_dim(value, peer * here, here, 1)
        if offset:
            block = swap_context(block, offset, parts)
        whole = lax.dynamic_update_slice_in_dim(whole, block, peer * own, 0)
    return whole


def norm_stats(value):
    centered = value - jnp.mean(value, axis=-1, keepdims=True)
    variance = jnp.mean(centered * centered, axis=-1, keepdims=True)
    scale = lax.rsqrt(variance + NORM_EPS)
    return centered * scale, scale


def norm_back(grad, gain, unit, scale):
    scaled = grad * gain
    return scale * (
        scaled
        - jnp.mean(scaled, axis=-1, keepdims=True)
        - unit * jnp.mean(scaled * unit, axis=-1, keepdims=True)
    )


def split_heads(rows, seqs):
    return rows.reshape(seqs, -1, HEADS, HEAD)


def attend(query, key, value, valid):
    seqs = valid.shape[0]
    scores = jnp.einsum(
        "gqhc,gkhc->ghqk",
        split_heads(query, seqs),
        split_heads(key, seqs),
        preferred_element_type=WIDE,
    ) * HEAD ** (-0.5)
    masked = jnp.where(valid[:, None, None, :], scores, MASK_FILL)
    peak = jnp.max(masked, axis=-1, keepdims=True)
    exponent = jnp.exp(masked - peak)
    total = jnp.sum(exponent, axis=-1, keepdims=True)
    prob = exponent / total
    mixed = jnp.einsum(
        "ghqk,gkhc->gqhc", prob.astype(LOW), split_heads(value, seqs), preferred_element_type=WIDE
    )
    return mixed.astype(LOW).reshape(query.shape), peak + jnp.log(total)


def attend_back(query, key, value, valid, normalizer, mixed_grad):
    seqs = valid.shape[0]
    shape = query.shape
    query, key, value, mixed_grad = (
        split_heads(query, seqs),
        split_heads(key, seqs),
        split_heads(value, seqs),
        split_heads(mixed_grad, seqs),
    )
    scores = jnp.einsum("gqhc,gkhc->ghqk", query, key, preferred_element_type=WIDE) * HEAD ** (
        -0.5
    )
    prob = jnp.where(valid[:, None, None, :], jnp.exp(scores - normalizer), 0.0)
    prob_grad = jnp.einsum("gqhc,gkhc->ghqk", mixed_grad, value, preferred_element_type=WIDE)
    row_term = jnp.sum(prob_grad * prob, axis=-1, keepdims=True)
    score_low = (prob * (prob_grad - row_term)).astype(LOW)
    query_grad = jnp.einsum(
        "ghqk,gkhc->gqhc", score_low, key, preferred_element_type=WIDE
    ) * HEAD ** (-0.5)
    key_grad = jnp.einsum(
        "ghqk,gqhc->gkhc", score_low, query, preferred_element_type=WIDE
    ) * HEAD ** (-0.5)
    value_grad = jnp.einsum(
        "ghqk,gqhc->gkhc", prob.astype(LOW), mixed_grad, preferred_element_type=WIDE
    )
    return tuple(g.astype(LOW).reshape(shape) for g in (query_grad, key_grad, value_grad))


def local(
    tokens,
    cotangent,
    lengths,
    attention_weights,
    inner_weights,
    outer_weights,
    inner_bias,
    vectors,
    attention_first,
    attention_second,
    inner_first,
    inner_second,
    outer_moment_first,
    outer_second,
    bias_first,
    bias_second,
    vector_first,
    vector_second,
):
    parts = lax.axis_size("context")
    count = lax.axis_size("dp") * parts
    seq_count, local_len, width = tokens.shape
    hidden = inner_weights.shape[1]
    full_len = local_len * parts
    own_seqs = seq_count // parts
    rows = own_seqs * full_len
    att_rows, vec_cols, bias_cols = (
        attention_weights.shape[1],
        vectors.shape[1],
        inner_bias.shape[0],
    )

    small = jnp.concatenate([vectors.reshape(-1), inner_bias]).astype(LOW)
    small_size = small.shape[0]
    small = jnp.pad(small, (0, width - small_size)).reshape(1, width)
    att_shard = jnp.concatenate(
        [attention_weights.astype(LOW).reshape(4 * att_rows, width), small], axis=0
    )
    token_rows = to_sequences(tokens, parts).reshape(rows, width)
    att_all = gather_all(att_shard, count)
    inner_full = gather_all(inner_weights.astype(LOW), count).reshape(width, hidden)
    outer_full = gather_all(outer_weights.astype(LOW), count).reshape(hidden, width)
    cot_rows = to_sequences(cotangent.astype(LOW), parts).reshape(rows, width).astype(WIDE)

    attention_full = (
        att_all[:, : 4 * att_rows]
        .reshape(count, 4, att_rows, width)
        .transpose(1, 0, 2, 3)
        .reshape(4, width, width)
    )
    small_all = att_all[:, 4 * att_rows, :small_size].astype(WIDE)
    vec = (
        small_all[:, : 8 * vec_cols].reshape(count, 8, vec_cols).transpose(1, 0, 2).reshape(8, -1)
    )
    bias = small_all[:, 8 * vec_cols :].reshape(1, -1)

    me = lax.axis_index("context")
    own_lengths = lax.dynamic_slice_in_dim(lengths, me * own_seqs, own_seqs, 0)
    valid = jnp.arange(full_len, dtype=jnp.int32)[None, :] < own_lengths[:, None]

    query = (matmul(token_rows, attention_full[0]) + vec[0]).astype(LOW)
    key = matmul(token_rows, attention_full[1]).astype(LOW)
    value = (matmul(token_rows, attention_full[2]) + vec[1]).astype(LOW)
    mixed, normalizer = attend(query, key, value, valid)
    first_sum = token_rows.astype(WIDE) + matmul(mixed, attention_full[3]) + vec[2]
    unit_one, scale_one = norm_stats(first_sum)
    normed = unit_one * vec[4] + vec[5]
    normed_low = normed.astype(LOW)
    hidden_pre = matmul(normed_low, inner_full) + bias
    activated, gelu_back = jax.vjp(lambda v: jax.nn.gelu(v, approximate=False), hidden_pre)
    activated = activated.astype(LOW)
    second_sum = normed + matmul(activated, outer_full) + vec[3]
    unit_two, scale_two = norm_stats(second_sum)
    result = (unit_two * vec[6] + vec[7]).astype(LOW)
    output_tokens = to_positions(result.reshape(own_seqs, full_len, width), parts)

    second_grad = norm_back(cot_rows, vec[6], unit_two, scale_two)
    ffn_low = second_grad.astype(LOW)
    outer_grad = contract_rows(activated, ffn_low)
    outer_total = reduce_shards(outer_grad.reshape(count, -1, width), count)
    (hidden_grad,) = gelu_back(times_transpose(ffn_low, outer_full))
    hidden_low = hidden_grad.astype(LOW)
    inner_grad = contract_rows(normed_low, hidden_low)
    inner_total = reduce_shards(inner_grad.reshape(count, -1, hidden), count)
    normed_grad = times_transpose(hidden_low, inner_full) + second_grad
    first_grad = norm_back(normed_grad, vec[4], unit_one, scale_one)
    branch_low = first_grad.astype(LOW)
    proj_grad = contract_rows(mixed, branch_low)
    mixed_grad = times_transpose(branch_low, attention_full[3]).astype(LOW)
    query_low, key_low, value_low = attend_back(query, key, value, valid, normalizer, mixed_grad)

    att_grad = jnp.stack(
        [
            contract_rows(token_rows, query_low),
            contract_rows(token_rows, key_low),
            contract_rows(token_rows, value_low),
            proj_grad,
        ]
    )
    att_grad = (
        att_grad.astype(LOW)
        .reshape(4, count, att_rows, width)
        .transpose(1, 0, 2, 3)
        .reshape(count, 4 * att_rows, width)
    )
    attention_total = reduce_shards(att_grad, count).reshape(4, att_rows, width)

    vector_grad = jnp.stack(
        [
            jnp.sum(query_low.astype(WIDE), axis=0),
            jnp.sum(value_low.astype(WIDE), axis=0),
            jnp.sum(branch_low.astype(WIDE), axis=0),
            jnp.sum(ffn_low.astype(WIDE), axis=0),
            jnp.sum(normed_grad * unit_one, axis=0),
            jnp.sum(normed_grad, axis=0),
            jnp.sum(cot_rows * unit_two, axis=0),
            jnp.sum(cot_rows, axis=0),
        ]
    )
    small_grad = jnp.concatenate(
        [
            vector_grad.reshape(8, count, vec_cols).transpose(1, 0, 2).reshape(count, -1),
            jnp.sum(hidden_low.astype(WIDE), axis=0).reshape(count, bias_cols),
        ],
        axis=1,
    )
    small_total = reduce_shards(small_grad[:, None, :], count, WIDE).reshape(-1)
    vector_total = small_total[: 8 * vec_cols].reshape(8, vec_cols)
    bias_total = small_total[8 * vec_cols :]

    input_grad = (
        first_grad
        + times_transpose(query_low, attention_full[0])
        + times_transpose(key_low, attention_full[1])
        + times_transpose(value_low, attention_full[2])
    )
    input_grad = to_positions(
        input_grad.astype(LOW).reshape(own_seqs, full_len, width), parts
    ).astype(WIDE)

    attention_square, attention_new = adam_step(
        attention_weights,
        attention_total,
        attention_first,
        attention_second,
        MATRIX_LEARN_RATE,
        WEIGHT_DECAY,
    )
    inner_square, inner_new = adam_step(
        inner_weights, inner_total, inner_first, inner_second, MATRIX_LEARN_RATE, WEIGHT_DECAY
    )
    outer_square, outer_new = adam_step(
        outer_weights,
        outer_total,
        outer_moment_first,
        outer_second,
        MATRIX_LEARN_RATE,
        WEIGHT_DECAY,
    )
    bias_square, bias_new = adam_step(
        inner_bias, bias_total, bias_first, bias_second, VECTOR_RATE, 0.0
    )
    vector_square, vector_new = adam_step(
        vectors, vector_total, vector_first, vector_second, VECTOR_RATE, 0.0
    )
    return (
        output_tokens,
        input_grad,
        attention_total,
        attention_square,
        attention_new,
        inner_total,
        inner_square,
        inner_new,
        outer_total,
        outer_square,
        outer_new,
        bias_total,
        bias_square,
        bias_new,
        vector_total,
        vector_square,
        vector_new,
    )


def solution(mesh):
    rows3 = P("dp", "context", None)
    mid3 = P(None, BOTH, None)
    row2 = P(BOTH, None)
    col2 = P(None, BOTH)
    one = P(BOTH)
    return jax.shard_map(
        local,
        mesh=mesh,
        in_specs=(rows3, rows3, P("dp"), mid3, row2, row2, one, col2)
        + (mid3, mid3, row2, row2, row2, row2, one, one, col2, col2),
        out_specs=(rows3, rows3)
        + (mid3,) * 3
        + (row2,) * 6
        + (one,) * 3
        + (col2,) * 3,
        check_vma=False,
    )
```

```python
import functools

import jax
import jax.numpy as jnp
import numpy as np
from jax import lax
from jax.experimental import pallas as pl
from jax.experimental.pallas import tpu as pltpu
from jax.sharding import Mesh, PartitionSpec as P

HEADS = 12
HEAD = 64
PAIR = 2 * HEAD
PAIRS = HEADS // 2
STEP = 10

NORM_EPS = 1e-12
BETA_ONE = 0.9
BETA_TWO = 0.999
ADAM_EPS = 1e-06
MATRIX_LEARN_RATE = 0.05
VECTOR_RATE = 0.5
WEIGHT_DECAY = 0.01
MASK_FILL = -1e30
SCORE_SCALE = HEAD ** (-0.5)
ROOT_HALF = 0.5**0.5
DENSITY = 0.3989422804014327

CHIPS = ("dp_hi", "dp_lo", "ctx_hi")
SIDE = "ctx_lo"
ALL = CHIPS + (SIDE,)
CONTEXT = ("ctx_hi", "ctx_lo")
LOW = jnp.bfloat16
WIDE = jnp.float32
VMEM_BYTES = 60 * 1024 * 1024


def adam_step(weight, gradient, moment_one, moment_two, step_rate, decay_rate):
    first_new = BETA_ONE * moment_one + (1.0 - BETA_ONE) * gradient
    second_new = BETA_TWO * moment_two + (1.0 - BETA_TWO) * gradient * gradient
    first_hat = first_new / (1.0 - BETA_ONE**STEP)
    second_hat = second_new / (1.0 - BETA_TWO**STEP)
    updated = weight - step_rate * (
        first_hat / (jnp.sqrt(second_hat) + ADAM_EPS) + decay_rate * weight
    )
    return (second_new, updated)


def matmul(left, right):
    return jnp.dot(left, right, preferred_element_type=WIDE)


def contract_rows(left, right):
    return lax.dot_general(left, right, (((0,), (0,)), ((), ())), preferred_element_type=WIDE)


def times_transpose(left, right):
    return lax.dot_general(left, right, (((1,), (1,)), ((), ())), preferred_element_type=WIDE)


def flip(value):
    return value.astype(WIDE).T


def norm_stats(value):
    centered = value - jnp.mean(value, axis=-1, keepdims=True)
    variance = jnp.mean(centered * centered, axis=-1, keepdims=True)
    scale = lax.rsqrt(variance + NORM_EPS)
    return centered * scale, scale


def norm_back(grad, gain, unit, scale):
    scaled = grad * gain
    return scale * (
        scaled
        - jnp.mean(scaled, axis=-1, keepdims=True)
        - unit * jnp.mean(scaled * unit, axis=-1, keepdims=True)
    )


def load_matrices(picks, side, mine, other, target, sems):
    rows, half = target.shape[2], mine.shape[2]
    copies = []
    for place, pick in enumerate(picks):
        for which, source in enumerate((mine, other)):
            start = pl.multiple_of((side if which == 0 else 1 - side) * half, half)
            copies.append(
                pltpu.make_async_copy(
                    source.at[:, pl.ds(pick * rows, rows), :],
                    target.at[place, :, :, pl.ds(start, half)],
                    sems.at[2 * place + which],
                )
            )
    return copies


def load_halves(side, mine, other, target, sems, first):
    half = mine.shape[1]
    copies = []
    for which, source in enumerate((mine, other)):
        start = pl.multiple_of((side if which == 0 else 1 - side) * half, half)
        copies.append(
            pltpu.make_async_copy(source, target.at[:, pl.ds(start, half)], sems.at[first + which])
        )
    return copies


def half_slices(side, half):
    return [
        pl.ds(pl.multiple_of(side * half, half), half),
        pl.ds(pl.multiple_of((1 - side) * half, half), half),
    ]


def matrix_of(scratch, place):
    _, blocks, rows, width = scratch.shape
    return scratch[place].reshape(blocks * rows, width)


def head_masks():
    lane = lax.broadcasted_iota(jnp.int32, (1, PAIR), 1)
    return [lane < HEAD, lane >= HEAD]


def only(value, mask):
    return jnp.where(mask, value, 0.0).astype(LOW)


def attend_kernel(
    lengths,
    sides,
    tokens,
    vec,
    mine,
    other,
    query_out,
    key_out,
    value_out,
    mixed_out,
    sum_out,
    norm_out,
    weights,
    value_flip,
    mixed_flip,
    sems,
):
    step = pl.program_id(0)
    copies = load_matrices(range(4), sides[0], mine, other, weights, sems)

    @pl.when(step == 0)
    def _():
        for copy in copies:
            copy.start()
        for copy in copies:
            copy.wait()

    length = lengths[step]
    rows = tokens[...]
    query_out[...] = (matmul(rows, matrix_of(weights, 0)) + vec[0:1, :]).astype(LOW)
    key_out[...] = matmul(rows, matrix_of(weights, 1)).astype(LOW)
    value_low = (matmul(rows, matrix_of(weights, 2)) + vec[1:2, :]).astype(LOW)
    value_out[...] = value_low
    value_flip[...] = flip(value_low).astype(LOW)
    size = tokens.shape[0]
    key_valid = lax.broadcasted_iota(jnp.int32, (size, size), 0) < length
    masks = head_masks()

    def one_pair(pair, carry):
        lanes = pl.ds(pl.multiple_of(pair * PAIR, PAIR), PAIR)
        keys = key_out[:, lanes]
        queries = query_out[:, lanes].astype(WIDE) * SCORE_SCALE
        mixed, norms = [], []
        for head in range(2):
            scores = times_transpose(keys, only(queries, masks[head]))
            scores = jnp.where(key_valid, scores, MASK_FILL)
            peak = jnp.max(scores, axis=0, keepdims=True)
            exponent = jnp.exp(scores - peak)
            total = jnp.sum(exponent, axis=0, keepdims=True)
            prob = (exponent * (1.0 / total)).astype(LOW)
            start = pl.multiple_of(pair * PAIR + head * HEAD, HEAD)
            mixed.append(matmul(value_flip[pl.ds(start, HEAD), :], prob))
            norms.append(peak + jnp.log(total))
        mixed_flip[lanes, :] = jnp.concatenate(mixed, axis=0)
        norm_out[0, pair] = jnp.concatenate(norms, axis=0)
        return carry

    lax.fori_loop(0, PAIRS, one_pair, 0)
    mixed_low = mixed_flip[...].T.astype(LOW)
    mixed_out[...] = mixed_low
    sum_out[...] = (
        rows.astype(WIDE) + matmul(mixed_low, matrix_of(weights, 3)) + vec[2:3, :]
    )


def ffn_kernel(
    sides,
    first_sum,
    cotangent,
    vec,
    bias,
    inner_mine,
    inner_other,
    outer_mine,
    outer_other,
    result_out,
    second_out,
    hidden_out,
    keep_out,
    send_out,
    vec_grad,
    bias_grad,
    inner,
    outer,
    total,
    activated,
    slope,
    sems,
):
    step = pl.program_id(0)
    side = sides[0]
    copies = load_halves(side, inner_mine, inner_other, inner, sems, 0) + load_halves(
        side, outer_mine, outer_other, outer, sems, 2
    )

    @pl.when(step == 0)
    def _():
        for copy in copies:
            copy.start()
        vec_grad[...] = jnp.zeros_like(vec_grad)
        bias_grad[...] = jnp.zeros_like(bias_grad)
        total[...] = jnp.zeros_like(total)
        for copy in copies:
            copy.wait()

    unit, _ = norm_stats(first_sum[...])
    normed = unit * vec[4:5, :] + vec[5:6, :]
    normed_low = normed.astype(LOW)
    hidden = inner.shape[1]
    chunk = inner.shape[0]
    second = normed + vec[3:4, :]
    for start in range(0, hidden, chunk):
        part = slice(start, start + chunk)
        pre = matmul(normed_low, inner[:, part]) + bias[:, part]
        cdf = 0.5 * (1.0 + lax.erf(pre * ROOT_HALF))
        active = (pre * cdf).astype(LOW)
        activated[:, part] = active
        slope[:, part] = cdf + pre * (DENSITY * jnp.exp(-0.5 * pre * pre))
        second = second + matmul(active, outer[part, :])
    unit_two, scale_two = norm_stats(second)
    result_out[...] = (unit_two * vec[6:7, :] + vec[7:8, :]).astype(LOW)
    grad = cotangent[...].astype(WIDE)
    second_grad = norm_back(grad, vec[6:7, :], unit_two, scale_two)
    second_out[...] = second_grad
    grad_low = second_grad.astype(LOW)
    vec_grad[3:4, :] += jnp.sum(grad_low.astype(WIDE), axis=0, keepdims=True)
    vec_grad[6:7, :] += jnp.sum(grad * unit_two, axis=0, keepdims=True)
    vec_grad[7:8, :] += jnp.sum(grad, axis=0, keepdims=True)
    for start in range(0, hidden, chunk):
        part = slice(start, start + chunk)
        back = times_transpose(grad_low, outer[part, :])
        hidden_low = (back * slope[:, part]).astype(LOW)
        hidden_out[:, part] = hidden_low
        bias_grad[:, part] += jnp.sum(hidden_low.astype(WIDE), axis=0, keepdims=True)
        total[part, :] += contract_rows(activated[:, part], grad_low)

    @pl.when(step == pl.num_programs(0) - 1)
    def _():
        mine, theirs = half_slices(side, keep_out.shape[1])
        keep_out[...] = total[:, mine].astype(LOW)
        send_out[...] = total[:, theirs].astype(LOW)


def inner_kernel(
    sides,
    first_sum,
    second_grad,
    hidden_low,
    mixed,
    vec,
    inner_mine,
    inner_other,
    att_mine,
    att_other,
    first_out,
    mixed_grad_out,
    keep_out,
    send_out,
    vec_grad,
    inner,
    project,
    total,
    project_total,
    sems,
):
    step = pl.program_id(0)
    side = sides[0]
    copies = load_halves(side, inner_mine, inner_other, inner, sems, 2) + load_matrices(
        (3,), side, att_mine, att_other, project, sems
    )

    @pl.when(step == 0)
    def _():
        for copy in copies:
            copy.start()
        vec_grad[...] = jnp.zeros_like(vec_grad)
        total[...] = jnp.zeros_like(total)
        project_total[...] = jnp.zeros_like(project_total)
        for copy in copies:
            copy.wait()

    unit, scale = norm_stats(first_sum[...])
    normed_low = (unit * vec[4:5, :] + vec[5:6, :]).astype(LOW)
    normed_flip = flip(normed_low).astype(LOW)
    hidden = inner.shape[1]
    chunk = inner.shape[0]
    grad = second_grad[...]
    for start in range(0, hidden, chunk):
        part = slice(start, start + chunk)
        grad = grad + times_transpose(hidden_low[:, part], inner[:, part])
        total[:, part] += matmul(normed_flip, hidden_low[:, part])
    first_grad = norm_back(grad, vec[4:5, :], unit, scale)
    first_out[...] = first_grad
    branch = first_grad.astype(LOW)
    vec_grad[2:3, :] += jnp.sum(branch.astype(WIDE), axis=0, keepdims=True)
    vec_grad[4:5, :] += jnp.sum(grad * unit, axis=0, keepdims=True)
    vec_grad[5:6, :] += jnp.sum(grad, axis=0, keepdims=True)
    mixed_grad_out[...] = times_transpose(branch, matrix_of(project, 0)).astype(LOW)
    project_total[...] += contract_rows(mixed[...], branch)

    @pl.when(step == pl.num_programs(0) - 1)
    def _():
        half = inner_mine.shape[1]
        for out, wide, narrow in zip(
            (keep_out, send_out),
            half_slices(side, half),
            half_slices(side, att_mine.shape[2]),
        ):
            out[:, :half] = total[:, wide].astype(LOW)
            out[:, half:] = project_total[:, narrow].astype(LOW)


def attend_back_kernel(
    lengths,
    sides,
    tokens,
    query,
    key,
    value,
    mixed_grad,
    normalizer,
    query_out,
    key_out,
    value_out,
    keep_out,
    send_out,
    vec_grad,
    key_flip,
    query_flip,
    total,
):
    step = pl.program_id(0)
    side = sides[0]

    @pl.when(step == 0)
    def _():
        vec_grad[...] = jnp.zeros_like(vec_grad)
        total[...] = jnp.zeros_like(total)

    length = lengths[step]
    size = tokens.shape[0]
    key_flip[...] = flip(key[...]).astype(LOW)
    key_valid = lax.broadcasted_iota(jnp.int32, (size, size), 0) < length
    masks = head_masks()

    def one_pair(pair, carry):
        lanes = pl.ds(pl.multiple_of(pair * PAIR, PAIR), PAIR)
        keys = key[:, lanes]
        values = value[:, lanes]
        queries = query[:, lanes].astype(WIDE) * SCORE_SCALE
        grads = mixed_grad[:, lanes].astype(WIDE)
        norms = normalizer[0, pair]
        query_parts, key_part, value_part = [], 0.0, 0.0
        for head in range(2):
            own_query = only(queries, masks[head])
            own_grad = only(grads, masks[head])
            scores = times_transpose(keys, own_query)
            prob = jnp.where(key_valid, jnp.exp(scores - norms[head : head + 1, :]), 0.0)
            prob_grad = times_transpose(values, own_grad)
            row_term = jnp.sum(prob_grad * prob, axis=0, keepdims=True)
            score_low = (prob * (prob_grad - row_term)).astype(LOW)
            value_part = value_part + matmul(prob.astype(LOW), own_grad)
            key_part = key_part + matmul(score_low, own_query)
            start = pl.multiple_of(pair * PAIR + head * HEAD, HEAD)
            query_parts.append(matmul(key_flip[pl.ds(start, HEAD), :], score_low))
        query_flip[lanes, :] = jnp.concatenate(query_parts, axis=0) * SCORE_SCALE
        key_out[:, lanes] = key_part.astype(LOW)
        value_out[:, lanes] = value_part.astype(LOW)
        return carry

    lax.fori_loop(0, PAIRS, one_pair, 0)
    query_out[...] = query_flip[...].T.astype(LOW)
    token_flip = flip(tokens[...]).astype(LOW)
    for place, grads in enumerate((query_out, key_out, value_out)):
        total[place] += matmul(token_flip, grads[...])
    vec_grad[0:1, :] += jnp.sum(query_out[...].astype(WIDE), axis=0, keepdims=True)
    vec_grad[1:2, :] += jnp.sum(value_out[...].astype(WIDE), axis=0, keepdims=True)

    @pl.when(step == pl.num_programs(0) - 1)
    def _():
        blocks, _, rows, half = keep_out.shape
        for out, part in zip((keep_out, send_out), half_slices(side, half)):
            for place in range(3):
                out[:, place] = total[place, :, part].astype(LOW).reshape(blocks, rows, half)


def input_kernel(
    sides, first_grad, query, key, value, mine, other, grad_out, weights, sems
):
    copies = load_matrices(range(3), sides[0], mine, other, weights, sems)

    @pl.when(pl.program_id(0) == 0)
    def _():
        for copy in copies:
            copy.start()
        for copy in copies:
            copy.wait()

    grad = first_grad[...]
    for place, grads in enumerate((query, key, value)):
        grad = grad + times_transpose(grads[...], matrix_of(weights, place))
    grad_out[...] = grad.astype(grad_out.dtype)


def call(kernel, grid, inputs, outputs, scratch, flops, moved):
    return pl.pallas_call(
        kernel,
        grid=(grid,),
        in_specs=[spec for _, spec in inputs],
        out_specs=[spec for _, _, spec in outputs],
        out_shape=[jax.ShapeDtypeStruct(shape, kind) for shape, kind, _ in outputs],
        scratch_shapes=scratch,
        compiler_params=pltpu.CompilerParams(
            dimension_semantics=("arbitrary",), vmem_limit_bytes=VMEM_BYTES
        ),
        cost_estimate=pl.CostEstimate(flops=flops, bytes_accessed=moved, transcendentals=0),
    )(*[array for array, _ in inputs])


SCALARS = pl.BlockSpec(memory_space=pltpu.SMEM)
WHERE_IT_IS = pl.BlockSpec(memory_space=pl.ANY)


def tiles(rows, width):
    return pl.BlockSpec((rows, width), lambda i: (i, 0))


def whole(*shape):
    return pl.BlockSpec(shape, lambda i: (0,) * len(shape))


def swap_side(value):
    return lax.ppermute(value, SIDE, [(0, 1), (1, 0)])


def split_columns(value, side):
    half = value.shape[-1] // 2
    mine = lax.dynamic_slice_in_dim(value, side * half, half, value.ndim - 1)
    theirs = lax.dynamic_slice_in_dim(value, (1 - side) * half, half, value.ndim - 1)
    return mine, theirs


def in_order(mine, theirs, side, axis):
    return jnp.where(
        side == 0,
        jnp.concatenate([mine, theirs], axis=axis),
        jnp.concatenate([theirs, mine], axis=axis),
    )


def gather_half(shard, side):
    mine, theirs = split_columns(shard, side)
    pair = in_order(mine, swap_side(theirs), side, shard.ndim - 2)
    return pair


def own_rows(total, side):
    rows = total.shape[-2] // 2
    axis = total.ndim - 2
    mine = lax.dynamic_slice_in_dim(total, side * rows, rows, axis)
    theirs = lax.dynamic_slice_in_dim(total, (1 - side) * rows, rows, axis)
    return mine, swap_side(theirs)


def bit_of(bit):
    return (lax.axis_index(ALL) >> bit) & 1


def halve(partial, bit, axis, count):
    mine = bit_of(bit)
    sent = lax.dynamic_index_in_dim(partial, 1 - mine, axis, keepdims=False)
    kept = lax.dynamic_index_in_dim(partial, mine, axis, keepdims=False)
    return kept + lax.ppermute(sent, ALL, [(i, i ^ (1 << bit)) for i in range(count)])


def reduce_small(partial, count):
    bits = count.bit_length() - 1
    partial = partial.reshape((2,) * bits + partial.shape[1:])
    for bit in range(bits):
        partial = halve(partial, bit, bits - 1 - bit, count)
    return partial


def swap_context(value, offset, parts):
    return lax.ppermute(value, CONTEXT, [(i, i ^ offset) for i in range(parts)])


def to_sequences(value, parts):
    seqs, here, width = value.shape
    own = seqs // parts
    me = lax.axis_index(CONTEXT)
    full = jnp.zeros((own, parts * here, width), value.dtype)
    for offset in range(parts):
        peer = me ^ offset
        block = lax.dynamic_slice_in_dim(value, peer * own, own, 0)
        if offset:
            block = swap_context(block, offset, parts)
        full = lax.dynamic_update_slice_in_dim(full, block, peer * here, 1)
    return full


def to_positions(value, parts):
    own, length, width = value.shape
    here = length // parts
    me = lax.axis_index(CONTEXT)
    full = jnp.zeros((own * parts, here, width), value.dtype)
    for offset in range(parts):
        peer = me ^ offset
        block = lax.dynamic_slice_in_dim(value, peer * here, here, 1)
        if offset:
            block = swap_context(block, offset, parts)
        full = lax.dynamic_update_slice_in_dim(full, block, peer * own, 0)
    return full


def local(
    tokens,
    cotangent,
    lengths,
    attention_weights,
    inner_weights,
    outer_weights,
    inner_bias,
    vectors,
    attention_first,
    attention_second,
    inner_first,
    inner_second,
    outer_moment_first,
    outer_second,
    bias_first,
    bias_second,
    vector_first,
    vector_second,
):
    parts = lax.axis_size(CONTEXT)
    chips = lax.axis_size(CHIPS)
    count = 2 * chips
    side = lax.axis_index(SIDE)
    sides = jnp.reshape(side, (1,)).astype(jnp.int32)
    seq_count, local_len, width = tokens.shape
    hidden = inner_weights.shape[1]
    full_len = local_len * parts
    own_seqs = seq_count // parts
    rows = own_seqs * full_len
    att_rows, vec_cols, bias_cols = (
        attention_weights.shape[1],
        vectors.shape[1],
        inner_bias.shape[0],
    )
    half = width // 2
    hidden_half = hidden // 2
    pair_rows = 2 * att_rows
    tall = 16

    small = jnp.concatenate([vectors.reshape(-1), inner_bias]).astype(LOW)
    small_size = small.shape[0]
    small = jnp.pad(small.reshape(1, -1), ((0, tall - 1), (0, half - small_size)))
    att_pair = gather_half(attention_weights.astype(LOW), side).reshape(4 * pair_rows, half)
    att_mine = lax.all_gather(
        jnp.concatenate([att_pair, small], axis=0), CHIPS, axis=0, tiled=False
    )
    att_other = swap_side(att_mine)
    inner_mine = lax.all_gather(
        gather_half(inner_weights.astype(LOW), side), CHIPS, axis=0, tiled=True
    )
    inner_other = swap_side(inner_mine)
    outer_mine = lax.all_gather(
        gather_half(outer_weights.astype(LOW), side), CHIPS, axis=0, tiled=True
    )
    outer_other = swap_side(outer_mine)

    small_all = in_order(
        att_mine[:, None, 4 * pair_rows, :small_size],
        att_other[:, None, 4 * pair_rows, :small_size],
        side,
        1,
    ).reshape(count, small_size)
    small_all = small_all.astype(WIDE)
    vec = (
        small_all[:, : 8 * vec_cols].reshape(count, 8, vec_cols).transpose(1, 0, 2).reshape(8, -1)
    )
    bias = small_all[:, 8 * vec_cols :].reshape(1, -1)
    if pair_rows % tall:
        blocks, block_rows = 1, width

        def lay_out(value):
            value = value[:, : 4 * pair_rows].reshape(chips, 4, pair_rows, half)
            return value.transpose(1, 0, 2, 3).reshape(1, 4 * width, half)

        att_mine, att_other = lay_out(att_mine), lay_out(att_other)
    else:
        blocks, block_rows = chips, pair_rows

    token_rows = to_sequences(tokens, parts).reshape(rows, width)
    cot_rows = to_sequences(cotangent.astype(LOW), parts).reshape(rows, width)
    own_lengths = lax.dynamic_slice_in_dim(lengths, lax.axis_index(CONTEXT) * own_seqs, own_seqs)

    seq_tile = tiles(full_len, width)
    norm_spec = pl.BlockSpec((1, PAIRS, 2, full_len), lambda i: (i, 0, 0, 0))
    norm_shape = (own_seqs, PAIRS, 2, full_len)
    low_rows = ((rows, width), LOW, seq_tile)
    vec_spec = whole(8, width)
    square = 2 * rows * width * width
    attend_flops = 8 * rows * full_len * width

    query, key, value, mixed, first_sum, normalizer = call(
        attend_kernel,
        own_seqs,
        [
            (own_lengths, SCALARS),
            (sides, SCALARS),
            (token_rows, seq_tile),
            (vec, vec_spec),
            (att_mine, WHERE_IT_IS),
            (att_other, WHERE_IT_IS),
        ],
        [low_rows] * 4
        + [((rows, width), WIDE, seq_tile), (norm_shape, WIDE, norm_spec)],
        [
            pltpu.VMEM((4, blocks, block_rows, width), LOW),
            pltpu.VMEM((width, full_len), LOW),
            pltpu.VMEM((width, full_len), WIDE),
            pltpu.SemaphoreType.DMA((8,)),
        ],
        4 * square + 2 * attend_flops,
        20 * rows * width,
    )

    tile = 256
    row_tile = tiles(tile, width)
    hidden_tile = tiles(tile, hidden)
    result, second_grad, hidden_low, outer_keep, outer_send, vec_ffn, bias_grad = call(
        ffn_kernel,
        rows // tile,
        [
            (sides, SCALARS),
            (first_sum, row_tile),
            (cot_rows, row_tile),
            (vec, vec_spec),
            (bias, whole(1, hidden)),
            (inner_mine, WHERE_IT_IS),
            (inner_other, WHERE_IT_IS),
            (outer_mine, WHERE_IT_IS),
            (outer_other, WHERE_IT_IS),
        ],
        [
            ((rows, width), LOW, row_tile),
            ((rows, width), WIDE, row_tile),
            ((rows, hidden), LOW, hidden_tile),
            ((hidden, half), LOW, whole(hidden, half)),
            ((hidden, half), LOW, whole(hidden, half)),
            ((8, width), WIDE, vec_spec),
            ((1, hidden), WIDE, whole(1, hidden)),
        ],
        [
            pltpu.VMEM((width, hidden), LOW),
            pltpu.VMEM((hidden, width), LOW),
            pltpu.VMEM((hidden, width), WIDE),
            pltpu.VMEM((tile, hidden), LOW),
            pltpu.VMEM((tile, hidden), WIDE),
            pltpu.SemaphoreType.DMA((4,)),
        ],
        16 * square + 60 * rows * hidden,
        30 * rows * width,
    )
    outer_sum = lax.psum_scatter(
        outer_keep + swap_side(outer_send), CHIPS, scatter_dimension=0, tiled=True
    )
    output_tokens = to_positions(result.reshape(own_seqs, full_len, width), parts)

    first_grad, mixed_grad, inner_keep, inner_send, vec_mid = call(
        inner_kernel,
        rows // tile,
        [
            (sides, SCALARS),
            (first_sum, row_tile),
            (second_grad, row_tile),
            (hidden_low, hidden_tile),
            (mixed, row_tile),
            (vec, vec_spec),
            (inner_mine, WHERE_IT_IS),
            (inner_other, WHERE_IT_IS),
            (att_mine, WHERE_IT_IS),
            (att_other, WHERE_IT_IS),
        ],
        [
            ((rows, width), WIDE, row_tile),
            ((rows, width), LOW, row_tile),
            ((width, hidden_half + half), LOW, whole(width, hidden_half + half)),
            ((width, hidden_half + half), LOW, whole(width, hidden_half + half)),
            ((8, width), WIDE, vec_spec),
        ],
        [
            pltpu.VMEM((width, hidden), LOW),
            pltpu.VMEM((1, blocks, block_rows, width), LOW),
            pltpu.VMEM((width, hidden), WIDE),
            pltpu.VMEM((width, width), WIDE),
            pltpu.SemaphoreType.DMA((4,)),
        ],
        10 * square,
        26 * rows * width,
    )
    inner_sum = lax.psum_scatter(
        inner_keep + swap_side(inner_send), CHIPS, scatter_dimension=0, tiled=True
    )

    att_shape = (blocks, 3, block_rows, half)
    query_low, key_low, value_low, att_keep, att_send, vec_att = call(
        attend_back_kernel,
        own_seqs,
        [
            (own_lengths, SCALARS),
            (sides, SCALARS),
            (token_rows, seq_tile),
            (query, seq_tile),
            (key, seq_tile),
            (value, seq_tile),
            (mixed_grad, seq_tile),
            (normalizer, norm_spec),
        ],
        [low_rows] * 3
        + [
            (att_shape, LOW, whole(*att_shape)),
            (att_shape, LOW, whole(*att_shape)),
            ((8, width), WIDE, vec_spec),
        ],
        [
            pltpu.VMEM((width, full_len), LOW),
            pltpu.VMEM((width, full_len), WIDE),
            pltpu.VMEM((3, width, width), WIDE),
        ],
        3 * square + 5 * attend_flops,
        20 * rows * width,
    )
    att_partial = att_keep + swap_side(att_send)
    if blocks != chips:
        att_partial = att_partial.reshape(3, chips, pair_rows, half).transpose(1, 0, 2, 3)
    att_sum = lax.psum_scatter(att_partial, CHIPS, scatter_dimension=0, tiled=True)
    att_sum = att_sum.reshape(3, pair_rows, half)

    vector_grad = vec_ffn + vec_mid + vec_att
    small_grad = jnp.concatenate(
        [
            vector_grad.reshape(8, count, vec_cols).transpose(1, 0, 2).reshape(count, -1),
            bias_grad.reshape(count, bias_cols),
        ],
        axis=1,
    )
    small_total = reduce_small(small_grad, count)
    vector_total = small_total[: 8 * vec_cols].reshape(8, vec_cols)
    bias_total = small_total[8 * vec_cols :]

    (input_grad,) = call(
        input_kernel,
        own_seqs,
        [
            (sides, SCALARS),
            (first_grad, seq_tile),
            (query_low, seq_tile),
            (key_low, seq_tile),
            (value_low, seq_tile),
            (att_mine, WHERE_IT_IS),
            (att_other, WHERE_IT_IS),
        ],
        [((rows, width), LOW, seq_tile)],
        [
            pltpu.VMEM((3, blocks, block_rows, width), LOW),
            pltpu.SemaphoreType.DMA((6,)),
        ],
        3 * square,
        12 * rows * width,
    )
    input_grad = to_positions(input_grad.reshape(own_seqs, full_len, width), parts).astype(WIDE)

    outer_total = in_order(*own_rows(outer_sum, side), side, 1).astype(WIDE)
    inner_here, inner_there = own_rows(inner_sum, side)
    inner_total = in_order(
        inner_here[:, :hidden_half], inner_there[:, :hidden_half], side, 1
    ).astype(WIDE)
    project_total = in_order(
        inner_here[:, hidden_half:], inner_there[:, hidden_half:], side, 1
    )
    attention_total = jnp.concatenate(
        [in_order(*own_rows(att_sum, side), side, 2), project_total[None]], axis=0
    ).astype(WIDE)

    attention_square, attention_new = adam_step(
        attention_weights,
        attention_total,
        attention_first,
        attention_second,
        MATRIX_LEARN_RATE,
        WEIGHT_DECAY,
    )
    inner_square, inner_new = adam_step(
        inner_weights, inner_total, inner_first, inner_second, MATRIX_LEARN_RATE, WEIGHT_DECAY
    )
    outer_square, outer_new = adam_step(
        outer_weights,
        outer_total,
        outer_moment_first,
        outer_second,
        MATRIX_LEARN_RATE,
        WEIGHT_DECAY,
    )
    bias_square, bias_new = adam_step(
        inner_bias, bias_total, bias_first, bias_second, VECTOR_RATE, 0.0
    )
    vector_square, vector_new = adam_step(
        vectors, vector_total, vector_first, vector_second, VECTOR_RATE, 0.0
    )
    return (
        output_tokens,
        input_grad,
        attention_total,
        attention_square,
        attention_new,
        inner_total,
        inner_square,
        inner_new,
        outer_total,
        outer_square,
        outer_new,
        bias_total,
        bias_square,
        bias_new,
        vector_total,
        vector_square,
        vector_new,
    )


def solution(mesh):
    split = Mesh(
        np.asarray(mesh.devices).reshape(
            mesh.shape["dp"] // 2, 2, mesh.shape["context"] // 2, 2
        ),
        ALL,
    )
    dp = ("dp_hi", "dp_lo")
    rows3 = P(dp, CONTEXT, None)
    mid3 = P(None, ALL, None)
    row2 = P(ALL, None)
    col2 = P(None, ALL)
    one = P(ALL)
    return jax.shard_map(
        local,
        mesh=split,
        in_specs=(rows3, rows3, P(dp), mid3, row2, row2, one, col2)
        + (mid3, mid3, row2, row2, row2, row2, one, one, col2, col2),
        out_specs=(rows3, rows3)
        + (mid3,) * 3
        + (row2,) * 6
        + (one,) * 3
        + (col2,) * 3,
        check_vma=False,
    )
```

```python
import functools

import jax
import jax.numpy as jnp
import numpy as np
from jax import lax
from jax.experimental import pallas as pl
from jax.experimental.pallas import tpu as pltpu
from jax.sharding import Mesh, PartitionSpec as P

HEADS = 12
HEAD = 64
PAIR = 2 * HEAD
PAIRS = HEADS // 2
STEP = 10

NORM_EPS = 1e-12
BETA_ONE = 0.9
BETA_TWO = 0.999
ADAM_EPS = 1e-06
MATRIX_LEARN_RATE = 0.05
VECTOR_RATE = 0.5
WEIGHT_DECAY = 0.01
MASK_FILL = -1e30
SCORE_SCALE = HEAD ** (-0.5)
ROOT_HALF = 0.5**0.5
DENSITY = 0.3989422804014327

CHIPS = ("dp_hi", "dp_lo", "ctx_hi")
SIDE = "ctx_lo"
ALL = CHIPS + (SIDE,)
CONTEXT = ("ctx_hi", "ctx_lo")
LOW = jnp.bfloat16
WIDE = jnp.float32
VMEM_BYTES = 60 * 1024 * 1024


def adam_step(weight, gradient, moment_one, moment_two, step_rate, decay_rate):
    first_new = BETA_ONE * moment_one + (1.0 - BETA_ONE) * gradient
    second_new = BETA_TWO * moment_two + (1.0 - BETA_TWO) * gradient * gradient
    first_hat = first_new / (1.0 - BETA_ONE**STEP)
    second_hat = second_new / (1.0 - BETA_TWO**STEP)
    updated = weight - step_rate * (
        first_hat / (jnp.sqrt(second_hat) + ADAM_EPS) + decay_rate * weight
    )
    return (second_new, updated)


def matmul(left, right):
    return jnp.dot(left, right, preferred_element_type=WIDE)


def contract_rows(left, right):
    return lax.dot_general(left, right, (((0,), (0,)), ((), ())), preferred_element_type=WIDE)


def times_transpose(left, right):
    return lax.dot_general(left, right, (((1,), (1,)), ((), ())), preferred_element_type=WIDE)


def flip(value):
    return value.astype(WIDE).T


def norm_stats(value):
    centered = value - jnp.mean(value, axis=-1, keepdims=True)
    variance = jnp.mean(centered * centered, axis=-1, keepdims=True)
    scale = lax.rsqrt(variance + NORM_EPS)
    return centered * scale, scale


def norm_back(grad, gain, unit, scale):
    scaled = grad * gain
    return scale * (
        scaled
        - jnp.mean(scaled, axis=-1, keepdims=True)
        - unit * jnp.mean(scaled * unit, axis=-1, keepdims=True)
    )


def load_pieces(coords, picks, pieces, target, sems, first=0):
    rows = target.shape[4]
    side, y_here, x_here = coords[0], coords[1], coords[2]
    squares = target.shape[2] * target.shape[3]
    per_side = len(pieces) // 2
    half = pieces[0].shape[2]
    copies = []
    for place, pick in enumerate(picks):
        for number, source in enumerate(pieces):
            which, order = divmod(number, per_side)
            start = pl.multiple_of((side if which == 0 else 1 - side) * half, half)
            if squares == 1:
                planes, y_at, x_at = pl.ds(0, 1), 0, 0
            else:
                y_at = 1 - y_here if order >= 2 else y_here
                x_at = 1 - x_here if order in (1, 3, 4) else x_here
                low = pieces[3].shape[0]
                planes = pl.ds(low if order == 4 else 0, source.shape[0])
            copies.append(
                pltpu.make_async_copy(
                    source.at[:, pl.ds(pick * rows, rows), :],
                    target.at[place, planes, y_at, x_at, :, pl.ds(start, half)],
                    sems.at[first + len(copies)],
                )
            )
    return copies


def load_now(copies):
    for copy in copies:
        copy.start()
    for copy in copies:
        copy.wait()


def flat(target, place=0):
    _, planes, high, wide, rows, width = target.shape
    return target.at[place].reshape(planes * high * wide * rows, width)


def store_pieces(coords, keep_out, send_out, read, place=None):
    side, y_here, x_here = coords[0], coords[1], coords[2]
    squares, planes = keep_out.shape[:2]
    rows = keep_out.shape[-2]
    half = keep_out.shape[-1]
    for out, own_side in ((keep_out, side), (send_out, 1 - side)):
        columns = pl.ds(pl.multiple_of(own_side * half, half), half)
        for square in range(squares):
            for plane in range(planes):
                if squares == 1:
                    block = plane
                else:
                    y_at = 1 - y_here if square >= 2 else y_here
                    x_at = 1 - x_here if square % 2 else x_here
                    block = (plane * 2 + y_at) * 2 + x_at
                part = read(pl.ds(pl.multiple_of(block * rows, rows), rows), columns).astype(LOW)
                if place is None:
                    out[square, plane] = part
                else:
                    out[square, plane, place] = part


def head_masks():
    lane = lax.broadcasted_iota(jnp.int32, (1, PAIR), 1)
    return [lane < HEAD, lane >= HEAD]


def only(value, mask):
    return jnp.where(mask, value, 0.0).astype(LOW)


def attend_kernel(sequence, pieces, earlier, *refs):
    lengths, coords, tokens, vec = refs[:4]
    sources = refs[4 : 4 + pieces]
    query_out, key_out, value_out, mixed_out, sum_out, norm_out = refs[
        4 + pieces + earlier : 10 + pieces + earlier
    ]
    weights, value_flip, mixed_flip, sems = refs[10 + pieces + earlier :]
    copies = load_pieces(coords, range(4), sources, weights, sems)
    for copy in copies:
        copy.start()

    def need(place):
        for copy in copies[place * pieces : (place + 1) * pieces]:
            copy.wait()

    length = lengths[sequence]
    rows = tokens[...]
    need(0)
    query_out[...] = (matmul(rows, flat(weights, 0)[...]) + vec[0:1, :]).astype(LOW)
    need(1)
    key_out[...] = matmul(rows, flat(weights, 1)[...]).astype(LOW)
    need(2)
    value_low = (matmul(rows, flat(weights, 2)[...]) + vec[1:2, :]).astype(LOW)
    value_out[...] = value_low
    value_flip[...] = flip(value_low).astype(LOW)
    size = tokens.shape[0]
    key_valid = lax.broadcasted_iota(jnp.int32, (size, size), 0) < length
    masks = head_masks()

    def one_pair(pair, carry):
        lanes = pl.ds(pl.multiple_of(pair * PAIR, PAIR), PAIR)
        keys = key_out[:, lanes]
        queries = query_out[:, lanes].astype(WIDE) * SCORE_SCALE
        mixed, norms = [], []
        for head in range(2):
            scores = times_transpose(keys, only(queries, masks[head]))
            scores = jnp.where(key_valid, scores, MASK_FILL)
            peak = jnp.max(scores, axis=0, keepdims=True)
            exponent = jnp.exp(scores - peak)
            total = jnp.sum(exponent, axis=0, keepdims=True)
            prob = (exponent * (1.0 / total)).astype(LOW)
            start = pl.multiple_of(pair * PAIR + head * HEAD, HEAD)
            mixed.append(matmul(value_flip[pl.ds(start, HEAD), :], prob))
            norms.append(peak + jnp.log(total))
        mixed_flip[lanes, :] = jnp.concatenate(mixed, axis=0)
        norm_out[0, pair] = jnp.concatenate(norms, axis=0)
        return carry

    lax.fori_loop(0, PAIRS, one_pair, 0)
    need(3)
    mixed_low = mixed_flip[...].T.astype(LOW)
    mixed_out[...] = mixed_low
    sum_out[...] = rows.astype(WIDE) + matmul(mixed_low, flat(weights, 3)[...]) + vec[2:3, :]


def ffn_kernel(inner_pieces, outer_pieces, *refs):
    coords, first_sum, cotangent, vec, bias = refs[:5]
    inner_from = refs[5 : 5 + inner_pieces]
    outer_from = refs[5 + inner_pieces : 5 + inner_pieces + outer_pieces]
    result_out, second_out, hidden_out, keep_out, send_out, vec_grad, bias_grad = refs[
        5 + inner_pieces + outer_pieces : 12 + inner_pieces + outer_pieces
    ]
    inner_at, outer_at, total, activated, slope, sems = refs[12 + inner_pieces + outer_pieces :]
    step = pl.program_id(0)

    @pl.when(step == 0)
    def _():
        copies = load_pieces(coords, (0,), inner_from, inner_at, sems) + load_pieces(
            coords, (0,), outer_from, outer_at, sems, inner_pieces
        )
        for copy in copies:
            copy.start()
        vec_grad[...] = jnp.zeros_like(vec_grad)
        bias_grad[...] = jnp.zeros_like(bias_grad)
        total[...] = jnp.zeros_like(total)
        for copy in copies:
            copy.wait()

    inner, outer = flat(inner_at), flat(outer_at)
    unit, _ = norm_stats(first_sum[...])
    normed = unit * vec[4:5, :] + vec[5:6, :]
    normed_low = normed.astype(LOW)
    width, hidden = inner.shape
    second = normed + vec[3:4, :]
    for start in range(0, hidden, width):
        part = slice(start, start + width)
        pre = matmul(normed_low, inner[:, part]) + bias[:, part]
        cdf = 0.5 * (1.0 + lax.erf(pre * ROOT_HALF))
        active = (pre * cdf).astype(LOW)
        activated[:, part] = active
        slope[:, part] = cdf + pre * (DENSITY * jnp.exp(-0.5 * pre * pre))
        second = second + matmul(active, outer[part, :])
    unit_two, scale_two = norm_stats(second)
    result_out[...] = (unit_two * vec[6:7, :] + vec[7:8, :]).astype(LOW)
    grad = cotangent[...].astype(WIDE)
    second_grad = norm_back(grad, vec[6:7, :], unit_two, scale_two)
    second_out[...] = second_grad
    grad_low = second_grad.astype(LOW)
    vec_grad[3:4, :] += jnp.sum(grad_low.astype(WIDE), axis=0, keepdims=True)
    vec_grad[6:7, :] += jnp.sum(grad * unit_two, axis=0, keepdims=True)
    vec_grad[7:8, :] += jnp.sum(grad, axis=0, keepdims=True)
    for start in range(0, hidden, width):
        part = slice(start, start + width)
        back = times_transpose(grad_low, outer[part, :])
        hidden_low = (back * slope[:, part]).astype(LOW)
        hidden_out[:, part] = hidden_low
        bias_grad[:, part] += jnp.sum(hidden_low.astype(WIDE), axis=0, keepdims=True)
        total[part, :] += contract_rows(activated[:, part], grad_low)

    @pl.when(step == pl.num_programs(0) - 1)
    def _():
        store_pieces(coords, keep_out, send_out, lambda r, c: total[r, c])


def inner_grad_kernel(coords, first_sum, hidden_low, vec, keep_out, send_out, total):
    step = pl.program_id(0)

    @pl.when(step == 0)
    def _():
        total[...] = jnp.zeros_like(total)

    unit, _ = norm_stats(first_sum[...])
    normed_flip = flip(unit * vec[4:5, :] + vec[5:6, :]).astype(LOW)
    width, hidden = total.shape
    for start in range(0, hidden, width):
        part = slice(start, start + width)
        total[:, part] += matmul(normed_flip, hidden_low[:, part])

    @pl.when(step == pl.num_programs(0) - 1)
    def _():
        store_pieces(coords, keep_out, send_out, lambda r, c: total[r, c])


def back_kernel(inner_pieces, att_pieces, *refs):
    coords, first_sum, second_grad, hidden_low, mixed, vec = refs[:6]
    inner_from = refs[6 : 6 + inner_pieces]
    att_from = refs[6 + inner_pieces : 6 + inner_pieces + att_pieces]
    first_out, mixed_grad_out, keep_out, send_out, vec_grad = refs[
        6 + inner_pieces + att_pieces : 11 + inner_pieces + att_pieces
    ]
    inner_at, project_at, total, sems = refs[11 + inner_pieces + att_pieces :]
    step = pl.program_id(0)

    @pl.when(step == 0)
    def _():
        copies = load_pieces(coords, (0,), inner_from, inner_at, sems) + load_pieces(
            coords, (3,), att_from, project_at, sems, inner_pieces
        )
        for copy in copies:
            copy.start()
        vec_grad[...] = jnp.zeros_like(vec_grad)
        total[...] = jnp.zeros_like(total)
        for copy in copies:
            copy.wait()

    unit, scale = norm_stats(first_sum[...])
    grad = second_grad[...] + times_transpose(hidden_low[...], flat(inner_at)[...])
    first_grad = norm_back(grad, vec[4:5, :], unit, scale)
    first_out[...] = first_grad
    branch = first_grad.astype(LOW)
    vec_grad[2:3, :] += jnp.sum(branch.astype(WIDE), axis=0, keepdims=True)
    vec_grad[4:5, :] += jnp.sum(grad * unit, axis=0, keepdims=True)
    vec_grad[5:6, :] += jnp.sum(grad, axis=0, keepdims=True)
    mixed_grad_out[...] = times_transpose(branch, flat(project_at)[...]).astype(LOW)
    total[...] += contract_rows(mixed[...], branch)

    @pl.when(step == pl.num_programs(0) - 1)
    def _():
        store_pieces(coords, keep_out, send_out, lambda r, c: total[r, c])


def attend_back_kernel(sequence, last, *refs):
    lengths, coords, tokens, query, key, value, mixed_grad, normalizer = refs[:8]
    count = 3 * sequence if last else 0
    earlier = refs[8 : 8 + count]
    query_out, key_out, value_out = refs[8 + count : 11 + count]
    scratch = refs[11 + count :]
    if last:
        keep_out, send_out, vec_grad = scratch[:3]
        scratch = scratch[3:]
        total = scratch[2]
    key_flip, query_flip = scratch[:2]
    length = lengths[sequence]
    size = query.shape[0]
    key_flip[...] = flip(key[...]).astype(LOW)
    key_valid = lax.broadcasted_iota(jnp.int32, (size, size), 0) < length
    masks = head_masks()

    def one_pair(pair, carry):
        lanes = pl.ds(pl.multiple_of(pair * PAIR, PAIR), PAIR)
        keys = key[:, lanes]
        values = value[:, lanes]
        queries = query[:, lanes].astype(WIDE) * SCORE_SCALE
        grads = mixed_grad[:, lanes].astype(WIDE)
        norms = normalizer[0, pair]
        query_parts, key_part, value_part = [], 0.0, 0.0
        for head in range(2):
            own_query = only(queries, masks[head])
            own_grad = only(grads, masks[head])
            scores = times_transpose(keys, own_query)
            prob = jnp.where(key_valid, jnp.exp(scores - norms[head : head + 1, :]), 0.0)
            prob_grad = times_transpose(values, own_grad)
            row_term = jnp.sum(prob_grad * prob, axis=0, keepdims=True)
            score_low = (prob * (prob_grad - row_term)).astype(LOW)
            value_part = value_part + matmul(prob.astype(LOW), own_grad)
            key_part = key_part + matmul(score_low, own_query)
            start = pl.multiple_of(pair * PAIR + head * HEAD, HEAD)
            query_parts.append(matmul(key_flip[pl.ds(start, HEAD), :], score_low))
        query_flip[lanes, :] = jnp.concatenate(query_parts, axis=0) * SCORE_SCALE
        key_out[:, lanes] = key_part.astype(LOW)
        value_out[:, lanes] = value_part.astype(LOW)
        return carry

    lax.fori_loop(0, PAIRS, one_pair, 0)
    query_out[...] = query_flip[...].T.astype(LOW)
    if not last:
        return
    vec_grad[...] = jnp.zeros_like(vec_grad)
    token_flip = flip(tokens[...]).astype(LOW)
    for place, own in enumerate((query_out, key_out, value_out)):
        grads = [earlier[3 * i + place] for i in range(sequence)] + [own]
        sums = 0.0
        for i, grad in enumerate(grads):
            part = matmul(token_flip[:, i * size : (i + 1) * size], grad[...])
            total[...] = part if i == 0 else total[...] + part
            if place != 1:
                sums = sums + jnp.sum(grad[...].astype(WIDE), axis=0, keepdims=True)
        if place != 1:
            vec_grad[place // 2 : place // 2 + 1, :] = sums
        store_pieces(coords, keep_out, send_out, lambda r, c: total[r, c], place)


def input_kernel(pieces, *refs):
    coords, first_grad, query, key, value = refs[:5]
    sources = refs[5 : 5 + pieces]
    grad_out, weights, sems = refs[5 + pieces :]
    load_now(load_pieces(coords, range(3), sources, weights, sems))
    grad = first_grad[...]
    for place, grads in enumerate((query, key, value)):
        grad = grad + times_transpose(grads[...], flat(weights, place)[...])
    grad_out[...] = grad.astype(grad_out.dtype)


def call(kernel, grid, inputs, outputs, scratch, flops, moved, aliases=None):
    return pl.pallas_call(
        kernel,
        grid=(grid,),
        in_specs=[spec for _, spec in inputs],
        out_specs=[spec for _, _, spec in outputs],
        out_shape=[jax.ShapeDtypeStruct(shape, kind) for shape, kind, _ in outputs],
        scratch_shapes=scratch,
        input_output_aliases=aliases or {},
        compiler_params=pltpu.CompilerParams(
            dimension_semantics=("arbitrary",), vmem_limit_bytes=VMEM_BYTES
        ),
        cost_estimate=pl.CostEstimate(flops=flops, bytes_accessed=moved, transcendentals=0),
    )(*[array for array, _ in inputs])


SCALARS = pl.BlockSpec(memory_space=pltpu.SMEM)
WHERE_IT_IS = pl.BlockSpec(memory_space=pl.ANY)


def tiles(rows, width):
    return pl.BlockSpec((rows, width), lambda i: (i, 0))


def block(number, *shape):
    return pl.BlockSpec(shape, lambda i: (number,) + (0,) * (len(shape) - 1))


def whole(*shape):
    return pl.BlockSpec(shape, lambda i: (0,) * len(shape))


def swap(value, axis, offset=1):
    size = lax.axis_size(axis)
    return lax.ppermute(value, axis, [(i, i ^ offset) for i in range(size)])


def swap_side(value):
    return swap(value, SIDE)


def swap_x(value):
    return swap(value, "ctx_hi")


def swap_y(value):
    return swap(value, "dp_lo")


def together(*arrays):
    return lax.optimization_barrier(arrays)


def in_order(mine, theirs, here, axis):
    return jnp.where(
        here == 0,
        jnp.concatenate([mine, theirs], axis=axis),
        jnp.concatenate([theirs, mine], axis=axis),
    )


def pair_shards(shard, side):
    half = shard.shape[-1] // 2
    axis = shard.ndim - 1
    mine = lax.dynamic_slice_in_dim(shard, side * half, half, axis)
    theirs = lax.dynamic_slice_in_dim(shard, (1 - side) * half, half, axis)
    return in_order(mine, swap_side(theirs), side, shard.ndim - 2)


def gather_planes(value):
    count = lax.axis_size("dp_hi")
    here = lax.axis_index("dp_hi")
    full = jnp.zeros((count,) + value.shape, value.dtype)
    for offset in range(count):
        part = swap(value, "dp_hi", offset) if offset else value
        full = lax.dynamic_update_slice_in_dim(full, part[None], here ^ offset, 0)
    return full


def gather_diagonal(from_x, from_y, low):
    parts = [swap_y(from_x[:low])]
    if low < from_x.shape[0]:
        parts.append(swap_x(from_y[low:]))
    return parts


def wide_sum(*arrays):
    return functools.reduce(lambda a, b: a + b, [a.astype(WIDE) for a in arrays])


class Sum:
    def __init__(self, keep, send, low):
        self.keep, self.low, self.planes = keep, low, keep.shape[1]
        self.recv = swap_side(send)

    def part(self, square, planes):
        return wide_sum(self.keep[square, planes], self.recv[square, planes])

    def first(self):
        lower, upper = slice(0, self.low), slice(self.low, self.planes)
        self.lower, self.upper = lower, upper
        self.split = self.low < self.planes
        out = [self.part(3, lower), self.part(2, lower)]
        if self.split:
            out += [self.part(3, upper), self.part(1, upper)]
        self.ready = [value.astype(LOW) for value in out]
        return self.ready

    def second(self, ready):
        self.diagonal = [swap_y(ready[0])]
        self.from_y = [swap_y(ready[1])]
        self.from_x = []
        if self.split:
            self.diagonal.append(swap_x(ready[2]))
            self.from_x.append(swap_x(ready[3]))
        out = [(self.part(1, self.lower) + self.diagonal[0].astype(WIDE)).astype(LOW)]
        if self.split:
            out.append((self.part(2, self.upper) + self.diagonal[1].astype(WIDE)).astype(LOW))
        return out

    def third(self, ready):
        self.from_x.insert(0, swap_x(ready[0]))
        if self.split:
            self.from_y.append(swap_y(ready[1]))
        runs = [self.lower] + ([self.upper] if self.split else [])
        out = [
            wide_sum(self.part(0, run), from_x, from_y).astype(LOW)
            for run, from_x, from_y in zip(runs, self.from_x, self.from_y)
        ]
        return out[0] if len(out) == 1 else jnp.concatenate(out, axis=0)

    def last(self, ready):
        here = lax.axis_index("dp_hi")
        total = lax.dynamic_index_in_dim(ready, here, 0, keepdims=False).astype(WIDE)
        for offset in range(1, self.planes):
            sent = lax.dynamic_index_in_dim(ready, here ^ offset, 0, keepdims=False)
            total = total + swap(sent, "dp_hi", offset).astype(WIDE)
        return total


def own_rows(total, side):
    rows = total.shape[-2] // 2
    axis = total.ndim - 2
    total = total.astype(LOW)
    mine = lax.dynamic_slice_in_dim(total, side * rows, rows, axis)
    theirs = lax.dynamic_slice_in_dim(total, (1 - side) * rows, rows, axis)
    return in_order(mine, swap_side(theirs), side, total.ndim - 1).astype(WIDE)


def bit_of(bit):
    return (lax.axis_index(ALL) >> bit) & 1


def halve(partial, bit, axis, count):
    mine = bit_of(bit)
    sent = lax.dynamic_index_in_dim(partial, 1 - mine, axis, keepdims=False)
    kept = lax.dynamic_index_in_dim(partial, mine, axis, keepdims=False)
    return kept + lax.ppermute(sent, ALL, [(i, i ^ (1 << bit)) for i in range(count)])


def reduce_small(partial, count):
    bits = count.bit_length() - 1
    partial = partial.reshape((2,) * bits + partial.shape[1:])
    for bit in range(bits):
        partial = halve(partial, bit, bits - 1 - bit, count)
    return partial


def to_sequences(value, parts):
    seqs, here, width = value.shape
    own = seqs // parts
    me = lax.axis_index(CONTEXT)
    full = jnp.zeros((own, parts * here, width), value.dtype)
    for offset in range(parts):
        peer = me ^ offset
        part = lax.dynamic_slice_in_dim(value, peer * own, own, 0)
        if offset:
            part = swap(part, CONTEXT, offset)
        full = lax.dynamic_update_slice_in_dim(full, part, peer * here, 1)
    return full


def to_positions(values, parts):
    own = len(values)
    length, width = values[0].shape
    here = length // parts
    me = lax.axis_index(CONTEXT)
    full = jnp.zeros((own * parts, here, width), values[0].dtype)
    for number, value in enumerate(values):
        for offset in range(parts):
            peer = me ^ offset
            part = lax.dynamic_slice_in_dim(value, peer * here, here, 0)
            if offset:
                part = swap(part, CONTEXT, offset)
            full = lax.dynamic_update_slice(full, part[None], (peer * own + number, 0, 0))
    return full


def local(
    tokens,
    cotangent,
    lengths,
    attention_weights,
    inner_weights,
    outer_weights,
    inner_bias,
    vectors,
    attention_first,
    attention_second,
    inner_first,
    inner_second,
    outer_moment_first,
    outer_second,
    bias_first,
    bias_second,
    vector_first,
    vector_second,
):
    parts = lax.axis_size(CONTEXT)
    planes = lax.axis_size("dp_hi")
    chips = lax.axis_size(CHIPS)
    count = 2 * chips
    side = lax.axis_index(SIDE)
    coords = jnp.stack([side, lax.axis_index("dp_lo"), lax.axis_index("ctx_hi")]).astype(
        jnp.int32
    )
    seq_count, local_len, width = tokens.shape
    hidden = inner_weights.shape[1]
    full_len = local_len * parts
    own_seqs = seq_count // parts
    rows = own_seqs * full_len
    att_rows, vec_cols, bias_cols = (
        attention_weights.shape[1],
        vectors.shape[1],
        inner_bias.shape[0],
    )
    half = width // 2
    tall = 16
    in_pieces = (2 * att_rows) % tall == 0
    if in_pieces:
        dims, squares = (planes, 2, 2), 4
        att_block, inner_block, outer_block = (
            2 * att_rows,
            2 * inner_weights.shape[0],
            2 * outer_weights.shape[0],
        )
    else:
        dims, squares = (1, 1, 1), 1
        att_block, inner_block, outer_block = width, width, hidden

    small = jnp.concatenate([vectors.reshape(-1), inner_bias]).astype(LOW)
    small_size = small.shape[0]
    small = jnp.pad(small.reshape(1, -1), ((0, tall - 1), (0, half - small_size)))
    small_row = 8 * att_rows
    token_rows = to_sequences(tokens, parts).reshape(rows, width)
    att_pair = pair_shards(attention_weights.astype(LOW), side).reshape(small_row, half)
    att_pair = jnp.concatenate([att_pair, small], axis=0)
    inner_pair = pair_shards(inner_weights.astype(LOW), side)
    outer_pair = pair_shards(outer_weights.astype(LOW), side)
    if in_pieces:
        att = gather_planes(att_pair)
        inner = gather_planes(inner_pair)
        outer = gather_planes(outer_pair)
        att_x, att_y = swap_x(att), swap_y(att)
        att_x, att_y, token_rows = together(att_x, att_y, token_rows)
        att_mine = [att, att_x, att_y] + gather_diagonal(att_x, att_y, planes // 2)
        att_all = att_mine + [swap_side(piece) for piece in att_mine]
        token_rows, inner, outer = together(token_rows, inner, outer)
        inner_x, inner_y = swap_x(inner), swap_y(inner)
        outer_x, outer_y = swap_x(outer), swap_y(outer)

        def small_of(pieces):
            own, from_x, from_y = [
                piece[:, None, None, small_row, :small_size] for piece in pieces[:3]
            ]
            diagonal = jnp.concatenate(
                [piece[:, None, None, small_row, :small_size] for piece in pieces[3:]], axis=0
            )
            x_here, y_here = coords[2], coords[1]
            return in_order(
                in_order(own, from_x, x_here, 2), in_order(from_y, diagonal, x_here, 2), y_here, 1
            ).reshape(chips, 1, small_size)

        small_all = in_order(
            small_of(att_mine), small_of(att_all[len(att_mine) :]), side, 1
        )
    else:
        att = lax.all_gather(att_pair, CHIPS, axis=0, tiled=False)
        inner = lax.all_gather(inner_pair, CHIPS, axis=0, tiled=True)[None]
        outer = lax.all_gather(outer_pair, CHIPS, axis=0, tiled=True)[None]
        small_mine = att[:, None, small_row, :small_size]
        small_all = in_order(small_mine, swap_side(small_mine), side, 1)
        att = att[:, :small_row].reshape(chips, 4, 2 * att_rows, half)
        att = att.transpose(1, 0, 2, 3).reshape(1, 4 * width, half)
        att_all, inner_all, outer_all = [
            [value, swap_side(value)] for value in (att, inner, outer)
        ]
    small_all = small_all.reshape(count, small_size).astype(WIDE)
    vec = (
        small_all[:, : 8 * vec_cols].reshape(count, 8, vec_cols).transpose(1, 0, 2).reshape(8, -1)
    )
    bias = small_all[:, 8 * vec_cols :].reshape(1, -1)
    own_lengths = lax.dynamic_slice_in_dim(lengths, lax.axis_index(CONTEXT) * own_seqs, own_seqs)

    def in_place(pieces):
        return [(piece, WHERE_IT_IS) for piece in pieces]

    norm_shape = (own_seqs, PAIRS, 2, full_len)
    low_rows = (rows, width)
    vec_spec = whole(8, width)
    square = 2 * rows * width * width
    attend_flops = 8 * rows * full_len * width

    held = []
    for number in range(own_seqs):
        own_rows_spec = block(number, full_len, width)
        inputs = [
            (own_lengths, SCALARS),
            (coords, SCALARS),
            (token_rows, own_rows_spec),
            (vec, vec_spec),
        ] + in_place(att_all)
        held = call(
            functools.partial(attend_kernel, number, len(att_all), len(held)),
            1,
            inputs + in_place(held),
            [(low_rows, LOW, own_rows_spec)] * 4
            + [
                (low_rows, WIDE, own_rows_spec),
                (norm_shape, WIDE, block(number, 1, PAIRS, 2, full_len)),
            ],
            [
                pltpu.VMEM((4,) + dims + (att_block, width), LOW),
                pltpu.VMEM((width, full_len), LOW),
                pltpu.VMEM((width, full_len), WIDE),
                pltpu.SemaphoreType.DMA((4 * len(att_all),)),
            ],
            (4 * square + 2 * attend_flops) // own_seqs,
            20 * rows * width // own_seqs,
            {len(inputs) + i: i for i in range(len(held))},
        )
        if in_pieces and number == 0:
            *held, inner_x, inner_y, outer_x, outer_y = together(
                *held, inner_x, inner_y, outer_x, outer_y
            )
            inner_all = [inner, inner_x, inner_y] + gather_diagonal(inner_x, inner_y, planes)
            outer_all = [outer, outer_x, outer_y] + gather_diagonal(outer_x, outer_y, planes)
            inner_all = inner_all + [swap_side(piece) for piece in inner_all]
            outer_all = outer_all + [swap_side(piece) for piece in outer_all]
    query, key, value, mixed, first_sum, normalizer = held
    cot_rows = to_sequences(cotangent.astype(LOW), parts).reshape(rows, width)

    def grad_pieces(rows_here, columns, matrices=None):
        lead = (squares, dims[0]) + ((matrices,) if matrices else ())
        shape = lead + (rows_here, columns)
        return [(shape, LOW, whole(*shape))] * 2

    tile = 256
    row_tile = tiles(tile, width)
    hidden_tile = tiles(tile, hidden)
    result, second_grad, hidden_low, outer_keep, outer_send, vec_ffn, bias_grad = call(
        functools.partial(ffn_kernel, len(inner_all), len(outer_all)),
        rows // tile,
        [
            (coords, SCALARS),
            (first_sum, row_tile),
            (cot_rows, row_tile),
            (vec, vec_spec),
            (bias, whole(1, hidden)),
        ]
        + in_place(inner_all)
        + in_place(outer_all),
        [
            (low_rows, LOW, row_tile),
            (low_rows, WIDE, row_tile),
            ((rows, hidden), LOW, hidden_tile),
        ]
        + grad_pieces(outer_block, half)
        + [((8, width), WIDE, vec_spec), ((1, hidden), WIDE, whole(1, hidden))],
        [
            pltpu.VMEM((1,) + dims + (inner_block, hidden), LOW),
            pltpu.VMEM((1,) + dims + (outer_block, width), LOW),
            pltpu.VMEM((hidden, width), WIDE),
            pltpu.VMEM((tile, hidden), LOW),
            pltpu.VMEM((tile, hidden), WIDE),
            pltpu.SemaphoreType.DMA((len(inner_all) + len(outer_all),)),
        ],
        16 * square + 60 * rows * hidden,
        30 * rows * width,
    )
    output_tokens = to_positions(list(result.reshape(own_seqs, full_len, width)), parts)

    inner_keep, inner_send = call(
        inner_grad_kernel,
        rows // tile,
        [
            (coords, SCALARS),
            (first_sum, row_tile),
            (hidden_low, hidden_tile),
            (vec, vec_spec),
        ],
        grad_pieces(inner_block, hidden // 2),
        [pltpu.VMEM((width, hidden), WIDE)],
        4 * square,
        18 * rows * width,
    )
    if in_pieces:
        outer_sum = Sum(outer_keep, outer_send, planes)
        outer_ready = outer_sum.first()
        *outer_ready, second_grad, inner_send = together(*outer_ready, second_grad, inner_send)

    first_grad, mixed_grad, project_keep, project_send, vec_mid = call(
        functools.partial(back_kernel, len(inner_all), len(att_all)),
        rows // tile,
        [
            (coords, SCALARS),
            (first_sum, row_tile),
            (second_grad, row_tile),
            (hidden_low, hidden_tile),
            (mixed, row_tile),
            (vec, vec_spec),
        ]
        + in_place(inner_all)
        + in_place(att_all),
        [(low_rows, WIDE, row_tile), (low_rows, LOW, row_tile)]
        + grad_pieces(att_block, half)
        + [((8, width), WIDE, vec_spec)],
        [
            pltpu.VMEM((1,) + dims + (inner_block, hidden), LOW),
            pltpu.VMEM((1,) + dims + (att_block, width), LOW),
            pltpu.VMEM((width, width), WIDE),
            pltpu.SemaphoreType.DMA((len(inner_all) + len(att_all),)),
        ],
        6 * square,
        24 * rows * width,
    )
    if in_pieces:
        outer_ready = outer_sum.second(outer_ready)
        inner_sum = Sum(inner_keep, inner_send, planes)
        inner_ready = inner_sum.first()
        mixed_grad, *ready = together(mixed_grad, *outer_ready, *inner_ready)
        outer_ready, inner_ready = ready[: len(outer_ready)], ready[len(outer_ready) :]

    grads = []
    for number in range(own_seqs):
        last = number == own_seqs - 1
        own_rows_spec = block(number, full_len, width)
        seq_shape = (full_len, width)
        earlier = [value for three in grads for value in three] if last else []
        outputs = [(seq_shape, LOW, whole(*seq_shape))] * 3
        scratch = [pltpu.VMEM((width, full_len), LOW), pltpu.VMEM((width, full_len), WIDE)]
        if last:
            outputs = (
                outputs + grad_pieces(att_block, half, 3) + [((8, width), WIDE, vec_spec)]
            )
            scratch = scratch + [pltpu.VMEM((width, width), WIDE)]
        three = call(
            functools.partial(attend_back_kernel, number, last),
            1,
            [
                (own_lengths, SCALARS),
                (coords, SCALARS),
                (token_rows, whole(rows, width)),
                (query, own_rows_spec),
                (key, own_rows_spec),
                (value, own_rows_spec),
                (mixed_grad, own_rows_spec),
                (normalizer, block(number, 1, PAIRS, 2, full_len)),
            ]
            + [(value_, whole(*seq_shape)) for value_ in earlier],
            outputs,
            scratch,
            5 * attend_flops // own_seqs + (3 * square if last else 0),
            20 * rows * width // own_seqs,
        )
        grads.append(list(three[:3]))
        if in_pieces and number == 0:
            outer_ready = outer_sum.third(outer_ready)
            inner_ready = inner_sum.second(inner_ready)
            project_sum = Sum(project_keep, project_send, planes)
            project_ready = project_sum.first()
            mixed_grad, grads[0][0], outer_ready, *ready = together(
                mixed_grad, grads[0][0], outer_ready, *inner_ready, *project_ready
            )
            inner_ready, project_ready = ready[: len(inner_ready)], ready[len(inner_ready) :]
    att_keep, att_send, vec_att = three[3:]

    if in_pieces:
        att_sum = Sum(att_keep, att_send, planes // 2)
        att_total = att_sum.last(att_sum.third(att_sum.second(att_sum.first())))
        outer_total = outer_sum.last(outer_ready)
        inner_total = inner_sum.last(inner_sum.third(inner_ready))
        project_total = project_sum.last(project_sum.third(project_sum.second(project_ready)))
    else:

        def scatter(keep, send):
            partial = (keep + swap_side(send)).reshape((-1,) + keep.shape[-2:])
            matrices, length, columns = partial.shape
            partial = partial.reshape(matrices, chips, length // chips, columns)
            return lax.psum_scatter(
                partial.transpose(1, 0, 2, 3), CHIPS, scatter_dimension=0, tiled=False
            )

        att_total = scatter(att_keep, att_send)
        outer_total = scatter(outer_keep, outer_send)[0]
        inner_total = scatter(inner_keep, inner_send)[0]
        project_total = scatter(project_keep, project_send)[0]
    attention_total = jnp.concatenate(
        [own_rows(att_total, side), own_rows(project_total, side)[None]], axis=0
    )
    inner_total = own_rows(inner_total, side)
    outer_total = own_rows(outer_total, side)

    vector_grad = vec_ffn + vec_mid + vec_att
    small_grad = jnp.concatenate(
        [
            vector_grad.reshape(8, count, vec_cols).transpose(1, 0, 2).reshape(count, -1),
            bias_grad.reshape(count, bias_cols),
        ],
        axis=1,
    )
    small_total = reduce_small(small_grad, count)
    vector_total = small_total[: 8 * vec_cols].reshape(8, vec_cols)
    bias_total = small_total[8 * vec_cols :]

    input_grads = []
    for number in range(own_seqs):
        seq_shape = (full_len, width)
        (grad,) = call(
            functools.partial(input_kernel, len(att_all)),
            1,
            [(coords, SCALARS), (first_grad, block(number, full_len, width))]
            + [(value_, whole(*seq_shape)) for value_ in grads[number]]
            + in_place(att_all),
            [(seq_shape, LOW, whole(*seq_shape))],
            [
                pltpu.VMEM((3,) + dims + (att_block, width), LOW),
                pltpu.SemaphoreType.DMA((3 * len(att_all),)),
            ],
            3 * square // own_seqs,
            12 * rows * width // own_seqs,
        )
        input_grads.append(grad)
    input_grad = to_positions(input_grads, parts).astype(WIDE)

    attention_square, attention_new = adam_step(
        attention_weights,
        attention_total,
        attention_first,
        attention_second,
        MATRIX_LEARN_RATE,
        WEIGHT_DECAY,
    )
    inner_square, inner_new = adam_step(
        inner_weights, inner_total, inner_first, inner_second, MATRIX_LEARN_RATE, WEIGHT_DECAY
    )
    outer_square, outer_new = adam_step(
        outer_weights,
        outer_total,
        outer_moment_first,
        outer_second,
        MATRIX_LEARN_RATE,
        WEIGHT_DECAY,
    )
    bias_square, bias_new = adam_step(
        inner_bias, bias_total, bias_first, bias_second, VECTOR_RATE, 0.0
    )
    vector_square, vector_new = adam_step(
        vectors, vector_total, vector_first, vector_second, VECTOR_RATE, 0.0
    )
    return (
        output_tokens,
        input_grad,
        attention_total,
        attention_square,
        attention_new,
        inner_total,
        inner_square,
        inner_new,
        outer_total,
        outer_square,
        outer_new,
        bias_total,
        bias_square,
        bias_new,
        vector_total,
        vector_square,
        vector_new,
    )


def solution(mesh):
    split = Mesh(
        np.asarray(mesh.devices).reshape(
            mesh.shape["dp"] // 2, 2, mesh.shape["context"] // 2, 2
        ),
        ALL,
    )
    dp = ("dp_hi", "dp_lo")
    rows3 = P(dp, CONTEXT, None)
    mid3 = P(None, ALL, None)
    row2 = P(ALL, None)
    col2 = P(None, ALL)
    one = P(ALL)
    return jax.shard_map(
        local,
        mesh=split,
        in_specs=(rows3, rows3, P(dp), mid3, row2, row2, one, col2)
        + (mid3, mid3, row2, row2, row2, row2, one, one, col2, col2),
        out_specs=(rows3, rows3)
        + (mid3,) * 3
        + (row2,) * 6
        + (one,) * 3
        + (col2,) * 3,
        check_vma=False,
    )
```

```python
import functools

import jax
import jax.numpy as jnp
import numpy as np
from jax import lax
from jax.experimental import pallas as pl
from jax.experimental.pallas import tpu as pltpu
from jax.sharding import Mesh, PartitionSpec as P

HEADS = 12
HEAD = 64
PAIR = 2 * HEAD
PAIRS = HEADS // 2
STEP = 10

NORM_EPS = 1e-12
BETA_ONE = 0.9
BETA_TWO = 0.999
ADAM_EPS = 1e-06
MATRIX_LEARN_RATE = 0.05
VECTOR_RATE = 0.5
WEIGHT_DECAY = 0.01
MASK_FILL = -1e30
SCORE_SCALE = HEAD ** (-0.5)
ROOT_HALF = 0.5**0.5
DENSITY = 0.3989422804014327

CHIPS = ("dp_hi", "dp_lo", "ctx_hi")
SIDE = "ctx_lo"
ALL = CHIPS + (SIDE,)
CONTEXT = ("ctx_hi", "ctx_lo")
LOW = jnp.bfloat16
WIDE = jnp.float32
VMEM_BYTES = 60 * 1024 * 1024


def adam_step(weight, gradient, moment_one, moment_two, step_rate, decay_rate):
    first_new = BETA_ONE * moment_one + (1.0 - BETA_ONE) * gradient
    second_new = BETA_TWO * moment_two + (1.0 - BETA_TWO) * gradient * gradient
    first_hat = first_new / (1.0 - BETA_ONE**STEP)
    second_hat = second_new / (1.0 - BETA_TWO**STEP)
    updated = weight - step_rate * (
        first_hat / (jnp.sqrt(second_hat) + ADAM_EPS) + decay_rate * weight
    )
    return (second_new, updated)


def matmul(left, right):
    return jnp.dot(left, right, preferred_element_type=WIDE)


def contract_rows(left, right):
    return lax.dot_general(left, right, (((0,), (0,)), ((), ())), preferred_element_type=WIDE)


def times_transpose(left, right):
    return lax.dot_general(left, right, (((1,), (1,)), ((), ())), preferred_element_type=WIDE)


def flip(value):
    return value.astype(WIDE).T


def norm_stats(value):
    centered = value - jnp.mean(value, axis=-1, keepdims=True)
    variance = jnp.mean(centered * centered, axis=-1, keepdims=True)
    scale = lax.rsqrt(variance + NORM_EPS)
    return centered * scale, scale


def norm_back(grad, gain, unit, scale):
    scaled = grad * gain
    return scale * (
        scaled
        - jnp.mean(scaled, axis=-1, keepdims=True)
        - unit * jnp.mean(scaled * unit, axis=-1, keepdims=True)
    )


def load_pieces(coords, picks, pieces, layout, target, sems, first=0):
    rows = target.shape[4]
    side, y_here, x_here = coords[0], coords[1], coords[2]
    single = target.shape[2] == 1
    half = pieces[0].shape[-1]
    copies = []
    for place, pick in enumerate(picks):
        for number, source in enumerate(pieces):
            which, order = divmod(number, len(layout))
            y_other, x_other, plane, planes = layout[order]
            start = pl.multiple_of((side if which == 0 else 1 - side) * half, half)
            y_at = 0 if single else (1 - y_here if y_other else y_here)
            run = pl.ds(plane, planes)
            part, columns = pl.ds(pick * rows, rows), pl.ds(start, half)
            if x_other is None:
                source = source.at[:, :, part, :]
                goal = target.at[place, run, y_at, :, :, columns]
            else:
                x_at = 0 if single else (1 - x_here if x_other else x_here)
                source = source.at[:, part, :]
                goal = target.at[place, run, y_at, x_at, :, columns]
            copies.append(pltpu.make_async_copy(source, goal, sems.at[first + len(copies)]))
    return copies


def load_now(copies):
    for copy in copies:
        copy.start()
    for copy in copies:
        copy.wait()


def flat(target, place=0):
    _, planes, high, wide, rows, width = target.shape
    return target.at[place].reshape(planes * high * wide * rows, width)


def store_pieces(coords, keep_out, send_out, read, place=None):
    side, y_here, x_here = coords[0], coords[1], coords[2]
    squares, planes = keep_out.shape[:2]
    rows = keep_out.shape[-2]
    half = keep_out.shape[-1]
    for out, own_side in ((keep_out, side), (send_out, 1 - side)):
        columns = pl.ds(pl.multiple_of(own_side * half, half), half)
        for square in range(squares):
            for plane in range(planes):
                if squares == 1:
                    block = plane
                else:
                    y_at = 1 - y_here if square >= 2 else y_here
                    x_at = 1 - x_here if square % 2 else x_here
                    block = (plane * 2 + y_at) * 2 + x_at
                part = read(pl.ds(pl.multiple_of(block * rows, rows), rows), columns).astype(LOW)
                if place is None:
                    out[square, plane] = part
                else:
                    out[square, plane, place] = part


def head_masks():
    lane = lax.broadcasted_iota(jnp.int32, (1, PAIR), 1)
    return [lane < HEAD, lane >= HEAD]


def only(value, mask):
    return jnp.where(mask, value, 0.0).astype(LOW)


def attend_kernel(sequence, layout, earlier, *refs):
    pieces = 2 * len(layout)
    lengths, coords, tokens, vec = refs[:4]
    sources = refs[4 : 4 + pieces]
    query_out, key_out, value_out, mixed_out, sum_out, norm_out = refs[
        4 + pieces + earlier : 10 + pieces + earlier
    ]
    weights, value_flip, mixed_flip, sems = refs[10 + pieces + earlier :]
    copies = load_pieces(coords, range(4), sources, layout, weights, sems)
    for copy in copies:
        copy.start()

    def need(place):
        for copy in copies[place * pieces : (place + 1) * pieces]:
            copy.wait()

    length = lengths[sequence]
    rows = tokens[...]
    need(0)
    query_out[...] = (matmul(rows, flat(weights, 0)[...]) + vec[0:1, :]).astype(LOW)
    need(1)
    key_out[...] = matmul(rows, flat(weights, 1)[...]).astype(LOW)
    need(2)
    value_low = (matmul(rows, flat(weights, 2)[...]) + vec[1:2, :]).astype(LOW)
    value_out[...] = value_low
    value_flip[...] = flip(value_low).astype(LOW)
    size = tokens.shape[0]
    key_valid = lax.broadcasted_iota(jnp.int32, (size, size), 0) < length
    masks = head_masks()

    def one_pair(pair, carry):
        lanes = pl.ds(pl.multiple_of(pair * PAIR, PAIR), PAIR)
        keys = key_out[:, lanes]
        queries = query_out[:, lanes].astype(WIDE) * SCORE_SCALE
        mixed, norms = [], []
        for head in range(2):
            scores = times_transpose(keys, only(queries, masks[head]))
            scores = jnp.where(key_valid, scores, MASK_FILL)
            peak = jnp.max(scores, axis=0, keepdims=True)
            exponent = jnp.exp(scores - peak)
            total = jnp.sum(exponent, axis=0, keepdims=True)
            prob = (exponent * (1.0 / total)).astype(LOW)
            start = pl.multiple_of(pair * PAIR + head * HEAD, HEAD)
            mixed.append(matmul(value_flip[pl.ds(start, HEAD), :], prob))
            norms.append(peak + jnp.log(total))
        mixed_flip[lanes, :] = jnp.concatenate(mixed, axis=0)
        norm_out[0, pair] = jnp.concatenate(norms, axis=0)
        return carry

    lax.fori_loop(0, PAIRS, one_pair, 0)
    need(3)
    mixed_low = mixed_flip[...].T.astype(LOW)
    mixed_out[...] = mixed_low
    sum_out[...] = rows.astype(WIDE) + matmul(mixed_low, flat(weights, 3)[...]) + vec[2:3, :]


def ffn_kernel(inner_layout, outer_layout, *refs):
    inner_pieces, outer_pieces = 2 * len(inner_layout), 2 * len(outer_layout)
    coords, first_sum, cotangent, vec, bias = refs[:5]
    inner_from = refs[5 : 5 + inner_pieces]
    outer_from = refs[5 + inner_pieces : 5 + inner_pieces + outer_pieces]
    result_out, second_out, hidden_out, keep_out, send_out, vec_grad, bias_grad = refs[
        5 + inner_pieces + outer_pieces : 12 + inner_pieces + outer_pieces
    ]
    inner_at, outer_at, total, activated, slope, sems = refs[12 + inner_pieces + outer_pieces :]
    step = pl.program_id(0)

    @pl.when(step == 0)
    def _():
        copies = load_pieces(
            coords, (0,), inner_from, inner_layout, inner_at, sems
        ) + load_pieces(coords, (0,), outer_from, outer_layout, outer_at, sems, inner_pieces)
        for copy in copies:
            copy.start()
        vec_grad[...] = jnp.zeros_like(vec_grad)
        bias_grad[...] = jnp.zeros_like(bias_grad)
        total[...] = jnp.zeros_like(total)
        for copy in copies:
            copy.wait()

    inner, outer = flat(inner_at), flat(outer_at)
    unit, _ = norm_stats(first_sum[...])
    normed = unit * vec[4:5, :] + vec[5:6, :]
    normed_low = normed.astype(LOW)
    width, hidden = inner.shape
    second = normed + vec[3:4, :]
    for start in range(0, hidden, width):
        part = slice(start, start + width)
        pre = matmul(normed_low, inner[:, part]) + bias[:, part]
        cdf = 0.5 * (1.0 + lax.erf(pre * ROOT_HALF))
        active = (pre * cdf).astype(LOW)
        activated[:, part] = active
        slope[:, part] = cdf + pre * (DENSITY * jnp.exp(-0.5 * pre * pre))
        second = second + matmul(active, outer[part, :])
    unit_two, scale_two = norm_stats(second)
    result_out[...] = (unit_two * vec[6:7, :] + vec[7:8, :]).astype(LOW)
    grad = cotangent[...].astype(WIDE)
    second_grad = norm_back(grad, vec[6:7, :], unit_two, scale_two)
    second_out[...] = second_grad
    grad_low = second_grad.astype(LOW)
    vec_grad[3:4, :] += jnp.sum(grad_low.astype(WIDE), axis=0, keepdims=True)
    vec_grad[6:7, :] += jnp.sum(grad * unit_two, axis=0, keepdims=True)
    vec_grad[7:8, :] += jnp.sum(grad, axis=0, keepdims=True)
    for start in range(0, hidden, width):
        part = slice(start, start + width)
        back = times_transpose(grad_low, outer[part, :])
        hidden_low = (back * slope[:, part]).astype(LOW)
        hidden_out[:, part] = hidden_low
        bias_grad[:, part] += jnp.sum(hidden_low.astype(WIDE), axis=0, keepdims=True)
        total[part, :] += contract_rows(activated[:, part], grad_low)

    @pl.when(step == pl.num_programs(0) - 1)
    def _():
        store_pieces(coords, keep_out, send_out, lambda r, c: total[r, c])


def inner_grad_kernel(coords, first_sum, hidden_low, vec, keep_out, send_out, total):
    step = pl.program_id(0)

    @pl.when(step == 0)
    def _():
        total[...] = jnp.zeros_like(total)

    unit, _ = norm_stats(first_sum[...])
    normed_flip = flip(unit * vec[4:5, :] + vec[5:6, :]).astype(LOW)
    width, hidden = total.shape
    for start in range(0, hidden, width):
        part = slice(start, start + width)
        total[:, part] += matmul(normed_flip, hidden_low[:, part])

    @pl.when(step == pl.num_programs(0) - 1)
    def _():
        store_pieces(coords, keep_out, send_out, lambda r, c: total[r, c])


def back_kernel(inner_layout, att_layout, *refs):
    inner_pieces, att_pieces = 2 * len(inner_layout), 2 * len(att_layout)
    coords, first_sum, second_grad, hidden_low, mixed, vec = refs[:6]
    inner_from = refs[6 : 6 + inner_pieces]
    att_from = refs[6 + inner_pieces : 6 + inner_pieces + att_pieces]
    first_out, mixed_grad_out, keep_out, send_out, vec_grad = refs[
        6 + inner_pieces + att_pieces : 11 + inner_pieces + att_pieces
    ]
    inner_at, project_at, total, sems = refs[11 + inner_pieces + att_pieces :]
    step = pl.program_id(0)

    @pl.when(step == 0)
    def _():
        copies = load_pieces(
            coords, (0,), inner_from, inner_layout, inner_at, sems
        ) + load_pieces(coords, (3,), att_from, att_layout, project_at, sems, inner_pieces)
        for copy in copies:
            copy.start()
        vec_grad[...] = jnp.zeros_like(vec_grad)
        total[...] = jnp.zeros_like(total)
        for copy in copies:
            copy.wait()

    unit, scale = norm_stats(first_sum[...])
    grad = second_grad[...] + times_transpose(hidden_low[...], flat(inner_at)[...])
    first_grad = norm_back(grad, vec[4:5, :], unit, scale)
    first_out[...] = first_grad
    branch = first_grad.astype(LOW)
    vec_grad[2:3, :] += jnp.sum(branch.astype(WIDE), axis=0, keepdims=True)
    vec_grad[4:5, :] += jnp.sum(grad * unit, axis=0, keepdims=True)
    vec_grad[5:6, :] += jnp.sum(grad, axis=0, keepdims=True)
    mixed_grad_out[...] = times_transpose(branch, flat(project_at)[...]).astype(LOW)
    total[...] += contract_rows(mixed[...], branch)

    @pl.when(step == pl.num_programs(0) - 1)
    def _():
        store_pieces(coords, keep_out, send_out, lambda r, c: total[r, c])


def attend_back_kernel(sequence, last, *refs):
    lengths, coords, tokens, query, key, value, mixed_grad, normalizer = refs[:8]
    count = 3 * sequence if last else 0
    earlier = refs[8 : 8 + count]
    query_out, key_out, value_out = refs[8 + count : 11 + count]
    scratch = refs[11 + count :]
    if last:
        keep_out, send_out, vec_grad = scratch[:3]
        scratch = scratch[3:]
        total = scratch[2]
    key_flip, query_flip = scratch[:2]
    length = lengths[sequence]
    size = query.shape[0]
    key_flip[...] = flip(key[...]).astype(LOW)
    key_valid = lax.broadcasted_iota(jnp.int32, (size, size), 0) < length
    masks = head_masks()

    def one_pair(pair, carry):
        lanes = pl.ds(pl.multiple_of(pair * PAIR, PAIR), PAIR)
        keys = key[:, lanes]
        values = value[:, lanes]
        queries = query[:, lanes].astype(WIDE) * SCORE_SCALE
        grads = mixed_grad[:, lanes].astype(WIDE)
        norms = normalizer[0, pair]
        query_parts, key_part, value_part = [], 0.0, 0.0
        for head in range(2):
            own_query = only(queries, masks[head])
            own_grad = only(grads, masks[head])
            scores = times_transpose(keys, own_query)
            prob = jnp.where(key_valid, jnp.exp(scores - norms[head : head + 1, :]), 0.0)
            prob_grad = times_transpose(values, own_grad)
            row_term = jnp.sum(prob_grad * prob, axis=0, keepdims=True)
            score_low = (prob * (prob_grad - row_term)).astype(LOW)
            value_part = value_part + matmul(prob.astype(LOW), own_grad)
            key_part = key_part + matmul(score_low, own_query)
            start = pl.multiple_of(pair * PAIR + head * HEAD, HEAD)
            query_parts.append(matmul(key_flip[pl.ds(start, HEAD), :], score_low))
        query_flip[lanes, :] = jnp.concatenate(query_parts, axis=0) * SCORE_SCALE
        key_out[:, lanes] = key_part.astype(LOW)
        value_out[:, lanes] = value_part.astype(LOW)
        return carry

    lax.fori_loop(0, PAIRS, one_pair, 0)
    query_out[...] = query_flip[...].T.astype(LOW)
    if not last:
        return
    vec_grad[...] = jnp.zeros_like(vec_grad)
    token_flip = flip(tokens[...]).astype(LOW)
    for place, own in enumerate((query_out, key_out, value_out)):
        grads = [earlier[3 * i + place] for i in range(sequence)] + [own]
        sums = 0.0
        for i, grad in enumerate(grads):
            part = matmul(token_flip[:, i * size : (i + 1) * size], grad[...])
            total[...] = part if i == 0 else total[...] + part
            if place != 1:
                sums = sums + jnp.sum(grad[...].astype(WIDE), axis=0, keepdims=True)
        if place != 1:
            vec_grad[place // 2 : place // 2 + 1, :] = sums
        store_pieces(coords, keep_out, send_out, lambda r, c: total[r, c], place)


def input_kernel(layout, *refs):
    pieces = 2 * len(layout)
    coords, first_grad, query, key, value = refs[:5]
    sources = refs[5 : 5 + pieces]
    grad_out, weights, sems = refs[5 + pieces :]
    load_now(load_pieces(coords, range(3), sources, layout, weights, sems))
    grad = first_grad[...]
    for place, grads in enumerate((query, key, value)):
        grad = grad + times_transpose(grads[...], flat(weights, place)[...])
    grad_out[...] = grad.astype(grad_out.dtype)


def call(kernel, grid, inputs, outputs, scratch, flops, moved, aliases=None):
    return pl.pallas_call(
        kernel,
        grid=(grid,),
        in_specs=[spec for _, spec in inputs],
        out_specs=[spec for _, _, spec in outputs],
        out_shape=[jax.ShapeDtypeStruct(shape, kind) for shape, kind, _ in outputs],
        scratch_shapes=scratch,
        input_output_aliases=aliases or {},
        compiler_params=pltpu.CompilerParams(
            dimension_semantics=("arbitrary",), vmem_limit_bytes=VMEM_BYTES
        ),
        cost_estimate=pl.CostEstimate(flops=flops, bytes_accessed=moved, transcendentals=0),
    )(*[array for array, _ in inputs])


SCALARS = pl.BlockSpec(memory_space=pltpu.SMEM)
WHERE_IT_IS = pl.BlockSpec(memory_space=pl.ANY)


def tiles(rows, width):
    return pl.BlockSpec((rows, width), lambda i: (i, 0))


def block(number, *shape):
    return pl.BlockSpec(shape, lambda i: (number,) + (0,) * (len(shape) - 1))


def whole(*shape):
    return pl.BlockSpec(shape, lambda i: (0,) * len(shape))


def swap(value, axis, offset=1):
    size = lax.axis_size(axis)
    return lax.ppermute(value, axis, [(i, i ^ offset) for i in range(size)])


def swap_side(value):
    return swap(value, SIDE)


def swap_x(value):
    return swap(value, "ctx_hi")


def swap_y(value):
    return swap(value, "dp_lo")


def phase(*values):
    return lax.optimization_barrier(values)


def in_order(mine, theirs, here, axis):
    return jnp.where(
        here == 0,
        jnp.concatenate([mine, theirs], axis=axis),
        jnp.concatenate([theirs, mine], axis=axis),
    )


def pair_shards(shard, side):
    half = shard.shape[-1] // 2
    axis = shard.ndim - 1
    mine = lax.dynamic_slice_in_dim(shard, side * half, half, axis)
    theirs = lax.dynamic_slice_in_dim(shard, (1 - side) * half, half, axis)
    return in_order(mine, swap_side(theirs), side, shard.ndim - 2)


def swap_planes(value):
    return [swap(value, "dp_hi", offset) for offset in range(1, lax.axis_size("dp_hi"))]


def place_planes(value, others):
    here = lax.axis_index("dp_hi")
    full = jnp.zeros((len(others) + 1,) + value.shape, value.dtype)
    for offset, part in enumerate([value] + others):
        full = lax.dynamic_update_slice_in_dim(full, part[None], here ^ offset, 0)
    return full


def wide_sum(*arrays):
    return functools.reduce(lambda a, b: a + b, [a.astype(WIDE) for a in arrays])


class Sum:
    def __init__(self, keep, send):
        self.keep, self.planes = keep, keep.shape[1]
        self.lower = slice(0, self.planes // 2)
        self.upper = slice(self.planes // 2, self.planes)
        self.send = send

    def core(self):
        return [swap_side(self.send)]

    def part(self, square, planes):
        return wide_sum(self.keep[square, planes], self.other[square, planes])

    def diagonal(self, got):
        (self.other,) = got
        lower, upper = self.lower, self.upper
        return [
            swap_y(self.part(3, lower).astype(LOW)),
            swap_x(self.part(3, upper).astype(LOW)),
            swap_x(self.part(1, upper).astype(LOW)),
            swap_y(self.part(2, lower).astype(LOW)),
        ]

    def near(self, got):
        by_y, by_x, self.x_upper, self.y_lower = got
        return [
            swap_x(wide_sum(self.part(1, self.lower), by_y).astype(LOW)),
            swap_y(wide_sum(self.part(2, self.upper), by_x).astype(LOW)),
        ]

    def along(self, got):
        x_lower, y_upper = got
        whole_sum = jnp.concatenate(
            [
                wide_sum(self.part(0, self.lower), x_lower, self.y_lower).astype(LOW),
                wide_sum(self.part(0, self.upper), self.x_upper, y_upper).astype(LOW),
            ],
            axis=0,
        )
        here = lax.axis_index("dp_hi")
        pick = functools.partial(lax.dynamic_index_in_dim, whole_sum, axis=0, keepdims=False)
        self.own = pick(here)
        return [
            swap(pick(here ^ offset), "dp_hi", offset) for offset in range(1, self.planes)
        ]

    def pair(self, got, side):
        total = wide_sum(self.own, *got).astype(LOW)
        rows = total.shape[-2] // 2
        axis = total.ndim - 2
        self.rows = lax.dynamic_slice_in_dim(total, side * rows, rows, axis)
        return [swap_side(lax.dynamic_slice_in_dim(total, (1 - side) * rows, rows, axis))]

    def done(self, got, side):
        return in_order(self.rows, got[0], side, self.rows.ndim - 1).astype(WIDE)


def own_rows(total, side):
    rows = total.shape[-2] // 2
    axis = total.ndim - 2
    total = total.astype(LOW)
    mine = lax.dynamic_slice_in_dim(total, side * rows, rows, axis)
    theirs = lax.dynamic_slice_in_dim(total, (1 - side) * rows, rows, axis)
    return in_order(mine, swap_side(theirs), side, total.ndim - 1).astype(WIDE)


def swap_square(value):
    diagonal = [((y, x), (1 - y, 1 - x)) for y in range(2) for x in range(2)]
    index = lambda place: place[0] * 2 + place[1]
    return [
        swap_x(value),
        swap_y(value),
        lax.ppermute(value, ("dp_lo", "ctx_hi"), [(index(a), index(b)) for a, b in diagonal]),
    ]


def swap_sequences(value, parts):
    own = value.shape[0] // parts
    me = lax.axis_index(CONTEXT)
    blocks = [
        lax.dynamic_slice_in_dim(value, (me ^ offset) * own, own, 0) for offset in range(parts)
    ]
    return blocks[:1] + [swap(blocks[i], CONTEXT, i) for i in range(1, parts)]


def place_sequences(blocks):
    own, here, width = blocks[0].shape
    me = lax.axis_index(CONTEXT)
    full = jnp.zeros((own, len(blocks) * here, width), blocks[0].dtype)
    for offset, part in enumerate(blocks):
        full = lax.dynamic_update_slice_in_dim(full, part, (me ^ offset) * here, 1)
    return full


def swap_positions(value, parts):
    here = value.shape[0] // parts
    me = lax.axis_index(CONTEXT)
    blocks = [
        lax.dynamic_slice_in_dim(value, (me ^ offset) * here, here, 0) for offset in range(parts)
    ]
    return blocks[:1] + [swap(blocks[i], CONTEXT, i) for i in range(1, parts)]


def place_positions(sequences):
    own, parts = len(sequences), len(sequences[0])
    here, width = sequences[0][0].shape
    me = lax.axis_index(CONTEXT)
    full = jnp.zeros((own * parts, here, width), sequences[0][0].dtype)
    for number, blocks in enumerate(sequences):
        for offset, part in enumerate(blocks):
            full = lax.dynamic_update_slice(
                full, part[None], ((me ^ offset) * own + number, 0, 0)
            )
    return full


def local(
    tokens,
    cotangent,
    lengths,
    attention_weights,
    inner_weights,
    outer_weights,
    inner_bias,
    vectors,
    attention_first,
    attention_second,
    inner_first,
    inner_second,
    outer_moment_first,
    outer_second,
    bias_first,
    bias_second,
    vector_first,
    vector_second,
):
    parts = lax.axis_size(CONTEXT)
    planes = lax.axis_size("dp_hi")
    chips = lax.axis_size(CHIPS)
    count = 2 * chips
    side = lax.axis_index(SIDE)
    coords = jnp.stack([side, lax.axis_index("dp_lo"), lax.axis_index("ctx_hi")]).astype(
        jnp.int32
    )
    seq_count, local_len, width = tokens.shape
    hidden = inner_weights.shape[1]
    full_len = local_len * parts
    own_seqs = seq_count // parts
    rows = own_seqs * full_len
    att_rows, vec_cols, bias_cols = (
        attention_weights.shape[1],
        vectors.shape[1],
        inner_bias.shape[0],
    )
    half = width // 2
    tall = 16
    in_pieces = (2 * att_rows) % tall == 0
    if in_pieces:
        dims, squares = (planes, 2, 2), 4
        att_block, inner_block, outer_block = (
            2 * att_rows,
            2 * inner_weights.shape[0],
            2 * outer_weights.shape[0],
        )
    else:
        dims, squares = (1, 1, 1), 1
        att_block, inner_block, outer_block = width, width, hidden

    me = lax.axis_index(ALL)
    per_row = width // bias_cols
    small = jnp.zeros((tall, width), LOW)
    small = lax.dynamic_update_slice(small, vectors.astype(LOW), (0, me * vec_cols))
    small = lax.dynamic_update_slice(
        small, inner_bias.astype(LOW)[None], (8 + me // per_row, me % per_row * bias_cols)
    )
    token_blocks = swap_sequences(tokens, parts)
    att_pair = pair_shards(attention_weights.astype(LOW), side).reshape(8 * att_rows, half)
    inner_pair = pair_shards(inner_weights.astype(LOW), side)
    outer_pair = pair_shards(outer_weights.astype(LOW), side)
    cot_low = cotangent.astype(LOW)
    if in_pieces:
        middle = planes // 2
        small_part = swap_side(small)
        att_pair, inner_pair, outer_pair, small_part = phase(
            att_pair, inner_pair, outer_pair, small_part
        )
        small = small + small_part
        att_parts, inner_parts = swap_planes(att_pair), swap_planes(inner_pair)
        outer_x = swap_x(outer_pair)
        small_parts = swap_planes(small)
        att_parts, inner_parts, outer_x, small_parts, token_blocks = phase(
            att_parts, inner_parts, outer_x, small_parts, token_blocks
        )
        small = wide_sum(small, *small_parts).astype(LOW)
        att, inner = place_planes(att_pair, att_parts), place_planes(inner_pair, inner_parts)
        outer_row = in_order(outer_pair[None], outer_x[None], coords[2], 0)
        att_x, att_y = swap_x(att), swap_y(att)
        inner_x, inner_y = swap_x(inner), swap_y(inner)
        outer_parts = swap_planes(outer_row)
        small_parts = swap_square(small)
        token_rows = place_sequences(token_blocks)
        att_x, att_y, inner_x, inner_y, outer_parts, small_parts, token_rows = phase(
            att_x, att_y, inner_x, inner_y, outer_parts, small_parts, token_rows
        )
        small = wide_sum(small, *small_parts)
        outer = place_planes(outer_row, outer_parts)
        att_mine = [att, att_x, att_y, swap_y(att_x[:middle]), swap_x(att_y[middle:])]
        att_other = [swap_side(piece) for piece in att_mine[:3]]
        att_mine, att_other, small, outer = phase(att_mine, att_other, small, outer)
        att_all = att_mine + att_other + [swap_side(piece) for piece in att_mine[3:]]
        att_layout = [
            (0, 0, 0, planes),
            (0, 1, 0, planes),
            (1, 0, 0, planes),
            (1, 1, 0, middle),
            (1, 1, middle, planes - middle),
        ]
        inner_layout = [(y, x, 0, planes) for y in range(2) for x in range(2)]
        outer_layout = [
            (0, None, 0, planes),
            (1, None, 0, middle),
            (1, None, middle, planes - middle),
        ]
    else:
        small = lax.psum(small, ALL).astype(WIDE)
        att = lax.all_gather(att_pair, CHIPS, axis=0, tiled=False)
        inner = lax.all_gather(inner_pair, CHIPS, axis=0, tiled=True)[None]
        outer = lax.all_gather(outer_pair, CHIPS, axis=0, tiled=True)[None]
        att = att.reshape(chips, 4, 2 * att_rows, half)
        att = att.transpose(1, 0, 2, 3).reshape(1, 4 * width, half)
        att_all, inner_all, outer_all = [
            [value, swap_side(value)] for value in (att, inner, outer)
        ]
        att_layout = inner_layout = outer_layout = [(0, 0, 0, 1)]
        token_rows = place_sequences(token_blocks)
        cot_blocks = swap_sequences(cot_low, parts)
    token_rows = token_rows.reshape(rows, width)
    vec = small[:8]
    bias = small[8 : 8 + hidden // width].reshape(1, hidden)
    own_lengths = lax.dynamic_slice_in_dim(lengths, lax.axis_index(CONTEXT) * own_seqs, own_seqs)

    def in_place(pieces):
        return [(piece, WHERE_IT_IS) for piece in pieces]

    norm_shape = (own_seqs, PAIRS, 2, full_len)
    low_rows = (rows, width)
    vec_spec = whole(8, width)
    square = 2 * rows * width * width
    attend_flops = 8 * rows * full_len * width

    held = []
    for number in range(own_seqs):
        own_rows_spec = block(number, full_len, width)
        inputs = [
            (own_lengths, SCALARS),
            (coords, SCALARS),
            (token_rows, own_rows_spec),
            (vec, vec_spec),
        ] + in_place(att_all)
        held = call(
            functools.partial(attend_kernel, number, att_layout, len(held)),
            1,
            inputs + in_place(held),
            [(low_rows, LOW, own_rows_spec)] * 4
            + [
                (low_rows, WIDE, own_rows_spec),
                (norm_shape, WIDE, block(number, 1, PAIRS, 2, full_len)),
            ],
            [
                pltpu.VMEM((4,) + dims + (att_block, width), LOW),
                pltpu.VMEM((width, full_len), LOW),
                pltpu.VMEM((width, full_len), WIDE),
                pltpu.SemaphoreType.DMA((4 * len(att_all),)),
            ],
            (4 * square + 2 * attend_flops) // own_seqs,
            20 * rows * width // own_seqs,
            {len(inputs) + i: i for i in range(len(held))},
        )
        if not in_pieces:
            continue
        if number == 0:
            inner_far = swap_x(inner_y)
            outer_low = swap_y(outer[:middle])
            inner_other = [swap_side(piece) for piece in (inner, inner_x, inner_y)]
            outer_other = swap_side(outer)
            held, inner_far, outer_low, inner_other, outer_other = phase(
                held, inner_far, outer_low, inner_other, outer_other
            )
        if number == min(1, own_seqs - 1):
            outer_high = swap_y(outer[middle:])
            cot_blocks = swap_sequences(cot_low, parts)
            inner_all = [inner, inner_x, inner_y, inner_far] + inner_other
            inner_all = inner_all + [swap_side(inner_far)]
            outer_low_other = swap_side(outer_low)
            held, outer_high, cot_blocks, inner_all, outer_low_other = phase(
                held, outer_high, cot_blocks, inner_all, outer_low_other
            )
            outer_all = [
                outer,
                outer_low,
                outer_high,
                outer_other,
                outer_low_other,
                swap_side(outer_high),
            ]
    query, key, value, mixed, first_sum, normalizer = held
    cot_rows = place_sequences(cot_blocks).reshape(rows, width)

    def grad_pieces(rows_here, columns, matrices=None):
        lead = (squares, dims[0]) + ((matrices,) if matrices else ())
        shape = lead + (rows_here, columns)
        return [(shape, LOW, whole(*shape))] * 2

    tile = 256
    row_tile = tiles(tile, width)
    hidden_tile = tiles(tile, hidden)
    result, second_grad, hidden_low, outer_keep, outer_send, vec_ffn, bias_grad = phase(
        *call(
            functools.partial(ffn_kernel, inner_layout, outer_layout),
            rows // tile,
            [
                (coords, SCALARS),
                (first_sum, row_tile),
                (cot_rows, row_tile),
                (vec, vec_spec),
                (bias, whole(1, hidden)),
            ]
            + in_place(inner_all)
            + in_place(outer_all),
            [
                (low_rows, LOW, row_tile),
                (low_rows, WIDE, row_tile),
                ((rows, hidden), LOW, hidden_tile),
            ]
            + grad_pieces(outer_block, half)
            + [((8, width), WIDE, vec_spec), ((1, hidden), WIDE, whole(1, hidden))],
            [
                pltpu.VMEM((1,) + dims + (inner_block, hidden), LOW),
                pltpu.VMEM((1,) + dims + (outer_block, width), LOW),
                pltpu.VMEM((hidden, width), WIDE),
                pltpu.VMEM((tile, hidden), LOW),
                pltpu.VMEM((tile, hidden), WIDE),
                pltpu.SemaphoreType.DMA((len(inner_all) + len(outer_all),)),
            ],
            16 * square + 60 * rows * hidden,
            30 * rows * width,
        )
    )
    results = result.reshape(own_seqs, full_len, width)

    inner_grads = call(
        inner_grad_kernel,
        rows // tile,
        [
            (coords, SCALARS),
            (first_sum, row_tile),
            (hidden_low, hidden_tile),
            (vec, vec_spec),
        ],
        grad_pieces(inner_block, hidden // 2),
        [pltpu.VMEM((width, hidden), WIDE)],
        4 * square,
        18 * rows * width,
    )
    result_blocks = [swap_positions(results[0], parts)]
    if in_pieces:
        outer_sum = Sum(outer_keep, outer_send)
        inner_grads, outer_got, result_blocks, second_grad = phase(
            inner_grads, outer_sum.core(), result_blocks, second_grad
        )
        inner_sum = Sum(*inner_grads)
        outer_got, inner_got = outer_sum.diagonal(outer_got), inner_sum.core()

    first_grad, mixed_grad, project_keep, project_send, vec_mid = call(
        functools.partial(back_kernel, inner_layout, att_layout),
        rows // tile,
        [
            (coords, SCALARS),
            (first_sum, row_tile),
            (second_grad, row_tile),
            (hidden_low, hidden_tile),
            (mixed, row_tile),
            (vec, vec_spec),
        ]
        + in_place(inner_all)
        + in_place(att_all),
        [(low_rows, WIDE, row_tile), (low_rows, LOW, row_tile)]
        + grad_pieces(att_block, half)
        + [((8, width), WIDE, vec_spec)],
        [
            pltpu.VMEM((1,) + dims + (inner_block, hidden), LOW),
            pltpu.VMEM((1,) + dims + (att_block, width), LOW),
            pltpu.VMEM((width, width), WIDE),
            pltpu.SemaphoreType.DMA((len(inner_all) + len(att_all),)),
        ],
        6 * square,
        24 * rows * width,
    )
    if in_pieces:
        (
            first_grad,
            mixed_grad,
            project_keep,
            project_send,
            vec_mid,
            outer_got,
            inner_got,
        ) = phase(
            first_grad, mixed_grad, project_keep, project_send, vec_mid, outer_got, inner_got
        )
        project_sum = Sum(project_keep, project_send)
        outer_got, inner_got = outer_sum.near(outer_got), inner_sum.diagonal(inner_got)
        project_got = project_sum.core()

    grads = []
    for number in range(own_seqs):
        last = number == own_seqs - 1
        own_rows_spec = block(number, full_len, width)
        seq_shape = (full_len, width)
        earlier = [value_ for three in grads for value_ in three] if last else []
        outputs = [(seq_shape, LOW, whole(*seq_shape))] * 3
        scratch = [pltpu.VMEM((width, full_len), LOW), pltpu.VMEM((width, full_len), WIDE)]
        if last:
            outputs = (
                outputs + grad_pieces(att_block, half, 3) + [((8, width), WIDE, vec_spec)]
            )
            scratch = scratch + [pltpu.VMEM((width, width), WIDE)]
        found = call(
            functools.partial(attend_back_kernel, number, last),
            1,
            [
                (own_lengths, SCALARS),
                (coords, SCALARS),
                (token_rows, whole(rows, width)),
                (query, own_rows_spec),
                (key, own_rows_spec),
                (value, own_rows_spec),
                (mixed_grad, own_rows_spec),
                (normalizer, block(number, 1, PAIRS, 2, full_len)),
            ]
            + [(value_, whole(*seq_shape)) for value_ in earlier],
            outputs,
            scratch,
            5 * attend_flops // own_seqs + (3 * square if last else 0),
            20 * rows * width // own_seqs,
        )
        if number:
            result_blocks.append(swap_positions(results[number], parts))
        if in_pieces:
            found, outer_got, inner_got, project_got, mixed_grad, result_blocks = phase(
                found, outer_got, inner_got, project_got, mixed_grad, result_blocks
            )
            if number == 0:
                outer_got, inner_got = outer_sum.along(outer_got), inner_sum.near(inner_got)
                project_got = project_sum.diagonal(project_got)
        grads.append(list(found[:3]))
    att_keep, att_send, vec_att = found[3:]
    output_tokens = place_positions(result_blocks)

    small_grad = jnp.concatenate(
        [
            vec_ffn + vec_mid + vec_att,
            bias_grad.reshape(-1, width),
            jnp.zeros((tall - 8 - hidden // width, width), WIDE),
        ],
        axis=0,
    )
    if in_pieces:
        att_sum = Sum(att_keep, att_send)
        att_got = att_sum.core()
        outer_got, inner_got = outer_sum.pair(outer_got, side), inner_sum.along(inner_got)
        project_got = project_sum.near(project_got)
        small_got = [swap_side(small_grad)]

    input_blocks = []
    for number in range(own_seqs):
        seq_shape = (full_len, width)
        (grad,) = call(
            functools.partial(input_kernel, att_layout),
            1,
            [(coords, SCALARS), (first_grad, block(number, full_len, width))]
            + [(value_, whole(*seq_shape)) for value_ in grads[number]]
            + in_place(att_all),
            [(seq_shape, LOW, whole(*seq_shape))],
            [
                pltpu.VMEM((3,) + dims + (att_block, width), LOW),
                pltpu.SemaphoreType.DMA((3 * len(att_all),)),
            ],
            3 * square // own_seqs,
            12 * rows * width // own_seqs,
        )
        if in_pieces and number == 0:
            grad, first_grad, att_got, outer_got, inner_got, project_got, small_got = phase(
                grad, first_grad, att_got, outer_got, inner_got, project_got, small_got
            )
            outer_total = outer_sum.done(outer_got, side)
            small_grad = wide_sum(small_grad, *small_got)
            att_got, inner_got = att_sum.diagonal(att_got), inner_sum.pair(inner_got, side)
            project_got, small_got = project_sum.along(project_got), swap_planes(small_grad)
        input_blocks.append(swap_positions(grad, parts))
    if in_pieces:
        input_blocks[:-1], att_got, inner_got, project_got, small_got, input_blocks[-1][0] = (
            phase(
                input_blocks[:-1], att_got, inner_got, project_got, small_got, input_blocks[-1][0]
            )
        )
        inner_total = inner_sum.done(inner_got, side)
        small_grad = wide_sum(small_grad, *small_got)
        att_got, small_got = att_sum.near(att_got), swap_square(small_grad)
        project_got = project_sum.pair(project_got, side)
        att_got, small_got, project_got = phase(att_got, small_got, project_got)
        small_total = wide_sum(small_grad, *small_got)
        project_total = project_sum.done(project_got, side)
        att_total = att_sum.done(att_sum.pair(att_sum.along(att_got), side), side)
    else:

        def scatter(keep, send):
            partial = (keep + swap_side(send)).reshape((-1,) + keep.shape[-2:])
            matrices, length, columns = partial.shape
            partial = partial.reshape(matrices, chips, length // chips, columns)
            partial = lax.psum_scatter(
                partial.transpose(1, 0, 2, 3), CHIPS, scatter_dimension=0, tiled=False
            )
            return own_rows(partial, side)

        att_total = scatter(att_keep, att_send)
        outer_total = scatter(outer_keep, outer_send)[0]
        inner_total = scatter(*inner_grads)[0]
        project_total = scatter(project_keep, project_send)[0]
        small_total = lax.psum(small_grad, ALL)
    attention_total = jnp.concatenate([att_total, project_total[None]], axis=0)
    vector_total = lax.dynamic_slice(small_total, (0, me * vec_cols), (8, vec_cols))
    bias_total = lax.dynamic_slice(
        small_total, (8 + me // per_row, me % per_row * bias_cols), (1, bias_cols)
    ).reshape(bias_cols)
    input_grad = place_positions(input_blocks).astype(WIDE)

    attention_square, attention_new = adam_step(
        attention_weights,
        attention_total,
        attention_first,
        attention_second,
        MATRIX_LEARN_RATE,
        WEIGHT_DECAY,
    )
    inner_square, inner_new = adam_step(
        inner_weights, inner_total, inner_first, inner_second, MATRIX_LEARN_RATE, WEIGHT_DECAY
    )
    outer_square, outer_new = adam_step(
        outer_weights,
        outer_total,
        outer_moment_first,
        outer_second,
        MATRIX_LEARN_RATE,
        WEIGHT_DECAY,
    )
    bias_square, bias_new = adam_step(
        inner_bias, bias_total, bias_first, bias_second, VECTOR_RATE, 0.0
    )
    vector_square, vector_new = adam_step(
        vectors, vector_total, vector_first, vector_second, VECTOR_RATE, 0.0
    )
    return (
        output_tokens,
        input_grad,
        attention_total,
        attention_square,
        attention_new,
        inner_total,
        inner_square,
        inner_new,
        outer_total,
        outer_square,
        outer_new,
        bias_total,
        bias_square,
        bias_new,
        vector_total,
        vector_square,
        vector_new,
    )


def solution(mesh):
    split = Mesh(
        np.asarray(mesh.devices).reshape(
            mesh.shape["dp"] // 2, 2, mesh.shape["context"] // 2, 2
        ),
        ALL,
    )
    dp = ("dp_hi", "dp_lo")
    rows3 = P(dp, CONTEXT, None)
    mid3 = P(None, ALL, None)
    row2 = P(ALL, None)
    col2 = P(None, ALL)
    one = P(ALL)
    return jax.shard_map(
        local,
        mesh=split,
        in_specs=(rows3, rows3, P(dp), mid3, row2, row2, one, col2)
        + (mid3, mid3, row2, row2, row2, row2, one, one, col2, col2),
        out_specs=(rows3, rows3)
        + (mid3,) * 3
        + (row2,) * 6
        + (one,) * 3
        + (col2,) * 3,
        check_vma=False,
    )
```

```python
import functools

import jax
import jax.numpy as jnp
import numpy as np
from jax import lax
from jax.experimental import pallas as pl
from jax.experimental.pallas import tpu as pltpu
from jax.sharding import Mesh, PartitionSpec as P

HEADS = 12
HEAD = 64
PAIR = 2 * HEAD
PAIRS = HEADS // 2
STEP = 10

NORM_EPS = 1e-12
BETA_ONE = 0.9
BETA_TWO = 0.999
ADAM_EPS = 1e-06
MATRIX_LEARN_RATE = 0.05
VECTOR_RATE = 0.5
WEIGHT_DECAY = 0.01
MASK_FILL = -1e30
SCORE_SCALE = HEAD ** (-0.5)
ROOT_HALF = 0.5**0.5
DENSITY = 0.3989422804014327

CHIPS = ("dp_hi", "dp_lo", "ctx_hi")
SIDE = "ctx_lo"
ALL = CHIPS + (SIDE,)
CONTEXT = ("ctx_hi", "ctx_lo")
LOW = jnp.bfloat16
WIDE = jnp.float32
VMEM_BYTES = 60 * 1024 * 1024


def adam_step(weight, gradient, moment_one, moment_two, step_rate, decay_rate):
    first_new = BETA_ONE * moment_one + (1.0 - BETA_ONE) * gradient
    second_new = BETA_TWO * moment_two + (1.0 - BETA_TWO) * gradient * gradient
    first_hat = first_new / (1.0 - BETA_ONE**STEP)
    second_hat = second_new / (1.0 - BETA_TWO**STEP)
    updated = weight - step_rate * (
        first_hat / (jnp.sqrt(second_hat) + ADAM_EPS) + decay_rate * weight
    )
    return (second_new, updated)


def matmul(left, right):
    return jnp.dot(left, right, preferred_element_type=WIDE)


def contract_rows(left, right):
    return lax.dot_general(left, right, (((0,), (0,)), ((), ())), preferred_element_type=WIDE)


def times_transpose(left, right):
    return lax.dot_general(left, right, (((1,), (1,)), ((), ())), preferred_element_type=WIDE)


def flip(value):
    return value.astype(WIDE).T


def norm_stats(value):
    centered = value - jnp.mean(value, axis=-1, keepdims=True)
    variance = jnp.mean(centered * centered, axis=-1, keepdims=True)
    scale = lax.rsqrt(variance + NORM_EPS)
    return centered * scale, scale


def norm_back(grad, gain, unit, scale):
    scaled = grad * gain
    return scale * (
        scaled
        - jnp.mean(scaled, axis=-1, keepdims=True)
        - unit * jnp.mean(scaled * unit, axis=-1, keepdims=True)
    )


def load_pieces(coords, moves, pieces, layout, target, sems, first=0):
    rows, half = target.shape[4], target.shape[5] // 2
    side, y_here, x_here = coords[0], coords[1], coords[2]
    single = target.shape[2] == 1
    wide = pieces[0].shape[-1]
    copies = []
    for row, place, column in moves:
        for number, source in enumerate(pieces):
            which, order = divmod(number, len(layout))
            y_other, x_other, plane, planes = layout[order]
            start = pl.multiple_of((side if which == 0 else 1 - side) * half + column, wide)
            y_at = 0 if single else (1 - y_here if y_other else y_here)
            x_at = 0 if single else (1 - x_here if x_other else x_here)
            copies.append(
                pltpu.make_async_copy(
                    source.at[:, pl.ds(row, rows), :],
                    target.at[place, pl.ds(plane, planes), y_at, x_at, :, pl.ds(start, wide)],
                    sems.at[first + len(copies)],
                )
            )
    return copies


def inner_moves(target, wide):
    rows, half = target.shape[4], target.shape[5] // 2
    return [(number * rows, 0, number * wide) for number in range(half // wide)]


def outer_moves(target, inner, wide):
    return [(inner.shape[4] * (inner.shape[5] // 2 // wide), 0, 0)]


def matrix_moves(picks, rows):
    return [(pick * rows, place, 0) for place, pick in enumerate(picks)]


def load_now(copies):
    for copy in copies:
        copy.start()
    for copy in copies:
        copy.wait()


def flat(target, place=0):
    _, planes, high, wide, rows, width = target.shape
    return target.at[place].reshape(planes * high * wide * rows, width)


def store_pieces(coords, keep_out, send_out, read, half, column=0, place=None):
    side, y_here, x_here = coords[0], coords[1], coords[2]
    runs, squares, planes = keep_out.shape[:3]
    rows = keep_out.shape[-2]
    into = pl.ds(column, half)
    for out, own_side in ((keep_out, side), (send_out, 1 - side)):
        columns = pl.ds(pl.multiple_of(own_side * half, half), half)
        for run in range(runs):
            for square in range(squares):
                high, low = square // 2, square % 2
                y_other, x_other = (high, low) if run == 0 else (low, high)
                for number in range(planes):
                    block = run * planes + number
                    if squares > 1:
                        y_at = 1 - y_here if y_other else y_here
                        x_at = 1 - x_here if x_other else x_here
                        block = (block * 2 + y_at) * 2 + x_at
                    start = pl.multiple_of(block * rows, rows)
                    part = read(pl.ds(start, rows), columns).astype(LOW)
                    if place is None:
                        out[run, square, number, :, into] = part
                    else:
                        out[run, square, number, place, :, into] = part


def head_masks():
    lane = lax.broadcasted_iota(jnp.int32, (1, PAIR), 1)
    return [lane < HEAD, lane >= HEAD]


def only(value, mask):
    return jnp.where(mask, value, 0.0).astype(LOW)


def attend_kernel(layout, *refs):
    pieces = 2 * len(layout)
    lengths, coords, tokens, vec = refs[:4]
    sources = refs[4 : 4 + pieces]
    query_out, key_out, value_out, mixed_out, sum_out, norm_out = refs[4 + pieces : 10 + pieces]
    weights, value_flip, mixed_flip, sems = refs[10 + pieces :]
    step = pl.program_id(0)
    copies = load_pieces(
        coords, matrix_moves(range(4), weights.shape[4]), sources, layout, weights, sems
    )

    @pl.when(step == 0)
    def _():
        for copy in copies:
            copy.start()

    def need(place):
        @pl.when(step == 0)
        def _():
            for copy in copies[place * pieces : (place + 1) * pieces]:
                copy.wait()

    length = lengths[step]
    rows = tokens[...]
    need(0)
    query_out[...] = (matmul(rows, flat(weights, 0)[...]) + vec[0:1, :]).astype(LOW)
    need(1)
    key_out[...] = matmul(rows, flat(weights, 1)[...]).astype(LOW)
    need(2)
    value_low = (matmul(rows, flat(weights, 2)[...]) + vec[1:2, :]).astype(LOW)
    value_out[...] = value_low
    value_flip[...] = flip(value_low).astype(LOW)
    size = tokens.shape[0]
    key_valid = lax.broadcasted_iota(jnp.int32, (size, size), 0) < length
    masks = head_masks()

    def one_pair(pair, carry):
        lanes = pl.ds(pl.multiple_of(pair * PAIR, PAIR), PAIR)
        keys = key_out[:, lanes]
        queries = query_out[:, lanes].astype(WIDE) * SCORE_SCALE
        mixed, norms = [], []
        for head in range(2):
            scores = times_transpose(keys, only(queries, masks[head]))
            scores = jnp.where(key_valid, scores, MASK_FILL)
            peak = jnp.max(scores, axis=0, keepdims=True)
            exponent = jnp.exp(scores - peak)
            total = jnp.sum(exponent, axis=0, keepdims=True)
            prob = (exponent * (1.0 / total)).astype(LOW)
            start = pl.multiple_of(pair * PAIR + head * HEAD, HEAD)
            mixed.append(matmul(value_flip[pl.ds(start, HEAD), :], prob))
            norms.append(peak + jnp.log(total))
        mixed_flip[lanes, :] = jnp.concatenate(mixed, axis=0)
        norm_out[0, pair] = jnp.concatenate(norms, axis=0)
        return carry

    lax.fori_loop(0, PAIRS, one_pair, 0)
    need(3)
    mixed_low = mixed_flip[...].T.astype(LOW)
    mixed_out[...] = mixed_low
    sum_out[...] = rows.astype(WIDE) + matmul(mixed_low, flat(weights, 3)[...]) + vec[2:3, :]


def ffn_kernel(layout, *refs):
    pieces = 2 * len(layout)
    coords, first_sum, cotangent, vec, bias = refs[:5]
    sources = refs[5 : 5 + pieces]
    result_out, second_out, hidden_out, keep_out, send_out, vec_grad, bias_grad = refs[
        5 + pieces : 12 + pieces
    ]
    inner_at, outer_at, total, activated, slope, sems = refs[12 + pieces :]
    step = pl.program_id(0)

    @pl.when(step == 0)
    def _():
        wide = sources[0].shape[-1]
        copies = load_pieces(
            coords, inner_moves(inner_at, wide), sources, layout, inner_at, sems
        )
        copies = copies + load_pieces(
            coords,
            outer_moves(outer_at, inner_at, wide),
            sources,
            layout,
            outer_at,
            sems,
            len(copies),
        )
        for copy in copies:
            copy.start()
        vec_grad[...] = jnp.zeros_like(vec_grad)
        bias_grad[...] = jnp.zeros_like(bias_grad)
        total[...] = jnp.zeros_like(total)
        for copy in copies:
            copy.wait()

    inner, outer = flat(inner_at), flat(outer_at)
    unit, _ = norm_stats(first_sum[...])
    normed = unit * vec[4:5, :] + vec[5:6, :]
    normed_low = normed.astype(LOW)
    width, hidden = inner.shape
    second = normed + vec[3:4, :]
    for start in range(0, hidden, width):
        part = slice(start, start + width)
        pre = matmul(normed_low, inner[:, part]) + bias[:, part]
        cdf = 0.5 * (1.0 + lax.erf(pre * ROOT_HALF))
        active = (pre * cdf).astype(LOW)
        activated[:, part] = active
        slope[:, part] = cdf + pre * (DENSITY * jnp.exp(-0.5 * pre * pre))
        second = second + matmul(active, outer[part, :])
    unit_two, scale_two = norm_stats(second)
    result_out[...] = (unit_two * vec[6:7, :] + vec[7:8, :]).astype(LOW)
    grad = cotangent[...].astype(WIDE)
    second_grad = norm_back(grad, vec[6:7, :], unit_two, scale_two)
    second_out[...] = second_grad
    grad_low = second_grad.astype(LOW)
    vec_grad[3:4, :] += jnp.sum(grad_low.astype(WIDE), axis=0, keepdims=True)
    vec_grad[6:7, :] += jnp.sum(grad * unit_two, axis=0, keepdims=True)
    vec_grad[7:8, :] += jnp.sum(grad, axis=0, keepdims=True)
    for start in range(0, hidden, width):
        part = slice(start, start + width)
        back = times_transpose(grad_low, outer[part, :])
        hidden_low = (back * slope[:, part]).astype(LOW)
        hidden_out[:, part] = hidden_low
        bias_grad[:, part] += jnp.sum(hidden_low.astype(WIDE), axis=0, keepdims=True)
        total[part, :] += contract_rows(activated[:, part], grad_low)

    @pl.when(step == pl.num_programs(0) - 1)
    def _():
        store_pieces(
            coords, keep_out, send_out, lambda r, c: total[r, c], keep_out.shape[-1]
        )


def back_kernel(pack_layout, att_layout, *refs):
    pack_pieces, att_pieces = 2 * len(pack_layout), 2 * len(att_layout)
    coords, first_sum, second_grad, hidden_low, mixed, vec = refs[:6]
    pack_from = refs[6 : 6 + pack_pieces]
    att_from = refs[6 + pack_pieces : 6 + pack_pieces + att_pieces]
    first_out, mixed_grad_out, keep_out, send_out, vec_grad = refs[
        6 + pack_pieces + att_pieces : 11 + pack_pieces + att_pieces
    ]
    inner_at, project_at, total, project_total, sems = refs[11 + pack_pieces + att_pieces :]
    step = pl.program_id(0)

    @pl.when(step == 0)
    def _():
        copies = load_pieces(
            coords,
            inner_moves(inner_at, pack_from[0].shape[-1]),
            pack_from,
            pack_layout,
            inner_at,
            sems,
        )
        copies = copies + load_pieces(
            coords,
            matrix_moves((3,), project_at.shape[4]),
            att_from,
            att_layout,
            project_at,
            sems,
            len(copies),
        )
        for copy in copies:
            copy.start()
        vec_grad[...] = jnp.zeros_like(vec_grad)
        total[...] = jnp.zeros_like(total)
        project_total[...] = jnp.zeros_like(project_total)
        for copy in copies:
            copy.wait()

    inner = flat(inner_at)
    unit, scale = norm_stats(first_sum[...])
    normed_flip = flip(unit * vec[4:5, :] + vec[5:6, :]).astype(LOW)
    width, hidden = total.shape
    grad = second_grad[...]
    for start in range(0, hidden, width):
        part = slice(start, start + width)
        grad = grad + times_transpose(hidden_low[:, part], inner[:, part])
        total[:, part] += matmul(normed_flip, hidden_low[:, part])
    first_grad = norm_back(grad, vec[4:5, :], unit, scale)
    first_out[...] = first_grad
    branch = first_grad.astype(LOW)
    vec_grad[2:3, :] += jnp.sum(branch.astype(WIDE), axis=0, keepdims=True)
    vec_grad[4:5, :] += jnp.sum(grad * unit, axis=0, keepdims=True)
    vec_grad[5:6, :] += jnp.sum(grad, axis=0, keepdims=True)
    mixed_grad_out[...] = times_transpose(branch, flat(project_at)[...]).astype(LOW)
    project_total[...] += contract_rows(mixed[...], branch)

    @pl.when(step == pl.num_programs(0) - 1)
    def _():
        store_pieces(coords, keep_out, send_out, lambda r, c: total[r, c], hidden // 2)
        store_pieces(
            coords,
            keep_out,
            send_out,
            lambda r, c: project_total[r, c],
            width // 2,
            hidden // 2,
        )


def attend_back_kernel(sequence, last, *refs):
    lengths, coords, tokens, query, key, value, mixed_grad, normalizer = refs[:8]
    count = 3 * sequence if last else 0
    earlier = refs[8 : 8 + count]
    query_out, key_out, value_out = refs[8 + count : 11 + count]
    scratch = refs[11 + count :]
    if last:
        keep_out, send_out, vec_grad = scratch[:3]
        scratch = scratch[3:]
        total = scratch[2]
    key_flip, query_flip = scratch[:2]
    length = lengths[sequence]
    size = query.shape[0]
    key_flip[...] = flip(key[...]).astype(LOW)
    key_valid = lax.broadcasted_iota(jnp.int32, (size, size), 0) < length
    masks = head_masks()

    def one_pair(pair, carry):
        lanes = pl.ds(pl.multiple_of(pair * PAIR, PAIR), PAIR)
        keys = key[:, lanes]
        values = value[:, lanes]
        queries = query[:, lanes].astype(WIDE) * SCORE_SCALE
        grads = mixed_grad[:, lanes].astype(WIDE)
        norms = normalizer[0, pair]
        query_parts, key_part, value_part = [], 0.0, 0.0
        for head in range(2):
            own_query = only(queries, masks[head])
            own_grad = only(grads, masks[head])
            scores = times_transpose(keys, own_query)
            prob = jnp.where(key_valid, jnp.exp(scores - norms[head : head + 1, :]), 0.0)
            prob_grad = times_transpose(values, own_grad)
            row_term = jnp.sum(prob_grad * prob, axis=0, keepdims=True)
            score_low = (prob * (prob_grad - row_term)).astype(LOW)
            value_part = value_part + matmul(prob.astype(LOW), own_grad)
            key_part = key_part + matmul(score_low, own_query)
            start = pl.multiple_of(pair * PAIR + head * HEAD, HEAD)
            query_parts.append(matmul(key_flip[pl.ds(start, HEAD), :], score_low))
        query_flip[lanes, :] = jnp.concatenate(query_parts, axis=0) * SCORE_SCALE
        key_out[:, lanes] = key_part.astype(LOW)
        value_out[:, lanes] = value_part.astype(LOW)
        return carry

    lax.fori_loop(0, PAIRS, one_pair, 0)
    query_out[...] = query_flip[...].T.astype(LOW)
    if not last:
        return
    vec_grad[...] = jnp.zeros_like(vec_grad)
    token_flip = flip(tokens[...]).astype(LOW)
    for place, own in enumerate((query_out, key_out, value_out)):
        grads = [earlier[3 * i + place] for i in range(sequence)] + [own]
        sums = 0.0
        for i, grad in enumerate(grads):
            part = matmul(token_flip[:, i * size : (i + 1) * size], grad[...])
            total[...] = part if i == 0 else total[...] + part
            if place != 1:
                sums = sums + jnp.sum(grad[...].astype(WIDE), axis=0, keepdims=True)
        if place != 1:
            vec_grad[place // 2 : place // 2 + 1, :] = sums
        store_pieces(
            coords,
            keep_out,
            send_out,
            lambda r, c: total[r, c],
            keep_out.shape[-1],
            place=place,
        )


def input_kernel(layout, sequences, *refs):
    pieces = 2 * len(layout)
    coords, first_grad = refs[:2]
    grads = refs[2 : 2 + 3 * sequences]
    sources = refs[2 + 3 * sequences : 2 + 3 * sequences + pieces]
    grad_out, weights, sems = refs[2 + 3 * sequences + pieces :]
    load_now(
        load_pieces(
            coords, matrix_moves(range(3), weights.shape[4]), sources, layout, weights, sems
        )
    )
    size = grads[0].shape[0]
    for number in range(sequences):
        part = slice(number * size, (number + 1) * size)
        grad = first_grad[part, :]
        for place in range(3):
            grad = grad + times_transpose(
                grads[3 * number + place][...], flat(weights, place)[...]
            )
        grad_out[part, :] = grad.astype(grad_out.dtype)


def call(kernel, grid, inputs, outputs, scratch, flops, moved, aliases=None):
    return pl.pallas_call(
        kernel,
        grid=(grid,),
        in_specs=[spec for _, spec in inputs],
        out_specs=[spec for _, _, spec in outputs],
        out_shape=[jax.ShapeDtypeStruct(shape, kind) for shape, kind, _ in outputs],
        scratch_shapes=scratch,
        input_output_aliases=aliases or {},
        compiler_params=pltpu.CompilerParams(
            dimension_semantics=("arbitrary",), vmem_limit_bytes=VMEM_BYTES
        ),
        cost_estimate=pl.CostEstimate(flops=flops, bytes_accessed=moved, transcendentals=0),
    )(*[array for array, _ in inputs])


SCALARS = pl.BlockSpec(memory_space=pltpu.SMEM)
WHERE_IT_IS = pl.BlockSpec(memory_space=pl.ANY)


def tiles(rows, width):
    return pl.BlockSpec((rows, width), lambda i: (i, 0))


def block(number, *shape):
    return pl.BlockSpec(shape, lambda i: (number,) + (0,) * (len(shape) - 1))


def whole(*shape):
    return pl.BlockSpec(shape, lambda i: (0,) * len(shape))


def swap(value, axis, offset=1):
    size = lax.axis_size(axis)
    return lax.ppermute(value, axis, [(i, i ^ offset) for i in range(size)])


def swap_side(value):
    return swap(value, SIDE)


def swap_x(value):
    return swap(value, "ctx_hi")


def swap_y(value):
    return swap(value, "dp_lo")


def phase(*values):
    return lax.optimization_barrier(values)


def in_order(mine, theirs, here, axis):
    return jnp.where(
        here == 0,
        jnp.concatenate([mine, theirs], axis=axis),
        jnp.concatenate([theirs, mine], axis=axis),
    )


def pair_shards(shard, side):
    half = shard.shape[-1] // 2
    axis = shard.ndim - 1
    mine = lax.dynamic_slice_in_dim(shard, side * half, half, axis)
    theirs = lax.dynamic_slice_in_dim(shard, (1 - side) * half, half, axis)
    return in_order(mine, swap_side(theirs), side, shard.ndim - 2)


def swap_planes(value):
    return [swap(value, "dp_hi", offset) for offset in range(1, lax.axis_size("dp_hi"))]


def place_planes(value, others):
    here = lax.axis_index("dp_hi")
    full = jnp.zeros((len(others) + 1,) + value.shape, value.dtype)
    for offset, part in enumerate([value] + others):
        full = lax.dynamic_update_slice_in_dim(full, part[None], here ^ offset, 0)
    return full


def wide_sum(*arrays):
    return functools.reduce(lambda a, b: a + b, [a.astype(WIDE) for a in arrays])


class Sum:
    def __init__(self, keep, send):
        self.keep, self.send = keep, send
        self.planes = 2 * keep.shape[2]

    def core(self):
        return swap_side(self.send)

    def part(self, run, squares):
        return wide_sum(self.keep[run, squares], self.other[run, squares])

    def first(self, got):
        self.other = got
        far = slice(2, 4)
        return [swap_y(self.part(0, far).astype(LOW)), swap_x(self.part(1, far).astype(LOW))]

    def second(self, got):
        self.got = got
        sent = [wide_sum(self.part(run, 1), got[run][1]).astype(LOW) for run in range(2)]
        return [swap_x(sent[0]), swap_y(sent[1])]

    def along(self, got):
        total = jnp.concatenate(
            [
                wide_sum(self.part(run, 0), self.got[run][0], got[run]).astype(LOW)
                for run in range(2)
            ],
            axis=0,
        )
        here = lax.axis_index("dp_hi")
        pick = functools.partial(lax.dynamic_index_in_dim, total, axis=0, keepdims=False)
        self.own = pick(here)
        return [
            swap(pick(here ^ offset), "dp_hi", offset) for offset in range(1, self.planes)
        ]

    def pair(self, got, side):
        total = wide_sum(self.own, *got).astype(LOW)
        rows = total.shape[-2] // 2
        axis = total.ndim - 2
        self.rows = lax.dynamic_slice_in_dim(total, side * rows, rows, axis)
        return swap_side(lax.dynamic_slice_in_dim(total, (1 - side) * rows, rows, axis))

    def done(self, got, side, columns=slice(None)):
        axis = self.rows.ndim - 1
        return in_order(self.rows[..., columns], got[..., columns], side, axis).astype(WIDE)


def own_rows(total, side):
    rows = total.shape[-2] // 2
    axis = total.ndim - 2
    total = total.astype(LOW)
    mine = lax.dynamic_slice_in_dim(total, side * rows, rows, axis)
    theirs = lax.dynamic_slice_in_dim(total, (1 - side) * rows, rows, axis)
    return in_order(mine, swap_side(theirs), side, total.ndim - 1).astype(WIDE)


def pick(value, index, axis=0):
    return lax.dynamic_index_in_dim(value, index, axis, keepdims=False)


class Exchange:
    def __init__(self, blocks):
        self.x_here, self.side = lax.axis_index("ctx_hi"), lax.axis_index(SIDE)
        self.own = pick(blocks, self.x_here)
        self.sent = pick(blocks, 1 - self.x_here)

    def far(self):
        return [swap_x(self.sent), swap_side(pick(self.own, 1 - self.side))]

    def near(self, got):
        self.from_x, self.from_side = got
        return swap_side(pick(self.from_x, 1 - self.side))

    def place(self, got):
        own = pick(self.own, self.side)
        x_here, side = self.x_here, self.side
        full = jnp.zeros((2, 2) + own.shape, own.dtype)
        zeros = (0,) * own.ndim
        for block, x_at, side_at in (
            (own, x_here, side),
            (self.from_side, x_here, 1 - side),
            (pick(self.from_x, side), 1 - x_here, side),
            (got, 1 - x_here, 1 - side),
        ):
            full = lax.dynamic_update_slice(full, block[None, None], (x_at, side_at) + zeros)
        return full


def by_sequence(value):
    return value.reshape((2, 2, -1) + value.shape[1:])


def sequences_of(blocks):
    parts = blocks.shape[0] * blocks.shape[1]
    own, here, width = blocks.shape[2:]
    blocks = blocks.reshape(parts, own, here, width)
    return blocks.transpose(1, 0, 2, 3).reshape(own * parts * here, width)


def by_position(value, sequences):
    width = value.shape[-1]
    blocks = value.reshape(sequences, 2, 2, -1, width)
    return blocks.transpose(1, 2, 0, 3, 4)


def positions_of(blocks):
    return blocks.reshape((-1,) + blocks.shape[3:])


def local(
    tokens,
    cotangent,
    lengths,
    attention_weights,
    inner_weights,
    outer_weights,
    inner_bias,
    vectors,
    attention_first,
    attention_second,
    inner_first,
    inner_second,
    outer_moment_first,
    outer_second,
    bias_first,
    bias_second,
    vector_first,
    vector_second,
):
    parts = lax.axis_size(CONTEXT)
    planes = lax.axis_size("dp_hi")
    chips = lax.axis_size(CHIPS)
    count = 2 * chips
    side = lax.axis_index(SIDE)
    coords = jnp.stack([side, lax.axis_index("dp_lo"), lax.axis_index("ctx_hi")]).astype(
        jnp.int32
    )
    seq_count, local_len, width = tokens.shape
    hidden = inner_weights.shape[1]
    full_len = local_len * parts
    own_seqs = seq_count // parts
    rows = own_seqs * full_len
    att_rows, vec_cols, bias_cols = (
        attention_weights.shape[1],
        vectors.shape[1],
        inner_bias.shape[0],
    )
    half = width // 2
    tall = 16
    in_pieces = (2 * att_rows) % tall == 0
    if in_pieces:
        dims, squares = (planes, 2, 2), 4
        att_block, inner_block, outer_block = (
            2 * att_rows,
            2 * inner_weights.shape[0],
            2 * outer_weights.shape[0],
        )
    else:
        dims, squares = (1, 1, 1), 1
        att_block, inner_block, outer_block = width, width, hidden

    me = lax.axis_index(ALL)
    per_row = width // bias_cols
    small = jnp.zeros((tall, width), LOW)
    small = lax.dynamic_update_slice(small, vectors.astype(LOW), (0, me * vec_cols))
    small = lax.dynamic_update_slice(
        small, inner_bias.astype(LOW)[None], (8 + me // per_row, me % per_row * bias_cols)
    )
    token_swap = Exchange(by_sequence(tokens))
    cot_swap = Exchange(by_sequence(cotangent.astype(LOW)))
    att_pair = pair_shards(attention_weights.astype(LOW), side).reshape(8 * att_rows, half)
    inner_pair = pair_shards(inner_weights.astype(LOW), side)
    outer_pair = pair_shards(outer_weights.astype(LOW), side)
    strips = hidden // width
    pack_pair = jnp.concatenate(
        [
            inner_pair.reshape(-1, strips, half).transpose(1, 0, 2).reshape(-1, half),
            outer_pair,
        ],
        axis=0,
    )
    if in_pieces:
        middle = planes // 2
        small_mine = lax.dynamic_slice_in_dim(small, side * half, half, 1)
        small_theirs = lax.dynamic_slice_in_dim(small, (1 - side) * half, half, 1)
        small = small_mine + swap_side(small_theirs)
        att_pair = jnp.concatenate([att_pair, small], axis=0)
        att_parts, token_far = swap_planes(att_pair), token_swap.far()
        att_parts, pack_pair = phase(att_parts, pack_pair)
        att = place_planes(att_pair, att_parts)
        pack_parts = swap_planes(pack_pair)
        att_x, att_y = swap_x(att), swap_y(att)
        att_x, att_y, token_far = phase(att_x, att_y, token_far)
        token_near = token_swap.near(token_far)
        att_mine = [att, att_x, att_y, swap_y(att_x[:middle]), swap_x(att_y[middle:])]
        att_other = [swap_side(piece) for piece in att_mine[:3]]
        att_mine, att_other, token_near = phase(att_mine, att_other, token_near)
        token_rows = sequences_of(token_swap.place(token_near))
        small = sum(
            jnp.sum(piece[:, 8 * att_rows :].astype(WIDE), axis=0) for piece in att_mine
        )
        small = in_order(small, swap_side(small.astype(LOW)).astype(WIDE), side, 1)
        att_all = att_mine + att_other + [swap_side(piece) for piece in att_mine[3:]]
        pack = place_planes(pack_pair, pack_parts)
        att_all, pack, token_rows, small = phase(att_all, pack, token_rows, small)
        pack_x, pack_y, cot_far = swap_x(pack), swap_y(pack), cot_swap.far()
        layout = [
            (0, 0, 0, planes),
            (0, 1, 0, planes),
            (1, 0, 0, planes),
            (1, 1, 0, middle),
            (1, 1, middle, planes - middle),
        ]
    else:
        small = lax.psum(small, ALL).astype(WIDE)
        att = lax.all_gather(att_pair, CHIPS, axis=0, tiled=False)
        pack = lax.all_gather(pack_pair, CHIPS, axis=0, tiled=False)

        def lay_out(value, matrices):
            value = value.reshape(chips, matrices, -1, half)
            return value.transpose(1, 0, 2, 3).reshape(1, -1, half)

        att = lay_out(att, 4)
        pack_rows = inner_pair.shape[0] * strips
        pack = jnp.concatenate(
            [lay_out(pack[:, :pack_rows], strips), lay_out(pack[:, pack_rows:], 1)], axis=1
        )
        att_all, pack_all = [[value, swap_side(value)] for value in (att, pack)]
        layout = [(0, 0, 0, 1)]
        token_rows = sequences_of(token_swap.place(token_swap.near(token_swap.far())))
        cot_rows = sequences_of(cot_swap.place(cot_swap.near(cot_swap.far())))
    vec = small[:8]
    bias = small[8 : 8 + strips].reshape(1, hidden)
    own_lengths = lax.dynamic_slice_in_dim(lengths, lax.axis_index(CONTEXT) * own_seqs, own_seqs)

    def in_place(pieces):
        return [(piece, WHERE_IT_IS) for piece in pieces]

    norm_shape = (own_seqs, PAIRS, 2, full_len)
    low_rows = (rows, width)
    seq_tile = tiles(full_len, width)
    vec_spec = whole(8, width)
    square = 2 * rows * width * width
    attend_flops = 8 * rows * full_len * width

    held = call(
        functools.partial(attend_kernel, layout),
        own_seqs,
        [
            (own_lengths, SCALARS),
            (coords, SCALARS),
            (token_rows, seq_tile),
            (vec, vec_spec),
        ]
        + in_place(att_all),
        [(low_rows, LOW, seq_tile)] * 4
        + [
            (low_rows, WIDE, seq_tile),
            (
                norm_shape,
                WIDE,
                pl.BlockSpec((1, PAIRS, 2, full_len), lambda i: (i, 0, 0, 0)),
            ),
        ],
        [
            pltpu.VMEM((4,) + dims + (att_block, width), LOW),
            pltpu.VMEM((width, full_len), LOW),
            pltpu.VMEM((width, full_len), WIDE),
            pltpu.SemaphoreType.DMA((4 * len(att_all),)),
        ],
        4 * square + 2 * attend_flops,
        20 * rows * width,
    )
    if in_pieces:
        held, pack_x, pack_y, cot_far = phase(held, pack_x, pack_y, cot_far)
        pack_mine = [pack, pack_x, pack_y, swap_y(pack_x[:middle]), swap_x(pack_y[middle:])]
        pack_other = [swap_side(piece) for piece in pack_mine[:3]]
        cot_near = cot_swap.near(cot_far)
        pack_mine, pack_other, cot_near = phase(pack_mine, pack_other, cot_near)
        cot_rows = sequences_of(cot_swap.place(cot_near))
        pack_all = pack_mine + pack_other + [swap_side(piece) for piece in pack_mine[3:]]
    query, key, value, mixed, first_sum, normalizer = held

    def grad_pieces(rows_here, columns, matrices=None):
        runs = 2 if in_pieces else 1
        lead = (runs, squares, dims[0] // runs) + ((matrices,) if matrices else ())
        shape = lead + (rows_here, columns)
        return [(shape, LOW, whole(*shape))] * 2

    tile = 256
    row_tile = tiles(tile, width)
    hidden_tile = tiles(tile, hidden)
    result, second_grad, hidden_low, outer_keep, outer_send, vec_ffn, bias_grad = phase(
        *call(
            functools.partial(ffn_kernel, layout),
            rows // tile,
            [
                (coords, SCALARS),
                (first_sum, row_tile),
                (cot_rows, row_tile),
                (vec, vec_spec),
                (bias, whole(1, hidden)),
            ]
            + in_place(pack_all),
            [
                (low_rows, LOW, row_tile),
                (low_rows, WIDE, row_tile),
                ((rows, hidden), LOW, hidden_tile),
            ]
            + grad_pieces(outer_block, half)
            + [((8, width), WIDE, vec_spec), ((1, hidden), WIDE, whole(1, hidden))],
            [
                pltpu.VMEM((1,) + dims + (inner_block, hidden), LOW),
                pltpu.VMEM((1,) + dims + (outer_block, width), LOW),
                pltpu.VMEM((hidden, width), WIDE),
                pltpu.VMEM((tile, hidden), LOW),
                pltpu.VMEM((tile, hidden), WIDE),
                pltpu.SemaphoreType.DMA(((strips + 1) * len(pack_all),)),
            ],
            16 * square + 60 * rows * hidden,
            30 * rows * width,
        )
    )
    result_swap = Exchange(by_position(result, own_seqs))
    if in_pieces:
        outer_sum = Sum(outer_keep, outer_send)
        outer_got, second_grad = phase(outer_sum.core(), second_grad)
        outer_got = outer_sum.first(outer_got)
    result_far = result_swap.far()

    first_grad, mixed_grad, mid_keep, mid_send, vec_mid = call(
        functools.partial(back_kernel, layout, layout),
        rows // tile,
        [
            (coords, SCALARS),
            (first_sum, row_tile),
            (second_grad, row_tile),
            (hidden_low, hidden_tile),
            (mixed, row_tile),
            (vec, vec_spec),
        ]
        + in_place(pack_all)
        + in_place(att_all),
        [(low_rows, WIDE, row_tile), (low_rows, LOW, row_tile)]
        + grad_pieces(inner_block, hidden // 2 + half)
        + [((8, width), WIDE, vec_spec)],
        [
            pltpu.VMEM((1,) + dims + (inner_block, hidden), LOW),
            pltpu.VMEM((1,) + dims + (att_block, width), LOW),
            pltpu.VMEM((width, hidden), WIDE),
            pltpu.VMEM((width, width), WIDE),
            pltpu.SemaphoreType.DMA((strips * len(pack_all) + len(att_all),)),
        ],
        10 * square,
        26 * rows * width,
    )
    if in_pieces:
        first_grad, mixed_grad, mid_keep, mid_send, vec_mid, outer_got, result_far = phase(
            first_grad, mixed_grad, mid_keep, mid_send, vec_mid, outer_got, result_far
        )
        mid_sum = Sum(mid_keep, mid_send)
        outer_got, mid_got = outer_sum.second(outer_got), mid_sum.core()
        outer_got, mid_got, mixed_grad = phase(outer_got, mid_got, mixed_grad)
        outer_got, mid_got = outer_sum.along(outer_got), mid_sum.first(mid_got)
    result_near = result_swap.near(result_far)

    grads = []
    for number in range(own_seqs):
        last = number == own_seqs - 1
        own_rows_spec = block(number, full_len, width)
        seq_shape = (full_len, width)
        earlier = grads if last else []
        outputs = [(seq_shape, LOW, whole(*seq_shape))] * 3
        scratch = [pltpu.VMEM((width, full_len), LOW), pltpu.VMEM((width, full_len), WIDE)]
        if last:
            outputs = (
                outputs + grad_pieces(att_block, half, 3) + [((8, width), WIDE, vec_spec)]
            )
            scratch = scratch + [pltpu.VMEM((width, width), WIDE)]
        found = call(
            functools.partial(attend_back_kernel, number, last),
            1,
            [
                (own_lengths, SCALARS),
                (coords, SCALARS),
                (token_rows, whole(rows, width)),
                (query, own_rows_spec),
                (key, own_rows_spec),
                (value, own_rows_spec),
                (mixed_grad, own_rows_spec),
                (normalizer, block(number, 1, PAIRS, 2, full_len)),
            ]
            + [(value_, whole(*seq_shape)) for value_ in earlier],
            outputs,
            scratch,
            5 * attend_flops // own_seqs + (3 * square if last else 0),
            20 * rows * width // own_seqs,
        )
        if in_pieces:
            found, outer_got, mid_got, mixed_grad, result_near = phase(
                found, outer_got, mid_got, mixed_grad, result_near
            )
            if number == 0:
                outer_got, mid_got = outer_sum.pair(outer_got, side), mid_sum.second(mid_got)
        grads = grads + list(found[:3])
    att_keep, att_send, vec_att = found[3:]

    small_grad = jnp.concatenate(
        [
            vec_ffn + vec_mid + vec_att,
            bias_grad.reshape(-1, width),
            jnp.zeros((tall - 8 - strips, width), WIDE),
        ],
        axis=0,
    )
    if in_pieces:
        att_sum = Sum(att_keep, att_send)
        att_got, small_got, grads = phase(att_sum.core(), swap_side(small_grad), grads)
        small_grad = small_grad + small_got
        att_got, mid_got = att_sum.first(att_got), mid_sum.along(mid_got)
        small_got = swap_y(small_grad)

    seq_shape = (full_len, width)
    (input_grad,) = call(
        functools.partial(input_kernel, layout, own_seqs),
        1,
        [(coords, SCALARS), (first_grad, whole(rows, width))]
        + [(value_, whole(*seq_shape)) for value_ in grads]
        + in_place(att_all),
        [(low_rows, LOW, whole(rows, width))],
        [
            pltpu.VMEM((3,) + dims + (att_block, width), LOW),
            pltpu.SemaphoreType.DMA((3 * len(att_all),)),
        ],
        3 * square,
        12 * rows * width,
    )
    if in_pieces:
        input_grad, att_got, mid_got, small_got = phase(input_grad, att_got, mid_got, small_got)
    input_swap = Exchange(by_position(input_grad, own_seqs))
    if in_pieces:
        att_got = att_sum.second(att_got)
        small_grad = small_grad + small_got
        small_got = swap_x(small_grad)
        input_far = input_swap.far()
        mid_got = mid_sum.pair(mid_got, side)
        outer_total = outer_sum.done(outer_got, side)
        att_got, small_got, mid_got = phase(att_got, small_got, mid_got)
        att_got = att_sum.along(att_got)
        small_grad = small_grad + small_got
        small_got = swap_planes(small_grad)
        split = hidden // 2
        inner_total = mid_sum.done(mid_got, side, slice(0, split))
        project_total = mid_sum.done(mid_got, side, slice(split, split + half))
        att_got, small_got, input_far = phase(att_got, small_got, input_far)
        input_near = input_swap.near(input_far)
        small_total = wide_sum(small_grad, *small_got)
        att_total = att_sum.done(att_sum.pair(att_got, side), side)
    else:
        input_near = input_swap.near(input_swap.far())

        def scatter(value):
            value = value.reshape((-1,) + value.shape[-2:])
            matrices, length, columns = value.shape
            value = value.reshape(matrices, chips, length // chips, columns)
            value = lax.psum_scatter(
                value.transpose(1, 0, 2, 3), CHIPS, scatter_dimension=0, tiled=False
            )
            return own_rows(value, side)

        att_total = scatter(att_keep + swap_side(att_send))
        outer_total = scatter(outer_keep + swap_side(outer_send))[0]
        mid = mid_keep + swap_side(mid_send)
        inner_total = scatter(mid[..., : hidden // 2])[0]
        project_total = scatter(mid[..., hidden // 2 :])[0]
        small_total = lax.psum(small_grad, ALL)
    output_tokens = positions_of(result_swap.place(result_near))
    input_grad = positions_of(input_swap.place(input_near)).astype(WIDE)
    attention_total = jnp.concatenate([att_total, project_total[None]], axis=0)
    vector_total = lax.dynamic_slice(small_total, (0, me * vec_cols), (8, vec_cols))
    bias_total = lax.dynamic_slice(
        small_total, (8 + me // per_row, me % per_row * bias_cols), (1, bias_cols)
    ).reshape(bias_cols)

    attention_square, attention_new = adam_step(
        attention_weights,
        attention_total,
        attention_first,
        attention_second,
        MATRIX_LEARN_RATE,
        WEIGHT_DECAY,
    )
    inner_square, inner_new = adam_step(
        inner_weights, inner_total, inner_first, inner_second, MATRIX_LEARN_RATE, WEIGHT_DECAY
    )
    outer_square, outer_new = adam_step(
        outer_weights,
        outer_total,
        outer_moment_first,
        outer_second,
        MATRIX_LEARN_RATE,
        WEIGHT_DECAY,
    )
    bias_square, bias_new = adam_step(
        inner_bias, bias_total, bias_first, bias_second, VECTOR_RATE, 0.0
    )
    vector_square, vector_new = adam_step(
        vectors, vector_total, vector_first, vector_second, VECTOR_RATE, 0.0
    )
    return (
        output_tokens,
        input_grad,
        attention_total,
        attention_square,
        attention_new,
        inner_total,
        inner_square,
        inner_new,
        outer_total,
        outer_square,
        outer_new,
        bias_total,
        bias_square,
        bias_new,
        vector_total,
        vector_square,
        vector_new,
    )


def solution(mesh):
    split = Mesh(
        np.asarray(mesh.devices).reshape(
            mesh.shape["dp"] // 2, 2, mesh.shape["context"] // 2, 2
        ),
        ALL,
    )
    dp = ("dp_hi", "dp_lo")
    rows3 = P(dp, CONTEXT, None)
    mid3 = P(None, ALL, None)
    row2 = P(ALL, None)
    col2 = P(None, ALL)
    one = P(ALL)
    return jax.shard_map(
        local,
        mesh=split,
        in_specs=(rows3, rows3, P(dp), mid3, row2, row2, one, col2)
        + (mid3, mid3, row2, row2, row2, row2, one, one, col2, col2),
        out_specs=(rows3, rows3)
        + (mid3,) * 3
        + (row2,) * 6
        + (one,) * 3
        + (col2,) * 3,
        check_vma=False,
    )
```

```python
import functools

import jax
import jax.numpy as jnp
import numpy as np
from jax import lax
from jax.experimental import pallas as pl
from jax.experimental.pallas import tpu as pltpu
from jax.sharding import Mesh, PartitionSpec as P

HEADS = 12
HEAD = 64
PAIR = 2 * HEAD
PAIRS = HEADS // 2
STEP = 10

NORM_EPS = 1e-12
BETA_ONE = 0.9
BETA_TWO = 0.999
ADAM_EPS = 1e-06
MATRIX_LEARN_RATE = 0.05
VECTOR_RATE = 0.5
WEIGHT_DECAY = 0.01
MASK_FILL = -1e30
SCORE_SCALE = HEAD ** (-0.5)
ROOT_HALF = 0.5**0.5
DENSITY = 0.3989422804014327

CHIPS = ("dp_hi", "dp_lo", "ctx_hi")
SIDE = "ctx_lo"
ALL = CHIPS + (SIDE,)
CONTEXT = ("ctx_hi", "ctx_lo")
LOW = jnp.bfloat16
WIDE = jnp.float32
VMEM_BYTES = 60 * 1024 * 1024


def adam_step(weight, gradient, moment_one, moment_two, step_rate, decay_rate):
    first_new = BETA_ONE * moment_one + (1.0 - BETA_ONE) * gradient
    second_new = BETA_TWO * moment_two + (1.0 - BETA_TWO) * gradient * gradient
    first_hat = first_new / (1.0 - BETA_ONE**STEP)
    second_hat = second_new / (1.0 - BETA_TWO**STEP)
    updated = weight - step_rate * (
        first_hat / (jnp.sqrt(second_hat) + ADAM_EPS) + decay_rate * weight
    )
    return (second_new, updated)


def matmul(left, right):
    return jnp.dot(left, right, preferred_element_type=WIDE)


def contract_rows(left, right):
    return lax.dot_general(left, right, (((0,), (0,)), ((), ())), preferred_element_type=WIDE)


def times_transpose(left, right):
    return lax.dot_general(left, right, (((1,), (1,)), ((), ())), preferred_element_type=WIDE)


def flip(value):
    return value.astype(WIDE).T


def norm_stats(value):
    centered = value - jnp.mean(value, axis=-1, keepdims=True)
    variance = jnp.mean(centered * centered, axis=-1, keepdims=True)
    scale = lax.rsqrt(variance + NORM_EPS)
    return centered * scale, scale


def norm_back(grad, gain, unit, scale):
    scaled = grad * gain
    return scale * (
        scaled
        - jnp.mean(scaled, axis=-1, keepdims=True)
        - unit * jnp.mean(scaled * unit, axis=-1, keepdims=True)
    )


def load_pieces(coords, moves, pieces, layout, target, sems, first=0):
    rows, half = target.shape[4], target.shape[5] // 2
    side, y_here, x_here, z_here = [coords[i] for i in range(4)]
    single = target.shape[2] == 1
    wide = pieces[0].shape[-1]
    copies = []
    for row, place, column in moves:
        for number, source in enumerate(pieces):
            which, order = divmod(number, len(layout))
            start = pl.multiple_of((side if which == 0 else 1 - side) * half + column, wide)
            columns = pl.ds(start, wide)
            y_at = 0 if single else (1 - y_here if layout[order][0] else y_here)
            if len(layout[order]) == 2:
                z_at = jnp.bitwise_xor(z_here, layout[order][1])
                goal = target.at[place, z_at, y_at, :, :, columns]
            else:
                _, x_other, plane, planes = layout[order]
                x_at = 0 if single else (1 - x_here if x_other else x_here)
                goal = target.at[place, pl.ds(plane, planes), y_at, x_at, :, columns]
            copies.append(
                pltpu.make_async_copy(
                    source.at[:, pl.ds(row, rows), :], goal, sems.at[first + len(copies)]
                )
            )
    return copies


def inner_moves(target, wide):
    rows, half = target.shape[4], target.shape[5] // 2
    return [(number * rows, 0, number * wide) for number in range(half // wide)]


def outer_moves(target, inner, wide):
    return [(inner.shape[4] * (inner.shape[5] // 2 // wide), 0, 0)]


def matrix_moves(picks, rows):
    return [(pick * rows, place, 0) for place, pick in enumerate(picks)]


def load_now(copies):
    for copy in copies:
        copy.start()
    for copy in copies:
        copy.wait()


def flat(target, place=0):
    _, planes, high, wide, rows, width = target.shape
    return target.at[place].reshape(planes * high * wide * rows, width)


def store_pieces(coords, keep_out, send_out, read, half, column=0, place=None):
    side, y_here, x_here = coords[0], coords[1], coords[2]
    runs, squares, planes = keep_out.shape[:3]
    rows = keep_out.shape[-2]
    into = pl.ds(column, half)
    for out, own_side in ((keep_out, side), (send_out, 1 - side)):
        columns = pl.ds(pl.multiple_of(own_side * half, half), half)
        for run in range(runs):
            for square in range(squares):
                high, low = square // 2, square % 2
                y_other, x_other = (high, low) if run == 0 else (low, high)
                for number in range(planes):
                    block = run * planes + number
                    if squares > 1:
                        y_at = 1 - y_here if y_other else y_here
                        x_at = 1 - x_here if x_other else x_here
                        block = (block * 2 + y_at) * 2 + x_at
                    start = pl.multiple_of(block * rows, rows)
                    part = read(pl.ds(start, rows), columns).astype(LOW)
                    if place is None:
                        out[run, square, number, :, into] = part
                    else:
                        out[run, square, number, place, :, into] = part


def head_masks():
    lane = lax.broadcasted_iota(jnp.int32, (1, PAIR), 1)
    return [lane < HEAD, lane >= HEAD]


def only(value, mask):
    return jnp.where(mask, value, 0.0).astype(LOW)


def masked_pair(queries, keys, fill, head, masks):
    lane = lax.broadcasted_iota(jnp.int32, (1, PAIR), 1)
    marker = (lane == (1 - head) * HEAD).astype(WIDE)
    left = jnp.where(masks[head], queries, marker).astype(LOW)
    right = jnp.where(masks[head], keys.astype(WIDE), fill).astype(LOW)
    return left, right


def attend_kernel(layout, *refs):
    pieces = 2 * len(layout)
    lengths, coords, tokens, vec = refs[:4]
    sources = refs[4 : 4 + pieces]
    query_out, key_out, value_out, mixed_out, sum_out, norm_out = refs[4 + pieces : 10 + pieces]
    weights, value_flip, mixed_flip, sems = refs[10 + pieces :]
    step = pl.program_id(0)
    copies = load_pieces(
        coords, matrix_moves(range(4), weights.shape[4]), sources, layout, weights, sems
    )

    @pl.when(step == 0)
    def _():
        for copy in copies:
            copy.start()

    def need(place):
        @pl.when(step == 0)
        def _():
            for copy in copies[place * pieces : (place + 1) * pieces]:
                copy.wait()

    length = lengths[step]
    rows = tokens[...]
    need(0)
    query_out[...] = (matmul(rows, flat(weights, 0)[...]) + vec[0:1, :]).astype(LOW)
    need(1)
    key_out[...] = matmul(rows, flat(weights, 1)[...]).astype(LOW)
    need(2)
    value_low = (matmul(rows, flat(weights, 2)[...]) + vec[1:2, :]).astype(LOW)
    value_out[...] = value_low
    value_flip[...] = flip(value_low).astype(LOW)
    size = tokens.shape[0]
    position = lax.broadcasted_iota(jnp.int32, (size, PAIR), 0)
    fill = jnp.where(position < length, 0.0, MASK_FILL)
    masks = head_masks()

    def one_pair(pair, carry):
        lanes = pl.ds(pl.multiple_of(pair * PAIR, PAIR), PAIR)
        keys = key_out[:, lanes]
        queries = query_out[:, lanes].astype(WIDE) * SCORE_SCALE
        mixed, norms = [], []
        for head in range(2):
            own_query, own_key = masked_pair(queries, keys, fill, head, masks)
            scores = times_transpose(own_key, own_query)
            peak = jnp.max(scores, axis=0, keepdims=True)
            exponent = jnp.exp(scores - peak)
            total = jnp.sum(exponent, axis=0, keepdims=True)
            prob = (exponent * (1.0 / total)).astype(LOW)
            start = pl.multiple_of(pair * PAIR + head * HEAD, HEAD)
            mixed.append(matmul(value_flip[pl.ds(start, HEAD), :], prob))
            norms.append(peak + jnp.log(total))
        mixed_flip[lanes, :] = jnp.concatenate(mixed, axis=0)
        norm_out[0, pair] = jnp.concatenate(norms, axis=0)
        return carry

    lax.fori_loop(0, PAIRS, one_pair, 0)
    need(3)
    mixed_low = mixed_flip[...].T.astype(LOW)
    mixed_out[...] = mixed_low
    sum_out[...] = rows.astype(WIDE) + matmul(mixed_low, flat(weights, 3)[...]) + vec[2:3, :]


def ffn_kernel(layout, *refs):
    pieces = 2 * len(layout)
    coords, first_sum, cotangent, vec, bias = refs[:5]
    sources = refs[5 : 5 + pieces]
    result_out, second_out, hidden_out, keep_out, send_out, vec_grad, bias_grad = refs[
        5 + pieces : 12 + pieces
    ]
    inner_at, outer_at, total, activated, slope, sems = refs[12 + pieces :]
    step = pl.program_id(0)

    wide = sources[0].shape[-1]
    copies = load_pieces(coords, inner_moves(inner_at, wide), sources, layout, inner_at, sems)
    outer_copies = load_pieces(
        coords,
        outer_moves(outer_at, inner_at, wide),
        sources,
        layout,
        outer_at,
        sems,
        len(copies),
    )

    @pl.when(step == 0)
    def _():
        for copy in copies + outer_copies:
            copy.start()
        vec_grad[...] = jnp.zeros_like(vec_grad)
        bias_grad[...] = jnp.zeros_like(bias_grad)
        total[...] = jnp.zeros_like(total)
        for copy in copies:
            copy.wait()

    inner, outer = flat(inner_at), flat(outer_at)
    unit, _ = norm_stats(first_sum[...])
    normed = unit * vec[4:5, :] + vec[5:6, :]
    normed_low = normed.astype(LOW)
    width, hidden = inner.shape
    second = normed + vec[3:4, :]
    for start in range(0, hidden, width):
        part = slice(start, start + width)
        pre = matmul(normed_low, inner[:, part]) + bias[:, part]
        cdf = 0.5 * (1.0 + lax.erf(pre * ROOT_HALF))
        active = (pre * cdf).astype(LOW)
        activated[:, part] = active
        slope[:, part] = cdf + pre * (DENSITY * jnp.exp(-0.5 * pre * pre))
        if start == 0:

            @pl.when(step == 0)
            def _():
                for copy in outer_copies:
                    copy.wait()

        second = second + matmul(active, outer[part, :])
    unit_two, scale_two = norm_stats(second)
    result_out[...] = (unit_two * vec[6:7, :] + vec[7:8, :]).astype(LOW)
    grad = cotangent[...].astype(WIDE)
    second_grad = norm_back(grad, vec[6:7, :], unit_two, scale_two)
    second_out[...] = second_grad
    grad_low = second_grad.astype(LOW)
    vec_grad[3:4, :] += jnp.sum(grad_low.astype(WIDE), axis=0, keepdims=True)
    vec_grad[6:7, :] += jnp.sum(grad * unit_two, axis=0, keepdims=True)
    vec_grad[7:8, :] += jnp.sum(grad, axis=0, keepdims=True)
    for start in range(0, hidden, width):
        part = slice(start, start + width)
        back = times_transpose(grad_low, outer[part, :])
        hidden_low = (back * slope[:, part]).astype(LOW)
        hidden_out[:, part] = hidden_low
        bias_grad[:, part] += jnp.sum(hidden_low.astype(WIDE), axis=0, keepdims=True)
        total[part, :] += contract_rows(activated[:, part], grad_low)

    @pl.when(step == pl.num_programs(0) - 1)
    def _():
        store_pieces(
            coords, keep_out, send_out, lambda r, c: total[r, c], keep_out.shape[-1]
        )


def back_kernel(pack_layout, att_layout, *refs):
    pack_pieces, att_pieces = 2 * len(pack_layout), 2 * len(att_layout)
    coords, first_sum, second_grad, hidden_low, mixed, vec = refs[:6]
    pack_from = refs[6 : 6 + pack_pieces]
    att_from = refs[6 + pack_pieces : 6 + pack_pieces + att_pieces]
    first_out, mixed_grad_out, keep_out, send_out, vec_grad = refs[
        6 + pack_pieces + att_pieces : 11 + pack_pieces + att_pieces
    ]
    inner_at, project_at, total, project_total, sems = refs[11 + pack_pieces + att_pieces :]
    step = pl.program_id(0)

    @pl.when(step == 0)
    def _():
        copies = load_pieces(
            coords,
            inner_moves(inner_at, pack_from[0].shape[-1]),
            pack_from,
            pack_layout,
            inner_at,
            sems,
        )
        copies = copies + load_pieces(
            coords,
            matrix_moves((3,), project_at.shape[4]),
            att_from,
            att_layout,
            project_at,
            sems,
            len(copies),
        )
        for copy in copies:
            copy.start()
        vec_grad[...] = jnp.zeros_like(vec_grad)
        total[...] = jnp.zeros_like(total)
        project_total[...] = jnp.zeros_like(project_total)
        for copy in copies:
            copy.wait()

    inner = flat(inner_at)
    unit, scale = norm_stats(first_sum[...])
    normed_flip = flip(unit * vec[4:5, :] + vec[5:6, :]).astype(LOW)
    width, hidden = total.shape
    grad = second_grad[...]
    for start in range(0, hidden, width):
        part = slice(start, start + width)
        grad = grad + times_transpose(hidden_low[:, part], inner[:, part])
        total[:, part] += matmul(normed_flip, hidden_low[:, part])
    first_grad = norm_back(grad, vec[4:5, :], unit, scale)
    first_out[...] = first_grad
    branch = first_grad.astype(LOW)
    vec_grad[2:3, :] += jnp.sum(branch.astype(WIDE), axis=0, keepdims=True)
    vec_grad[4:5, :] += jnp.sum(grad * unit, axis=0, keepdims=True)
    vec_grad[5:6, :] += jnp.sum(grad, axis=0, keepdims=True)
    mixed_grad_out[...] = times_transpose(branch, flat(project_at)[...]).astype(LOW)
    project_total[...] += contract_rows(mixed[...], branch)

    @pl.when(step == pl.num_programs(0) - 1)
    def _():
        store_pieces(coords, keep_out, send_out, lambda r, c: total[r, c], hidden // 2)
        store_pieces(
            coords,
            keep_out,
            send_out,
            lambda r, c: project_total[r, c],
            width // 2,
            hidden // 2,
        )


def attend_back_kernel(sequence, last, *refs):
    lengths, coords, tokens, query, key, value, mixed_grad, normalizer = refs[:8]
    count = 3 * sequence if last else 0
    earlier = refs[8 : 8 + count]
    query_out, key_out, value_out = refs[8 + count : 11 + count]
    scratch = refs[11 + count :]
    if last:
        keep_out, send_out, vec_grad = scratch[:3]
        scratch = scratch[3:]
        total = scratch[2]
    key_flip, query_flip = scratch[:2]
    length = lengths[sequence]
    size = query.shape[0]
    key_flip[...] = flip(key[...]).astype(LOW)
    position = lax.broadcasted_iota(jnp.int32, (size, PAIR), 0)
    fill = jnp.where(position < length, 0.0, MASK_FILL)
    masks = head_masks()

    def one_pair(pair, carry):
        lanes = pl.ds(pl.multiple_of(pair * PAIR, PAIR), PAIR)
        keys = key[:, lanes]
        values = value[:, lanes]
        queries = query[:, lanes].astype(WIDE) * SCORE_SCALE
        grads = mixed_grad[:, lanes].astype(WIDE)
        norms = normalizer[0, pair]
        query_parts, key_part, value_part = [], 0.0, 0.0
        for head in range(2):
            own_query = only(queries, masks[head])
            marked_query, own_key = masked_pair(queries, keys, fill, head, masks)
            own_grad = only(grads, masks[head])
            scores = times_transpose(own_key, marked_query)
            prob = jnp.exp(scores - norms[head : head + 1, :])
            prob_grad = times_transpose(values, own_grad)
            row_term = jnp.sum(prob_grad * prob, axis=0, keepdims=True)
            score_low = (prob * (prob_grad - row_term)).astype(LOW)
            value_part = value_part + matmul(prob.astype(LOW), own_grad)
            key_part = key_part + matmul(score_low, own_query)
            start = pl.multiple_of(pair * PAIR + head * HEAD, HEAD)
            query_parts.append(matmul(key_flip[pl.ds(start, HEAD), :], score_low))
        query_flip[lanes, :] = jnp.concatenate(query_parts, axis=0) * SCORE_SCALE
        key_out[:, lanes] = key_part.astype(LOW)
        value_out[:, lanes] = value_part.astype(LOW)
        return carry

    lax.fori_loop(0, PAIRS, one_pair, 0)
    query_out[...] = query_flip[...].T.astype(LOW)
    if not last:
        return
    vec_grad[...] = jnp.zeros_like(vec_grad)
    token_flip = flip(tokens[...]).astype(LOW)
    for place, own in enumerate((query_out, key_out, value_out)):
        grads = [earlier[3 * i + place] for i in range(sequence)] + [own]
        sums = 0.0
        for i, grad in enumerate(grads):
            part = matmul(token_flip[:, i * size : (i + 1) * size], grad[...])
            total[...] = part if i == 0 else total[...] + part
            if place != 1:
                sums = sums + jnp.sum(grad[...].astype(WIDE), axis=0, keepdims=True)
        if place != 1:
            vec_grad[place // 2 : place // 2 + 1, :] = sums
        store_pieces(
            coords,
            keep_out,
            send_out,
            lambda r, c: total[r, c],
            keep_out.shape[-1],
            place=place,
        )


def input_kernel(layout, sequences, *refs):
    pieces = 2 * len(layout)
    coords, first_grad = refs[:2]
    grads = refs[2 : 2 + 3 * sequences]
    sources = refs[2 + 3 * sequences : 2 + 3 * sequences + pieces]
    grad_out, weights, sems = refs[2 + 3 * sequences + pieces :]
    load_now(
        load_pieces(
            coords, matrix_moves(range(3), weights.shape[4]), sources, layout, weights, sems
        )
    )
    size = grads[0].shape[0]
    for number in range(sequences):
        part = slice(number * size, (number + 1) * size)
        grad = first_grad[part, :]
        for place in range(3):
            grad = grad + times_transpose(
                grads[3 * number + place][...], flat(weights, place)[...]
            )
        grad_out[part, :] = grad.astype(grad_out.dtype)


def call(kernel, grid, inputs, outputs, scratch, flops, moved, aliases=None):
    return pl.pallas_call(
        kernel,
        grid=(grid,),
        in_specs=[spec for _, spec in inputs],
        out_specs=[spec for _, _, spec in outputs],
        out_shape=[jax.ShapeDtypeStruct(shape, kind) for shape, kind, _ in outputs],
        scratch_shapes=scratch,
        input_output_aliases=aliases or {},
        compiler_params=pltpu.CompilerParams(
            dimension_semantics=("arbitrary",), vmem_limit_bytes=VMEM_BYTES
        ),
        cost_estimate=pl.CostEstimate(flops=flops, bytes_accessed=moved, transcendentals=0),
    )(*[array for array, _ in inputs])


SCALARS = pl.BlockSpec(memory_space=pltpu.SMEM)
WHERE_IT_IS = pl.BlockSpec(memory_space=pl.ANY)


def tiles(rows, width):
    return pl.BlockSpec((rows, width), lambda i: (i, 0))


def block(number, *shape):
    return pl.BlockSpec(shape, lambda i: (number,) + (0,) * (len(shape) - 1))


def whole(*shape):
    return pl.BlockSpec(shape, lambda i: (0,) * len(shape))


def swap(value, axis, offset=1):
    size = lax.axis_size(axis)
    return lax.ppermute(value, axis, [(i, i ^ offset) for i in range(size)])


def swap_side(value):
    return swap(value, SIDE)


def swap_x(value):
    return swap(value, "ctx_hi")


def swap_y(value):
    return swap(value, "dp_lo")


def phase(*values):
    return lax.optimization_barrier(values)


def in_order(mine, theirs, here, axis):
    return jnp.where(
        here == 0,
        jnp.concatenate([mine, theirs], axis=axis),
        jnp.concatenate([theirs, mine], axis=axis),
    )


def pair_shards(shard, side):
    half = shard.shape[-1] // 2
    axis = shard.ndim - 1
    mine = lax.dynamic_slice_in_dim(shard, side * half, half, axis)
    theirs = lax.dynamic_slice_in_dim(shard, (1 - side) * half, half, axis)
    return in_order(mine, swap_side(theirs), side, shard.ndim - 2)


def swap_planes(value):
    return [swap(value, "dp_hi", offset) for offset in range(1, lax.axis_size("dp_hi"))]


def place_planes(value, others):
    here = lax.axis_index("dp_hi")
    parts = [part[None] for part in [value] + others]
    bit = 0
    while len(parts) > 1:
        flag = (here >> bit) & 1
        parts = [
            in_order(parts[i], parts[i + 1], flag, 0) for i in range(0, len(parts), 2)
        ]
        bit += 1
    return parts[0]


def wide_sum(*arrays):
    return functools.reduce(lambda a, b: a + b, [a.astype(WIDE) for a in arrays])


class Sum:
    def __init__(self, keep, send):
        self.keep, self.send = keep, send
        self.planes = 2 * keep.shape[2]

    def core(self):
        return swap_side(self.send)

    def part(self, run, squares):
        return wide_sum(self.keep[run, squares], self.other[run, squares])

    def first(self, got):
        self.other = got
        far = slice(2, 4)
        return [swap_y(self.part(0, far).astype(LOW)), swap_x(self.part(1, far).astype(LOW))]

    def second(self, got):
        self.got = got
        sent = [wide_sum(self.part(run, 1), got[run][1]).astype(LOW) for run in range(2)]
        return [swap_x(sent[0]), swap_y(sent[1])]

    def along(self, got):
        total = jnp.concatenate(
            [
                wide_sum(self.part(run, 0), self.got[run][0], got[run]).astype(LOW)
                for run in range(2)
            ],
            axis=0,
        )
        here = lax.axis_index("dp_hi")
        pick = functools.partial(lax.dynamic_index_in_dim, total, axis=0, keepdims=False)
        self.own = pick(here)
        return [
            swap(pick(here ^ offset), "dp_hi", offset) for offset in range(1, self.planes)
        ]

    def pair(self, got, side):
        total = wide_sum(self.own, *got).astype(LOW)
        rows = total.shape[-2] // 2
        axis = total.ndim - 2
        self.rows = lax.dynamic_slice_in_dim(total, side * rows, rows, axis)
        return swap_side(lax.dynamic_slice_in_dim(total, (1 - side) * rows, rows, axis))

    def done(self, got, side, columns=slice(None)):
        axis = self.rows.ndim - 1
        return in_order(self.rows[..., columns], got[..., columns], side, axis).astype(WIDE)


def own_rows(total, side):
    rows = total.shape[-2] // 2
    axis = total.ndim - 2
    total = total.astype(LOW)
    mine = lax.dynamic_slice_in_dim(total, side * rows, rows, axis)
    theirs = lax.dynamic_slice_in_dim(total, (1 - side) * rows, rows, axis)
    return in_order(mine, swap_side(theirs), side, total.ndim - 1).astype(WIDE)


def pick(value, index, axis=0):
    return lax.dynamic_index_in_dim(value, index, axis, keepdims=False)


class Exchange:
    def __init__(self, blocks):
        self.x_here, self.side = lax.axis_index("ctx_hi"), lax.axis_index(SIDE)
        self.own = pick(blocks, self.x_here)
        self.sent = pick(blocks, 1 - self.x_here)

    def far(self):
        return [swap_x(self.sent), swap_side(pick(self.own, 1 - self.side))]

    def near(self, got):
        self.from_x, self.from_side = got
        return swap_side(pick(self.from_x, 1 - self.side))

    def place(self, got):
        own = pick(self.own, self.side)[None]
        far = pick(self.from_x, self.side)[None]
        return in_order(
            in_order(own, self.from_side[None], self.side, 0)[None],
            in_order(far, got[None], self.side, 0)[None],
            self.x_here,
            0,
        )


def by_sequence(value):
    return value.reshape((2, 2, -1) + value.shape[1:])


def sequences_of(blocks):
    parts = blocks.shape[0] * blocks.shape[1]
    own, here, width = blocks.shape[2:]
    blocks = blocks.reshape(parts, own, here, width)
    return blocks.transpose(1, 0, 2, 3).reshape(own * parts * here, width)


def by_position(value, sequences):
    width = value.shape[-1]
    blocks = value.reshape(sequences, 2, 2, -1, width)
    return blocks.transpose(1, 2, 0, 3, 4)


def positions_of(blocks):
    return blocks.reshape((-1,) + blocks.shape[3:])


def local(
    tokens,
    cotangent,
    lengths,
    attention_weights,
    inner_weights,
    outer_weights,
    inner_bias,
    vectors,
    attention_first,
    attention_second,
    inner_first,
    inner_second,
    outer_moment_first,
    outer_second,
    bias_first,
    bias_second,
    vector_first,
    vector_second,
):
    parts = lax.axis_size(CONTEXT)
    planes = lax.axis_size("dp_hi")
    chips = lax.axis_size(CHIPS)
    count = 2 * chips
    side = lax.axis_index(SIDE)
    coords = jnp.stack([side] + [lax.axis_index(axis) for axis in ("dp_lo", "ctx_hi", "dp_hi")])
    coords = coords.astype(jnp.int32)
    seq_count, local_len, width = tokens.shape
    hidden = inner_weights.shape[1]
    full_len = local_len * parts
    own_seqs = seq_count // parts
    rows = own_seqs * full_len
    att_rows, vec_cols, bias_cols = (
        attention_weights.shape[1],
        vectors.shape[1],
        inner_bias.shape[0],
    )
    half = width // 2
    tall = 16
    in_pieces = (2 * att_rows) % tall == 0
    if in_pieces:
        dims, squares = (planes, 2, 2), 4
        att_block, inner_block, outer_block = (
            2 * att_rows,
            2 * inner_weights.shape[0],
            2 * outer_weights.shape[0],
        )
    else:
        dims, squares = (1, 1, 1), 1
        att_block, inner_block, outer_block = width, width, hidden

    me = lax.axis_index(ALL)
    per_row = width // bias_cols
    small = jnp.zeros((tall, width), LOW)
    small = lax.dynamic_update_slice(small, vectors.astype(LOW), (0, me * vec_cols))
    small = lax.dynamic_update_slice(
        small, inner_bias.astype(LOW)[None], (8 + me // per_row, me % per_row * bias_cols)
    )
    att_pair = pair_shards(attention_weights.astype(LOW), side).reshape(8 * att_rows, half)
    if in_pieces:
        att_pair = jnp.concatenate([att_pair, small[:, :half], small[:, half:]], axis=0)
        att_pair, tokens, cotangent, inner_own, outer_own = phase(
            att_pair, tokens, cotangent, inner_weights, outer_weights
        )
        att_parts = swap_planes(att_pair)
    else:
        inner_own, outer_own = inner_weights, outer_weights
    inner_pair = pair_shards(inner_own.astype(LOW), side)
    outer_pair = pair_shards(outer_own.astype(LOW), side)
    strips = hidden // width
    pack_pair = jnp.concatenate(
        [
            inner_pair.reshape(-1, strips, half).transpose(1, 0, 2).reshape(-1, half),
            outer_pair,
        ],
        axis=0,
    )
    token_swap = Exchange(by_sequence(tokens))
    cot_swap = Exchange(by_sequence(cotangent.astype(LOW)))
    if in_pieces:
        middle = planes // 2
        token_far = token_swap.far()
        pack_x = swap_x(pack_pair)
        att_parts, pack_x = phase(att_parts, pack_x)
        att = place_planes(att_pair, att_parts)
        att_x, att_y = swap_x(att), swap_y(att)
        pack = in_order(pack_pair[None], pack_x[None], coords[2], 0)
        pack_z = [pack] + swap_planes(pack)
        pack_y = [swap_y(pack)]
        att_x, att_y, token_far, pack_z[1] = phase(att_x, att_y, token_far, pack_z[1])
        token_near = token_swap.near(token_far)
        att_mine = [att, att_x, att_y, swap_y(att_x[:middle]), swap_x(att_y[middle:])]
        att_other = [swap_side(piece) for piece in att_mine[:3]]
        early = max(2, planes - 1)
        pack_y = pack_y + [swap_y(piece) for piece in pack_z[1 : early - 1]]
        att_mine, att_other, token_near, pack_z[1:early], pack_y[0] = phase(
            att_mine, att_other, token_near, pack_z[1:early], pack_y[0]
        )
        token_rows = sequences_of(token_swap.place(token_near))
        small = sum(
            jnp.sum(piece[:, 8 * att_rows :].astype(WIDE), axis=0) for piece in att_mine
        )
        small = small + swap_side(small.astype(LOW)).astype(WIDE)
        small = jnp.concatenate([small[:tall], small[tall:]], axis=1)
        att_all = att_mine + att_other + [swap_side(piece) for piece in att_mine[3:]]
        att_all, token_rows, small, cotangent_sent = phase(
            att_all, token_rows, small, cot_swap.sent
        )
        cot_swap.sent = cotangent_sent
        pack_y = pack_y + [swap_y(piece) for piece in pack_z[early - 1 : early]]
        cot_far = cot_swap.far()
        pack_z_other = [swap_side(piece) for piece in pack_z[:early]]
        pack_y_other = [swap_side(pack_y[0])]
        att_layout = [
            (0, 0, 0, planes),
            (0, 1, 0, planes),
            (1, 0, 0, planes),
            (1, 1, 0, middle),
            (1, 1, middle, planes - middle),
        ]
        pack_layout = [(y, offset) for y in range(2) for offset in range(planes)]
    else:
        small = lax.psum(small, ALL).astype(WIDE)
        att = lax.all_gather(att_pair, CHIPS, axis=0, tiled=False)
        pack = lax.all_gather(pack_pair, CHIPS, axis=0, tiled=False)

        def lay_out(value, matrices):
            value = value.reshape(chips, matrices, -1, half)
            return value.transpose(1, 0, 2, 3).reshape(1, -1, half)

        att = lay_out(att, 4)
        pack_rows = inner_pair.shape[0] * strips
        pack = jnp.concatenate(
            [lay_out(pack[:, :pack_rows], strips), lay_out(pack[:, pack_rows:], 1)], axis=1
        )
        att_all, pack_all = [[value, swap_side(value)] for value in (att, pack)]
        att_layout = pack_layout = [(0, 0, 0, 1)]
        token_rows = sequences_of(token_swap.place(token_swap.near(token_swap.far())))
        cot_rows = sequences_of(cot_swap.place(cot_swap.near(cot_swap.far())))
    vec = small[:8]
    bias = small[8 : 8 + strips].reshape(1, hidden)
    own_lengths = lax.dynamic_slice_in_dim(lengths, lax.axis_index(CONTEXT) * own_seqs, own_seqs)

    def in_place(pieces):
        return [(piece, WHERE_IT_IS) for piece in pieces]

    norm_shape = (own_seqs, PAIRS, 2, full_len)
    low_rows = (rows, width)
    seq_tile = tiles(full_len, width)
    vec_spec = whole(8, width)
    square = 2 * rows * width * width
    attend_flops = 8 * rows * full_len * width

    held = call(
        functools.partial(attend_kernel, att_layout),
        own_seqs,
        [
            (own_lengths, SCALARS),
            (coords, SCALARS),
            (token_rows, seq_tile),
            (vec, vec_spec),
        ]
        + in_place(att_all),
        [(low_rows, LOW, seq_tile)] * 4
        + [
            (low_rows, WIDE, seq_tile),
            (
                norm_shape,
                WIDE,
                pl.BlockSpec((1, PAIRS, 2, full_len), lambda i: (i, 0, 0, 0)),
            ),
        ],
        [
            pltpu.VMEM((4,) + dims + (att_block, width), LOW),
            pltpu.VMEM((width, full_len), LOW),
            pltpu.VMEM((width, full_len), WIDE),
            pltpu.SemaphoreType.DMA((4 * len(att_all),)),
        ],
        4 * square + 2 * attend_flops,
        20 * rows * width,
    )
    if in_pieces:
        held, pack_z, pack_y, pack_z_other, pack_y_other, cot_far = phase(
            held, pack_z, pack_y, pack_z_other, pack_y_other, cot_far
        )
        known = len(pack_y)
        pack_y = pack_y + [swap_y(piece) for piece in pack_z[known:]]
        pack_z_other = pack_z_other + [swap_side(piece) for piece in pack_z[early:]]
        pack_y_other = pack_y_other + [swap_side(piece) for piece in pack_y[1:known]]
        cot_near = cot_swap.near(cot_far)
        pack_y, pack_z_other, pack_y_other, cot_near = phase(
            pack_y, pack_z_other, pack_y_other, cot_near
        )
        cot_rows = sequences_of(cot_swap.place(cot_near))
        pack_y_other = pack_y_other + [swap_side(piece) for piece in pack_y[known:]]
        pack_all = pack_z + pack_y + pack_z_other + pack_y_other
    query, key, value, mixed, first_sum, normalizer = held

    def grad_pieces(rows_here, columns, matrices=None):
        runs = 2 if in_pieces else 1
        lead = (runs, squares, dims[0] // runs) + ((matrices,) if matrices else ())
        shape = lead + (rows_here, columns)
        return [(shape, LOW, whole(*shape))] * 2

    tile = 256
    row_tile = tiles(tile, width)
    hidden_tile = tiles(tile, hidden)
    result, second_grad, hidden_low, outer_keep, outer_send, vec_ffn, bias_grad = phase(
        *call(
            functools.partial(ffn_kernel, pack_layout),
            rows // tile,
            [
                (coords, SCALARS),
                (first_sum, row_tile),
                (cot_rows, row_tile),
                (vec, vec_spec),
                (bias, whole(1, hidden)),
            ]
            + in_place(pack_all),
            [
                (low_rows, LOW, row_tile),
                (low_rows, WIDE, row_tile),
                ((rows, hidden), LOW, hidden_tile),
            ]
            + grad_pieces(outer_block, half)
            + [((8, width), WIDE, vec_spec), ((1, hidden), WIDE, whole(1, hidden))],
            [
                pltpu.VMEM((1,) + dims + (inner_block, hidden), LOW),
                pltpu.VMEM((1,) + dims + (outer_block, width), LOW),
                pltpu.VMEM((hidden, width), WIDE),
                pltpu.VMEM((tile, hidden), LOW),
                pltpu.VMEM((tile, hidden), WIDE),
                pltpu.SemaphoreType.DMA(((strips + 1) * len(pack_all),)),
            ],
            16 * square + 60 * rows * hidden,
            30 * rows * width,
        )
    )
    result_swap = Exchange(by_position(result, own_seqs))
    if in_pieces:
        outer_sum = Sum(outer_keep, outer_send)
        outer_got, second_grad = phase(outer_sum.core(), second_grad)
        outer_got = outer_sum.first(outer_got)
    result_far = result_swap.far()

    first_grad, mixed_grad, mid_keep, mid_send, vec_mid = call(
        functools.partial(back_kernel, pack_layout, att_layout),
        rows // tile,
        [
            (coords, SCALARS),
            (first_sum, row_tile),
            (second_grad, row_tile),
            (hidden_low, hidden_tile),
            (mixed, row_tile),
            (vec, vec_spec),
        ]
        + in_place(pack_all)
        + in_place(att_all),
        [(low_rows, WIDE, row_tile), (low_rows, LOW, row_tile)]
        + grad_pieces(inner_block, hidden // 2 + half)
        + [((8, width), WIDE, vec_spec)],
        [
            pltpu.VMEM((1,) + dims + (inner_block, hidden), LOW),
            pltpu.VMEM((1,) + dims + (att_block, width), LOW),
            pltpu.VMEM((width, hidden), WIDE),
            pltpu.VMEM((width, width), WIDE),
            pltpu.SemaphoreType.DMA((strips * len(pack_all) + len(att_all),)),
        ],
        10 * square,
        26 * rows * width,
    )
    if in_pieces:
        first_grad, mixed_grad, mid_keep, mid_send, vec_mid, outer_got, result_far = phase(
            first_grad, mixed_grad, mid_keep, mid_send, vec_mid, outer_got, result_far
        )
        mid_sum = Sum(mid_keep, mid_send)
        outer_got, mid_got = outer_sum.second(outer_got), mid_sum.core()
    result_near = result_swap.near(result_far)

    grads = []
    for number in range(own_seqs):
        last = number == own_seqs - 1
        own_rows_spec = block(number, full_len, width)
        seq_shape = (full_len, width)
        earlier = grads if last else []
        outputs = [(seq_shape, LOW, whole(*seq_shape))] * 3
        scratch = [pltpu.VMEM((width, full_len), LOW), pltpu.VMEM((width, full_len), WIDE)]
        if last:
            outputs = (
                outputs + grad_pieces(att_block, half, 3) + [((8, width), WIDE, vec_spec)]
            )
            scratch = scratch + [pltpu.VMEM((width, width), WIDE)]
        found = call(
            functools.partial(attend_back_kernel, number, last),
            1,
            [
                (own_lengths, SCALARS),
                (coords, SCALARS),
                (token_rows, whole(rows, width)),
                (query, own_rows_spec),
                (key, own_rows_spec),
                (value, own_rows_spec),
                (mixed_grad, own_rows_spec),
                (normalizer, block(number, 1, PAIRS, 2, full_len)),
            ]
            + [(value_, whole(*seq_shape)) for value_ in earlier],
            outputs,
            scratch,
            5 * attend_flops // own_seqs + (3 * square if last else 0),
            20 * rows * width // own_seqs,
        )
        if in_pieces:
            found, outer_got, mid_got, mixed_grad, result_near = phase(
                found, outer_got, mid_got, mixed_grad, result_near
            )
            if number == 0:
                outer_got, mid_got = outer_sum.along(outer_got), mid_sum.first(mid_got)
        grads = grads + list(found[:3])
    att_keep, att_send, vec_att = found[3:]

    small_grad = jnp.concatenate(
        [
            vec_ffn + vec_mid + vec_att,
            bias_grad.reshape(-1, width),
            jnp.zeros((tall - 8 - strips, width), WIDE),
        ],
        axis=0,
    )
    if in_pieces:
        att_sum = Sum(att_keep, att_send)
        att_got, small_got, grads, outer_got, mid_got, first_grad = phase(
            att_sum.core(), swap_side(small_grad), grads, outer_got, mid_got, first_grad
        )
        small_grad = small_grad + small_got
        att_got, mid_got = att_sum.first(att_got), mid_sum.second(mid_got)
        outer_got = outer_sum.pair(outer_got, side)
        small_got = swap_y(small_grad)

    seq_shape = (full_len, width)
    (input_grad,) = call(
        functools.partial(input_kernel, att_layout, own_seqs),
        1,
        [(coords, SCALARS), (first_grad, whole(rows, width))]
        + [(value_, whole(*seq_shape)) for value_ in grads]
        + in_place(att_all),
        [(low_rows, LOW, whole(rows, width))],
        [
            pltpu.VMEM((3,) + dims + (att_block, width), LOW),
            pltpu.SemaphoreType.DMA((3 * len(att_all),)),
        ],
        3 * square,
        12 * rows * width,
    )
    if in_pieces:
        input_grad, att_got, mid_got, small_got, outer_got = phase(
            input_grad, att_got, mid_got, small_got, outer_got
        )
    input_swap = Exchange(by_position(input_grad, own_seqs))
    if in_pieces:
        att_got = att_sum.second(att_got)
        small_grad = small_grad + small_got
        small_got = swap_x(small_grad)
        input_far = input_swap.far()
        mid_got = mid_sum.along(mid_got)
        outer_total = outer_sum.done(outer_got, side)
        att_got, small_got, mid_got = phase(att_got, small_got, mid_got)
        att_got = att_sum.along(att_got)
        small_grad = small_grad + small_got
        small_got = swap_planes(small_grad)
        mid_got = mid_sum.pair(mid_got, side)
        split = hidden // 2
        inner_total = mid_sum.done(mid_got, side, slice(0, split))
        project_total = mid_sum.done(mid_got, side, slice(split, split + half))
        att_got, small_got, input_far = phase(att_got, small_got, input_far)
        input_near = input_swap.near(input_far)
        small_total = wide_sum(small_grad, *small_got)
        att_total = att_sum.done(att_sum.pair(att_got, side), side)
    else:
        input_near = input_swap.near(input_swap.far())

        def scatter(value):
            value = value.reshape((-1,) + value.shape[-2:])
            matrices, length, columns = value.shape
            value = value.reshape(matrices, chips, length // chips, columns)
            value = lax.psum_scatter(
                value.transpose(1, 0, 2, 3), CHIPS, scatter_dimension=0, tiled=False
            )
            return own_rows(value, side)

        att_total = scatter(att_keep + swap_side(att_send))
        outer_total = scatter(outer_keep + swap_side(outer_send))[0]
        mid = mid_keep + swap_side(mid_send)
        inner_total = scatter(mid[..., : hidden // 2])[0]
        project_total = scatter(mid[..., hidden // 2 :])[0]
        small_total = lax.psum(small_grad, ALL)
    output_tokens = positions_of(result_swap.place(result_near))
    input_grad = positions_of(input_swap.place(input_near)).astype(WIDE)
    attention_total = jnp.concatenate([att_total, project_total[None]], axis=0)
    vector_total = lax.dynamic_slice(small_total, (0, me * vec_cols), (8, vec_cols))
    bias_total = lax.dynamic_slice(
        small_total, (8 + me // per_row, me % per_row * bias_cols), (1, bias_cols)
    ).reshape(bias_cols)

    attention_square, attention_new = adam_step(
        attention_weights,
        attention_total,
        attention_first,
        attention_second,
        MATRIX_LEARN_RATE,
        WEIGHT_DECAY,
    )
    inner_square, inner_new = adam_step(
        inner_weights, inner_total, inner_first, inner_second, MATRIX_LEARN_RATE, WEIGHT_DECAY
    )
    outer_square, outer_new = adam_step(
        outer_weights,
        outer_total,
        outer_moment_first,
        outer_second,
        MATRIX_LEARN_RATE,
        WEIGHT_DECAY,
    )
    bias_square, bias_new = adam_step(
        inner_bias, bias_total, bias_first, bias_second, VECTOR_RATE, 0.0
    )
    vector_square, vector_new = adam_step(
        vectors, vector_total, vector_first, vector_second, VECTOR_RATE, 0.0
    )
    return (
        output_tokens,
        input_grad,
        attention_total,
        attention_square,
        attention_new,
        inner_total,
        inner_square,
        inner_new,
        outer_total,
        outer_square,
        outer_new,
        bias_total,
        bias_square,
        bias_new,
        vector_total,
        vector_square,
        vector_new,
    )


def solution(mesh):
    split = Mesh(
        np.asarray(mesh.devices).reshape(
            mesh.shape["dp"] // 2, 2, mesh.shape["context"] // 2, 2
        ),
        ALL,
    )
    dp = ("dp_hi", "dp_lo")
    rows3 = P(dp, CONTEXT, None)
    mid3 = P(None, ALL, None)
    row2 = P(ALL, None)
    col2 = P(None, ALL)
    one = P(ALL)
    return jax.shard_map(
        local,
        mesh=split,
        in_specs=(rows3, rows3, P(dp), mid3, row2, row2, one, col2)
        + (mid3, mid3, row2, row2, row2, row2, one, one, col2, col2),
        out_specs=(rows3, rows3)
        + (mid3,) * 3
        + (row2,) * 6
        + (one,) * 3
        + (col2,) * 3,
        check_vma=False,
    )
```

```python
import functools

import jax
import jax.numpy as jnp
import numpy as np
from jax import lax
from jax.experimental import pallas as pl
from jax.experimental.pallas import tpu as pltpu
from jax.sharding import Mesh, PartitionSpec as P

HEADS = 12
HEAD = 64
PAIR = 2 * HEAD
PAIRS = HEADS // 2
STEP = 10

NORM_EPS = 1e-12
BETA_ONE = 0.9
BETA_TWO = 0.999
ADAM_EPS = 1e-06
MATRIX_LEARN_RATE = 0.05
VECTOR_RATE = 0.5
WEIGHT_DECAY = 0.01
MASK_FILL = -1e30
SCORE_SCALE = HEAD ** (-0.5)
ROOT_HALF = 0.5**0.5
DENSITY = 0.3989422804014327

CHIPS = ("dp_hi", "dp_lo", "ctx_hi")
SIDE = "ctx_lo"
ALL = CHIPS + (SIDE,)
CONTEXT = ("ctx_hi", "ctx_lo")
LOW = jnp.bfloat16
WIDE = jnp.float32
VMEM_BYTES = 60 * 1024 * 1024


def adam_step(weight, gradient, moment_one, moment_two, step_rate, decay_rate):
    first_new = BETA_ONE * moment_one + (1.0 - BETA_ONE) * gradient
    second_new = BETA_TWO * moment_two + (1.0 - BETA_TWO) * gradient * gradient
    first_hat = first_new / (1.0 - BETA_ONE**STEP)
    second_hat = second_new / (1.0 - BETA_TWO**STEP)
    updated = weight - step_rate * (
        first_hat / (jnp.sqrt(second_hat) + ADAM_EPS) + decay_rate * weight
    )
    return (second_new, updated)


def matmul(left, right):
    return jnp.dot(left, right, preferred_element_type=WIDE)


def contract_rows(left, right):
    return lax.dot_general(left, right, (((0,), (0,)), ((), ())), preferred_element_type=WIDE)


def times_transpose(left, right):
    return lax.dot_general(left, right, (((1,), (1,)), ((), ())), preferred_element_type=WIDE)


def flip(value):
    return value.astype(WIDE).T


def norm_stats(value):
    centered = value - jnp.mean(value, axis=-1, keepdims=True)
    variance = jnp.mean(centered * centered, axis=-1, keepdims=True)
    scale = lax.rsqrt(variance + NORM_EPS)
    return centered * scale, scale


def norm_back(grad, gain, unit, scale):
    scaled = grad * gain
    return scale * (
        scaled
        - jnp.mean(scaled, axis=-1, keepdims=True)
        - unit * jnp.mean(scaled * unit, axis=-1, keepdims=True)
    )


def load_pieces(coords, moves, pieces, layout, target, sems, first=0):
    rows, half = target.shape[4], target.shape[5] // 2
    side, y_here, x_here, z_here = [coords[i] for i in range(4)]
    single = target.shape[2] == 1
    wide = pieces[0].shape[-1]
    copies = []
    for row, place, column in moves:
        for number, source in enumerate(pieces):
            which, order = divmod(number, len(layout))
            start = pl.multiple_of((side if which == 0 else 1 - side) * half + column, wide)
            columns = pl.ds(start, wide)
            y_at = 0 if single else (1 - y_here if layout[order][0] else y_here)
            if len(layout[order]) == 2:
                z_at = jnp.bitwise_xor(z_here, layout[order][1])
                goal = target.at[place, z_at, y_at, :, :, columns]
            else:
                _, x_other, plane, planes = layout[order]
                x_at = 0 if single else (1 - x_here if x_other else x_here)
                goal = target.at[place, pl.ds(plane, planes), y_at, x_at, :, columns]
            copies.append(
                pltpu.make_async_copy(
                    source.at[:, pl.ds(row, rows), :], goal, sems.at[first + len(copies)]
                )
            )
    return copies


def inner_moves(target, wide):
    rows, half = target.shape[4], target.shape[5] // 2
    return [(number * rows, 0, number * wide) for number in range(half // wide)]


def outer_moves(target, inner, wide):
    return [(inner.shape[4] * (inner.shape[5] // 2 // wide), 0, 0)]


def matrix_moves(picks, rows):
    return [(pick * rows, place, 0) for place, pick in enumerate(picks)]


def load_now(copies):
    for copy in copies:
        copy.start()
    for copy in copies:
        copy.wait()


def flat(target, place=0):
    _, planes, high, wide, rows, width = target.shape
    return target.at[place].reshape(planes * high * wide * rows, width)


def store_pieces(coords, keep_out, send_out, read, half, column=0, place=None):
    side, y_here, x_here = coords[0], coords[1], coords[2]
    runs, squares, planes = keep_out.shape[:3]
    rows = keep_out.shape[-2]
    into = pl.ds(column, half)
    for out, own_side in ((keep_out, side), (send_out, 1 - side)):
        columns = pl.ds(pl.multiple_of(own_side * half, half), half)
        for run in range(runs):
            for square in range(squares):
                high, low = square // 2, square % 2
                y_other, x_other = (high, low) if run == 0 else (low, high)
                for number in range(planes):
                    block = run * planes + number
                    if squares > 1:
                        y_at = 1 - y_here if y_other else y_here
                        x_at = 1 - x_here if x_other else x_here
                        block = (block * 2 + y_at) * 2 + x_at
                    start = pl.multiple_of(block * rows, rows)
                    part = read(pl.ds(start, rows), columns).astype(LOW)
                    if place is None:
                        out[run, square, number, :, into] = part
                    else:
                        out[run, square, number, place, :, into] = part


def head_masks():
    lane = lax.broadcasted_iota(jnp.int32, (1, PAIR), 1)
    return [lane < HEAD, lane >= HEAD]


def only(value, mask):
    return jnp.where(mask, value, 0.0).astype(LOW)


def masked_pair(queries, keys, fill, head, masks):
    lane = lax.broadcasted_iota(jnp.int32, (1, PAIR), 1)
    marker = (lane == (1 - head) * HEAD).astype(WIDE)
    left = jnp.where(masks[head], queries, marker).astype(LOW)
    right = jnp.where(masks[head], keys.astype(WIDE), fill).astype(LOW)
    return left, right


def attend_kernel(layout, *refs):
    pieces = 2 * len(layout)
    lengths, coords, tokens, vec = refs[:4]
    sources = refs[4 : 4 + pieces]
    query_out, key_out, value_out, mixed_out, sum_out, norm_out = refs[4 + pieces : 10 + pieces]
    weights, value_flip, mixed_flip, sems = refs[10 + pieces :]
    step = pl.program_id(0)
    copies = load_pieces(
        coords, matrix_moves(range(4), weights.shape[4]), sources, layout, weights, sems
    )

    @pl.when(step == 0)
    def _():
        for copy in copies:
            copy.start()

    def need(place):
        @pl.when(step == 0)
        def _():
            for copy in copies[place * pieces : (place + 1) * pieces]:
                copy.wait()

    length = lengths[step]
    rows = tokens[...]
    need(0)
    query_out[...] = (matmul(rows, flat(weights, 0)[...]) + vec[0:1, :]).astype(LOW)
    need(1)
    key_out[...] = matmul(rows, flat(weights, 1)[...]).astype(LOW)
    need(2)
    value_low = (matmul(rows, flat(weights, 2)[...]) + vec[1:2, :]).astype(LOW)
    value_out[...] = value_low
    value_flip[...] = flip(value_low).astype(LOW)
    size = tokens.shape[0]
    position = lax.broadcasted_iota(jnp.int32, (size, PAIR), 0)
    fill = jnp.where(position < length, 0.0, MASK_FILL)
    masks = head_masks()

    def one_pair(pair, carry):
        lanes = pl.ds(pl.multiple_of(pair * PAIR, PAIR), PAIR)
        keys = key_out[:, lanes]
        queries = query_out[:, lanes].astype(WIDE) * SCORE_SCALE
        mixed, norms = [], []
        for head in range(2):
            own_query, own_key = masked_pair(queries, keys, fill, head, masks)
            scores = times_transpose(own_key, own_query)
            peak = jnp.max(scores, axis=0, keepdims=True)
            exponent = jnp.exp(scores - peak)
            total = jnp.sum(exponent, axis=0, keepdims=True)
            prob = (exponent * (1.0 / total)).astype(LOW)
            start = pl.multiple_of(pair * PAIR + head * HEAD, HEAD)
            mixed.append(matmul(value_flip[pl.ds(start, HEAD), :], prob))
            norms.append(peak + jnp.log(total))
        mixed_flip[lanes, :] = jnp.concatenate(mixed, axis=0)
        norm_out[0, pair] = jnp.concatenate(norms, axis=0)
        return carry

    lax.fori_loop(0, PAIRS, one_pair, 0)
    need(3)
    mixed_low = mixed_flip[...].T.astype(LOW)
    mixed_out[...] = mixed_low
    sum_out[...] = rows.astype(WIDE) + matmul(mixed_low, flat(weights, 3)[...]) + vec[2:3, :]


def ffn_kernel(layout, *refs):
    pieces = 2 * len(layout)
    coords, first_sum, cotangent, vec, bias = refs[:5]
    sources = refs[5 : 5 + pieces]
    result_out, second_out, hidden_out, keep_out, send_out, vec_grad, bias_grad = refs[
        5 + pieces : 12 + pieces
    ]
    inner_at, outer_at, total, activated, slope, sems = refs[12 + pieces :]
    step = pl.program_id(0)

    wide = sources[0].shape[-1]
    copies = load_pieces(coords, inner_moves(inner_at, wide), sources, layout, inner_at, sems)
    outer_copies = load_pieces(
        coords,
        outer_moves(outer_at, inner_at, wide),
        sources,
        layout,
        outer_at,
        sems,
        len(copies),
    )

    @pl.when(step == 0)
    def _():
        for copy in copies + outer_copies:
            copy.start()
        vec_grad[...] = jnp.zeros_like(vec_grad)
        bias_grad[...] = jnp.zeros_like(bias_grad)
        total[...] = jnp.zeros_like(total)
        for copy in copies + outer_copies:
            copy.wait()

    inner, outer = flat(inner_at), flat(outer_at)
    unit, _ = norm_stats(first_sum[...])
    normed = unit * vec[4:5, :] + vec[5:6, :]
    normed_low = normed.astype(LOW)
    width, hidden = inner.shape
    second = normed + vec[3:4, :]
    for start in range(0, hidden, width):
        part = slice(start, start + width)
        pre = matmul(normed_low, inner[:, part]) + bias[:, part]
        cdf = 0.5 * (1.0 + lax.erf(pre * ROOT_HALF))
        active = (pre * cdf).astype(LOW)
        activated[:, part] = active
        slope[:, part] = cdf + pre * (DENSITY * jnp.exp(-0.5 * pre * pre))
        second = second + matmul(active, outer[part, :])
    unit_two, scale_two = norm_stats(second)
    result_out[...] = (unit_two * vec[6:7, :] + vec[7:8, :]).astype(LOW)
    grad = cotangent[...].astype(WIDE)
    second_grad = norm_back(grad, vec[6:7, :], unit_two, scale_two)
    second_out[...] = second_grad
    grad_low = second_grad.astype(LOW)
    vec_grad[3:4, :] += jnp.sum(grad_low.astype(WIDE), axis=0, keepdims=True)
    vec_grad[6:7, :] += jnp.sum(grad * unit_two, axis=0, keepdims=True)
    vec_grad[7:8, :] += jnp.sum(grad, axis=0, keepdims=True)
    for start in range(0, hidden, width):
        part = slice(start, start + width)
        back = times_transpose(grad_low, outer[part, :])
        hidden_low = (back * slope[:, part]).astype(LOW)
        hidden_out[:, part] = hidden_low
        bias_grad[:, part] += jnp.sum(hidden_low.astype(WIDE), axis=0, keepdims=True)
        total[part, :] += contract_rows(activated[:, part], grad_low)

    @pl.when(step == pl.num_programs(0) - 1)
    def _():
        store_pieces(
            coords, keep_out, send_out, lambda r, c: total[r, c], keep_out.shape[-1]
        )


def back_kernel(pack_layout, att_layout, *refs):
    pack_pieces, att_pieces = 2 * len(pack_layout), 2 * len(att_layout)
    coords, first_sum, second_grad, hidden_low, mixed, vec = refs[:6]
    pack_from = refs[6 : 6 + pack_pieces]
    att_from = refs[6 + pack_pieces : 6 + pack_pieces + att_pieces]
    first_out, mixed_grad_out, keep_out, send_out, vec_grad = refs[
        6 + pack_pieces + att_pieces : 11 + pack_pieces + att_pieces
    ]
    inner_at, project_at, total, project_total, sems = refs[11 + pack_pieces + att_pieces :]
    step = pl.program_id(0)

    @pl.when(step == 0)
    def _():
        copies = load_pieces(
            coords,
            inner_moves(inner_at, pack_from[0].shape[-1]),
            pack_from,
            pack_layout,
            inner_at,
            sems,
        )
        copies = copies + load_pieces(
            coords,
            matrix_moves((3,), project_at.shape[4]),
            att_from,
            att_layout,
            project_at,
            sems,
            len(copies),
        )
        for copy in copies:
            copy.start()
        vec_grad[...] = jnp.zeros_like(vec_grad)
        total[...] = jnp.zeros_like(total)
        project_total[...] = jnp.zeros_like(project_total)
        for copy in copies:
            copy.wait()

    inner = flat(inner_at)
    unit, scale = norm_stats(first_sum[...])
    normed_flip = flip(unit * vec[4:5, :] + vec[5:6, :]).astype(LOW)
    width, hidden = total.shape
    grad = second_grad[...]
    for start in range(0, hidden, width):
        part = slice(start, start + width)
        grad = grad + times_transpose(hidden_low[:, part], inner[:, part])
        total[:, part] += matmul(normed_flip, hidden_low[:, part])
    first_grad = norm_back(grad, vec[4:5, :], unit, scale)
    first_out[...] = first_grad
    branch = first_grad.astype(LOW)
    vec_grad[2:3, :] += jnp.sum(branch.astype(WIDE), axis=0, keepdims=True)
    vec_grad[4:5, :] += jnp.sum(grad * unit, axis=0, keepdims=True)
    vec_grad[5:6, :] += jnp.sum(grad, axis=0, keepdims=True)
    mixed_grad_out[...] = times_transpose(branch, flat(project_at)[...]).astype(LOW)
    project_total[...] += contract_rows(mixed[...], branch)

    @pl.when(step == pl.num_programs(0) - 1)
    def _():
        store_pieces(coords, keep_out, send_out, lambda r, c: total[r, c], hidden // 2)
        store_pieces(
            coords,
            keep_out,
            send_out,
            lambda r, c: project_total[r, c],
            width // 2,
            hidden // 2,
        )


def attend_back_kernel(sequence, last, *refs):
    lengths, coords, tokens, query, key, value, mixed_grad, normalizer = refs[:8]
    count = 3 * sequence if last else 0
    earlier = refs[8 : 8 + count]
    query_out, key_out, value_out = refs[8 + count : 11 + count]
    scratch = refs[11 + count :]
    if last:
        keep_out, send_out, vec_grad = scratch[:3]
        scratch = scratch[3:]
        total = scratch[2]
    key_flip, query_flip = scratch[:2]
    length = lengths[sequence]
    size = query.shape[0]
    key_flip[...] = flip(key[...]).astype(LOW)
    position = lax.broadcasted_iota(jnp.int32, (size, PAIR), 0)
    fill = jnp.where(position < length, 0.0, MASK_FILL)
    masks = head_masks()

    def one_pair(pair, carry):
        lanes = pl.ds(pl.multiple_of(pair * PAIR, PAIR), PAIR)
        keys = key[:, lanes]
        values = value[:, lanes]
        queries = query[:, lanes].astype(WIDE) * SCORE_SCALE
        grads = mixed_grad[:, lanes].astype(WIDE)
        norms = normalizer[0, pair]
        query_parts, key_part, value_part = [], 0.0, 0.0
        for head in range(2):
            own_query = only(queries, masks[head])
            marked_query, own_key = masked_pair(queries, keys, fill, head, masks)
            own_grad = only(grads, masks[head])
            scores = times_transpose(own_key, marked_query)
            prob = jnp.exp(scores - norms[head : head + 1, :])
            prob_grad = times_transpose(values, own_grad)
            row_term = jnp.sum(prob_grad * prob, axis=0, keepdims=True)
            score_low = (prob * (prob_grad - row_term)).astype(LOW)
            value_part = value_part + matmul(prob.astype(LOW), own_grad)
            key_part = key_part + matmul(score_low, own_query)
            start = pl.multiple_of(pair * PAIR + head * HEAD, HEAD)
            query_parts.append(matmul(key_flip[pl.ds(start, HEAD), :], score_low))
        query_flip[lanes, :] = jnp.concatenate(query_parts, axis=0) * SCORE_SCALE
        key_out[:, lanes] = key_part.astype(LOW)
        value_out[:, lanes] = value_part.astype(LOW)
        return carry

    lax.fori_loop(0, PAIRS, one_pair, 0)
    query_out[...] = query_flip[...].T.astype(LOW)
    if not last:
        return
    vec_grad[...] = jnp.zeros_like(vec_grad)
    token_flip = flip(tokens[...]).astype(LOW)
    for place, own in enumerate((query_out, key_out, value_out)):
        grads = [earlier[3 * i + place] for i in range(sequence)] + [own]
        sums = 0.0
        for i, grad in enumerate(grads):
            part = matmul(token_flip[:, i * size : (i + 1) * size], grad[...])
            total[...] = part if i == 0 else total[...] + part
            if place != 1:
                sums = sums + jnp.sum(grad[...].astype(WIDE), axis=0, keepdims=True)
        if place != 1:
            vec_grad[place // 2 : place // 2 + 1, :] = sums
        store_pieces(
            coords,
            keep_out,
            send_out,
            lambda r, c: total[r, c],
            keep_out.shape[-1],
            place=place,
        )


def input_kernel(layout, sequences, *refs):
    pieces = 2 * len(layout)
    coords, first_grad = refs[:2]
    grads = refs[2 : 2 + 3 * sequences]
    sources = refs[2 + 3 * sequences : 2 + 3 * sequences + pieces]
    grad_out, weights, sems = refs[2 + 3 * sequences + pieces :]
    load_now(
        load_pieces(
            coords, matrix_moves(range(3), weights.shape[4]), sources, layout, weights, sems
        )
    )
    size = grads[0].shape[0]
    for number in range(sequences):
        part = slice(number * size, (number + 1) * size)
        grad = first_grad[part, :]
        for place in range(3):
            grad = grad + times_transpose(
                grads[3 * number + place][...], flat(weights, place)[...]
            )
        grad_out[part, :] = grad.astype(grad_out.dtype)


def call(kernel, grid, inputs, outputs, scratch, flops, moved, aliases=None):
    return pl.pallas_call(
        kernel,
        grid=(grid,),
        in_specs=[spec for _, spec in inputs],
        out_specs=[spec for _, _, spec in outputs],
        out_shape=[jax.ShapeDtypeStruct(shape, kind) for shape, kind, _ in outputs],
        scratch_shapes=scratch,
        input_output_aliases=aliases or {},
        compiler_params=pltpu.CompilerParams(
            dimension_semantics=("arbitrary",), vmem_limit_bytes=VMEM_BYTES
        ),
        cost_estimate=pl.CostEstimate(flops=flops, bytes_accessed=moved, transcendentals=0),
    )(*[array for array, _ in inputs])


SCALARS = pl.BlockSpec(memory_space=pltpu.SMEM)
WHERE_IT_IS = pl.BlockSpec(memory_space=pl.ANY)


def tiles(rows, width):
    return pl.BlockSpec((rows, width), lambda i: (i, 0))


def block(number, *shape):
    return pl.BlockSpec(shape, lambda i: (number,) + (0,) * (len(shape) - 1))


def whole(*shape):
    return pl.BlockSpec(shape, lambda i: (0,) * len(shape))


def swap(value, axis, offset=1):
    size = lax.axis_size(axis)
    return lax.ppermute(value, axis, [(i, i ^ offset) for i in range(size)])


def swap_side(value):
    return swap(value, SIDE)


def swap_x(value):
    return swap(value, "ctx_hi")


def swap_y(value):
    return swap(value, "dp_lo")


def phase(*values):
    return lax.optimization_barrier(values)


def in_order(mine, theirs, here, axis):
    return jnp.where(
        here == 0,
        jnp.concatenate([mine, theirs], axis=axis),
        jnp.concatenate([theirs, mine], axis=axis),
    )


def pair_shards(shard, side):
    half = shard.shape[-1] // 2
    axis = shard.ndim - 1
    mine = lax.dynamic_slice_in_dim(shard, side * half, half, axis)
    theirs = lax.dynamic_slice_in_dim(shard, (1 - side) * half, half, axis)
    return in_order(mine, swap_side(theirs), side, shard.ndim - 2)


def swap_planes(value):
    return [swap(value, "dp_hi", offset) for offset in range(1, lax.axis_size("dp_hi"))]


def place_planes(value, others):
    here = lax.axis_index("dp_hi")
    parts = [part[None] for part in [value] + others]
    bit = 0
    while len(parts) > 1:
        flag = (here >> bit) & 1
        parts = [
            in_order(parts[i], parts[i + 1], flag, 0) for i in range(0, len(parts), 2)
        ]
        bit += 1
    return parts[0]


def wide_sum(*arrays):
    return functools.reduce(lambda a, b: a + b, [a.astype(WIDE) for a in arrays])


class Sum:
    def __init__(self, keep, send):
        self.keep, self.send = keep, send
        self.planes = 2 * keep.shape[2]

    def core(self):
        return swap_side(self.send)

    def part(self, run, squares):
        return wide_sum(self.keep[run, squares], self.other[run, squares])

    def first(self, got):
        self.other = got
        far = slice(2, 4)
        return [swap_y(self.part(0, far).astype(LOW)), swap_x(self.part(1, far).astype(LOW))]

    def second(self, got):
        self.got = got
        sent = [wide_sum(self.part(run, 1), got[run][1]).astype(LOW) for run in range(2)]
        return [swap_x(sent[0]), swap_y(sent[1])]

    def total(self, got):
        return jnp.concatenate(
            [
                wide_sum(self.part(run, 0), self.got[run][0], got[run]).astype(LOW)
                for run in range(2)
            ],
            axis=0,
        )


def sum_planes(total):
    here = lax.axis_index("dp_hi")
    planes = total.shape[0]
    return pick(total, here), [
        swap(pick(total, here ^ offset), "dp_hi", offset) for offset in range(1, planes)
    ]


def own_rows(total, side):
    rows = total.shape[-2] // 2
    axis = total.ndim - 2
    total = total.astype(LOW)
    mine = lax.dynamic_slice_in_dim(total, side * rows, rows, axis)
    theirs = lax.dynamic_slice_in_dim(total, (1 - side) * rows, rows, axis)
    return in_order(mine, swap_side(theirs), side, total.ndim - 1).astype(WIDE)


def pick(value, index, axis=0):
    return lax.dynamic_index_in_dim(value, index, axis, keepdims=False)


class Exchange:
    def __init__(self, blocks):
        self.x_here, self.side = lax.axis_index("ctx_hi"), lax.axis_index(SIDE)
        self.own = pick(blocks, self.x_here)
        self.sent = pick(blocks, 1 - self.x_here)

    def far(self):
        return [swap_x(self.sent), swap_side(pick(self.own, 1 - self.side))]

    def near(self, got):
        self.from_x, self.from_side = got
        return swap_side(pick(self.from_x, 1 - self.side))

    def place(self, got):
        own = pick(self.own, self.side)[None]
        far = pick(self.from_x, self.side)[None]
        return in_order(
            in_order(own, self.from_side[None], self.side, 0)[None],
            in_order(far, got[None], self.side, 0)[None],
            self.x_here,
            0,
        )


def by_sequence(value):
    return value.reshape((2, 2, -1) + value.shape[1:])


def sequences_of(blocks):
    parts = blocks.shape[0] * blocks.shape[1]
    own, here, width = blocks.shape[2:]
    blocks = blocks.reshape(parts, own, here, width)
    return blocks.transpose(1, 0, 2, 3).reshape(own * parts * here, width)


def by_position(value, sequences):
    width = value.shape[-1]
    blocks = value.reshape(sequences, 2, 2, -1, width)
    return blocks.transpose(1, 2, 0, 3, 4)


def positions_of(blocks):
    return blocks.reshape((-1,) + blocks.shape[3:])


def local(
    tokens,
    cotangent,
    lengths,
    attention_weights,
    inner_weights,
    outer_weights,
    inner_bias,
    vectors,
    attention_first,
    attention_second,
    inner_first,
    inner_second,
    outer_moment_first,
    outer_second,
    bias_first,
    bias_second,
    vector_first,
    vector_second,
):
    parts = lax.axis_size(CONTEXT)
    planes = lax.axis_size("dp_hi")
    chips = lax.axis_size(CHIPS)
    count = 2 * chips
    side = lax.axis_index(SIDE)
    coords = jnp.stack([side] + [lax.axis_index(axis) for axis in ("dp_lo", "ctx_hi", "dp_hi")])
    coords = coords.astype(jnp.int32)
    seq_count, local_len, width = tokens.shape
    hidden = inner_weights.shape[1]
    full_len = local_len * parts
    own_seqs = seq_count // parts
    rows = own_seqs * full_len
    att_rows, vec_cols, bias_cols = (
        attention_weights.shape[1],
        vectors.shape[1],
        inner_bias.shape[0],
    )
    half = width // 2
    tall = 16
    in_pieces = (2 * att_rows) % tall == 0
    if in_pieces:
        dims, squares = (planes, 2, 2), 4
        att_block, inner_block, outer_block = (
            2 * att_rows,
            2 * inner_weights.shape[0],
            2 * outer_weights.shape[0],
        )
    else:
        dims, squares = (1, 1, 1), 1
        att_block, inner_block, outer_block = width, width, hidden

    me = lax.axis_index(ALL)
    per_row = width // bias_cols
    small = jnp.zeros((tall, width), LOW)
    small = lax.dynamic_update_slice(small, vectors.astype(LOW), (0, me * vec_cols))
    small = lax.dynamic_update_slice(
        small, inner_bias.astype(LOW)[None], (8 + me // per_row, me % per_row * bias_cols)
    )
    att_pair = pair_shards(attention_weights.astype(LOW), side).reshape(8 * att_rows, half)
    if in_pieces:
        att_pair = jnp.concatenate([att_pair, small[:, :half], small[:, half:]], axis=0)
        att_pair, tokens, inner_own, outer_own = phase(
            att_pair, tokens, inner_weights, outer_weights
        )
        att_parts = swap_planes(att_pair)
    else:
        inner_own, outer_own = inner_weights, outer_weights
    inner_pair = pair_shards(inner_own.astype(LOW), side)
    outer_pair = pair_shards(outer_own.astype(LOW), side)
    strips = hidden // width
    pack_pair = jnp.concatenate(
        [
            inner_pair.reshape(-1, strips, half).transpose(1, 0, 2).reshape(-1, half),
            outer_pair,
        ],
        axis=0,
    )
    token_swap = Exchange(by_sequence(tokens))
    if in_pieces:
        middle = planes // 2
        token_far = token_swap.far()
        pack_x = swap_x(pack_pair)
        att_parts, pack_x = phase(att_parts, pack_x)
        att = place_planes(att_pair, att_parts)
        att_x, att_y = swap_x(att), swap_y(att)
        pack = in_order(pack_pair[None], pack_x[None], coords[2], 0)
        pack_z = [pack] + swap_planes(pack)
        pack_y = [swap_y(pack)]
        att_x, att_y, token_far, pack_z[1] = phase(att_x, att_y, token_far, pack_z[1])
        token_near = token_swap.near(token_far)
        att_mine = [att, att_x, att_y, swap_y(att_x[:middle]), swap_x(att_y[middle:])]
        att_other = [swap_side(piece) for piece in att_mine[:3]]
        early = max(2, planes - 1)
        att_mine, att_other, token_near, pack_z[1:early], pack_y[0], cotangent = phase(
            att_mine, att_other, token_near, pack_z[1:early], pack_y[0], cotangent
        )
        cot_swap = Exchange(by_sequence(cotangent.astype(LOW)))
        token_rows = sequences_of(token_swap.place(token_near))
        small = sum(
            jnp.sum(piece[:, 8 * att_rows :].astype(WIDE), axis=0) for piece in att_mine
        )
        small = small + swap_side(small.astype(LOW)).astype(WIDE)
        small = jnp.concatenate([small[:tall], small[tall:]], axis=1)
        att_all = att_mine + att_other + [swap_side(piece) for piece in att_mine[3:]]
        att_all, token_rows, small, cotangent_sent = phase(
            att_all, token_rows, small, cot_swap.sent
        )
        cot_swap.sent = cotangent_sent
        pack_y = pack_y + [swap_y(piece) for piece in pack_z[1:early]]
        cot_far = cot_swap.far()
        pack_z_other = [swap_side(piece) for piece in pack_z[:early]]
        pack_y_other = [swap_side(pack_y[0])]
        att_layout = [
            (0, 0, 0, planes),
            (0, 1, 0, planes),
            (1, 0, 0, planes),
            (1, 1, 0, middle),
            (1, 1, middle, planes - middle),
        ]
        pack_layout = [(y, offset) for y in range(2) for offset in range(planes)]
    else:
        small = lax.psum(small, ALL).astype(WIDE)
        att = lax.all_gather(att_pair, CHIPS, axis=0, tiled=False)
        pack = lax.all_gather(pack_pair, CHIPS, axis=0, tiled=False)

        def lay_out(value, matrices):
            value = value.reshape(chips, matrices, -1, half)
            return value.transpose(1, 0, 2, 3).reshape(1, -1, half)

        att = lay_out(att, 4)
        pack_rows = inner_pair.shape[0] * strips
        pack = jnp.concatenate(
            [lay_out(pack[:, :pack_rows], strips), lay_out(pack[:, pack_rows:], 1)], axis=1
        )
        att_all, pack_all = [[value, swap_side(value)] for value in (att, pack)]
        att_layout = pack_layout = [(0, 0, 0, 1)]
        token_rows = sequences_of(token_swap.place(token_swap.near(token_swap.far())))
        cot_swap = Exchange(by_sequence(cotangent.astype(LOW)))
        cot_rows = sequences_of(cot_swap.place(cot_swap.near(cot_swap.far())))
    vec = small[:8]
    bias = small[8 : 8 + strips].reshape(1, hidden)
    own_lengths = lax.dynamic_slice_in_dim(lengths, lax.axis_index(CONTEXT) * own_seqs, own_seqs)

    def in_place(pieces):
        return [(piece, WHERE_IT_IS) for piece in pieces]

    norm_shape = (own_seqs, PAIRS, 2, full_len)
    low_rows = (rows, width)
    seq_tile = tiles(full_len, width)
    vec_spec = whole(8, width)
    square = 2 * rows * width * width
    attend_flops = 8 * rows * full_len * width

    held = call(
        functools.partial(attend_kernel, att_layout),
        own_seqs,
        [
            (own_lengths, SCALARS),
            (coords, SCALARS),
            (token_rows, seq_tile),
            (vec, vec_spec),
        ]
        + in_place(att_all),
        [(low_rows, LOW, seq_tile)] * 4
        + [
            (low_rows, WIDE, seq_tile),
            (
                norm_shape,
                WIDE,
                pl.BlockSpec((1, PAIRS, 2, full_len), lambda i: (i, 0, 0, 0)),
            ),
        ],
        [
            pltpu.VMEM((4,) + dims + (att_block, width), LOW),
            pltpu.VMEM((width, full_len), LOW),
            pltpu.VMEM((width, full_len), WIDE),
            pltpu.SemaphoreType.DMA((4 * len(att_all),)),
        ],
        4 * square + 2 * attend_flops,
        20 * rows * width,
    )
    if in_pieces:
        held, pack_z, pack_y, pack_z_other, pack_y_other, cot_far = phase(
            held, pack_z, pack_y, pack_z_other, pack_y_other, cot_far
        )
        known = len(pack_y)
        pack_y = pack_y + [swap_y(piece) for piece in pack_z[known:]]
        pack_z_other = pack_z_other + [swap_side(piece) for piece in pack_z[early:]]
        pack_y_other = pack_y_other + [swap_side(piece) for piece in pack_y[1:known]]
        cot_near = cot_swap.near(cot_far)
        pack_y, pack_z_other, pack_y_other, cot_near = phase(
            pack_y, pack_z_other, pack_y_other, cot_near
        )
        cot_rows = sequences_of(cot_swap.place(cot_near))
        pack_y_other = pack_y_other + [swap_side(piece) for piece in pack_y[known:]]
        pack_all = pack_z + pack_y + pack_z_other + pack_y_other
    query, key, value, mixed, first_sum, normalizer = held

    def grad_pieces(rows_here, columns, matrices=None):
        runs = 2 if in_pieces else 1
        lead = (runs, squares, dims[0] // runs) + ((matrices,) if matrices else ())
        shape = lead + (rows_here, columns)
        return [(shape, LOW, whole(*shape))] * 2

    tile = 256
    row_tile = tiles(tile, width)
    hidden_tile = tiles(tile, hidden)
    result, second_grad, hidden_low, outer_keep, outer_send, vec_ffn, bias_grad = phase(
        *call(
            functools.partial(ffn_kernel, pack_layout),
            rows // tile,
            [
                (coords, SCALARS),
                (first_sum, row_tile),
                (cot_rows, row_tile),
                (vec, vec_spec),
                (bias, whole(1, hidden)),
            ]
            + in_place(pack_all),
            [
                (low_rows, LOW, row_tile),
                (low_rows, WIDE, row_tile),
                ((rows, hidden), LOW, hidden_tile),
            ]
            + grad_pieces(outer_block, half)
            + [((8, width), WIDE, vec_spec), ((1, hidden), WIDE, whole(1, hidden))],
            [
                pltpu.VMEM((1,) + dims + (inner_block, hidden), LOW),
                pltpu.VMEM((1,) + dims + (outer_block, width), LOW),
                pltpu.VMEM((hidden, width), WIDE),
                pltpu.VMEM((tile, hidden), LOW),
                pltpu.VMEM((tile, hidden), WIDE),
                pltpu.SemaphoreType.DMA(((strips + 1) * len(pack_all),)),
            ],
            16 * square + 60 * rows * hidden,
            30 * rows * width,
        )
    )
    result_swap = Exchange(by_position(result, own_seqs))
    if in_pieces:
        outer_sum = Sum(outer_keep, outer_send)
        outer_got, second_grad = phase(outer_sum.core(), second_grad)
        outer_got = outer_sum.first(outer_got)
    result_far = result_swap.far()

    first_grad, mixed_grad, mid_keep, mid_send, vec_mid = call(
        functools.partial(back_kernel, pack_layout, att_layout),
        rows // tile,
        [
            (coords, SCALARS),
            (first_sum, row_tile),
            (second_grad, row_tile),
            (hidden_low, hidden_tile),
            (mixed, row_tile),
            (vec, vec_spec),
        ]
        + in_place(pack_all)
        + in_place(att_all),
        [(low_rows, WIDE, row_tile), (low_rows, LOW, row_tile)]
        + grad_pieces(inner_block, hidden // 2 + half)
        + [((8, width), WIDE, vec_spec)],
        [
            pltpu.VMEM((1,) + dims + (inner_block, hidden), LOW),
            pltpu.VMEM((1,) + dims + (att_block, width), LOW),
            pltpu.VMEM((width, hidden), WIDE),
            pltpu.VMEM((width, width), WIDE),
            pltpu.SemaphoreType.DMA((strips * len(pack_all) + len(att_all),)),
        ],
        10 * square,
        26 * rows * width,
    )
    if in_pieces:
        first_grad, mixed_grad, mid_keep, mid_send, vec_mid, outer_got, result_far = phase(
            first_grad, mixed_grad, mid_keep, mid_send, vec_mid, outer_got, result_far
        )
        mid_sum = Sum(mid_keep, mid_send)
        outer_got = outer_sum.second(outer_got)
        mid_got, mixed_grad = phase(mid_sum.core(), mixed_grad)
        mid_got = mid_sum.first(mid_got)
    result_near = result_swap.near(result_far)

    grads = []
    for number in range(own_seqs):
        last = number == own_seqs - 1
        own_rows_spec = block(number, full_len, width)
        seq_shape = (full_len, width)
        earlier = grads if last else []
        outputs = [(seq_shape, LOW, whole(*seq_shape))] * 3
        scratch = [pltpu.VMEM((width, full_len), LOW), pltpu.VMEM((width, full_len), WIDE)]
        if last:
            outputs = (
                outputs + grad_pieces(att_block, half, 3) + [((8, width), WIDE, vec_spec)]
            )
            scratch = scratch + [pltpu.VMEM((width, width), WIDE)]
        found = call(
            functools.partial(attend_back_kernel, number, last),
            1,
            [
                (own_lengths, SCALARS),
                (coords, SCALARS),
                (token_rows, whole(rows, width)),
                (query, own_rows_spec),
                (key, own_rows_spec),
                (value, own_rows_spec),
                (mixed_grad, own_rows_spec),
                (normalizer, block(number, 1, PAIRS, 2, full_len)),
            ]
            + [(value_, whole(*seq_shape)) for value_ in earlier],
            outputs,
            scratch,
            5 * attend_flops // own_seqs + (3 * square if last else 0),
            20 * rows * width // own_seqs,
        )
        if in_pieces:
            found, outer_got, mid_got, mixed_grad, result_near = phase(
                found, outer_got, mid_got, mixed_grad, result_near
            )
            if number == 0:
                outer_got, mid_got = outer_sum.total(outer_got), mid_sum.second(mid_got)
        grads = grads + list(found[:3])
    att_keep, att_send, vec_att = found[3:]

    small_grad = jnp.concatenate(
        [
            vec_ffn + vec_mid + vec_att,
            bias_grad.reshape(-1, width),
            jnp.zeros((tall - 8 - strips, width), WIDE),
        ],
        axis=0,
    )
    if in_pieces:
        att_sum = Sum(att_keep, att_send)
        strip = inner_block
        merged = jnp.concatenate(
            [mid_sum.total(mid_got)]
            + [
                outer_got[:, start : start + strip]
                for start in range(0, outer_block, strip)
            ],
            axis=2,
        )
        att_got, small_got, grads, merged, first_grad = phase(
            att_sum.core(), swap_side(small_grad), grads, merged, first_grad
        )
        small_grad = small_grad + small_got
        att_got = att_sum.first(att_got)
        merged, merged_got = sum_planes(merged)
        small_got = swap_y(small_grad)

    seq_shape = (full_len, width)
    (input_grad,) = call(
        functools.partial(input_kernel, att_layout, own_seqs),
        1,
        [(coords, SCALARS), (first_grad, whole(rows, width))]
        + [(value_, whole(*seq_shape)) for value_ in grads]
        + in_place(att_all),
        [(low_rows, LOW, whole(rows, width))],
        [
            pltpu.VMEM((3,) + dims + (att_block, width), LOW),
            pltpu.SemaphoreType.DMA((3 * len(att_all),)),
        ],
        3 * square,
        12 * rows * width,
    )
    if in_pieces:
        input_grad, att_got, small_got = phase(input_grad, att_got, small_got)
    input_blocks = by_position(input_grad, own_seqs)
    input_swaps = [Exchange(input_blocks[:, :, i : i + 1]) for i in range(own_seqs)]
    if in_pieces:
        att_got = att_sum.second(att_got)
        small_grad = small_grad + small_got
        small_got = swap_x(small_grad)
        input_far = [one.far() for one in input_swaps]
        att_got, small_got, merged_got, input_far[0] = phase(
            att_got, small_got, merged_got, input_far[0]
        )
        small_grad = small_grad + small_got
        att_own, att_got = sum_planes(att_sum.total(att_got))
        att_got[0], small_grad, merged, merged_got = phase(
            att_got[0], small_grad, merged, merged_got
        )
        small_got = swap_planes(small_grad)
        merged = wide_sum(merged, *merged_got)
        inner_total = own_rows(merged[:, : hidden // 2], side)
        project_total = own_rows(merged[:, hidden // 2 : hidden // 2 + half], side)
        outer_total = own_rows(
            jnp.concatenate(
                [
                    merged[:, start : start + half]
                    for start in range(hidden // 2 + half, merged.shape[1], half)
                ],
                axis=0,
            ),
            side,
        )
        att_total = own_rows(wide_sum(att_own, *att_got), side)
        input_near = [one.near(far) for one, far in zip(input_swaps, input_far)]
        small_total = wide_sum(small_grad, *small_got)
    else:
        input_near = [one.near(one.far()) for one in input_swaps]

        def scatter(value):
            value = value.reshape((-1,) + value.shape[-2:])
            matrices, length, columns = value.shape
            value = value.reshape(matrices, chips, length // chips, columns)
            value = lax.psum_scatter(
                value.transpose(1, 0, 2, 3), CHIPS, scatter_dimension=0, tiled=False
            )
            return own_rows(value, side)

        att_total = scatter(att_keep + swap_side(att_send))
        outer_total = scatter(outer_keep + swap_side(outer_send))[0]
        mid = mid_keep + swap_side(mid_send)
        inner_total = scatter(mid[..., : hidden // 2])[0]
        project_total = scatter(mid[..., hidden // 2 :])[0]
        small_total = lax.psum(small_grad, ALL)
    output_tokens = positions_of(result_swap.place(result_near))
    input_grad = jnp.concatenate(
        [one.place(near) for one, near in zip(input_swaps, input_near)], axis=2
    )
    input_grad = positions_of(input_grad).astype(WIDE)
    attention_total = jnp.concatenate([att_total, project_total[None]], axis=0)
    vector_total = lax.dynamic_slice(small_total, (0, me * vec_cols), (8, vec_cols))
    bias_total = lax.dynamic_slice(
        small_total, (8 + me // per_row, me % per_row * bias_cols), (1, bias_cols)
    ).reshape(bias_cols)

    attention_square, attention_new = adam_step(
        attention_weights,
        attention_total,
        attention_first,
        attention_second,
        MATRIX_LEARN_RATE,
        WEIGHT_DECAY,
    )
    inner_square, inner_new = adam_step(
        inner_weights, inner_total, inner_first, inner_second, MATRIX_LEARN_RATE, WEIGHT_DECAY
    )
    outer_square, outer_new = adam_step(
        outer_weights,
        outer_total,
        outer_moment_first,
        outer_second,
        MATRIX_LEARN_RATE,
        WEIGHT_DECAY,
    )
    bias_square, bias_new = adam_step(
        inner_bias, bias_total, bias_first, bias_second, VECTOR_RATE, 0.0
    )
    vector_square, vector_new = adam_step(
        vectors, vector_total, vector_first, vector_second, VECTOR_RATE, 0.0
    )
    return (
        output_tokens,
        input_grad,
        attention_total,
        attention_square,
        attention_new,
        inner_total,
        inner_square,
        inner_new,
        outer_total,
        outer_square,
        outer_new,
        bias_total,
        bias_square,
        bias_new,
        vector_total,
        vector_square,
        vector_new,
    )


def solution(mesh):
    split = Mesh(
        np.asarray(mesh.devices).reshape(
            mesh.shape["dp"] // 2, 2, mesh.shape["context"] // 2, 2
        ),
        ALL,
    )
    dp = ("dp_hi", "dp_lo")
    rows3 = P(dp, CONTEXT, None)
    mid3 = P(None, ALL, None)
    row2 = P(ALL, None)
    col2 = P(None, ALL)
    one = P(ALL)
    return jax.shard_map(
        local,
        mesh=split,
        in_specs=(rows3, rows3, P(dp), mid3, row2, row2, one, col2)
        + (mid3, mid3, row2, row2, row2, row2, one, one, col2, col2),
        out_specs=(rows3, rows3)
        + (mid3,) * 3
        + (row2,) * 6
        + (one,) * 3
        + (col2,) * 3,
        check_vma=False,
    )
```

```python
import functools

import jax
import jax.numpy as jnp
import numpy as np
from jax import lax
from jax.experimental import pallas as pl
from jax.experimental.pallas import tpu as pltpu
from jax.sharding import Mesh, PartitionSpec as P

HEADS = 12
HEAD = 64
PAIR = 2 * HEAD
PAIRS = HEADS // 2
STEP = 10

NORM_EPS = 1e-12
BETA_ONE = 0.9
BETA_TWO = 0.999
ADAM_EPS = 1e-06
MATRIX_LEARN_RATE = 0.05
VECTOR_RATE = 0.5
WEIGHT_DECAY = 0.01
MASK_FILL = -1e30
SCORE_SCALE = HEAD ** (-0.5)
ROOT_HALF = 0.5**0.5
DENSITY = 0.3989422804014327

CHIPS = ("dp_hi", "dp_lo", "ctx_hi")
SIDE = "ctx_lo"
ALL = CHIPS + (SIDE,)
CONTEXT = ("ctx_hi", "ctx_lo")
LOW = jnp.bfloat16
WIDE = jnp.float32
VMEM_BYTES = 60 * 1024 * 1024


def adam_step(weight, gradient, moment_one, moment_two, step_rate, decay_rate):
    first_new = BETA_ONE * moment_one + (1.0 - BETA_ONE) * gradient
    second_new = BETA_TWO * moment_two + (1.0 - BETA_TWO) * gradient * gradient
    first_hat = first_new / (1.0 - BETA_ONE**STEP)
    second_hat = second_new / (1.0 - BETA_TWO**STEP)
    updated = weight - step_rate * (
        first_hat / (jnp.sqrt(second_hat) + ADAM_EPS) + decay_rate * weight
    )
    return (second_new, updated)


def matmul(left, right):
    return jnp.dot(left, right, preferred_element_type=WIDE)


def contract_rows(left, right):
    return lax.dot_general(left, right, (((0,), (0,)), ((), ())), preferred_element_type=WIDE)


def times_transpose(left, right):
    return lax.dot_general(left, right, (((1,), (1,)), ((), ())), preferred_element_type=WIDE)


def flip(value):
    return value.astype(WIDE).T


def norm_stats(value):
    centered = value - jnp.mean(value, axis=-1, keepdims=True)
    variance = jnp.mean(centered * centered, axis=-1, keepdims=True)
    scale = lax.rsqrt(variance + NORM_EPS)
    return centered * scale, scale


def norm_back(grad, gain, unit, scale):
    scaled = grad * gain
    return scale * (
        scaled
        - jnp.mean(scaled, axis=-1, keepdims=True)
        - unit * jnp.mean(scaled * unit, axis=-1, keepdims=True)
    )


def load_pieces(coords, moves, pieces, layout, target, sems, first=0):
    rows, half = target.shape[4], target.shape[5] // 2
    side, y_here, x_here, z_here = [coords[i] for i in range(4)]
    single = target.shape[2] == 1
    wide = pieces[0].shape[-1]
    copies = []
    for row, place, column in moves:
        for number, source in enumerate(pieces):
            which, order = divmod(number, len(layout))
            start = pl.multiple_of((side if which == 0 else 1 - side) * half + column, wide)
            columns = pl.ds(start, wide)
            y_at = 0 if single else (1 - y_here if layout[order][0] else y_here)
            if len(layout[order]) == 2:
                z_at = jnp.bitwise_xor(z_here, layout[order][1])
                goal = target.at[place, z_at, y_at, :, :, columns]
            else:
                _, x_other, plane, planes = layout[order]
                x_at = 0 if single else (1 - x_here if x_other else x_here)
                goal = target.at[place, pl.ds(plane, planes), y_at, x_at, :, columns]
            copies.append(
                pltpu.make_async_copy(
                    source.at[:, pl.ds(row, rows), :], goal, sems.at[first + len(copies)]
                )
            )
    return copies


def inner_moves(target, wide):
    rows, half = target.shape[4], target.shape[5] // 2
    return [(number * rows, 0, number * wide) for number in range(half // wide)]


def outer_moves(target, inner, wide):
    return [(inner.shape[4] * (inner.shape[5] // 2 // wide), 0, 0)]


def matrix_moves(picks, rows):
    return [(pick * rows, place, 0) for place, pick in enumerate(picks)]


def load_now(copies):
    for copy in copies:
        copy.start()
    for copy in copies:
        copy.wait()


def flat(target, place=0):
    _, planes, high, wide, rows, width = target.shape
    return target.at[place].reshape(planes * high * wide * rows, width)


def store_pieces(coords, keep_out, send_out, read, half, column=0, place=None):
    side, y_here, x_here = coords[0], coords[1], coords[2]
    runs, squares, planes = keep_out.shape[:3]
    rows = keep_out.shape[-2]
    into = pl.ds(column, half)
    for out, own_side in ((keep_out, side), (send_out, 1 - side)):
        columns = pl.ds(pl.multiple_of(own_side * half, half), half)
        for run in range(runs):
            for square in range(squares):
                high, low = square // 2, square % 2
                y_other, x_other = (high, low) if run == 0 else (low, high)
                for number in range(planes):
                    block = run * planes + number
                    if squares > 1:
                        y_at = 1 - y_here if y_other else y_here
                        x_at = 1 - x_here if x_other else x_here
                        block = (block * 2 + y_at) * 2 + x_at
                    start = pl.multiple_of(block * rows, rows)
                    part = read(pl.ds(start, rows), columns).astype(LOW)
                    if place is None:
                        out[run, square, number, :, into] = part
                    else:
                        out[run, square, number, place, :, into] = part


def head_masks():
    lane = lax.broadcasted_iota(jnp.int32, (1, PAIR), 1)
    return [lane < HEAD, lane >= HEAD]


def only(value, mask):
    return jnp.where(mask, value, 0.0).astype(LOW)


def masked_pair(queries, keys, fill, head, masks):
    lane = lax.broadcasted_iota(jnp.int32, (1, PAIR), 1)
    marker = (lane == (1 - head) * HEAD).astype(WIDE)
    left = jnp.where(masks[head], queries, marker).astype(LOW)
    right = jnp.where(masks[head], keys.astype(WIDE), fill).astype(LOW)
    return left, right


def attend_kernel(layout, *refs):
    pieces = 2 * len(layout)
    lengths, coords, tokens, vec = refs[:4]
    sources = refs[4 : 4 + pieces]
    query_out, key_out, value_out, mixed_out, sum_out, norm_out = refs[4 + pieces : 10 + pieces]
    weights, value_flip, mixed_flip, sems = refs[10 + pieces :]
    step = pl.program_id(0)
    copies = load_pieces(
        coords, matrix_moves(range(4), weights.shape[4]), sources, layout, weights, sems
    )

    @pl.when(step == 0)
    def _():
        for copy in copies:
            copy.start()

    def need(place):
        @pl.when(step == 0)
        def _():
            for copy in copies[place * pieces : (place + 1) * pieces]:
                copy.wait()

    length = lengths[step]
    rows = tokens[...]
    need(0)
    query_out[...] = (matmul(rows, flat(weights, 0)[...]) + vec[0:1, :]).astype(LOW)
    need(1)
    key_out[...] = matmul(rows, flat(weights, 1)[...]).astype(LOW)
    need(2)
    value_low = (matmul(rows, flat(weights, 2)[...]) + vec[1:2, :]).astype(LOW)
    value_out[...] = value_low
    value_flip[...] = flip(value_low).astype(LOW)
    size = tokens.shape[0]
    position = lax.broadcasted_iota(jnp.int32, (size, PAIR), 0)
    fill = jnp.where(position < length, 0.0, MASK_FILL)
    masks = head_masks()

    def one_pair(pair, carry):
        lanes = pl.ds(pl.multiple_of(pair * PAIR, PAIR), PAIR)
        keys = key_out[:, lanes]
        queries = query_out[:, lanes].astype(WIDE) * SCORE_SCALE
        mixed, norms = [], []
        for head in range(2):
            own_query, own_key = masked_pair(queries, keys, fill, head, masks)
            scores = times_transpose(own_key, own_query)
            peak = jnp.max(scores, axis=0, keepdims=True)
            exponent = jnp.exp(scores - peak)
            total = jnp.sum(exponent, axis=0, keepdims=True)
            prob = (exponent * (1.0 / total)).astype(LOW)
            start = pl.multiple_of(pair * PAIR + head * HEAD, HEAD)
            mixed.append(matmul(value_flip[pl.ds(start, HEAD), :], prob))
            norms.append(peak + jnp.log(total))
        mixed_flip[lanes, :] = jnp.concatenate(mixed, axis=0)
        norm_out[0, pair] = jnp.concatenate(norms, axis=0)
        return carry

    lax.fori_loop(0, PAIRS, one_pair, 0)
    need(3)
    mixed_low = mixed_flip[...].T.astype(LOW)
    mixed_out[...] = mixed_low
    sum_out[...] = rows.astype(WIDE) + matmul(mixed_low, flat(weights, 3)[...]) + vec[2:3, :]


def ffn_kernel(layout, *refs):
    pieces = 2 * len(layout)
    coords, first_sum, cotangent, vec, bias = refs[:5]
    sources = refs[5 : 5 + pieces]
    result_out, second_out, hidden_out, keep_out, send_out, vec_grad, bias_grad = refs[
        5 + pieces : 12 + pieces
    ]
    inner_at, outer_at, total, activated, slope, sems = refs[12 + pieces :]
    step = pl.program_id(0)

    wide = sources[0].shape[-1]
    copies = load_pieces(coords, inner_moves(inner_at, wide), sources, layout, inner_at, sems)
    outer_copies = load_pieces(
        coords,
        outer_moves(outer_at, inner_at, wide),
        sources,
        layout,
        outer_at,
        sems,
        len(copies),
    )

    @pl.when(step == 0)
    def _():
        for copy in copies + outer_copies:
            copy.start()
        vec_grad[...] = jnp.zeros_like(vec_grad)
        bias_grad[...] = jnp.zeros_like(bias_grad)
        total[...] = jnp.zeros_like(total)
        for copy in copies + outer_copies:
            copy.wait()

    inner, outer = flat(inner_at), flat(outer_at)
    unit, _ = norm_stats(first_sum[...])
    normed = unit * vec[4:5, :] + vec[5:6, :]
    normed_low = normed.astype(LOW)
    width, hidden = inner.shape
    second = normed + vec[3:4, :]
    for start in range(0, hidden, width):
        part = slice(start, start + width)
        pre = matmul(normed_low, inner[:, part]) + bias[:, part]
        cdf = 0.5 * (1.0 + lax.erf(pre * ROOT_HALF))
        active = (pre * cdf).astype(LOW)
        activated[:, part] = active
        slope[:, part] = cdf + pre * (DENSITY * jnp.exp(-0.5 * pre * pre))
        second = second + matmul(active, outer[part, :])
    unit_two, scale_two = norm_stats(second)
    result_out[...] = (unit_two * vec[6:7, :] + vec[7:8, :]).astype(LOW)
    grad = cotangent[...].astype(WIDE)
    second_grad = norm_back(grad, vec[6:7, :], unit_two, scale_two)
    second_out[...] = second_grad
    grad_low = second_grad.astype(LOW)
    vec_grad[3:4, :] += jnp.sum(grad_low.astype(WIDE), axis=0, keepdims=True)
    vec_grad[6:7, :] += jnp.sum(grad * unit_two, axis=0, keepdims=True)
    vec_grad[7:8, :] += jnp.sum(grad, axis=0, keepdims=True)
    for start in range(0, hidden, width):
        part = slice(start, start + width)
        back = times_transpose(grad_low, outer[part, :])
        hidden_low = (back * slope[:, part]).astype(LOW)
        hidden_out[:, part] = hidden_low
        bias_grad[:, part] += jnp.sum(hidden_low.astype(WIDE), axis=0, keepdims=True)
        total[part, :] += contract_rows(activated[:, part], grad_low)

    @pl.when(step == pl.num_programs(0) - 1)
    def _():
        store_pieces(
            coords, keep_out, send_out, lambda r, c: total[r, c], keep_out.shape[-1]
        )


def back_kernel(pack_layout, att_layout, *refs):
    pack_pieces, att_pieces = 2 * len(pack_layout), 2 * len(att_layout)
    coords, first_sum, second_grad, hidden_low, mixed, vec = refs[:6]
    pack_from = refs[6 : 6 + pack_pieces]
    att_from = refs[6 + pack_pieces : 6 + pack_pieces + att_pieces]
    first_out, mixed_grad_out, keep_out, send_out, vec_grad = refs[
        6 + pack_pieces + att_pieces : 11 + pack_pieces + att_pieces
    ]
    inner_at, project_at, total, project_total, sems = refs[11 + pack_pieces + att_pieces :]
    step = pl.program_id(0)

    @pl.when(step == 0)
    def _():
        copies = load_pieces(
            coords,
            inner_moves(inner_at, pack_from[0].shape[-1]),
            pack_from,
            pack_layout,
            inner_at,
            sems,
        )
        copies = copies + load_pieces(
            coords,
            matrix_moves((3,), project_at.shape[4]),
            att_from,
            att_layout,
            project_at,
            sems,
            len(copies),
        )
        for copy in copies:
            copy.start()
        vec_grad[...] = jnp.zeros_like(vec_grad)
        total[...] = jnp.zeros_like(total)
        project_total[...] = jnp.zeros_like(project_total)
        for copy in copies:
            copy.wait()

    inner = flat(inner_at)
    unit, scale = norm_stats(first_sum[...])
    normed_flip = flip(unit * vec[4:5, :] + vec[5:6, :]).astype(LOW)
    width, hidden = total.shape
    grad = second_grad[...]
    for start in range(0, hidden, width):
        part = slice(start, start + width)
        grad = grad + times_transpose(hidden_low[:, part], inner[:, part])
        total[:, part] += matmul(normed_flip, hidden_low[:, part])
    first_grad = norm_back(grad, vec[4:5, :], unit, scale)
    first_out[...] = first_grad
    branch = first_grad.astype(LOW)
    vec_grad[2:3, :] += jnp.sum(branch.astype(WIDE), axis=0, keepdims=True)
    vec_grad[4:5, :] += jnp.sum(grad * unit, axis=0, keepdims=True)
    vec_grad[5:6, :] += jnp.sum(grad, axis=0, keepdims=True)
    mixed_grad_out[...] = times_transpose(branch, flat(project_at)[...]).astype(LOW)
    project_total[...] += contract_rows(mixed[...], branch)

    @pl.when(step == pl.num_programs(0) - 1)
    def _():
        store_pieces(coords, keep_out, send_out, lambda r, c: total[r, c], hidden // 2)
        store_pieces(
            coords,
            keep_out,
            send_out,
            lambda r, c: project_total[r, c],
            width // 2,
            hidden // 2,
        )


def attend_back_kernel(sequence, last, *refs):
    lengths, coords, tokens, query, key, value, mixed_grad, normalizer = refs[:8]
    count = 3 * sequence if last else 0
    earlier = refs[8 : 8 + count]
    query_out, key_out, value_out = refs[8 + count : 11 + count]
    scratch = refs[11 + count :]
    if last:
        keep_out, send_out, vec_grad = scratch[:3]
        scratch = scratch[3:]
        total = scratch[2]
    key_flip, query_flip = scratch[:2]
    length = lengths[sequence]
    size = query.shape[0]
    key_flip[...] = flip(key[...]).astype(LOW)
    position = lax.broadcasted_iota(jnp.int32, (size, PAIR), 0)
    fill = jnp.where(position < length, 0.0, MASK_FILL)
    masks = head_masks()

    def one_pair(pair, carry):
        lanes = pl.ds(pl.multiple_of(pair * PAIR, PAIR), PAIR)
        keys = key[:, lanes]
        values = value[:, lanes]
        queries = query[:, lanes].astype(WIDE) * SCORE_SCALE
        grads = mixed_grad[:, lanes].astype(WIDE)
        norms = normalizer[0, pair]
        query_parts, key_part, value_part = [], 0.0, 0.0
        for head in range(2):
            own_query = only(queries, masks[head])
            marked_query, own_key = masked_pair(queries, keys, fill, head, masks)
            own_grad = only(grads, masks[head])
            scores = times_transpose(own_key, marked_query)
            prob = jnp.exp(scores - norms[head : head + 1, :])
            prob_grad = times_transpose(values, own_grad)
            row_term = jnp.sum(prob_grad * prob, axis=0, keepdims=True)
            score_low = (prob * (prob_grad - row_term)).astype(LOW)
            value_part = value_part + matmul(prob.astype(LOW), own_grad)
            key_part = key_part + matmul(score_low, own_query)
            start = pl.multiple_of(pair * PAIR + head * HEAD, HEAD)
            query_parts.append(matmul(key_flip[pl.ds(start, HEAD), :], score_low))
        query_flip[lanes, :] = jnp.concatenate(query_parts, axis=0) * SCORE_SCALE
        key_out[:, lanes] = key_part.astype(LOW)
        value_out[:, lanes] = value_part.astype(LOW)
        return carry

    lax.fori_loop(0, PAIRS, one_pair, 0)
    query_out[...] = query_flip[...].T.astype(LOW)
    if not last:
        return
    vec_grad[...] = jnp.zeros_like(vec_grad)
    token_flip = flip(tokens[...]).astype(LOW)
    for place, own in enumerate((query_out, key_out, value_out)):
        grads = [earlier[3 * i + place] for i in range(sequence)] + [own]
        sums = 0.0
        for i, grad in enumerate(grads):
            part = matmul(token_flip[:, i * size : (i + 1) * size], grad[...])
            total[...] = part if i == 0 else total[...] + part
            if place != 1:
                sums = sums + jnp.sum(grad[...].astype(WIDE), axis=0, keepdims=True)
        if place != 1:
            vec_grad[place // 2 : place // 2 + 1, :] = sums
        store_pieces(
            coords,
            keep_out,
            send_out,
            lambda r, c: total[r, c],
            keep_out.shape[-1],
            place=place,
        )


def input_kernel(layout, sequences, *refs):
    pieces = 2 * len(layout)
    coords, first_grad = refs[:2]
    grads = refs[2 : 2 + 3 * sequences]
    sources = refs[2 + 3 * sequences : 2 + 3 * sequences + pieces]
    grad_out, weights, sems = refs[2 + 3 * sequences + pieces :]
    load_now(
        load_pieces(
            coords, matrix_moves(range(3), weights.shape[4]), sources, layout, weights, sems
        )
    )
    size = grads[0].shape[0]
    for number in range(sequences):
        part = slice(number * size, (number + 1) * size)
        grad = first_grad[part, :]
        for place in range(3):
            grad = grad + times_transpose(
                grads[3 * number + place][...], flat(weights, place)[...]
            )
        grad_out[part, :] = grad.astype(grad_out.dtype)


def call(kernel, grid, inputs, outputs, scratch, flops, moved, aliases=None):
    return pl.pallas_call(
        kernel,
        grid=(grid,),
        in_specs=[spec for _, spec in inputs],
        out_specs=[spec for _, _, spec in outputs],
        out_shape=[jax.ShapeDtypeStruct(shape, kind) for shape, kind, _ in outputs],
        scratch_shapes=scratch,
        input_output_aliases=aliases or {},
        compiler_params=pltpu.CompilerParams(
            dimension_semantics=("arbitrary",), vmem_limit_bytes=VMEM_BYTES
        ),
        cost_estimate=pl.CostEstimate(flops=flops, bytes_accessed=moved, transcendentals=0),
    )(*[array for array, _ in inputs])


SCALARS = pl.BlockSpec(memory_space=pltpu.SMEM)
WHERE_IT_IS = pl.BlockSpec(memory_space=pl.ANY)


def tiles(rows, width):
    return pl.BlockSpec((rows, width), lambda i: (i, 0))


def block(number, *shape):
    return pl.BlockSpec(shape, lambda i: (number,) + (0,) * (len(shape) - 1))


def whole(*shape):
    return pl.BlockSpec(shape, lambda i: (0,) * len(shape))


def swap(value, axis, offset=1):
    size = lax.axis_size(axis)
    return lax.ppermute(value, axis, [(i, i ^ offset) for i in range(size)])


def swap_side(value):
    return swap(value, SIDE)


def swap_x(value):
    return swap(value, "ctx_hi")


def swap_y(value):
    return swap(value, "dp_lo")


def phase(*values):
    return lax.optimization_barrier(values)


def in_order(mine, theirs, here, axis):
    return jnp.where(
        here == 0,
        jnp.concatenate([mine, theirs], axis=axis),
        jnp.concatenate([theirs, mine], axis=axis),
    )


def pair_shards(shard, side):
    half = shard.shape[-1] // 2
    axis = shard.ndim - 1
    mine = lax.dynamic_slice_in_dim(shard, side * half, half, axis)
    theirs = lax.dynamic_slice_in_dim(shard, (1 - side) * half, half, axis)
    return in_order(mine, swap_side(theirs), side, shard.ndim - 2)


def swap_planes(value):
    return [swap(value, "dp_hi", offset) for offset in range(1, lax.axis_size("dp_hi"))]


def place_planes(value, others):
    here = lax.axis_index("dp_hi")
    parts = [part[None] for part in [value] + others]
    bit = 0
    while len(parts) > 1:
        flag = (here >> bit) & 1
        parts = [
            in_order(parts[i], parts[i + 1], flag, 0) for i in range(0, len(parts), 2)
        ]
        bit += 1
    return parts[0]


def wide_sum(*arrays):
    return functools.reduce(lambda a, b: a + b, [a.astype(WIDE) for a in arrays])


class Sum:
    def __init__(self, keep, send):
        self.keep, self.send = keep, send
        self.planes = 2 * keep.shape[2]

    def core(self):
        return swap_side(self.send)

    def part(self, run, squares):
        return wide_sum(self.keep[run, squares], self.other[run, squares])

    def first(self, got):
        self.other = got
        far = slice(2, 4)
        return [swap_y(self.part(0, far).astype(LOW)), swap_x(self.part(1, far).astype(LOW))]

    def middle(self, got):
        self.got = got
        return [wide_sum(self.part(run, 1), got[run][1]).astype(LOW) for run in range(2)]

    def second(self, got):
        return self.turn(self.middle(got))

    def turn(self, sent):
        return [swap_x(sent[0]), swap_y(sent[1])]

    def total(self, got):
        return jnp.concatenate(
            [
                wide_sum(self.part(run, 0), self.got[run][0], got[run]).astype(LOW)
                for run in range(2)
            ],
            axis=0,
        )


def sum_planes(total):
    here = lax.axis_index("dp_hi")
    planes = total.shape[0]
    return pick(total, here), [
        swap(pick(total, here ^ offset), "dp_hi", offset) for offset in range(1, planes)
    ]


def own_rows(total, side):
    rows = total.shape[-2] // 2
    axis = total.ndim - 2
    total = total.astype(LOW)
    mine = lax.dynamic_slice_in_dim(total, side * rows, rows, axis)
    theirs = lax.dynamic_slice_in_dim(total, (1 - side) * rows, rows, axis)
    return in_order(mine, swap_side(theirs), side, total.ndim - 1).astype(WIDE)


def pick(value, index, axis=0):
    return lax.dynamic_index_in_dim(value, index, axis, keepdims=False)


class Exchange:
    def __init__(self, blocks):
        self.x_here, self.side = lax.axis_index("ctx_hi"), lax.axis_index(SIDE)
        self.own = pick(blocks, self.x_here)
        self.sent = pick(blocks, 1 - self.x_here)

    def far(self):
        return [swap_x(self.sent), swap_side(pick(self.own, 1 - self.side))]

    def near(self, got):
        self.from_x, self.from_side = got
        return swap_side(pick(self.from_x, 1 - self.side))

    def place(self, got):
        own = pick(self.own, self.side)[None]
        far = pick(self.from_x, self.side)[None]
        return in_order(
            in_order(own, self.from_side[None], self.side, 0)[None],
            in_order(far, got[None], self.side, 0)[None],
            self.x_here,
            0,
        )


def by_sequence(value):
    return value.reshape((2, 2, -1) + value.shape[1:])


def sequences_of(blocks):
    parts = blocks.shape[0] * blocks.shape[1]
    own, here, width = blocks.shape[2:]
    blocks = blocks.reshape(parts, own, here, width)
    return blocks.transpose(1, 0, 2, 3).reshape(own * parts * here, width)


def by_position(value, sequences):
    width = value.shape[-1]
    blocks = value.reshape(sequences, 2, 2, -1, width)
    return blocks.transpose(1, 2, 0, 3, 4)


def positions_of(blocks):
    return blocks.reshape((-1,) + blocks.shape[3:])


def local(
    tokens,
    cotangent,
    lengths,
    attention_weights,
    inner_weights,
    outer_weights,
    inner_bias,
    vectors,
    attention_first,
    attention_second,
    inner_first,
    inner_second,
    outer_moment_first,
    outer_second,
    bias_first,
    bias_second,
    vector_first,
    vector_second,
):
    parts = lax.axis_size(CONTEXT)
    planes = lax.axis_size("dp_hi")
    chips = lax.axis_size(CHIPS)
    count = 2 * chips
    side = lax.axis_index(SIDE)
    coords = jnp.stack([side] + [lax.axis_index(axis) for axis in ("dp_lo", "ctx_hi", "dp_hi")])
    coords = coords.astype(jnp.int32)
    seq_count, local_len, width = tokens.shape
    hidden = inner_weights.shape[1]
    full_len = local_len * parts
    own_seqs = seq_count // parts
    rows = own_seqs * full_len
    att_rows, vec_cols, bias_cols = (
        attention_weights.shape[1],
        vectors.shape[1],
        inner_bias.shape[0],
    )
    half = width // 2
    tall = 16
    in_pieces = (2 * att_rows) % tall == 0
    if in_pieces:
        dims, squares = (planes, 2, 2), 4
        att_block, inner_block, outer_block = (
            2 * att_rows,
            2 * inner_weights.shape[0],
            2 * outer_weights.shape[0],
        )
    else:
        dims, squares = (1, 1, 1), 1
        att_block, inner_block, outer_block = width, width, hidden

    me = lax.axis_index(ALL)
    per_row = width // bias_cols
    small = jnp.zeros((tall, width), LOW)
    small = lax.dynamic_update_slice(small, vectors.astype(LOW), (0, me * vec_cols))
    small = lax.dynamic_update_slice(
        small, inner_bias.astype(LOW)[None], (8 + me // per_row, me % per_row * bias_cols)
    )
    att_pair = pair_shards(attention_weights.astype(LOW), side).reshape(8 * att_rows, half)
    if in_pieces:
        att_pair = jnp.concatenate([att_pair, small[:, :half], small[:, half:]], axis=0)
        att_pair, tokens, inner_own, outer_own = phase(
            att_pair, tokens, inner_weights, outer_weights
        )
        att_parts = swap_planes(att_pair)
    else:
        inner_own, outer_own = inner_weights, outer_weights
    inner_pair = pair_shards(inner_own.astype(LOW), side)
    outer_pair = pair_shards(outer_own.astype(LOW), side)
    strips = hidden // width
    pack_pair = jnp.concatenate(
        [
            inner_pair.reshape(-1, strips, half).transpose(1, 0, 2).reshape(-1, half),
            outer_pair,
        ],
        axis=0,
    )
    token_swap = Exchange(by_sequence(tokens))
    if in_pieces:
        middle = planes // 2
        token_far = token_swap.far()
        pack_x = swap_x(pack_pair)
        att_parts, pack_x = phase(att_parts, pack_x)
        att = place_planes(att_pair, att_parts)
        att_x, att_y = swap_x(att), swap_y(att)
        pack = in_order(pack_pair[None], pack_x[None], coords[2], 0)
        pack_z = [pack] + swap_planes(pack)
        pack_y = [swap_y(pack)]
        cot_low = cotangent.astype(LOW)
        att_x, att_y, token_far, pack_z[1], cot_low = phase(
            att_x, att_y, token_far, pack_z[1], cot_low
        )
        token_near = token_swap.near(token_far)
        att_mine = [att, att_x, att_y, swap_y(att_x[:middle]), swap_x(att_y[middle:])]
        early = max(2, planes - 1)
        att_mine, token_near, pack_z[1:early], pack_y[0], cot_low = phase(
            att_mine, token_near, pack_z[1:early], pack_y[0], cot_low
        )
        cot_swap = Exchange(by_sequence(cot_low))
        token_rows = sequences_of(token_swap.place(token_near))
        small = sum(
            jnp.sum(piece[:, 8 * att_rows :].astype(WIDE), axis=0) for piece in att_mine
        )
        small = small + swap_side(small.astype(LOW)).astype(WIDE)
        small = jnp.concatenate([small[:tall], small[tall:]], axis=1)
        att_all = att_mine + [swap_side(piece) for piece in att_mine]
        att_all, token_rows, small, cotangent_sent = phase(
            att_all, token_rows, small, cot_swap.sent
        )
        cot_swap.sent = cotangent_sent
        pack_y = pack_y + [swap_y(piece) for piece in pack_z[1:early]]
        cot_far = cot_swap.far()
        att_layout = [
            (0, 0, 0, planes),
            (0, 1, 0, planes),
            (1, 0, 0, planes),
            (1, 1, 0, middle),
            (1, 1, middle, planes - middle),
        ]
        pack_layout = [(y, offset) for y in range(2) for offset in range(planes)]
    else:
        small = lax.psum(small, ALL).astype(WIDE)
        att = lax.all_gather(att_pair, CHIPS, axis=0, tiled=False)
        pack = lax.all_gather(pack_pair, CHIPS, axis=0, tiled=False)

        def lay_out(value, matrices):
            value = value.reshape(chips, matrices, -1, half)
            return value.transpose(1, 0, 2, 3).reshape(1, -1, half)

        att = lay_out(att, 4)
        pack_rows = inner_pair.shape[0] * strips
        pack = jnp.concatenate(
            [lay_out(pack[:, :pack_rows], strips), lay_out(pack[:, pack_rows:], 1)], axis=1
        )
        att_all, pack_all = [[value, swap_side(value)] for value in (att, pack)]
        att_layout = pack_layout = [(0, 0, 0, 1)]
        token_rows = sequences_of(token_swap.place(token_swap.near(token_swap.far())))
        cot_swap = Exchange(by_sequence(cotangent.astype(LOW)))
        cot_rows = sequences_of(cot_swap.place(cot_swap.near(cot_swap.far())))
    vec = small[:8]
    bias = small[8 : 8 + strips].reshape(1, hidden)
    own_lengths = lax.dynamic_slice_in_dim(lengths, lax.axis_index(CONTEXT) * own_seqs, own_seqs)

    def in_place(pieces):
        return [(piece, WHERE_IT_IS) for piece in pieces]

    norm_shape = (own_seqs, PAIRS, 2, full_len)
    low_rows = (rows, width)
    seq_tile = tiles(full_len, width)
    vec_spec = whole(8, width)
    square = 2 * rows * width * width
    attend_flops = 8 * rows * full_len * width

    held = call(
        functools.partial(attend_kernel, att_layout),
        own_seqs,
        [
            (own_lengths, SCALARS),
            (coords, SCALARS),
            (token_rows, seq_tile),
            (vec, vec_spec),
        ]
        + in_place(att_all),
        [(low_rows, LOW, seq_tile)] * 4
        + [
            (low_rows, WIDE, seq_tile),
            (
                norm_shape,
                WIDE,
                pl.BlockSpec((1, PAIRS, 2, full_len), lambda i: (i, 0, 0, 0)),
            ),
        ],
        [
            pltpu.VMEM((4,) + dims + (att_block, width), LOW),
            pltpu.VMEM((width, full_len), LOW),
            pltpu.VMEM((width, full_len), WIDE),
            pltpu.SemaphoreType.DMA((4 * len(att_all),)),
        ],
        4 * square + 2 * attend_flops,
        20 * rows * width,
    )
    if in_pieces:
        held, pack_z, pack_y, cot_far = phase(held, pack_z, pack_y, cot_far)
        known = len(pack_y)
        pack_y = pack_y + [swap_y(piece) for piece in pack_z[known:]]
        pack_z_other = [swap_side(piece) for piece in pack_z]
        pack_y_other = [swap_side(piece) for piece in pack_y[:known]]
        cot_near = cot_swap.near(cot_far)
        pack_y, pack_z_other, pack_y_other, cot_near = phase(
            pack_y, pack_z_other, pack_y_other, cot_near
        )
        cot_rows = sequences_of(cot_swap.place(cot_near))
        pack_y_other = pack_y_other + [swap_side(piece) for piece in pack_y[known:]]
        pack_all = pack_z + pack_y + pack_z_other + pack_y_other
    query, key, value, mixed, first_sum, normalizer = held

    def grad_pieces(rows_here, columns, matrices=None):
        runs = 2 if in_pieces else 1
        lead = (runs, squares, dims[0] // runs) + ((matrices,) if matrices else ())
        shape = lead + (rows_here, columns)
        return [(shape, LOW, whole(*shape))] * 2

    tile = 256
    row_tile = tiles(tile, width)
    hidden_tile = tiles(tile, hidden)
    result, second_grad, hidden_low, outer_keep, outer_send, vec_ffn, bias_grad = phase(
        *call(
            functools.partial(ffn_kernel, pack_layout),
            rows // tile,
            [
                (coords, SCALARS),
                (first_sum, row_tile),
                (cot_rows, row_tile),
                (vec, vec_spec),
                (bias, whole(1, hidden)),
            ]
            + in_place(pack_all),
            [
                (low_rows, LOW, row_tile),
                (low_rows, WIDE, row_tile),
                ((rows, hidden), LOW, hidden_tile),
            ]
            + grad_pieces(outer_block, half)
            + [((8, width), WIDE, vec_spec), ((1, hidden), WIDE, whole(1, hidden))],
            [
                pltpu.VMEM((1,) + dims + (inner_block, hidden), LOW),
                pltpu.VMEM((1,) + dims + (outer_block, width), LOW),
                pltpu.VMEM((hidden, width), WIDE),
                pltpu.VMEM((tile, hidden), LOW),
                pltpu.VMEM((tile, hidden), WIDE),
                pltpu.SemaphoreType.DMA(((strips + 1) * len(pack_all),)),
            ],
            16 * square + 60 * rows * hidden,
            30 * rows * width,
        )
    )
    result_swap = Exchange(by_position(result, own_seqs))
    if in_pieces:
        outer_sum = Sum(outer_keep, outer_send)
        outer_got, second_grad = phase(outer_sum.core(), second_grad)
        outer_got = outer_sum.first(outer_got)
    result_far = result_swap.far()

    first_grad, mixed_grad, mid_keep, mid_send, vec_mid = call(
        functools.partial(back_kernel, pack_layout, att_layout),
        rows // tile,
        [
            (coords, SCALARS),
            (first_sum, row_tile),
            (second_grad, row_tile),
            (hidden_low, hidden_tile),
            (mixed, row_tile),
            (vec, vec_spec),
        ]
        + in_place(pack_all)
        + in_place(att_all),
        [(low_rows, WIDE, row_tile), (low_rows, LOW, row_tile)]
        + grad_pieces(inner_block, hidden // 2 + half)
        + [((8, width), WIDE, vec_spec)],
        [
            pltpu.VMEM((1,) + dims + (inner_block, hidden), LOW),
            pltpu.VMEM((1,) + dims + (att_block, width), LOW),
            pltpu.VMEM((width, hidden), WIDE),
            pltpu.VMEM((width, width), WIDE),
            pltpu.SemaphoreType.DMA((strips * len(pack_all) + len(att_all),)),
        ],
        10 * square,
        26 * rows * width,
    )
    if in_pieces:
        first_grad, mixed_grad, mid_keep, mid_send, vec_mid, outer_got, result_far = phase(
            first_grad, mixed_grad, mid_keep, mid_send, vec_mid, outer_got, result_far
        )
        mid_sum = Sum(mid_keep, mid_send)
        outer_got = outer_sum.second(outer_got)
        mid_got, mixed_grad = phase(mid_sum.core(), mixed_grad)
        mid_got = mid_sum.first(mid_got)
    result_near = result_swap.near(result_far)

    def input_of(number):
        seq_shape = (full_len, width)
        (grad,) = call(
            functools.partial(input_kernel, att_layout, 1),
            1,
            [(coords, SCALARS), (first_grad, block(number, full_len, width))]
            + [(value_, whole(*seq_shape)) for value_ in grads[3 * number : 3 * number + 3]]
            + in_place(att_all),
            [(seq_shape, LOW, whole(*seq_shape))],
            [
                pltpu.VMEM((3,) + dims + (att_block, width), LOW),
                pltpu.SemaphoreType.DMA((3 * len(att_all),)),
            ],
            3 * square // own_seqs,
            12 * rows * width // own_seqs,
        )
        return grad

    grads, input_swaps, input_far = [], [], []
    for number in range(own_seqs):
        last = number == own_seqs - 1
        own_rows_spec = block(number, full_len, width)
        seq_shape = (full_len, width)
        earlier = grads if last else []
        outputs = [(seq_shape, LOW, whole(*seq_shape))] * 3
        scratch = [pltpu.VMEM((width, full_len), LOW), pltpu.VMEM((width, full_len), WIDE)]
        if last:
            outputs = (
                outputs + grad_pieces(att_block, half, 3) + [((8, width), WIDE, vec_spec)]
            )
            scratch = scratch + [pltpu.VMEM((width, width), WIDE)]
        found = call(
            functools.partial(attend_back_kernel, number, last),
            1,
            [
                (own_lengths, SCALARS),
                (coords, SCALARS),
                (token_rows, whole(rows, width)),
                (query, own_rows_spec),
                (key, own_rows_spec),
                (value, own_rows_spec),
                (mixed_grad, own_rows_spec),
                (normalizer, block(number, 1, PAIRS, 2, full_len)),
            ]
            + [(value_, whole(*seq_shape)) for value_ in earlier],
            outputs,
            scratch,
            5 * attend_flops // own_seqs + (3 * square if last else 0),
            20 * rows * width // own_seqs,
        )
        if in_pieces:
            found, outer_got, mid_got, mixed_grad, result_near, input_far = phase(
                found, outer_got, mid_got, mixed_grad, result_near, input_far
            )
            if number == 0:
                outer_got, mid_got = outer_sum.total(outer_got), mid_sum.middle(mid_got)
        grads = grads + list(found[:3])
        if not last:
            swap_first = Exchange(by_position(input_of(number), 1))
            swap_first.sent, swap_first.own, mixed_grad = phase(
                swap_first.sent, swap_first.own, mixed_grad
            )
            if in_pieces and number == 0:
                mid_got, outer_got, mixed_grad = phase(mid_got, outer_got, mixed_grad)
                mid_got = mid_sum.turn(mid_got)
            input_swaps.append(swap_first)
            input_far.append(swap_first.far())
    att_keep, att_send, vec_att = found[3:]

    small_grad = jnp.concatenate(
        [
            vec_ffn + vec_mid + vec_att,
            bias_grad.reshape(-1, width),
            jnp.zeros((tall - 8 - strips, width), WIDE),
        ],
        axis=0,
    )
    if in_pieces:
        att_sum = Sum(att_keep, att_send)
        strip = inner_block
        merged = jnp.concatenate(
            [mid_sum.total(mid_got)]
            + [
                outer_got[:, start : start + strip]
                for start in range(0, outer_block, strip)
            ],
            axis=2,
        )
        att_got, small_got, grads, merged, first_grad = phase(
            att_sum.core(), swap_side(small_grad), grads, merged, first_grad
        )
        small_grad = small_grad + small_got
        att_got = att_sum.first(att_got)
        merged, merged_got = sum_planes(merged)
        small_got = swap_y(small_grad)

    input_grad = input_of(own_seqs - 1)
    if in_pieces:
        input_grad, att_got, small_got = phase(input_grad, att_got, small_got)
    input_swaps.append(Exchange(by_position(input_grad, 1)))
    if in_pieces:
        att_got = att_sum.second(att_got)
        small_grad = small_grad + small_got
        small_got = swap_x(small_grad)
        swap_last = input_swaps[-1]
        att_got, small_got, merged_got, swap_last.sent, swap_last.own = phase(
            att_got, small_got, merged_got, swap_last.sent, swap_last.own
        )
        input_far.append(swap_last.far())
        small_grad = small_grad + small_got
        att_own, att_got = sum_planes(att_sum.total(att_got))
        att_got[0], small_grad, merged, merged_got = phase(
            att_got[0], small_grad, merged, merged_got
        )
        small_got = swap_planes(small_grad)
        merged = wide_sum(merged, *merged_got)
        inner_total = own_rows(merged[:, : hidden // 2], side)
        project_total = own_rows(merged[:, hidden // 2 : hidden // 2 + half], side)
        outer_total = own_rows(
            jnp.concatenate(
                [
                    merged[:, start : start + half]
                    for start in range(hidden // 2 + half, merged.shape[1], half)
                ],
                axis=0,
            ),
            side,
        )
        att_total = own_rows(wide_sum(att_own, *att_got), side)
        input_near = [one.near(far) for one, far in zip(input_swaps, input_far)]
        small_total = wide_sum(small_grad, *small_got)
    else:
        input_far.append(input_swaps[-1].far())
        input_near = [one.near(far) for one, far in zip(input_swaps, input_far)]

        def scatter(value):
            value = value.reshape((-1,) + value.shape[-2:])
            matrices, length, columns = value.shape
            value = value.reshape(matrices, chips, length // chips, columns)
            value = lax.psum_scatter(
                value.transpose(1, 0, 2, 3), CHIPS, scatter_dimension=0, tiled=False
            )
            return own_rows(value, side)

        att_total = scatter(att_keep + swap_side(att_send))
        outer_total = scatter(outer_keep + swap_side(outer_send))[0]
        mid = mid_keep + swap_side(mid_send)
        inner_total = scatter(mid[..., : hidden // 2])[0]
        project_total = scatter(mid[..., hidden // 2 :])[0]
        small_total = lax.psum(small_grad, ALL)
    output_tokens = positions_of(result_swap.place(result_near))
    input_grad = jnp.concatenate(
        [one.place(near) for one, near in zip(input_swaps, input_near)], axis=2
    )
    input_grad = positions_of(input_grad).astype(WIDE)
    attention_total = jnp.concatenate([att_total, project_total[None]], axis=0)
    vector_total = lax.dynamic_slice(small_total, (0, me * vec_cols), (8, vec_cols))
    bias_total = lax.dynamic_slice(
        small_total, (8 + me // per_row, me % per_row * bias_cols), (1, bias_cols)
    ).reshape(bias_cols)

    attention_square, attention_new = adam_step(
        attention_weights,
        attention_total,
        attention_first,
        attention_second,
        MATRIX_LEARN_RATE,
        WEIGHT_DECAY,
    )
    inner_square, inner_new = adam_step(
        inner_weights, inner_total, inner_first, inner_second, MATRIX_LEARN_RATE, WEIGHT_DECAY
    )
    outer_square, outer_new = adam_step(
        outer_weights,
        outer_total,
        outer_moment_first,
        outer_second,
        MATRIX_LEARN_RATE,
        WEIGHT_DECAY,
    )
    bias_square, bias_new = adam_step(
        inner_bias, bias_total, bias_first, bias_second, VECTOR_RATE, 0.0
    )
    vector_square, vector_new = adam_step(
        vectors, vector_total, vector_first, vector_second, VECTOR_RATE, 0.0
    )
    return (
        output_tokens,
        input_grad,
        attention_total,
        attention_square,
        attention_new,
        inner_total,
        inner_square,
        inner_new,
        outer_total,
        outer_square,
        outer_new,
        bias_total,
        bias_square,
        bias_new,
        vector_total,
        vector_square,
        vector_new,
    )


def solution(mesh):
    split = Mesh(
        np.asarray(mesh.devices).reshape(
            mesh.shape["dp"] // 2, 2, mesh.shape["context"] // 2, 2
        ),
        ALL,
    )
    dp = ("dp_hi", "dp_lo")
    rows3 = P(dp, CONTEXT, None)
    mid3 = P(None, ALL, None)
    row2 = P(ALL, None)
    col2 = P(None, ALL)
    one = P(ALL)
    return jax.shard_map(
        local,
        mesh=split,
        in_specs=(rows3, rows3, P(dp), mid3, row2, row2, one, col2)
        + (mid3, mid3, row2, row2, row2, row2, one, one, col2, col2),
        out_specs=(rows3, rows3)
        + (mid3,) * 3
        + (row2,) * 6
        + (one,) * 3
        + (col2,) * 3,
        check_vma=False,
    )
```

```python
import functools

import jax
import jax.numpy as jnp
import numpy as np
from jax import lax
from jax.experimental import pallas as pl
from jax.experimental.pallas import tpu as pltpu
from jax.sharding import Mesh, PartitionSpec as P

HEADS = 12
HEAD = 64
PAIR = 2 * HEAD
PAIRS = HEADS // 2
STEP = 10

NORM_EPS = 1e-12
BETA_ONE = 0.9
BETA_TWO = 0.999
ADAM_EPS = 1e-06
MATRIX_LEARN_RATE = 0.05
VECTOR_RATE = 0.5
WEIGHT_DECAY = 0.01
MASK_FILL = -1e30
SCORE_SCALE = HEAD ** (-0.5)
ROOT_HALF = 0.5**0.5
DENSITY = 0.3989422804014327

CHIPS = ("dp_hi", "dp_lo", "ctx_hi")
SIDE = "ctx_lo"
ALL = CHIPS + (SIDE,)
CONTEXT = ("ctx_hi", "ctx_lo")
LOW = jnp.bfloat16
WIDE = jnp.float32
VMEM_BYTES = 60 * 1024 * 1024


def adam_step(weight, gradient, moment_one, moment_two, step_rate, decay_rate):
    first_new = BETA_ONE * moment_one + (1.0 - BETA_ONE) * gradient
    second_new = BETA_TWO * moment_two + (1.0 - BETA_TWO) * gradient * gradient
    first_hat = first_new / (1.0 - BETA_ONE**STEP)
    second_hat = second_new / (1.0 - BETA_TWO**STEP)
    updated = weight - step_rate * (
        first_hat / (jnp.sqrt(second_hat) + ADAM_EPS) + decay_rate * weight
    )
    return (second_new, updated)


def matmul(left, right):
    return jnp.dot(left, right, preferred_element_type=WIDE)


def contract_rows(left, right):
    return lax.dot_general(left, right, (((0,), (0,)), ((), ())), preferred_element_type=WIDE)


def times_transpose(left, right):
    return lax.dot_general(left, right, (((1,), (1,)), ((), ())), preferred_element_type=WIDE)


def flip(value):
    return value.astype(WIDE).T


def norm_stats(value):
    centered = value - jnp.mean(value, axis=-1, keepdims=True)
    variance = jnp.mean(centered * centered, axis=-1, keepdims=True)
    scale = lax.rsqrt(variance + NORM_EPS)
    return centered * scale, scale


def norm_back(grad, gain, unit, scale):
    scaled = grad * gain
    return scale * (
        scaled
        - jnp.mean(scaled, axis=-1, keepdims=True)
        - unit * jnp.mean(scaled * unit, axis=-1, keepdims=True)
    )


def load_pieces(coords, moves, pieces, layout, target, sems, first=0):
    rows, half = target.shape[4], target.shape[5] // 2
    side, y_here, x_here, z_here = [coords[i] for i in range(4)]
    single = target.shape[2] == 1
    wide = pieces[0].shape[-1]
    copies = []
    for row, place, column in moves:
        for number, source in enumerate(pieces):
            which, order = divmod(number, len(layout))
            start = pl.multiple_of((side if which == 0 else 1 - side) * half + column, wide)
            columns = pl.ds(start, wide)
            y_at = 0 if single else (1 - y_here if layout[order][0] else y_here)
            if len(layout[order]) == 2:
                z_at = jnp.bitwise_xor(z_here, layout[order][1])
                goal = target.at[place, z_at, y_at, :, :, columns]
            else:
                _, x_other, plane, planes = layout[order]
                x_at = 0 if single else (1 - x_here if x_other else x_here)
                goal = target.at[place, pl.ds(plane, planes), y_at, x_at, :, columns]
            copies.append(
                pltpu.make_async_copy(
                    source.at[:, pl.ds(row, rows), :], goal, sems.at[first + len(copies)]
                )
            )
    return copies


def inner_moves(target, wide):
    rows, half = target.shape[4], target.shape[5] // 2
    return [(number * rows, 0, number * wide) for number in range(half // wide)]


def outer_moves(target, inner, wide):
    return [(inner.shape[4] * (inner.shape[5] // 2 // wide), 0, 0)]


def matrix_moves(picks, rows):
    return [(pick * rows, place, 0) for place, pick in enumerate(picks)]


def load_now(copies):
    for copy in copies:
        copy.start()
    for copy in copies:
        copy.wait()


def flat(target, place=0):
    _, planes, high, wide, rows, width = target.shape
    return target.at[place].reshape(planes * high * wide * rows, width)


def store_pieces(coords, keep_out, send_out, read, half, column=0, place=None):
    side, y_here, x_here = coords[0], coords[1], coords[2]
    runs, squares, planes = keep_out.shape[:3]
    rows = keep_out.shape[-2]
    into = pl.ds(column, half)
    for out, own_side in ((keep_out, side), (send_out, 1 - side)):
        columns = pl.ds(pl.multiple_of(own_side * half, half), half)
        for run in range(runs):
            for square in range(squares):
                high, low = square // 2, square % 2
                y_other, x_other = (high, low) if run == 0 else (low, high)
                for number in range(planes):
                    block = run * planes + number
                    if squares > 1:
                        y_at = 1 - y_here if y_other else y_here
                        x_at = 1 - x_here if x_other else x_here
                        block = (block * 2 + y_at) * 2 + x_at
                    start = pl.multiple_of(block * rows, rows)
                    part = read(pl.ds(start, rows), columns).astype(LOW)
                    if place is None:
                        out[run, square, number, :, into] = part
                    else:
                        out[run, square, number, place, :, into] = part


def head_masks():
    lane = lax.broadcasted_iota(jnp.int32, (1, PAIR), 1)
    return [lane < HEAD, lane >= HEAD]


def only(value, mask):
    return jnp.where(mask, value, 0.0).astype(LOW)


def masked_pair(queries, keys, fill, head, masks):
    lane = lax.broadcasted_iota(jnp.int32, (1, PAIR), 1)
    marker = (lane == (1 - head) * HEAD).astype(WIDE)
    left = jnp.where(masks[head], queries, marker).astype(LOW)
    right = jnp.where(masks[head], keys.astype(WIDE), fill).astype(LOW)
    return left, right


def attend_kernel(layout, *refs):
    pieces = 2 * len(layout)
    lengths, coords, tokens, vec = refs[:4]
    sources = refs[4 : 4 + pieces]
    query_out, key_out, value_out, mixed_out, sum_out, norm_out = refs[4 + pieces : 10 + pieces]
    weights, value_flip, mixed_flip, sems = refs[10 + pieces :]
    step = pl.program_id(0)
    copies = load_pieces(
        coords, matrix_moves(range(4), weights.shape[4]), sources, layout, weights, sems
    )

    @pl.when(step == 0)
    def _():
        for copy in copies:
            copy.start()

    def need(place):
        @pl.when(step == 0)
        def _():
            for copy in copies[place * pieces : (place + 1) * pieces]:
                copy.wait()

    length = lengths[step]
    rows = tokens[...]
    need(0)
    query_out[...] = (matmul(rows, flat(weights, 0)[...]) + vec[0:1, :]).astype(LOW)
    need(1)
    key_out[...] = matmul(rows, flat(weights, 1)[...]).astype(LOW)
    need(2)
    value_low = (matmul(rows, flat(weights, 2)[...]) + vec[1:2, :]).astype(LOW)
    value_out[...] = value_low
    value_flip[...] = flip(value_low).astype(LOW)
    size = tokens.shape[0]
    position = lax.broadcasted_iota(jnp.int32, (size, PAIR), 0)
    fill = jnp.where(position < length, 0.0, MASK_FILL)
    masks = head_masks()

    def one_pair(pair, carry):
        lanes = pl.ds(pl.multiple_of(pair * PAIR, PAIR), PAIR)
        keys = key_out[:, lanes]
        queries = query_out[:, lanes].astype(WIDE) * SCORE_SCALE
        mixed, norms = [], []
        for head in range(2):
            own_query, own_key = masked_pair(queries, keys, fill, head, masks)
            scores = times_transpose(own_key, own_query)
            peak = jnp.max(scores, axis=0, keepdims=True)
            exponent = jnp.exp(scores - peak)
            total = jnp.sum(exponent, axis=0, keepdims=True)
            prob = (exponent * (1.0 / total)).astype(LOW)
            start = pl.multiple_of(pair * PAIR + head * HEAD, HEAD)
            mixed.append(matmul(value_flip[pl.ds(start, HEAD), :], prob))
            norms.append(peak + jnp.log(total))
        mixed_flip[lanes, :] = jnp.concatenate(mixed, axis=0)
        norm_out[0, pair] = jnp.concatenate(norms, axis=0)
        return carry

    lax.fori_loop(0, PAIRS, one_pair, 0)
    need(3)
    mixed_low = mixed_flip[...].T.astype(LOW)
    mixed_out[...] = mixed_low
    sum_out[...] = rows.astype(WIDE) + matmul(mixed_low, flat(weights, 3)[...]) + vec[2:3, :]


def ffn_kernel(layout, *refs):
    pieces = 2 * len(layout)
    coords, first_sum, cotangent, vec, bias = refs[:5]
    sources = refs[5 : 5 + pieces]
    result_out, second_out, hidden_out, keep_out, send_out, vec_grad, bias_grad = refs[
        5 + pieces : 12 + pieces
    ]
    inner_at, outer_at, total, activated, slope, sems = refs[12 + pieces :]
    step = pl.program_id(0)

    wide = sources[0].shape[-1]
    copies = load_pieces(coords, inner_moves(inner_at, wide), sources, layout, inner_at, sems)
    outer_copies = load_pieces(
        coords,
        outer_moves(outer_at, inner_at, wide),
        sources,
        layout,
        outer_at,
        sems,
        len(copies),
    )

    @pl.when(step == 0)
    def _():
        for copy in copies + outer_copies:
            copy.start()
        vec_grad[...] = jnp.zeros_like(vec_grad)
        bias_grad[...] = jnp.zeros_like(bias_grad)
        total[...] = jnp.zeros_like(total)
        for copy in copies + outer_copies:
            copy.wait()

    inner, outer = flat(inner_at), flat(outer_at)
    unit, _ = norm_stats(first_sum[...])
    normed = unit * vec[4:5, :] + vec[5:6, :]
    normed_low = normed.astype(LOW)
    width, hidden = inner.shape
    second = normed + vec[3:4, :]
    for start in range(0, hidden, width):
        part = slice(start, start + width)
        pre = matmul(normed_low, inner[:, part]) + bias[:, part]
        cdf = 0.5 * (1.0 + lax.erf(pre * ROOT_HALF))
        active = (pre * cdf).astype(LOW)
        activated[:, part] = active
        slope[:, part] = cdf + pre * (DENSITY * jnp.exp(-0.5 * pre * pre))
        second = second + matmul(active, outer[part, :])
    unit_two, scale_two = norm_stats(second)
    result_out[...] = (unit_two * vec[6:7, :] + vec[7:8, :]).astype(LOW)
    grad = cotangent[...].astype(WIDE)
    second_grad = norm_back(grad, vec[6:7, :], unit_two, scale_two)
    second_out[...] = second_grad
    grad_low = second_grad.astype(LOW)
    vec_grad[3:4, :] += jnp.sum(grad_low.astype(WIDE), axis=0, keepdims=True)
    vec_grad[6:7, :] += jnp.sum(grad * unit_two, axis=0, keepdims=True)
    vec_grad[7:8, :] += jnp.sum(grad, axis=0, keepdims=True)
    for start in range(0, hidden, width):
        part = slice(start, start + width)
        back = times_transpose(grad_low, outer[part, :])
        hidden_low = (back * slope[:, part]).astype(LOW)
        hidden_out[:, part] = hidden_low
        bias_grad[:, part] += jnp.sum(hidden_low.astype(WIDE), axis=0, keepdims=True)
        total[part, :] += contract_rows(activated[:, part], grad_low)

    @pl.when(step == pl.num_programs(0) - 1)
    def _():
        store_pieces(
            coords, keep_out, send_out, lambda r, c: total[r, c], keep_out.shape[-1]
        )


def back_kernel(pack_layout, att_layout, *refs):
    pack_pieces, att_pieces = 2 * len(pack_layout), 2 * len(att_layout)
    coords, first_sum, second_grad, hidden_low, mixed, vec = refs[:6]
    pack_from = refs[6 : 6 + pack_pieces]
    att_from = refs[6 + pack_pieces : 6 + pack_pieces + att_pieces]
    first_out, mixed_grad_out, keep_out, send_out, vec_grad = refs[
        6 + pack_pieces + att_pieces : 11 + pack_pieces + att_pieces
    ]
    inner_at, project_at, total, project_total, sems = refs[11 + pack_pieces + att_pieces :]
    step = pl.program_id(0)

    @pl.when(step == 0)
    def _():
        copies = load_pieces(
            coords,
            inner_moves(inner_at, pack_from[0].shape[-1]),
            pack_from,
            pack_layout,
            inner_at,
            sems,
        )
        copies = copies + load_pieces(
            coords,
            matrix_moves((3,), project_at.shape[4]),
            att_from,
            att_layout,
            project_at,
            sems,
            len(copies),
        )
        for copy in copies:
            copy.start()
        vec_grad[...] = jnp.zeros_like(vec_grad)
        total[...] = jnp.zeros_like(total)
        project_total[...] = jnp.zeros_like(project_total)
        for copy in copies:
            copy.wait()

    inner = flat(inner_at)
    unit, scale = norm_stats(first_sum[...])
    normed_flip = flip(unit * vec[4:5, :] + vec[5:6, :]).astype(LOW)
    width, hidden = total.shape
    grad = second_grad[...]
    for start in range(0, hidden, width):
        part = slice(start, start + width)
        grad = grad + times_transpose(hidden_low[:, part], inner[:, part])
        total[:, part] += matmul(normed_flip, hidden_low[:, part])
    first_grad = norm_back(grad, vec[4:5, :], unit, scale)
    first_out[...] = first_grad
    branch = first_grad.astype(LOW)
    vec_grad[2:3, :] += jnp.sum(branch.astype(WIDE), axis=0, keepdims=True)
    vec_grad[4:5, :] += jnp.sum(grad * unit, axis=0, keepdims=True)
    vec_grad[5:6, :] += jnp.sum(grad, axis=0, keepdims=True)
    mixed_grad_out[...] = times_transpose(branch, flat(project_at)[...]).astype(LOW)
    project_total[...] += contract_rows(mixed[...], branch)

    @pl.when(step == pl.num_programs(0) - 1)
    def _():
        store_pieces(coords, keep_out, send_out, lambda r, c: total[r, c], hidden // 2)
        store_pieces(
            coords,
            keep_out,
            send_out,
            lambda r, c: project_total[r, c],
            width // 2,
            hidden // 2,
        )


def attend_back_kernel(sequence, last, *refs):
    lengths, coords, tokens, query, key, value, mixed_grad, normalizer = refs[:8]
    count = 3 * sequence if last else 0
    earlier = refs[8 : 8 + count]
    query_out, key_out, value_out = refs[8 + count : 11 + count]
    scratch = refs[11 + count :]
    if last:
        keep_out, send_out, vec_grad = scratch[:3]
        scratch = scratch[3:]
        total = scratch[2]
    key_flip, query_flip = scratch[:2]
    length = lengths[sequence]
    size = query.shape[0]
    key_flip[...] = flip(key[...]).astype(LOW)
    position = lax.broadcasted_iota(jnp.int32, (size, PAIR), 0)
    fill = jnp.where(position < length, 0.0, MASK_FILL)
    masks = head_masks()

    def one_pair(pair, carry):
        lanes = pl.ds(pl.multiple_of(pair * PAIR, PAIR), PAIR)
        keys = key[:, lanes]
        values = value[:, lanes]
        queries = query[:, lanes].astype(WIDE) * SCORE_SCALE
        grads = mixed_grad[:, lanes].astype(WIDE)
        norms = normalizer[0, pair]
        query_parts, key_part, value_part = [], 0.0, 0.0
        for head in range(2):
            own_query = only(queries, masks[head])
            marked_query, own_key = masked_pair(queries, keys, fill, head, masks)
            own_grad = only(grads, masks[head])
            scores = times_transpose(own_key, marked_query)
            prob = jnp.exp(scores - norms[head : head + 1, :])
            prob_grad = times_transpose(values, own_grad)
            row_term = jnp.sum(prob_grad * prob, axis=0, keepdims=True)
            score_low = (prob * (prob_grad - row_term)).astype(LOW)
            value_part = value_part + matmul(prob.astype(LOW), own_grad)
            key_part = key_part + matmul(score_low, own_query)
            start = pl.multiple_of(pair * PAIR + head * HEAD, HEAD)
            query_parts.append(matmul(key_flip[pl.ds(start, HEAD), :], score_low))
        query_flip[lanes, :] = jnp.concatenate(query_parts, axis=0) * SCORE_SCALE
        key_out[:, lanes] = key_part.astype(LOW)
        value_out[:, lanes] = value_part.astype(LOW)
        return carry

    lax.fori_loop(0, PAIRS, one_pair, 0)
    query_out[...] = query_flip[...].T.astype(LOW)
    if not last:
        return
    vec_grad[...] = jnp.zeros_like(vec_grad)
    token_flip = flip(tokens[...]).astype(LOW)
    for place, own in enumerate((query_out, key_out, value_out)):
        grads = [earlier[3 * i + place] for i in range(sequence)] + [own]
        sums = 0.0
        for i, grad in enumerate(grads):
            part = matmul(token_flip[:, i * size : (i + 1) * size], grad[...])
            total[...] = part if i == 0 else total[...] + part
            if place != 1:
                sums = sums + jnp.sum(grad[...].astype(WIDE), axis=0, keepdims=True)
        if place != 1:
            vec_grad[place // 2 : place // 2 + 1, :] = sums
        store_pieces(
            coords,
            keep_out,
            send_out,
            lambda r, c: total[r, c],
            keep_out.shape[-1],
            place=place,
        )


def input_kernel(layout, sequences, *refs):
    pieces = 2 * len(layout)
    coords, first_grad = refs[:2]
    grads = refs[2 : 2 + 3 * sequences]
    sources = refs[2 + 3 * sequences : 2 + 3 * sequences + pieces]
    grad_out, weights, sems = refs[2 + 3 * sequences + pieces :]
    load_now(
        load_pieces(
            coords, matrix_moves(range(3), weights.shape[4]), sources, layout, weights, sems
        )
    )
    size = grads[0].shape[0]
    for number in range(sequences):
        part = slice(number * size, (number + 1) * size)
        grad = first_grad[part, :]
        for place in range(3):
            grad = grad + times_transpose(
                grads[3 * number + place][...], flat(weights, place)[...]
            )
        grad_out[part, :] = grad.astype(grad_out.dtype)


def call(kernel, grid, inputs, outputs, scratch, flops, moved, aliases=None):
    return pl.pallas_call(
        kernel,
        grid=(grid,),
        in_specs=[spec for _, spec in inputs],
        out_specs=[spec for _, _, spec in outputs],
        out_shape=[jax.ShapeDtypeStruct(shape, kind) for shape, kind, _ in outputs],
        scratch_shapes=scratch,
        input_output_aliases=aliases or {},
        compiler_params=pltpu.CompilerParams(
            dimension_semantics=("arbitrary",), vmem_limit_bytes=VMEM_BYTES
        ),
        cost_estimate=pl.CostEstimate(flops=flops, bytes_accessed=moved, transcendentals=0),
    )(*[array for array, _ in inputs])


SCALARS = pl.BlockSpec(memory_space=pltpu.SMEM)
WHERE_IT_IS = pl.BlockSpec(memory_space=pl.ANY)


def tiles(rows, width):
    return pl.BlockSpec((rows, width), lambda i: (i, 0))


def block(number, *shape):
    return pl.BlockSpec(shape, lambda i: (number,) + (0,) * (len(shape) - 1))


def whole(*shape):
    return pl.BlockSpec(shape, lambda i: (0,) * len(shape))


def swap(value, axis, offset=1):
    size = lax.axis_size(axis)
    return lax.ppermute(value, axis, [(i, i ^ offset) for i in range(size)])


def swap_side(value):
    return swap(value, SIDE)


def swap_x(value):
    return swap(value, "ctx_hi")


def swap_y(value):
    return swap(value, "dp_lo")


def phase(*values):
    return lax.optimization_barrier(values)


def in_order(mine, theirs, here, axis):
    return jnp.where(
        here == 0,
        jnp.concatenate([mine, theirs], axis=axis),
        jnp.concatenate([theirs, mine], axis=axis),
    )


def pair_shards(shard, side):
    half = shard.shape[-1] // 2
    axis = shard.ndim - 1
    mine = lax.dynamic_slice_in_dim(shard, side * half, half, axis)
    theirs = lax.dynamic_slice_in_dim(shard, (1 - side) * half, half, axis)
    return in_order(mine, swap_side(theirs), side, shard.ndim - 2)


def swap_planes(value):
    return [swap(value, "dp_hi", offset) for offset in range(1, lax.axis_size("dp_hi"))]


def place_planes(value, others):
    here = lax.axis_index("dp_hi")
    parts = [part[None] for part in [value] + others]
    bit = 0
    while len(parts) > 1:
        flag = (here >> bit) & 1
        parts = [
            in_order(parts[i], parts[i + 1], flag, 0) for i in range(0, len(parts), 2)
        ]
        bit += 1
    return parts[0]


def wide_sum(*arrays):
    return functools.reduce(lambda a, b: a + b, [a.astype(WIDE) for a in arrays])


class Sum:
    def __init__(self, keep, send):
        self.keep, self.send = keep, send
        self.planes = 2 * keep.shape[2]

    def core(self):
        return swap_side(self.send)

    def part(self, run, squares):
        return wide_sum(self.keep[run, squares], self.other[run, squares])

    def first(self, got):
        self.other = got
        far = slice(2, 4)
        return [swap_y(self.part(0, far).astype(LOW)), swap_x(self.part(1, far).astype(LOW))]

    def middle(self, got):
        self.got = got
        return [wide_sum(self.part(run, 1), got[run][1]).astype(LOW) for run in range(2)]

    def second(self, got):
        return self.turn(self.middle(got))

    def turn(self, sent):
        return [swap_x(sent[0]), swap_y(sent[1])]

    def total(self, got):
        return jnp.concatenate(
            [
                wide_sum(self.part(run, 0), self.got[run][0], got[run]).astype(LOW)
                for run in range(2)
            ],
            axis=0,
        )


def sum_planes(total):
    here = lax.axis_index("dp_hi")
    planes = total.shape[0]
    return pick(total, here), [
        swap(pick(total, here ^ offset), "dp_hi", offset) for offset in range(1, planes)
    ]


def own_rows(total, side):
    rows = total.shape[-2] // 2
    axis = total.ndim - 2
    total = total.astype(LOW)
    mine = lax.dynamic_slice_in_dim(total, side * rows, rows, axis)
    theirs = lax.dynamic_slice_in_dim(total, (1 - side) * rows, rows, axis)
    return in_order(mine, swap_side(theirs), side, total.ndim - 1).astype(WIDE)


def pick(value, index, axis=0):
    return lax.dynamic_index_in_dim(value, index, axis, keepdims=False)


class Exchange:
    def __init__(self, blocks):
        self.x_here, self.side = lax.axis_index("ctx_hi"), lax.axis_index(SIDE)
        self.own = pick(blocks, self.x_here)
        self.sent = pick(blocks, 1 - self.x_here)

    def far(self):
        return [swap_x(self.sent), swap_side(pick(self.own, 1 - self.side))]

    def near(self, got):
        self.from_x, self.from_side = got
        return swap_side(pick(self.from_x, 1 - self.side))

    def place(self, got):
        own = pick(self.own, self.side)[None]
        far = pick(self.from_x, self.side)[None]
        return in_order(
            in_order(own, self.from_side[None], self.side, 0)[None],
            in_order(far, got[None], self.side, 0)[None],
            self.x_here,
            0,
        )


def by_sequence(value):
    return value.reshape((2, 2, -1) + value.shape[1:])


def sequences_of(blocks):
    parts = blocks.shape[0] * blocks.shape[1]
    own, here, width = blocks.shape[2:]
    blocks = blocks.reshape(parts, own, here, width)
    return blocks.transpose(1, 0, 2, 3).reshape(own * parts * here, width)


def by_position(value, sequences):
    width = value.shape[-1]
    blocks = value.reshape(sequences, 2, 2, -1, width)
    return blocks.transpose(1, 2, 0, 3, 4)


def positions_of(blocks):
    return blocks.reshape((-1,) + blocks.shape[3:])


def local(
    tokens,
    cotangent,
    lengths,
    attention_weights,
    inner_weights,
    outer_weights,
    inner_bias,
    vectors,
    attention_first,
    attention_second,
    inner_first,
    inner_second,
    outer_moment_first,
    outer_second,
    bias_first,
    bias_second,
    vector_first,
    vector_second,
):
    parts = lax.axis_size(CONTEXT)
    planes = lax.axis_size("dp_hi")
    chips = lax.axis_size(CHIPS)
    count = 2 * chips
    side = lax.axis_index(SIDE)
    coords = jnp.stack([side] + [lax.axis_index(axis) for axis in ("dp_lo", "ctx_hi", "dp_hi")])
    coords = coords.astype(jnp.int32)
    seq_count, local_len, width = tokens.shape
    hidden = inner_weights.shape[1]
    full_len = local_len * parts
    own_seqs = seq_count // parts
    rows = own_seqs * full_len
    att_rows, vec_cols, bias_cols = (
        attention_weights.shape[1],
        vectors.shape[1],
        inner_bias.shape[0],
    )
    half = width // 2
    tall = 16
    in_pieces = (2 * att_rows) % tall == 0
    if in_pieces:
        dims, squares = (planes, 2, 2), 4
        att_block, inner_block, outer_block = (
            2 * att_rows,
            2 * inner_weights.shape[0],
            2 * outer_weights.shape[0],
        )
    else:
        dims, squares = (1, 1, 1), 1
        att_block, inner_block, outer_block = width, width, hidden

    me = lax.axis_index(ALL)
    per_row = width // bias_cols
    small = jnp.zeros((tall, width), LOW)
    small = lax.dynamic_update_slice(small, vectors.astype(LOW), (0, me * vec_cols))
    small = lax.dynamic_update_slice(
        small, inner_bias.astype(LOW)[None], (8 + me // per_row, me % per_row * bias_cols)
    )
    att_pair = pair_shards(attention_weights.astype(LOW), side).reshape(8 * att_rows, half)
    if in_pieces:
        att_pair = jnp.concatenate([att_pair, small[:, :half], small[:, half:]], axis=0)
        att_pair, tokens, inner_own, outer_own = phase(
            att_pair, tokens, inner_weights, outer_weights
        )
        att_parts = swap_planes(att_pair)
    else:
        inner_own, outer_own = inner_weights, outer_weights
    inner_pair = pair_shards(inner_own.astype(LOW), side)
    outer_pair = pair_shards(outer_own.astype(LOW), side)
    strips = hidden // width
    pack_pair = jnp.concatenate(
        [
            inner_pair.reshape(-1, strips, half).transpose(1, 0, 2).reshape(-1, half),
            outer_pair,
        ],
        axis=0,
    )
    token_swap = Exchange(by_sequence(tokens))
    if in_pieces:
        middle = planes // 2
        token_far = token_swap.far()
        pack_x = swap_x(pack_pair)
        att_parts, pack_x = phase(att_parts, pack_x)
        att = place_planes(att_pair, att_parts)
        att_x, att_y = swap_x(att), swap_y(att)
        pack = in_order(pack_pair[None], pack_x[None], coords[2], 0)
        pack_z = [pack] + swap_planes(pack)
        pack_y = [swap_y(pack)]
        cot_low = cotangent.astype(LOW)
        att_x, att_y, token_far, pack_z[1], cot_low = phase(
            att_x, att_y, token_far, pack_z[1], cot_low
        )
        token_near = token_swap.near(token_far)
        att_mine = [att, att_x, att_y, swap_y(att_x[:middle]), swap_x(att_y[middle:])]
        early = max(2, planes - 1)
        att_mine, token_near, pack_z[1:early], pack_y[0], cot_low = phase(
            att_mine, token_near, pack_z[1:early], pack_y[0], cot_low
        )
        cot_swap = Exchange(by_sequence(cot_low))
        token_rows = sequences_of(token_swap.place(token_near))
        small = sum(
            jnp.sum(piece[:, 8 * att_rows :].astype(WIDE), axis=0) for piece in att_mine
        )
        small = small + swap_side(small.astype(LOW)).astype(WIDE)
        small = jnp.concatenate([small[:tall], small[tall:]], axis=1)
        att_all = att_mine + [swap_side(piece) for piece in att_mine]
        att_all, token_rows, small, cotangent_sent = phase(
            att_all, token_rows, small, cot_swap.sent
        )
        cot_swap.sent = cotangent_sent
        pack_y = pack_y + [swap_y(piece) for piece in pack_z[1:early]]
        cot_far = cot_swap.far()
        att_layout = [
            (0, 0, 0, planes),
            (0, 1, 0, planes),
            (1, 0, 0, planes),
            (1, 1, 0, middle),
            (1, 1, middle, planes - middle),
        ]
        pack_layout = [(y, offset) for y in range(2) for offset in range(planes)]
    else:
        small = lax.psum(small, ALL).astype(WIDE)
        att = lax.all_gather(att_pair, CHIPS, axis=0, tiled=False)
        pack = lax.all_gather(pack_pair, CHIPS, axis=0, tiled=False)

        def lay_out(value, matrices):
            value = value.reshape(chips, matrices, -1, half)
            return value.transpose(1, 0, 2, 3).reshape(1, -1, half)

        att = lay_out(att, 4)
        pack_rows = inner_pair.shape[0] * strips
        pack = jnp.concatenate(
            [lay_out(pack[:, :pack_rows], strips), lay_out(pack[:, pack_rows:], 1)], axis=1
        )
        att_all, pack_all = [[value, swap_side(value)] for value in (att, pack)]
        att_layout = pack_layout = [(0, 0, 0, 1)]
        token_rows = sequences_of(token_swap.place(token_swap.near(token_swap.far())))
        cot_swap = Exchange(by_sequence(cotangent.astype(LOW)))
        cot_rows = sequences_of(cot_swap.place(cot_swap.near(cot_swap.far())))
    vec = small[:8]
    bias = small[8 : 8 + strips].reshape(1, hidden)
    own_lengths = lax.dynamic_slice_in_dim(lengths, lax.axis_index(CONTEXT) * own_seqs, own_seqs)

    def in_place(pieces):
        return [(piece, WHERE_IT_IS) for piece in pieces]

    norm_shape = (own_seqs, PAIRS, 2, full_len)
    low_rows = (rows, width)
    seq_tile = tiles(full_len, width)
    vec_spec = whole(8, width)
    square = 2 * rows * width * width
    attend_flops = 8 * rows * full_len * width

    held = call(
        functools.partial(attend_kernel, att_layout),
        own_seqs,
        [
            (own_lengths, SCALARS),
            (coords, SCALARS),
            (token_rows, seq_tile),
            (vec, vec_spec),
        ]
        + in_place(att_all),
        [(low_rows, LOW, seq_tile)] * 4
        + [
            (low_rows, WIDE, seq_tile),
            (
                norm_shape,
                WIDE,
                pl.BlockSpec((1, PAIRS, 2, full_len), lambda i: (i, 0, 0, 0)),
            ),
        ],
        [
            pltpu.VMEM((4,) + dims + (att_block, width), LOW),
            pltpu.VMEM((width, full_len), LOW),
            pltpu.VMEM((width, full_len), WIDE),
            pltpu.SemaphoreType.DMA((4 * len(att_all),)),
        ],
        4 * square + 2 * attend_flops,
        20 * rows * width,
    )
    if in_pieces:
        held, pack_z, pack_y, cot_far = phase(held, pack_z, pack_y, cot_far)
        known = len(pack_y)
        pack_y = pack_y + [swap_y(piece) for piece in pack_z[known:]]
        pack_z_other = [swap_side(piece) for piece in pack_z]
        pack_y_other = [swap_side(piece) for piece in pack_y[:known]]
        cot_near = cot_swap.near(cot_far)
        pack_y, pack_z_other, pack_y_other, cot_near = phase(
            pack_y, pack_z_other, pack_y_other, cot_near
        )
        cot_rows = sequences_of(cot_swap.place(cot_near))
        pack_y_other = pack_y_other + [swap_side(piece) for piece in pack_y[known:]]
        pack_all = pack_z + pack_y + pack_z_other + pack_y_other
    query, key, value, mixed, first_sum, normalizer = held

    def grad_pieces(rows_here, columns, matrices=None):
        runs = 2 if in_pieces else 1
        lead = (runs, squares, dims[0] // runs) + ((matrices,) if matrices else ())
        shape = lead + (rows_here, columns)
        return [(shape, LOW, whole(*shape))] * 2

    tile = 256
    row_tile = tiles(tile, width)
    hidden_tile = tiles(tile, hidden)
    result, second_grad, hidden_low, outer_keep, outer_send, vec_ffn, bias_grad = phase(
        *call(
            functools.partial(ffn_kernel, pack_layout),
            rows // tile,
            [
                (coords, SCALARS),
                (first_sum, row_tile),
                (cot_rows, row_tile),
                (vec, vec_spec),
                (bias, whole(1, hidden)),
            ]
            + in_place(pack_all),
            [
                (low_rows, LOW, row_tile),
                (low_rows, WIDE, row_tile),
                ((rows, hidden), LOW, hidden_tile),
            ]
            + grad_pieces(outer_block, half)
            + [((8, width), WIDE, vec_spec), ((1, hidden), WIDE, whole(1, hidden))],
            [
                pltpu.VMEM((1,) + dims + (inner_block, hidden), LOW),
                pltpu.VMEM((1,) + dims + (outer_block, width), LOW),
                pltpu.VMEM((hidden, width), WIDE),
                pltpu.VMEM((tile, hidden), LOW),
                pltpu.VMEM((tile, hidden), WIDE),
                pltpu.SemaphoreType.DMA(((strips + 1) * len(pack_all),)),
            ],
            16 * square + 60 * rows * hidden,
            30 * rows * width,
        )
    )
    result_swap = Exchange(by_position(result, own_seqs))
    if in_pieces:
        outer_sum = Sum(outer_keep, outer_send)
        outer_got, second_grad = phase(outer_sum.core(), second_grad)
        outer_got = outer_sum.first(outer_got)
    result_far = result_swap.far()

    first_grad, mixed_grad, mid_keep, mid_send, vec_mid = call(
        functools.partial(back_kernel, pack_layout, att_layout),
        rows // tile,
        [
            (coords, SCALARS),
            (first_sum, row_tile),
            (second_grad, row_tile),
            (hidden_low, hidden_tile),
            (mixed, row_tile),
            (vec, vec_spec),
        ]
        + in_place(pack_all)
        + in_place(att_all),
        [(low_rows, WIDE, row_tile), (low_rows, LOW, row_tile)]
        + grad_pieces(inner_block, hidden // 2 + half)
        + [((8, width), WIDE, vec_spec)],
        [
            pltpu.VMEM((1,) + dims + (inner_block, hidden), LOW),
            pltpu.VMEM((1,) + dims + (att_block, width), LOW),
            pltpu.VMEM((width, hidden), WIDE),
            pltpu.VMEM((width, width), WIDE),
            pltpu.SemaphoreType.DMA((strips * len(pack_all) + len(att_all),)),
        ],
        10 * square,
        26 * rows * width,
    )
    if in_pieces:
        first_grad, mixed_grad, mid_keep, mid_send, vec_mid, outer_got, result_far = phase(
            first_grad, mixed_grad, mid_keep, mid_send, vec_mid, outer_got, result_far
        )
        mid_sum = Sum(mid_keep, mid_send)
        outer_got = outer_sum.second(outer_got)
        mid_got, mixed_grad = phase(mid_sum.core(), mixed_grad)
        mid_got = mid_sum.first(mid_got)
    result_near = result_swap.near(result_far)

    def input_of(number):
        seq_shape = (full_len, width)
        (grad,) = call(
            functools.partial(input_kernel, att_layout, 1),
            1,
            [(coords, SCALARS), (first_grad, block(number, full_len, width))]
            + [(value_, whole(*seq_shape)) for value_ in grads[3 * number : 3 * number + 3]]
            + in_place(att_all),
            [(seq_shape, LOW, whole(*seq_shape))],
            [
                pltpu.VMEM((3,) + dims + (att_block, width), LOW),
                pltpu.SemaphoreType.DMA((3 * len(att_all),)),
            ],
            3 * square // own_seqs,
            12 * rows * width // own_seqs,
        )
        return grad

    grads, input_swaps, input_far = [], [], []
    for number in range(own_seqs):
        last = number == own_seqs - 1
        own_rows_spec = block(number, full_len, width)
        seq_shape = (full_len, width)
        earlier = grads if last else []
        outputs = [(seq_shape, LOW, whole(*seq_shape))] * 3
        scratch = [pltpu.VMEM((width, full_len), LOW), pltpu.VMEM((width, full_len), WIDE)]
        if last:
            outputs = (
                outputs + grad_pieces(att_block, half, 3) + [((8, width), WIDE, vec_spec)]
            )
            scratch = scratch + [pltpu.VMEM((width, width), WIDE)]
        found = call(
            functools.partial(attend_back_kernel, number, last),
            1,
            [
                (own_lengths, SCALARS),
                (coords, SCALARS),
                (token_rows, whole(rows, width)),
                (query, own_rows_spec),
                (key, own_rows_spec),
                (value, own_rows_spec),
                (mixed_grad, own_rows_spec),
                (normalizer, block(number, 1, PAIRS, 2, full_len)),
            ]
            + [(value_, whole(*seq_shape)) for value_ in earlier],
            outputs,
            scratch,
            5 * attend_flops // own_seqs + (3 * square if last else 0),
            20 * rows * width // own_seqs,
        )
        if in_pieces:
            found, outer_got, mid_got, mixed_grad, result_near, input_far = phase(
                found, outer_got, mid_got, mixed_grad, result_near, input_far
            )
            if number == 0:
                outer_got, mid_got = outer_sum.total(outer_got), mid_sum.middle(mid_got)
        grads = grads + list(found[:3])
        if not last:
            swap_first = Exchange(by_position(input_of(number), 1))
            swap_first.sent, swap_first.own, mixed_grad = phase(
                swap_first.sent, swap_first.own, mixed_grad
            )
            if in_pieces and number == 0:
                mid_got, outer_got, mixed_grad = phase(mid_got, outer_got, mixed_grad)
                mid_got = mid_sum.turn(mid_got)
            input_swaps.append(swap_first)
            input_far.append(swap_first.far())
    att_keep, att_send, vec_att = found[3:]

    small_grad = jnp.concatenate(
        [
            vec_ffn + vec_mid + vec_att,
            bias_grad.reshape(-1, width),
            jnp.zeros((tall - 8 - strips, width), WIDE),
        ],
        axis=0,
    )
    if in_pieces:
        att_sum = Sum(att_keep, att_send)
        strip = inner_block
        merged = jnp.concatenate(
            [mid_sum.total(mid_got)]
            + [
                outer_got[:, start : start + strip]
                for start in range(0, outer_block, strip)
            ],
            axis=2,
        )
        att_got, small_got, grads, merged, first_grad = phase(
            att_sum.core(), swap_side(small_grad), grads, merged, first_grad
        )
        small_grad = small_grad + small_got
        att_got = att_sum.first(att_got)
        merged, merged_got = sum_planes(merged)
        small_got = swap_y(small_grad)

    input_grad = input_of(own_seqs - 1)
    if in_pieces:
        input_grad, att_got, small_got = phase(input_grad, att_got, small_got)
    input_swaps.append(Exchange(by_position(input_grad, 1)))
    if in_pieces:
        att_got = att_sum.second(att_got)
        small_grad = small_grad + small_got
        small_got = swap_x(small_grad)
        swap_last = input_swaps[-1]
        (
            att_got,
            small_got,
            merged_got,
            swap_last.sent,
            swap_last.own,
            result_near,
            input_far,
        ) = phase(
            att_got,
            small_got,
            merged_got,
            swap_last.sent,
            swap_last.own,
            result_near,
            input_far,
        )
        input_far.append(swap_last.far())
        small_grad = small_grad + small_got
        att_own, att_got = sum_planes(att_sum.total(att_got))
        att_got[0], small_grad, merged, merged_got, input_far = phase(
            att_got[0], small_grad, merged, merged_got, input_far
        )
        small_got = swap_planes(small_grad)
        merged = wide_sum(merged, *merged_got)
        inner_total = own_rows(merged[:, : hidden // 2], side)
        project_total = own_rows(merged[:, hidden // 2 : hidden // 2 + half], side)
        outer_total = own_rows(
            jnp.concatenate(
                [
                    merged[:, start : start + half]
                    for start in range(hidden // 2 + half, merged.shape[1], half)
                ],
                axis=0,
            ),
            side,
        )
        att_total = own_rows(wide_sum(att_own, *att_got), side)
        input_near = [one.near(far) for one, far in zip(input_swaps, input_far)]
        small_total = wide_sum(small_grad, *small_got)
    else:
        input_far.append(input_swaps[-1].far())
        input_near = [one.near(far) for one, far in zip(input_swaps, input_far)]

        def scatter(value):
            value = value.reshape((-1,) + value.shape[-2:])
            matrices, length, columns = value.shape
            value = value.reshape(matrices, chips, length // chips, columns)
            value = lax.psum_scatter(
                value.transpose(1, 0, 2, 3), CHIPS, scatter_dimension=0, tiled=False
            )
            return own_rows(value, side)

        att_total = scatter(att_keep + swap_side(att_send))
        outer_total = scatter(outer_keep + swap_side(outer_send))[0]
        mid = mid_keep + swap_side(mid_send)
        inner_total = scatter(mid[..., : hidden // 2])[0]
        project_total = scatter(mid[..., hidden // 2 :])[0]
        small_total = lax.psum(small_grad, ALL)
    output_tokens = positions_of(result_swap.place(result_near))
    input_grad = jnp.concatenate(
        [one.place(near) for one, near in zip(input_swaps, input_near)], axis=2
    )
    input_grad = positions_of(input_grad).astype(WIDE)
    attention_total = jnp.concatenate([att_total, project_total[None]], axis=0)
    vector_total = lax.dynamic_slice(small_total, (0, me * vec_cols), (8, vec_cols))
    bias_total = lax.dynamic_slice(
        small_total, (8 + me // per_row, me % per_row * bias_cols), (1, bias_cols)
    ).reshape(bias_cols)

    attention_square, attention_new = adam_step(
        attention_weights,
        attention_total,
        attention_first,
        attention_second,
        MATRIX_LEARN_RATE,
        WEIGHT_DECAY,
    )
    inner_square, inner_new = adam_step(
        inner_weights, inner_total, inner_first, inner_second, MATRIX_LEARN_RATE, WEIGHT_DECAY
    )
    outer_square, outer_new = adam_step(
        outer_weights,
        outer_total,
        outer_moment_first,
        outer_second,
        MATRIX_LEARN_RATE,
        WEIGHT_DECAY,
    )
    bias_square, bias_new = adam_step(
        inner_bias, bias_total, bias_first, bias_second, VECTOR_RATE, 0.0
    )
    vector_square, vector_new = adam_step(
        vectors, vector_total, vector_first, vector_second, VECTOR_RATE, 0.0
    )
    return (
        output_tokens,
        input_grad,
        attention_total,
        attention_square,
        attention_new,
        inner_total,
        inner_square,
        inner_new,
        outer_total,
        outer_square,
        outer_new,
        bias_total,
        bias_square,
        bias_new,
        vector_total,
        vector_square,
        vector_new,
    )


def solution(mesh):
    split = Mesh(
        np.asarray(mesh.devices).reshape(
            mesh.shape["dp"] // 2, 2, mesh.shape["context"] // 2, 2
        ),
        ALL,
    )
    dp = ("dp_hi", "dp_lo")
    rows3 = P(dp, CONTEXT, None)
    mid3 = P(None, ALL, None)
    row2 = P(ALL, None)
    col2 = P(None, ALL)
    one = P(ALL)
    return jax.shard_map(
        local,
        mesh=split,
        in_specs=(rows3, rows3, P(dp), mid3, row2, row2, one, col2)
        + (mid3, mid3, row2, row2, row2, row2, one, one, col2, col2),
        out_specs=(rows3, rows3)
        + (mid3,) * 3
        + (row2,) * 6
        + (one,) * 3
        + (col2,) * 3,
        check_vma=False,
    )
```

```python
import functools

import jax
import jax.numpy as jnp
import numpy as np
from jax import lax
from jax.experimental import pallas as pl
from jax.experimental.pallas import tpu as pltpu
from jax.sharding import Mesh, PartitionSpec as P

HEADS = 12
HEAD = 64
PAIR = 2 * HEAD
PAIRS = HEADS // 2
STEP = 10

NORM_EPS = 1e-12
BETA_ONE = 0.9
BETA_TWO = 0.999
ADAM_EPS = 1e-06
MATRIX_LEARN_RATE = 0.05
VECTOR_RATE = 0.5
WEIGHT_DECAY = 0.01
MASK_FILL = -1e30
SCORE_SCALE = HEAD ** (-0.5)
ROOT_HALF = 0.5**0.5
DENSITY = 0.3989422804014327

CHIPS = ("dp_hi", "dp_lo", "ctx_hi")
SIDE = "ctx_lo"
ALL = CHIPS + (SIDE,)
CONTEXT = ("ctx_hi", "ctx_lo")
LOW = jnp.bfloat16
WIDE = jnp.float32
VMEM_BYTES = 60 * 1024 * 1024


def adam_step(weight, gradient, moment_one, moment_two, step_rate, decay_rate):
    first_new = BETA_ONE * moment_one + (1.0 - BETA_ONE) * gradient
    second_new = BETA_TWO * moment_two + (1.0 - BETA_TWO) * gradient * gradient
    first_hat = first_new / (1.0 - BETA_ONE**STEP)
    second_hat = second_new / (1.0 - BETA_TWO**STEP)
    updated = weight - step_rate * (
        first_hat / (jnp.sqrt(second_hat) + ADAM_EPS) + decay_rate * weight
    )
    return (second_new, updated)


def matmul(left, right):
    return jnp.dot(left, right, preferred_element_type=WIDE)


def contract_rows(left, right):
    return lax.dot_general(left, right, (((0,), (0,)), ((), ())), preferred_element_type=WIDE)


def times_transpose(left, right):
    return lax.dot_general(left, right, (((1,), (1,)), ((), ())), preferred_element_type=WIDE)


def flip(value):
    return value.astype(WIDE).T


def norm_stats(value):
    centered = value - jnp.mean(value, axis=-1, keepdims=True)
    variance = jnp.mean(centered * centered, axis=-1, keepdims=True)
    scale = lax.rsqrt(variance + NORM_EPS)
    return centered * scale, scale


def norm_back(grad, gain, unit, scale):
    scaled = grad * gain
    return scale * (
        scaled
        - jnp.mean(scaled, axis=-1, keepdims=True)
        - unit * jnp.mean(scaled * unit, axis=-1, keepdims=True)
    )


def load_pieces(coords, moves, pieces, layout, target, sems, first=0):
    rows, half = target.shape[4], target.shape[5] // 2
    side, y_here, x_here, z_here = [coords[i] for i in range(4)]
    single = target.shape[2] == 1
    wide = pieces[0].shape[-1]
    copies = []
    for row, place, column in moves:
        for number, source in enumerate(pieces):
            which, order = divmod(number, len(layout))
            start = pl.multiple_of((side if which == 0 else 1 - side) * half + column, wide)
            columns = pl.ds(start, wide)
            y_at = 0 if single else (1 - y_here if layout[order][0] else y_here)
            if len(layout[order]) == 2:
                z_at = jnp.bitwise_xor(z_here, layout[order][1])
                goal = target.at[place, z_at, y_at, :, :, columns]
            else:
                _, x_other, plane, planes = layout[order]
                x_at = 0 if single else (1 - x_here if x_other else x_here)
                goal = target.at[place, pl.ds(plane, planes), y_at, x_at, :, columns]
            copies.append(
                pltpu.make_async_copy(
                    source.at[:, pl.ds(row, rows), :], goal, sems.at[first + len(copies)]
                )
            )
    return copies


def inner_moves(target, wide):
    rows, half = target.shape[4], target.shape[5] // 2
    return [(number * rows, 0, number * wide) for number in range(half // wide)]


def outer_moves(target, inner, wide):
    return [(inner.shape[4] * (inner.shape[5] // 2 // wide), 0, 0)]


def matrix_moves(picks, rows):
    return [(pick * rows, place, 0) for place, pick in enumerate(picks)]


def load_now(copies):
    for copy in copies:
        copy.start()
    for copy in copies:
        copy.wait()


def flat(target, place=0):
    _, planes, high, wide, rows, width = target.shape
    return target.at[place].reshape(planes * high * wide * rows, width)


def store_pieces(coords, keep_out, send_out, read, half, column=0, place=None):
    side, y_here, x_here = coords[0], coords[1], coords[2]
    runs, squares, planes = keep_out.shape[:3]
    rows = keep_out.shape[-2]
    into = pl.ds(column, half)
    for out, own_side in ((keep_out, side), (send_out, 1 - side)):
        columns = pl.ds(pl.multiple_of(own_side * half, half), half)
        for run in range(runs):
            for square in range(squares):
                high, low = square // 2, square % 2
                y_other, x_other = (high, low) if run == 0 else (low, high)
                for number in range(planes):
                    block = run * planes + number
                    if squares > 1:
                        y_at = 1 - y_here if y_other else y_here
                        x_at = 1 - x_here if x_other else x_here
                        block = (block * 2 + y_at) * 2 + x_at
                    start = pl.multiple_of(block * rows, rows)
                    part = read(pl.ds(start, rows), columns).astype(LOW)
                    if place is None:
                        out[run, square, number, :, into] = part
                    else:
                        out[run, square, number, place, :, into] = part


def head_masks():
    lane = lax.broadcasted_iota(jnp.int32, (1, PAIR), 1)
    return [lane < HEAD, lane >= HEAD]


def only(value, mask):
    return jnp.where(mask, value, 0.0).astype(LOW)


def masked_pair(queries, keys, fill, head, masks):
    lane = lax.broadcasted_iota(jnp.int32, (1, PAIR), 1)
    marker = (lane == (1 - head) * HEAD).astype(WIDE)
    left = jnp.where(masks[head], queries, marker).astype(LOW)
    right = jnp.where(masks[head], keys.astype(WIDE), fill).astype(LOW)
    return left, right


def attend_kernel(layout, *refs):
    pieces = 2 * len(layout)
    lengths, coords, tokens, vec = refs[:4]
    sources = refs[4 : 4 + pieces]
    query_out, key_out, value_out, mixed_out, sum_out, norm_out = refs[4 + pieces : 10 + pieces]
    weights, value_flip, mixed_flip, sems = refs[10 + pieces :]
    step = pl.program_id(0)
    copies = load_pieces(
        coords, matrix_moves(range(4), weights.shape[4]), sources, layout, weights, sems
    )

    @pl.when(step == 0)
    def _():
        for copy in copies:
            copy.start()

    def need(place):
        @pl.when(step == 0)
        def _():
            for copy in copies[place * pieces : (place + 1) * pieces]:
                copy.wait()

    length = lengths[step]
    rows = tokens[...]
    need(0)
    query_out[...] = (matmul(rows, flat(weights, 0)[...]) + vec[0:1, :]).astype(LOW)
    need(1)
    key_out[...] = matmul(rows, flat(weights, 1)[...]).astype(LOW)
    need(2)
    value_low = (matmul(rows, flat(weights, 2)[...]) + vec[1:2, :]).astype(LOW)
    value_out[...] = value_low
    value_flip[...] = flip(value_low).astype(LOW)
    size = tokens.shape[0]
    position = lax.broadcasted_iota(jnp.int32, (size, PAIR), 0)
    fill = jnp.where(position < length, 0.0, MASK_FILL)
    masks = head_masks()

    def one_pair(pair, carry):
        lanes = pl.ds(pl.multiple_of(pair * PAIR, PAIR), PAIR)
        keys = key_out[:, lanes]
        queries = query_out[:, lanes].astype(WIDE) * SCORE_SCALE
        mixed, norms = [], []
        for head in range(2):
            own_query, own_key = masked_pair(queries, keys, fill, head, masks)
            scores = times_transpose(own_key, own_query)
            peak = jnp.max(scores, axis=0, keepdims=True)
            exponent = jnp.exp(scores - peak)
            total = jnp.sum(exponent, axis=0, keepdims=True)
            prob = (exponent * (1.0 / total)).astype(LOW)
            start = pl.multiple_of(pair * PAIR + head * HEAD, HEAD)
            mixed.append(matmul(value_flip[pl.ds(start, HEAD), :], prob))
            norms.append(peak + jnp.log(total))
        mixed_flip[lanes, :] = jnp.concatenate(mixed, axis=0)
        norm_out[0, pair] = jnp.concatenate(norms, axis=0)
        return carry

    lax.fori_loop(0, PAIRS, one_pair, 0)
    need(3)
    mixed_low = mixed_flip[...].T.astype(LOW)
    mixed_out[...] = mixed_low
    sum_out[...] = rows.astype(WIDE) + matmul(mixed_low, flat(weights, 3)[...]) + vec[2:3, :]


def ffn_kernel(layout, *refs):
    pieces = 2 * len(layout)
    coords, first_sum, cotangent, vec, bias = refs[:5]
    sources = refs[5 : 5 + pieces]
    result_out, second_out, hidden_out, keep_out, send_out, vec_grad, bias_grad = refs[
        5 + pieces : 12 + pieces
    ]
    inner_at, outer_at, total, activated, slope, sems = refs[12 + pieces :]
    step = pl.program_id(0)

    wide = sources[0].shape[-1]
    copies = load_pieces(coords, inner_moves(inner_at, wide), sources, layout, inner_at, sems)
    outer_copies = load_pieces(
        coords,
        outer_moves(outer_at, inner_at, wide),
        sources,
        layout,
        outer_at,
        sems,
        len(copies),
    )

    @pl.when(step == 0)
    def _():
        for copy in copies + outer_copies:
            copy.start()
        vec_grad[...] = jnp.zeros_like(vec_grad)
        bias_grad[...] = jnp.zeros_like(bias_grad)
        total[...] = jnp.zeros_like(total)
        for copy in copies + outer_copies:
            copy.wait()

    inner, outer = flat(inner_at), flat(outer_at)
    unit, _ = norm_stats(first_sum[...])
    normed = unit * vec[4:5, :] + vec[5:6, :]
    normed_low = normed.astype(LOW)
    width, hidden = inner.shape
    second = normed + vec[3:4, :]
    for start in range(0, hidden, width):
        part = slice(start, start + width)
        pre = matmul(normed_low, inner[:, part]) + bias[:, part]
        cdf = 0.5 * (1.0 + lax.erf(pre * ROOT_HALF))
        active = (pre * cdf).astype(LOW)
        activated[:, part] = active
        slope[:, part] = cdf + pre * (DENSITY * jnp.exp(-0.5 * pre * pre))
        second = second + matmul(active, outer[part, :])
    unit_two, scale_two = norm_stats(second)
    result_out[...] = (unit_two * vec[6:7, :] + vec[7:8, :]).astype(LOW)
    grad = cotangent[...].astype(WIDE)
    second_grad = norm_back(grad, vec[6:7, :], unit_two, scale_two)
    second_out[...] = second_grad
    grad_low = second_grad.astype(LOW)
    vec_grad[3:4, :] += jnp.sum(grad_low.astype(WIDE), axis=0, keepdims=True)
    vec_grad[6:7, :] += jnp.sum(grad * unit_two, axis=0, keepdims=True)
    vec_grad[7:8, :] += jnp.sum(grad, axis=0, keepdims=True)
    for start in range(0, hidden, width):
        part = slice(start, start + width)
        back = times_transpose(grad_low, outer[part, :])
        hidden_low = (back * slope[:, part]).astype(LOW)
        hidden_out[:, part] = hidden_low
        bias_grad[:, part] += jnp.sum(hidden_low.astype(WIDE), axis=0, keepdims=True)
        total[part, :] += contract_rows(activated[:, part], grad_low)

    @pl.when(step == pl.num_programs(0) - 1)
    def _():
        store_pieces(
            coords, keep_out, send_out, lambda r, c: total[r, c], keep_out.shape[-1]
        )


def back_kernel(pack_layout, att_layout, *refs):
    pack_pieces, att_pieces = 2 * len(pack_layout), 2 * len(att_layout)
    coords, first_sum, second_grad, hidden_low, mixed, vec = refs[:6]
    pack_from = refs[6 : 6 + pack_pieces]
    att_from = refs[6 + pack_pieces : 6 + pack_pieces + att_pieces]
    first_out, mixed_grad_out, keep_out, send_out, vec_grad = refs[
        6 + pack_pieces + att_pieces : 11 + pack_pieces + att_pieces
    ]
    inner_at, project_at, total, project_total, sems = refs[11 + pack_pieces + att_pieces :]
    step = pl.program_id(0)

    @pl.when(step == 0)
    def _():
        copies = load_pieces(
            coords,
            inner_moves(inner_at, pack_from[0].shape[-1]),
            pack_from,
            pack_layout,
            inner_at,
            sems,
        )
        copies = copies + load_pieces(
            coords,
            matrix_moves((3,), project_at.shape[4]),
            att_from,
            att_layout,
            project_at,
            sems,
            len(copies),
        )
        for copy in copies:
            copy.start()
        vec_grad[...] = jnp.zeros_like(vec_grad)
        total[...] = jnp.zeros_like(total)
        project_total[...] = jnp.zeros_like(project_total)
        for copy in copies:
            copy.wait()

    inner = flat(inner_at)
    unit, scale = norm_stats(first_sum[...])
    normed_flip = flip(unit * vec[4:5, :] + vec[5:6, :]).astype(LOW)
    width, hidden = total.shape
    grad = second_grad[...]
    for start in range(0, hidden, width):
        part = slice(start, start + width)
        grad = grad + times_transpose(hidden_low[:, part], inner[:, part])
        total[:, part] += matmul(normed_flip, hidden_low[:, part])
    first_grad = norm_back(grad, vec[4:5, :], unit, scale)
    first_out[...] = first_grad
    branch = first_grad.astype(LOW)
    vec_grad[2:3, :] += jnp.sum(branch.astype(WIDE), axis=0, keepdims=True)
    vec_grad[4:5, :] += jnp.sum(grad * unit, axis=0, keepdims=True)
    vec_grad[5:6, :] += jnp.sum(grad, axis=0, keepdims=True)
    mixed_grad_out[...] = times_transpose(branch, flat(project_at)[...]).astype(LOW)
    project_total[...] += contract_rows(mixed[...], branch)

    @pl.when(step == pl.num_programs(0) - 1)
    def _():
        store_pieces(coords, keep_out, send_out, lambda r, c: total[r, c], hidden // 2)
        store_pieces(
            coords,
            keep_out,
            send_out,
            lambda r, c: project_total[r, c],
            width // 2,
            hidden // 2,
        )


def attend_back_kernel(sequence, last, *refs):
    lengths, coords, tokens, query, key, value, mixed_grad, normalizer = refs[:8]
    count = 3 * sequence if last else 0
    earlier = refs[8 : 8 + count]
    query_out, key_out, value_out = refs[8 + count : 11 + count]
    scratch = refs[11 + count :]
    if last:
        keep_out, send_out, vec_grad = scratch[:3]
        scratch = scratch[3:]
        total = scratch[2]
    key_flip, query_flip = scratch[:2]
    length = lengths[sequence]
    size = query.shape[0]
    key_flip[...] = flip(key[...]).astype(LOW)
    position = lax.broadcasted_iota(jnp.int32, (size, PAIR), 0)
    fill = jnp.where(position < length, 0.0, MASK_FILL)
    masks = head_masks()

    def one_pair(pair, carry):
        lanes = pl.ds(pl.multiple_of(pair * PAIR, PAIR), PAIR)
        keys = key[:, lanes]
        values = value[:, lanes]
        queries = query[:, lanes].astype(WIDE) * SCORE_SCALE
        grads = mixed_grad[:, lanes].astype(WIDE)
        norms = normalizer[0, pair]
        query_parts, key_part, value_part = [], 0.0, 0.0
        for head in range(2):
            own_query = only(queries, masks[head])
            marked_query, own_key = masked_pair(queries, keys, fill, head, masks)
            own_grad = only(grads, masks[head])
            scores = times_transpose(own_key, marked_query)
            prob = jnp.exp(scores - norms[head : head + 1, :])
            prob_grad = times_transpose(values, own_grad)
            row_term = jnp.sum(prob_grad * prob, axis=0, keepdims=True)
            score_low = (prob * (prob_grad - row_term)).astype(LOW)
            value_part = value_part + matmul(prob.astype(LOW), own_grad)
            key_part = key_part + matmul(score_low, own_query)
            start = pl.multiple_of(pair * PAIR + head * HEAD, HEAD)
            query_parts.append(matmul(key_flip[pl.ds(start, HEAD), :], score_low))
        query_flip[lanes, :] = jnp.concatenate(query_parts, axis=0) * SCORE_SCALE
        key_out[:, lanes] = key_part.astype(LOW)
        value_out[:, lanes] = value_part.astype(LOW)
        return carry

    lax.fori_loop(0, PAIRS, one_pair, 0)
    query_out[...] = query_flip[...].T.astype(LOW)
    if not last:
        return
    vec_grad[...] = jnp.zeros_like(vec_grad)
    token_flip = flip(tokens[...]).astype(LOW)
    for place, own in enumerate((query_out, key_out, value_out)):
        grads = [earlier[3 * i + place] for i in range(sequence)] + [own]
        sums = 0.0
        for i, grad in enumerate(grads):
            part = matmul(token_flip[:, i * size : (i + 1) * size], grad[...])
            total[...] = part if i == 0 else total[...] + part
            if place != 1:
                sums = sums + jnp.sum(grad[...].astype(WIDE), axis=0, keepdims=True)
        if place != 1:
            vec_grad[place // 2 : place // 2 + 1, :] = sums
        store_pieces(
            coords,
            keep_out,
            send_out,
            lambda r, c: total[r, c],
            keep_out.shape[-1],
            place=place,
        )


def input_kernel(layout, sequences, *refs):
    pieces = 2 * len(layout)
    coords, first_grad = refs[:2]
    grads = refs[2 : 2 + 3 * sequences]
    sources = refs[2 + 3 * sequences : 2 + 3 * sequences + pieces]
    grad_out, weights, sems = refs[2 + 3 * sequences + pieces :]
    load_now(
        load_pieces(
            coords, matrix_moves(range(3), weights.shape[4]), sources, layout, weights, sems
        )
    )
    size = grads[0].shape[0]
    for number in range(sequences):
        part = slice(number * size, (number + 1) * size)
        grad = first_grad[part, :]
        for place in range(3):
            grad = grad + times_transpose(
                grads[3 * number + place][...], flat(weights, place)[...]
            )
        grad_out[part, :] = grad.astype(grad_out.dtype)


def call(kernel, grid, inputs, outputs, scratch, flops, moved, aliases=None):
    return pl.pallas_call(
        kernel,
        grid=(grid,),
        in_specs=[spec for _, spec in inputs],
        out_specs=[spec for _, _, spec in outputs],
        out_shape=[jax.ShapeDtypeStruct(shape, kind) for shape, kind, _ in outputs],
        scratch_shapes=scratch,
        input_output_aliases=aliases or {},
        compiler_params=pltpu.CompilerParams(
            dimension_semantics=("arbitrary",), vmem_limit_bytes=VMEM_BYTES
        ),
        cost_estimate=pl.CostEstimate(flops=flops, bytes_accessed=moved, transcendentals=0),
    )(*[array for array, _ in inputs])


SCALARS = pl.BlockSpec(memory_space=pltpu.SMEM)
WHERE_IT_IS = pl.BlockSpec(memory_space=pl.ANY)


def tiles(rows, width):
    return pl.BlockSpec((rows, width), lambda i: (i, 0))


def block(number, *shape):
    return pl.BlockSpec(shape, lambda i: (number,) + (0,) * (len(shape) - 1))


def whole(*shape):
    return pl.BlockSpec(shape, lambda i: (0,) * len(shape))


def swap(value, axis, offset=1):
    size = lax.axis_size(axis)
    return lax.ppermute(value, axis, [(i, i ^ offset) for i in range(size)])


def swap_side(value):
    return swap(value, SIDE)


def swap_x(value):
    return swap(value, "ctx_hi")


def swap_y(value):
    return swap(value, "dp_lo")


def phase(*values):
    return lax.optimization_barrier(values)


def in_order(mine, theirs, here, axis):
    return jnp.where(
        here == 0,
        jnp.concatenate([mine, theirs], axis=axis),
        jnp.concatenate([theirs, mine], axis=axis),
    )


def pair_shards(shard, side):
    half = shard.shape[-1] // 2
    axis = shard.ndim - 1
    mine = lax.dynamic_slice_in_dim(shard, side * half, half, axis)
    theirs = lax.dynamic_slice_in_dim(shard, (1 - side) * half, half, axis)
    return in_order(mine, swap_side(theirs), side, shard.ndim - 2)


def swap_planes(value):
    return [swap(value, "dp_hi", offset) for offset in range(1, lax.axis_size("dp_hi"))]


def place_planes(value, others):
    here = lax.axis_index("dp_hi")
    parts = [part[None] for part in [value] + others]
    bit = 0
    while len(parts) > 1:
        flag = (here >> bit) & 1
        parts = [
            in_order(parts[i], parts[i + 1], flag, 0) for i in range(0, len(parts), 2)
        ]
        bit += 1
    return parts[0]


def wide_sum(*arrays):
    return functools.reduce(lambda a, b: a + b, [a.astype(WIDE) for a in arrays])


class Sum:
    def __init__(self, keep, send):
        self.keep, self.send = keep, send
        self.planes = 2 * keep.shape[2]

    def core(self):
        return swap_side(self.send)

    def part(self, run, squares):
        return wide_sum(self.keep[run, squares], self.other[run, squares])

    def first(self, got):
        self.other = got
        far = slice(2, 4)
        return [swap_y(self.part(0, far).astype(LOW)), swap_x(self.part(1, far).astype(LOW))]

    def middle(self, got):
        self.got = got
        return [wide_sum(self.part(run, 1), got[run][1]).astype(LOW) for run in range(2)]

    def second(self, got):
        return self.turn(self.middle(got))

    def turn(self, sent):
        return [swap_x(sent[0]), swap_y(sent[1])]

    def total(self, got):
        return jnp.concatenate(
            [
                wide_sum(self.part(run, 0), self.got[run][0], got[run]).astype(LOW)
                for run in range(2)
            ],
            axis=0,
        )


def sum_planes(total):
    here = lax.axis_index("dp_hi")
    planes = total.shape[0]
    return pick(total, here), [
        swap(pick(total, here ^ offset), "dp_hi", offset) for offset in range(1, planes)
    ]


def own_rows(total, side):
    rows = total.shape[-2] // 2
    axis = total.ndim - 2
    total = total.astype(LOW)
    mine = lax.dynamic_slice_in_dim(total, side * rows, rows, axis)
    theirs = lax.dynamic_slice_in_dim(total, (1 - side) * rows, rows, axis)
    return in_order(mine, swap_side(theirs), side, total.ndim - 1).astype(WIDE)


def pick(value, index, axis=0):
    return lax.dynamic_index_in_dim(value, index, axis, keepdims=False)


class Exchange:
    def __init__(self, blocks):
        self.x_here, self.side = lax.axis_index("ctx_hi"), lax.axis_index(SIDE)
        self.own = pick(blocks, self.x_here)
        self.sent = pick(blocks, 1 - self.x_here)

    def far(self):
        return [swap_x(self.sent), swap_side(pick(self.own, 1 - self.side))]

    def near(self, got):
        self.from_x, self.from_side = got
        return swap_side(pick(self.from_x, 1 - self.side))

    def place(self, got):
        own = pick(self.own, self.side)[None]
        far = pick(self.from_x, self.side)[None]
        return in_order(
            in_order(own, self.from_side[None], self.side, 0)[None],
            in_order(far, got[None], self.side, 0)[None],
            self.x_here,
            0,
        )


def by_sequence(value):
    return value.reshape((2, 2, -1) + value.shape[1:])


def sequences_of(blocks):
    parts = blocks.shape[0] * blocks.shape[1]
    own, here, width = blocks.shape[2:]
    blocks = blocks.reshape(parts, own, here, width)
    return blocks.transpose(1, 0, 2, 3).reshape(own * parts * here, width)


def by_position(value, sequences):
    width = value.shape[-1]
    blocks = value.reshape(sequences, 2, 2, -1, width)
    return blocks.transpose(1, 2, 0, 3, 4)


def positions_of(blocks):
    return blocks.reshape((-1,) + blocks.shape[3:])


def local(
    tokens,
    cotangent,
    lengths,
    attention_weights,
    inner_weights,
    outer_weights,
    inner_bias,
    vectors,
    attention_first,
    attention_second,
    inner_first,
    inner_second,
    outer_moment_first,
    outer_second,
    bias_first,
    bias_second,
    vector_first,
    vector_second,
):
    parts = lax.axis_size(CONTEXT)
    planes = lax.axis_size("dp_hi")
    chips = lax.axis_size(CHIPS)
    count = 2 * chips
    side = lax.axis_index(SIDE)
    coords = jnp.stack([side] + [lax.axis_index(axis) for axis in ("dp_lo", "ctx_hi", "dp_hi")])
    coords = coords.astype(jnp.int32)
    seq_count, local_len, width = tokens.shape
    hidden = inner_weights.shape[1]
    full_len = local_len * parts
    own_seqs = seq_count // parts
    rows = own_seqs * full_len
    att_rows, vec_cols, bias_cols = (
        attention_weights.shape[1],
        vectors.shape[1],
        inner_bias.shape[0],
    )
    half = width // 2
    tall = 16
    in_pieces = (2 * att_rows) % tall == 0
    if in_pieces:
        dims, squares = (planes, 2, 2), 4
        att_block, inner_block, outer_block = (
            2 * att_rows,
            2 * inner_weights.shape[0],
            2 * outer_weights.shape[0],
        )
    else:
        dims, squares = (1, 1, 1), 1
        att_block, inner_block, outer_block = width, width, hidden

    me = lax.axis_index(ALL)
    per_row = width // bias_cols
    small = jnp.zeros((tall, width), LOW)
    small = lax.dynamic_update_slice(small, vectors.astype(LOW), (0, me * vec_cols))
    small = lax.dynamic_update_slice(
        small, inner_bias.astype(LOW)[None], (8 + me // per_row, me % per_row * bias_cols)
    )
    att_pair = pair_shards(attention_weights.astype(LOW), side).reshape(8 * att_rows, half)
    if in_pieces:
        att_pair = jnp.concatenate([att_pair, small[:, :half], small[:, half:]], axis=0)
        att_pair, tokens, inner_own, outer_own = phase(
            att_pair, tokens, inner_weights, outer_weights
        )
        att_parts = swap_planes(att_pair)
    else:
        inner_own, outer_own = inner_weights, outer_weights
    inner_pair = pair_shards(inner_own.astype(LOW), side)
    outer_pair = pair_shards(outer_own.astype(LOW), side)
    strips = hidden // width
    pack_pair = jnp.concatenate(
        [
            inner_pair.reshape(-1, strips, half).transpose(1, 0, 2).reshape(-1, half),
            outer_pair,
        ],
        axis=0,
    )
    token_swap = Exchange(by_sequence(tokens))
    if in_pieces:
        middle = planes // 2
        token_far = token_swap.far()
        pack_x = swap_x(pack_pair)
        att_parts, pack_x = phase(att_parts, pack_x)
        att = place_planes(att_pair, att_parts)
        att_x, att_y = swap_x(att), swap_y(att)
        pack = in_order(pack_pair[None], pack_x[None], coords[2], 0)
        pack_z = [pack] + swap_planes(pack)
        pack_y = [swap_y(pack)]
        cot_low = cotangent.astype(LOW)
        att_x, att_y, token_far, pack_z[1], cot_low = phase(
            att_x, att_y, token_far, pack_z[1], cot_low
        )
        token_near = token_swap.near(token_far)
        att_mine = [att, att_x, att_y, swap_y(att_x[:middle]), swap_x(att_y[middle:])]
        early = max(2, planes - 1)
        att_mine, token_near, pack_z[1:early], pack_y[0], cot_low = phase(
            att_mine, token_near, pack_z[1:early], pack_y[0], cot_low
        )
        cot_swap = Exchange(by_sequence(cot_low))
        token_rows = sequences_of(token_swap.place(token_near))
        small = sum(
            jnp.sum(piece[:, 8 * att_rows :].astype(WIDE), axis=0) for piece in att_mine
        )
        small = small + swap_side(small.astype(LOW)).astype(WIDE)
        small = jnp.concatenate([small[:tall], small[tall:]], axis=1)
        att_all = att_mine + [swap_side(piece) for piece in att_mine]
        att_all, token_rows, small, cotangent_sent = phase(
            att_all, token_rows, small, cot_swap.sent
        )
        cot_swap.sent = cotangent_sent
        pack_y = pack_y + [swap_y(piece) for piece in pack_z[1:early]]
        cot_far = cot_swap.far()
        att_layout = [
            (0, 0, 0, planes),
            (0, 1, 0, planes),
            (1, 0, 0, planes),
            (1, 1, 0, middle),
            (1, 1, middle, planes - middle),
        ]
        pack_layout = [(y, offset) for y in range(2) for offset in range(planes)]
    else:
        small = lax.psum(small, ALL).astype(WIDE)
        att = lax.all_gather(att_pair, CHIPS, axis=0, tiled=False)
        pack = lax.all_gather(pack_pair, CHIPS, axis=0, tiled=False)

        def lay_out(value, matrices):
            value = value.reshape(chips, matrices, -1, half)
            return value.transpose(1, 0, 2, 3).reshape(1, -1, half)

        att = lay_out(att, 4)
        pack_rows = inner_pair.shape[0] * strips
        pack = jnp.concatenate(
            [lay_out(pack[:, :pack_rows], strips), lay_out(pack[:, pack_rows:], 1)], axis=1
        )
        att_all, pack_all = [[value, swap_side(value)] for value in (att, pack)]
        att_layout = pack_layout = [(0, 0, 0, 1)]
        token_rows = sequences_of(token_swap.place(token_swap.near(token_swap.far())))
        cot_swap = Exchange(by_sequence(cotangent.astype(LOW)))
        cot_rows = sequences_of(cot_swap.place(cot_swap.near(cot_swap.far())))
    vec = small[:8]
    bias = small[8 : 8 + strips].reshape(1, hidden)
    own_lengths = lax.dynamic_slice_in_dim(lengths, lax.axis_index(CONTEXT) * own_seqs, own_seqs)

    def in_place(pieces):
        return [(piece, WHERE_IT_IS) for piece in pieces]

    norm_shape = (own_seqs, PAIRS, 2, full_len)
    low_rows = (rows, width)
    seq_tile = tiles(full_len, width)
    vec_spec = whole(8, width)
    square = 2 * rows * width * width
    attend_flops = 8 * rows * full_len * width

    held = call(
        functools.partial(attend_kernel, att_layout),
        own_seqs,
        [
            (own_lengths, SCALARS),
            (coords, SCALARS),
            (token_rows, seq_tile),
            (vec, vec_spec),
        ]
        + in_place(att_all),
        [(low_rows, LOW, seq_tile)] * 4
        + [
            (low_rows, WIDE, seq_tile),
            (
                norm_shape,
                WIDE,
                pl.BlockSpec((1, PAIRS, 2, full_len), lambda i: (i, 0, 0, 0)),
            ),
        ],
        [
            pltpu.VMEM((4,) + dims + (att_block, width), LOW),
            pltpu.VMEM((width, full_len), LOW),
            pltpu.VMEM((width, full_len), WIDE),
            pltpu.SemaphoreType.DMA((4 * len(att_all),)),
        ],
        4 * square + 2 * attend_flops,
        20 * rows * width,
    )
    if in_pieces:
        held, pack_z, pack_y, cot_far = phase(held, pack_z, pack_y, cot_far)
        known = len(pack_y)
        pack_y = pack_y + [swap_y(piece) for piece in pack_z[known:]]
        pack_z_other = [swap_side(piece) for piece in pack_z]
        pack_y_other = [swap_side(piece) for piece in pack_y[:known]]
        cot_near = cot_swap.near(cot_far)
        cot_rows = sequences_of(cot_swap.place(cot_near))
        pack_y, pack_z_other, pack_y_other, cot_rows = phase(
            pack_y, pack_z_other, pack_y_other, cot_rows
        )
        pack_y_other = pack_y_other + [swap_side(piece) for piece in pack_y[known:]]
        pack_all = pack_z + pack_y + pack_z_other + pack_y_other
    query, key, value, mixed, first_sum, normalizer = held

    def grad_pieces(rows_here, columns, matrices=None):
        runs = 2 if in_pieces else 1
        lead = (runs, squares, dims[0] // runs) + ((matrices,) if matrices else ())
        shape = lead + (rows_here, columns)
        return [(shape, LOW, whole(*shape))] * 2

    tile = 256
    row_tile = tiles(tile, width)
    hidden_tile = tiles(tile, hidden)
    result, second_grad, hidden_low, outer_keep, outer_send, vec_ffn, bias_grad = phase(
        *call(
            functools.partial(ffn_kernel, pack_layout),
            rows // tile,
            [
                (coords, SCALARS),
                (first_sum, row_tile),
                (cot_rows, row_tile),
                (vec, vec_spec),
                (bias, whole(1, hidden)),
            ]
            + in_place(pack_all),
            [
                (low_rows, LOW, row_tile),
                (low_rows, WIDE, row_tile),
                ((rows, hidden), LOW, hidden_tile),
            ]
            + grad_pieces(outer_block, half)
            + [((8, width), WIDE, vec_spec), ((1, hidden), WIDE, whole(1, hidden))],
            [
                pltpu.VMEM((1,) + dims + (inner_block, hidden), LOW),
                pltpu.VMEM((1,) + dims + (outer_block, width), LOW),
                pltpu.VMEM((hidden, width), WIDE),
                pltpu.VMEM((tile, hidden), LOW),
                pltpu.VMEM((tile, hidden), WIDE),
                pltpu.SemaphoreType.DMA(((strips + 1) * len(pack_all),)),
            ],
            16 * square + 60 * rows * hidden,
            30 * rows * width,
        )
    )
    result_swap = Exchange(by_position(result, own_seqs))
    if in_pieces:
        outer_sum = Sum(outer_keep, outer_send)
        outer_got, second_grad = phase(outer_sum.core(), second_grad)
        outer_got = outer_sum.first(outer_got)
    result_far = result_swap.far()

    first_grad, mixed_grad, mid_keep, mid_send, vec_mid = call(
        functools.partial(back_kernel, pack_layout, att_layout),
        rows // tile,
        [
            (coords, SCALARS),
            (first_sum, row_tile),
            (second_grad, row_tile),
            (hidden_low, hidden_tile),
            (mixed, row_tile),
            (vec, vec_spec),
        ]
        + in_place(pack_all)
        + in_place(att_all),
        [(low_rows, WIDE, row_tile), (low_rows, LOW, row_tile)]
        + grad_pieces(inner_block, hidden // 2 + half)
        + [((8, width), WIDE, vec_spec)],
        [
            pltpu.VMEM((1,) + dims + (inner_block, hidden), LOW),
            pltpu.VMEM((1,) + dims + (att_block, width), LOW),
            pltpu.VMEM((width, hidden), WIDE),
            pltpu.VMEM((width, width), WIDE),
            pltpu.SemaphoreType.DMA((strips * len(pack_all) + len(att_all),)),
        ],
        10 * square,
        26 * rows * width,
    )
    if in_pieces:
        first_grad, mixed_grad, mid_keep, mid_send, vec_mid, outer_got, result_far = phase(
            first_grad, mixed_grad, mid_keep, mid_send, vec_mid, outer_got, result_far
        )
        mid_sum = Sum(mid_keep, mid_send)
        outer_got = outer_sum.second(outer_got)
        mid_got, mixed_grad = phase(mid_sum.core(), mixed_grad)
        mid_got = mid_sum.first(mid_got)
    result_near = result_swap.near(result_far)

    def input_of(number):
        seq_shape = (full_len, width)
        (grad,) = call(
            functools.partial(input_kernel, att_layout, 1),
            1,
            [(coords, SCALARS), (first_grad, block(number, full_len, width))]
            + [(value_, whole(*seq_shape)) for value_ in grads[3 * number : 3 * number + 3]]
            + in_place(att_all),
            [(seq_shape, LOW, whole(*seq_shape))],
            [
                pltpu.VMEM((3,) + dims + (att_block, width), LOW),
                pltpu.SemaphoreType.DMA((3 * len(att_all),)),
            ],
            3 * square // own_seqs,
            12 * rows * width // own_seqs,
        )
        return grad

    grads, input_swaps, input_far = [], [], []
    for number in range(own_seqs):
        last = number == own_seqs - 1
        own_rows_spec = block(number, full_len, width)
        seq_shape = (full_len, width)
        earlier = grads if last else []
        outputs = [(seq_shape, LOW, whole(*seq_shape))] * 3
        scratch = [pltpu.VMEM((width, full_len), LOW), pltpu.VMEM((width, full_len), WIDE)]
        if last:
            outputs = (
                outputs + grad_pieces(att_block, half, 3) + [((8, width), WIDE, vec_spec)]
            )
            scratch = scratch + [pltpu.VMEM((width, width), WIDE)]
        found = call(
            functools.partial(attend_back_kernel, number, last),
            1,
            [
                (own_lengths, SCALARS),
                (coords, SCALARS),
                (token_rows, whole(rows, width)),
                (query, own_rows_spec),
                (key, own_rows_spec),
                (value, own_rows_spec),
                (mixed_grad, own_rows_spec),
                (normalizer, block(number, 1, PAIRS, 2, full_len)),
            ]
            + [(value_, whole(*seq_shape)) for value_ in earlier],
            outputs,
            scratch,
            5 * attend_flops // own_seqs + (3 * square if last else 0),
            20 * rows * width // own_seqs,
        )
        if in_pieces:
            found, outer_got, mid_got, mixed_grad, result_near, input_far = phase(
                found, outer_got, mid_got, mixed_grad, result_near, input_far
            )
            if number == 0:
                outer_got, mid_got = outer_sum.total(outer_got), mid_sum.middle(mid_got)
        grads = grads + list(found[:3])
        if not last:
            swap_first = Exchange(by_position(input_of(number), 1))
            swap_first.sent, swap_first.own, mixed_grad = phase(
                swap_first.sent, swap_first.own, mixed_grad
            )
            if in_pieces and number == 0:
                mid_got, outer_got, mixed_grad = phase(mid_got, outer_got, mixed_grad)
                mid_got = mid_sum.turn(mid_got)
            input_swaps.append(swap_first)
            input_far.append(swap_first.far())
    att_keep, att_send, vec_att = found[3:]

    small_grad = jnp.concatenate(
        [
            vec_ffn + vec_mid + vec_att,
            bias_grad.reshape(-1, width),
            jnp.zeros((tall - 8 - strips, width), WIDE),
        ],
        axis=0,
    )
    if in_pieces:
        att_sum = Sum(att_keep, att_send)
        strip = inner_block
        merged = jnp.concatenate(
            [mid_sum.total(mid_got)]
            + [
                outer_got[:, start : start + strip]
                for start in range(0, outer_block, strip)
            ],
            axis=2,
        )
        att_got, small_got, grads, merged, first_grad = phase(
            att_sum.core(), swap_side(small_grad), grads, merged, first_grad
        )
        small_grad = small_grad + small_got
        att_got = att_sum.first(att_got)
        merged, merged_got = sum_planes(merged)
        small_got = swap_y(small_grad)

    input_grad = input_of(own_seqs - 1)
    if in_pieces:
        input_grad, att_got, small_got = phase(input_grad, att_got, small_got)
    input_swaps.append(Exchange(by_position(input_grad, 1)))
    if in_pieces:
        att_got = att_sum.second(att_got)
        small_grad = small_grad + small_got
        small_got = swap_x(small_grad)
        swap_last = input_swaps[-1]
        (
            att_got,
            small_got,
            merged_got,
            swap_last.sent,
            swap_last.own,
            result_near,
            input_far,
        ) = phase(
            att_got,
            small_got,
            merged_got,
            swap_last.sent,
            swap_last.own,
            result_near,
            input_far,
        )
        input_far.append(swap_last.far())
        small_grad = small_grad + small_got
        att_own, att_got = sum_planes(att_sum.total(att_got))
        att_got[0], small_grad, merged, merged_got, input_far = phase(
            att_got[0], small_grad, merged, merged_got, input_far
        )
        small_got = swap_planes(small_grad)
        merged = wide_sum(merged, *merged_got)
        inner_total = own_rows(merged[:, : hidden // 2], side)
        project_total = own_rows(merged[:, hidden // 2 : hidden // 2 + half], side)
        outer_total = own_rows(
            jnp.concatenate(
                [
                    merged[:, start : start + half]
                    for start in range(hidden // 2 + half, merged.shape[1], half)
                ],
                axis=0,
            ),
            side,
        )
        att_total = own_rows(wide_sum(att_own, *att_got), side)
        input_near = [one.near(far) for one, far in zip(input_swaps, input_far)]
        small_total = wide_sum(small_grad, *small_got)
    else:
        input_far.append(input_swaps[-1].far())
        input_near = [one.near(far) for one, far in zip(input_swaps, input_far)]

        def scatter(value):
            value = value.reshape((-1,) + value.shape[-2:])
            matrices, length, columns = value.shape
            value = value.reshape(matrices, chips, length // chips, columns)
            value = lax.psum_scatter(
                value.transpose(1, 0, 2, 3), CHIPS, scatter_dimension=0, tiled=False
            )
            return own_rows(value, side)

        att_total = scatter(att_keep + swap_side(att_send))
        outer_total = scatter(outer_keep + swap_side(outer_send))[0]
        mid = mid_keep + swap_side(mid_send)
        inner_total = scatter(mid[..., : hidden // 2])[0]
        project_total = scatter(mid[..., hidden // 2 :])[0]
        small_total = lax.psum(small_grad, ALL)
    output_tokens = positions_of(result_swap.place(result_near))
    input_grad = jnp.concatenate(
        [one.place(near) for one, near in zip(input_swaps, input_near)], axis=2
    )
    input_grad = positions_of(input_grad).astype(WIDE)
    attention_total = jnp.concatenate([att_total, project_total[None]], axis=0)
    vector_total = lax.dynamic_slice(small_total, (0, me * vec_cols), (8, vec_cols))
    bias_total = lax.dynamic_slice(
        small_total, (8 + me // per_row, me % per_row * bias_cols), (1, bias_cols)
    ).reshape(bias_cols)

    attention_square, attention_new = adam_step(
        attention_weights,
        attention_total,
        attention_first,
        attention_second,
        MATRIX_LEARN_RATE,
        WEIGHT_DECAY,
    )
    inner_square, inner_new = adam_step(
        inner_weights, inner_total, inner_first, inner_second, MATRIX_LEARN_RATE, WEIGHT_DECAY
    )
    outer_square, outer_new = adam_step(
        outer_weights,
        outer_total,
        outer_moment_first,
        outer_second,
        MATRIX_LEARN_RATE,
        WEIGHT_DECAY,
    )
    bias_square, bias_new = adam_step(
        inner_bias, bias_total, bias_first, bias_second, VECTOR_RATE, 0.0
    )
    vector_square, vector_new = adam_step(
        vectors, vector_total, vector_first, vector_second, VECTOR_RATE, 0.0
    )
    return (
        output_tokens,
        input_grad,
        attention_total,
        attention_square,
        attention_new,
        inner_total,
        inner_square,
        inner_new,
        outer_total,
        outer_square,
        outer_new,
        bias_total,
        bias_square,
        bias_new,
        vector_total,
        vector_square,
        vector_new,
    )


def solution(mesh):
    split = Mesh(
        np.asarray(mesh.devices).reshape(
            mesh.shape["dp"] // 2, 2, mesh.shape["context"] // 2, 2
        ),
        ALL,
    )
    dp = ("dp_hi", "dp_lo")
    rows3 = P(dp, CONTEXT, None)
    mid3 = P(None, ALL, None)
    row2 = P(ALL, None)
    col2 = P(None, ALL)
    one = P(ALL)
    return jax.shard_map(
        local,
        mesh=split,
        in_specs=(rows3, rows3, P(dp), mid3, row2, row2, one, col2)
        + (mid3, mid3, row2, row2, row2, row2, one, one, col2, col2),
        out_specs=(rows3, rows3)
        + (mid3,) * 3
        + (row2,) * 6
        + (one,) * 3
        + (col2,) * 3,
        check_vma=False,
    )
```
